32 devices in a mesh: fsdp: 2 (over z_hi), seq: 8 (over y, x, core), tp: 2 (over z_lo).
Axes of the slice: x: 2, y: 2, z: 4 (z_hi: 2, z_lo: 2; z = z_hi * 2 + z_lo), core: 2. Of those that a mesh axis runs over, the one named last changes fastest.
Arguments:
- tokens: bfloat16 [4096, 8192], P(('fsdp', 'seq', 'tp')), may hold values from -6 to 6
- proj_mean: bfloat16 [8192, 4096], P(('fsdp', 'seq'), 'tp'), may hold values from -0.0625 to 0.0625
- proj_devs: bfloat16 [4, 8192, 4096], P(None, ('fsdp', 'seq'), 'tp'), may hold values from -0.0625 to 0.0625
- bc_mean: bfloat16 [8192, 2, 1024], P(('fsdp', 'seq'), None, 'tp'), may hold values from -0.0625 to 0.0625
- bc_devs: bfloat16 [4, 8192, 2, 1024], P(None, ('fsdp', 'seq'), None, 'tp'), may hold values from -0.0625 to 0.0625
- swag_coef: float32 [4], replicated, may hold values from -4 to 4
- dt_weight: bfloat16 [8192, 64], P(('fsdp', 'seq'), 'tp'), may hold values from -0.0625 to 0.0625
- dt_bias: float32 [64], P('tp'), may hold values from -12 to -2, as said below
- decay_rate: float32 [64], P('tp'), may hold values from 0 to 16, as said below
- skip_gain: float32 [64], P('tp'), may hold values from 0.5 to 1.5
- conv_proj: float32 [4, 4096], P(None, 'tp'), may hold values from -3 to 3
- conv_bc: float32 [4, 2, 1024], P(None, None, 'tp'), may hold values from -1.5 to 1.5
Outputs:
- ssm_out: bfloat16 [4096, 4096], P(('fsdp', 'seq'), 'tp')
The draws below stay inside these ranges and needn't reach their ends.
Inputs may be any that keep to these rules, and one draw needn't show every extreme that they name: `dt_bias`: every bias is the inverse softplus of a positive step size. `decay_rate`: every rate is positive.
All inputs are finite; a program needn't handle non-finite values.
Results may differ from the reference program's by a relative error of at most 0.0059.
Values may be sent and summed in bfloat16 or wider, within the bound.
No kernel may reach another device: no remote copies, remote signals or barrier semaphores. Data moves between devices by JAX's collectives and lax.ppermute only.
A program may use at most 128 MiB of HBM per device.

```python
import math
import jax
import jax.numpy as jnp
from jax import lax

D = 8192
HEADS = 64
P_SIZE = 64
N = 128
GROUPS = 8
DEVS = 4
CONV = 4
SPAN = 128
LENGTH = 2048
DOCS = 2
TOKENS = 4096


def head_law(key):
    base = jax.random.fold_in(key, 11)
    pick_key, reach_key, keep_key, step_key, rate_key = jax.random.split(base, 5)
    slow_share = 0.5
    reach = jnp.exp(jax.random.uniform(reach_key, (HEADS,), jnp.float32, math.log(2.0), math.log(4.0)))
    keep = jnp.exp(jax.random.uniform(keep_key, (HEADS,), jnp.float32, math.log(0.3), math.log(1.2)))
    fast_step = jnp.exp(jax.random.uniform(step_key, (HEADS,), jnp.float32, math.log(0.01), math.log(0.1)))
    fast_rate = jnp.exp(jax.random.uniform(rate_key, (HEADS,), jnp.float32, math.log(1.0), math.log(16.0)))
    is_slow = jax.random.uniform(pick_key, (HEADS,), jnp.float32) < slow_share
    step_level = jnp.where(is_slow, reach / LENGTH, fast_step)
    rate_level = jnp.where(is_slow, keep / reach, fast_rate)
    return (step_level, rate_level)


def draw_decay_rate(key, part):
    step_level, rate_level = head_law(key)
    return rate_level


def draw_dt_bias(key, part):
    step_level, rate_level = head_law(key)
    return jnp.log(jnp.expm1(step_level))


def level_of(key, dims, shards, least, high):
    loudness = 1.0
    for axis_at, shards_of in shards:
        steps = jax.random.uniform(jax.random.fold_in(jax.random.fold_in(key, 6), axis_at), (shards_of,), jnp.float32, least / len(shards), high / len(shards))
        loudness = loudness * jnp.repeat(jnp.exp(steps), dims[axis_at] // shards_of).reshape((-1,) + (1,) * (len(dims) - 1 - axis_at))
    return loudness


def bell_draw(rng, dims, deviation, bound, pieces=(), dtype=jnp.bfloat16):
    factor_of = level_of(rng, dims, pieces, -0.22, 0.18) if pieces else 1.0
    entries = jax.random.normal(rng, dims, jnp.float32) * deviation * factor_of
    return jnp.minimum(jnp.maximum(entries, -bound), bound).astype(dtype)


def setup_inputs(seed: int = 0) -> dict:
    seeds = jax.random.split(jax.random.key(seed), 13)
    tokens = bell_draw(seeds[0], (TOKENS, D), 1.0, 6.0, ((0, 32),))
    proj_mean = bell_draw(seeds[1], (D, HEADS * P_SIZE), D ** -0.5, 0.0625, ((0, 16), (1, 2)))
    proj_devs = bell_draw(seeds[2], (DEVS, D, HEADS * P_SIZE), D ** -0.5, 0.0625, ((1, 16), (2, 2)))
    bc_mean = bell_draw(seeds[3], (D, 2, GROUPS * N), D ** -0.5, 0.0625, ((0, 16), (2, 2)))
    bc_devs = bell_draw(seeds[4], (DEVS, D, 2, GROUPS * N), D ** -0.5, 0.0625, ((1, 16), (3, 2)))
    swag_coef = bell_draw(seeds[5], (DEVS,), 1.0, 4.0, (), jnp.float32)
    dt_weight = bell_draw(seeds[6], (D, HEADS), D ** -0.5, 0.0625, ((0, 16), (1, 2)))
    dt_bias = draw_dt_bias(jax.random.fold_in(seeds[12], 71), 0)
    decay_rate = draw_decay_rate(jax.random.fold_in(seeds[12], 71), 0)
    skip_gain = jnp.clip(0.5 + 1.0 * jax.random.uniform(seeds[9], (HEADS,), jnp.float32) ** level_of(seeds[9], (HEADS,), ((0, 2),), -0.2, 0.2), 0.5, 1.5)
    conv_proj = bell_draw(seeds[10], (CONV, HEADS * P_SIZE), CONV ** -0.5, 3.0, ((1, 2),), jnp.float32)
    conv_bc = bell_draw(seeds[11], (CONV, 2, GROUPS * N), 0.25, 1.5, ((2, 2),), jnp.float32)
    return {"tokens": tokens, "proj_mean": proj_mean, "proj_devs": proj_devs, "bc_mean": bc_mean, "bc_devs": bc_devs, "swag_coef": swag_coef, "dt_weight": dt_weight, "dt_bias": dt_bias, "decay_rate": decay_rate, "skip_gain": skip_gain, "conv_proj": conv_proj, "conv_bc": conv_bc}


def sampled(mean_part, dev_part, swag_coef):
    factor = (2.0 * (DEVS - 1)) ** -0.5
    accum = mean_part.astype(jnp.float32)
    for member in range(DEVS):
        accum = accum + factor * swag_coef[member] * dev_part[member].astype(jnp.float32)
    return accum.astype(jnp.bfloat16)


def rounded(source):
    narrow = lax.optimization_barrier(source.astype(jnp.bfloat16))
    return narrow.astype(jnp.float32)


def causal_conv(projected, kernel):
    padded = jnp.concatenate([jnp.zeros((CONV - 1, projected.shape[1]), jnp.float32), projected.astype(jnp.float32)], axis=0)
    conv_sum = kernel[0] * padded[0:LENGTH]
    for offset in range(1, CONV):
        conv_sum = conv_sum + kernel[offset] * padded[offset:offset + LENGTH]
    return jax.nn.silu(conv_sum).astype(jnp.bfloat16)


def reference(tokens, proj_mean, proj_devs, bc_mean, bc_devs, swag_coef, dt_weight, dt_bias, decay_rate, skip_gain, conv_proj, conv_bc):
    weight_x = sampled(proj_mean, proj_devs, swag_coef)
    weight_bc = sampled(bc_mean, bc_devs, swag_coef).reshape(D, 2 * GROUPS * N)
    proj_x = jnp.dot(tokens, weight_x, preferred_element_type=jnp.float32).astype(jnp.bfloat16)
    proj_bc = jnp.dot(tokens, weight_bc, preferred_element_type=jnp.float32).astype(jnp.bfloat16)
    logits = jnp.dot(tokens, dt_weight, preferred_element_type=jnp.float32)
    kernel_bc = conv_bc.reshape(CONV, 2 * GROUPS * N)
    per_group = HEADS // GROUPS
    blocks = LENGTH // SPAN
    causal_mask = jnp.tril(jnp.ones((SPAN, SPAN), bool))

    def document(items):
        doc_x, doc_bc, doc_logits = items
        values = causal_conv(doc_x, conv_proj).astype(jnp.float32).reshape(blocks, SPAN, HEADS, P_SIZE)
        both_parts = causal_conv(doc_bc, kernel_bc).astype(jnp.float32).reshape(LENGTH, 2, GROUPS, N)
        keys_h = jnp.repeat(both_parts[:, 0], per_group, axis=1).reshape(blocks, SPAN, HEADS, N)
        reads_h = jnp.repeat(both_parts[:, 1], per_group, axis=1).reshape(blocks, SPAN, HEADS, N)
        steps_b = jax.nn.softplus(doc_logits + dt_bias).reshape(blocks, SPAN, HEADS)
        cum_log = jnp.cumsum(-steps_b * decay_rate, axis=1)
        scores = jnp.einsum("bqhn,bshn->bhqs", reads_h, keys_h)
        later_cum = jnp.transpose(cum_log, (0, 2, 1))
        cum_gaps = later_cum[:, :, :, None] - later_cum[:, :, None, :]
        decays = jnp.where(causal_mask, jnp.exp(jnp.minimum(cum_gaps, 0.0)), 0.0)
        weights = rounded(scores * decays * jnp.transpose(steps_b, (0, 2, 1))[:, :, None, :])
        inner_part = jnp.einsum("bhqs,bshp->bqhp", weights, values)
        last_cum = cum_log[:, SPAN - 1:, :]
        scaled = rounded(values * (jnp.exp(last_cum - cum_log) * steps_b)[..., None])
        states = jnp.einsum("bshn,bshp->bhnp", keys_h, scaled)
        block_decay = jnp.exp(last_cum[:, 0, :])

        def advance(carried, pair):
            return pair[0][:, None, None] * carried + pair[1], carried

        unused, entering = lax.scan(advance, jnp.zeros((HEADS, N, P_SIZE), jnp.float32), (block_decay, states))
        entering_bf = rounded(entering)
        outer_part = jnp.exp(cum_log)[..., None] * jnp.einsum("bqhn,bhnp->bqhp", reads_h, entering_bf)
        result = inner_part + outer_part + skip_gain[:, None] * values
        return result.reshape(LENGTH, HEADS * P_SIZE).astype(jnp.bfloat16)

    outputs = lax.map(document, (proj_x.reshape(DOCS, LENGTH, HEADS * P_SIZE), proj_bc.reshape(DOCS, LENGTH, 2 * GROUPS * N), logits.reshape(DOCS, LENGTH, HEADS)))
    return outputs.reshape(TOKENS, HEADS * P_SIZE)
```

```python
import jax
import jax.numpy as jnp
from jax import lax
from jax.sharding import Mesh, PartitionSpec as P

P_SIZE = 64
N = 128
CONV = 4
SPAN = 128
LANES = 128
SEQ = ("chip", "core")


def swapped(part, axis):
    return lax.ppermute(part, axis, [(0, 1), (1, 0)])


def sampled(mean_part, dev_part, swag_coef):
    factor = (2.0 * (dev_part.shape[0] - 1)) ** (-0.5)
    accum = mean_part.astype(jnp.float32)
    for member in range(dev_part.shape[0]):
        accum = accum + factor * swag_coef[member] * dev_part[member].astype(jnp.float32)
    return accum.astype(jnp.bfloat16)


def split_two(wide):
    high = lax.reduce_precision(wide, 8, 7)
    return high.astype(jnp.bfloat16), (wide - high).astype(jnp.bfloat16)


def narrowed(part, width, heads_here):
    body_part = part[:, :width].astype(jnp.bfloat16)
    if part.shape[1] == width:
        return body_part
    high, low = split_two(part[:, width : width + heads_here])
    fill = jnp.zeros((part.shape[0], part.shape[1] - width - 2 * heads_here), jnp.bfloat16)
    return jnp.concatenate([body_part, high, low, fill], axis=1)


def widened(part, width, heads_here):
    wide = part.astype(jnp.float32)
    if part.shape[1] == width:
        return wide
    logits = wide[:, width : width + heads_here] + wide[:, width + heads_here : width + 2 * heads_here]
    fill = jnp.zeros((part.shape[0], part.shape[1] - width - heads_here), jnp.float32)
    return jnp.concatenate([wide[:, :width], logits, fill], axis=1)


def gathered_rows(part):
    if lax.axis_size("tp") == 2:
        return jnp.concatenate([part, swapped(part, "tp")], axis=1)
    return lax.all_gather(part, "tp", axis=1, tiled=True)


def in_order(rows):
    if lax.axis_size("tp") != 2:
        return rows
    half = rows.shape[0] // 2
    flipped = jnp.concatenate([rows[half:], rows[:half]], axis=0)
    return jnp.where(lax.axis_index("tp") == 0, rows, flipped)


def prefix_decays(decay):
    place = lax.axis_index(SEQ)
    count = lax.axis_size(SEQ)
    before = jnp.ones_like(decay)
    total = decay
    levels = []
    by = 1
    while by < count:
        other = lax.ppermute(total, SEQ, [(i, i ^ by) for i in range(count)])
        upper = (place & by) != 0
        levels.append((upper, before, total, other))
        before = jnp.where(upper, other * before, before)
        total = total * other
        by *= 2
    return levels


def prefix_states(state, levels, part):
    count = lax.axis_size(SEQ)
    before = jnp.zeros_like(state)
    total = state
    by = 1
    for upper, before_decay, total_decay, other_decay in levels:
        other = lax.ppermute(
            total.astype(jnp.bfloat16), SEQ, [(i, i ^ by) for i in range(count)]
        ).astype(jnp.float32)
        before_decay, total_decay, other_decay = (
            d[part][:, None, None] for d in (before_decay, total_decay, other_decay)
        )
        before = before + jnp.where(upper, before_decay, 0.0) * other
        total = jnp.where(upper, total_decay * other + total, other_decay * total + other)
        by *= 2
    return before


def body(
    tokens,
    proj_mean,
    proj_devs,
    bc_mean,
    bc_devs,
    swag_coef,
    dt_weight,
    dt_bias,
    decay_rate,
    skip_gain,
    conv_proj,
    conv_bc,
):
    heads_here = decay_rate.shape[0]
    groups_here = bc_mean.shape[2] // N
    per_group = heads_here // groups_here
    width_x = proj_mean.shape[1]
    width_bc = 2 * bc_mean.shape[2]
    rows_k = proj_mean.shape[0]
    f_at, c_at = lax.axis_index("fsdp"), lax.axis_index("core")

    shares = tokens.reshape(tokens.shape[0], 2, -1, 2, rows_k)
    pick = lambda a, at, axis: lax.dynamic_index_in_dim(a, at, axis, keepdims=False)
    half_kept, half_sent = pick(shares, f_at, 1), pick(shares, 1 - f_at, 1)

    def rows_of(half):
        kept = pick(half, c_at, 2).reshape(1, tokens.shape[0], -1)
        sent = pick(half, 1 - c_at, 2).reshape(1, tokens.shape[0], -1)
        both = jnp.concatenate([kept, swapped(sent, "core")], axis=0)
        both = gathered_rows(both)
        return both.reshape(-1, both.shape[2])

    half_got = swapped(half_sent, "fsdp")
    rows_own = rows_of(half_kept)
    rows_other = rows_of(half_got)
    tok_count = rows_own.shape[0] // 2

    def projected(weight, width):
        whole = lax.all_gather(weight, "chip", axis=0, tiled=True)
        part_other = jnp.dot(rows_other, whole, preferred_element_type=jnp.float32)
        part_own = jnp.dot(rows_own, whole, preferred_element_type=jnp.float32)
        sent = jnp.concatenate([part_other[tok_count:], part_own[tok_count:]], axis=0)
        got = widened(swapped(narrowed(sent, width, heads_here), "core"), width, heads_here)
        back = part_other[:tok_count] + got[:tok_count]
        back = widened(swapped(narrowed(back, width, heads_here), "fsdp"), width, heads_here)
        return in_order(part_own[:tok_count] + got[tok_count:] + back)

    def convolved(proj, kernel):
        proj = proj.astype(jnp.bfloat16)
        count = lax.axis_size(SEQ)
        rim = lax.ppermute(
            proj[tok_count - (CONV - 1) :], SEQ, [(i, i + 1) for i in range(count - 1)]
        )
        padded = jnp.concatenate([rim, proj], axis=0).astype(jnp.float32)
        conv_sum = kernel[0] * padded[0:tok_count]
        for offset in range(1, CONV):
            conv_sum = conv_sum + kernel[offset] * padded[offset : offset + tok_count]
        return jax.nn.silu(conv_sum).astype(jnp.bfloat16)

    blocks = tok_count // SPAN
    fill = -heads_here % LANES
    weight_bc = sampled(bc_mean, bc_devs, swag_coef).reshape(rows_k, width_bc)
    weight_bc = jnp.concatenate([weight_bc, dt_weight, jnp.zeros((rows_k, fill), jnp.bfloat16)], axis=1)
    proj_bc = projected(weight_bc, width_bc)
    step_size = jax.nn.softplus(proj_bc[:, width_bc : width_bc + heads_here] + dt_bias)
    steps_b = step_size.reshape(blocks, SPAN, heads_here)
    cum_log = jnp.cumsum(-steps_b * decay_rate, axis=1)
    last_cum = cum_log[:, SPAN - 1 :, :]
    block_decay = jnp.exp(last_cum[:, 0, :])
    levels = prefix_decays(jnp.exp(jnp.sum(last_cum[:, 0, :], axis=0)))
    conv_out = convolved(proj_bc[:, :width_bc], conv_bc.reshape(CONV, width_bc))
    keys_b = conv_out[:, : width_bc // 2].reshape(blocks, SPAN, groups_here, N)
    reads_c = conv_out[:, width_bc // 2 :].reshape(blocks, SPAN, groups_here, N)
    scores = jnp.einsum("bqgn,bsgn->bgqs", reads_c, keys_b, preferred_element_type=jnp.float32)
    causal_mask = jnp.tril(jnp.ones((SPAN, SPAN), bool))

    def finished(first, group_count):
        heads = group_count * per_group
        part = slice(first * per_group, first * per_group + heads)
        cols = slice(part.start * P_SIZE, part.stop * P_SIZE)
        weight_x = sampled(proj_mean[:, cols], proj_devs[:, :, cols], swag_coef)
        values = convolved(projected(weight_x, heads * P_SIZE), conv_proj[:, cols])
        values = values.reshape(blocks, SPAN, heads, P_SIZE)
        cum, steps = cum_log[:, :, part], steps_b[:, :, part]
        scaled = (
            values.astype(jnp.float32) * (jnp.exp(last_cum[:, :, part] - cum) * steps)[..., None]
        ).astype(jnp.bfloat16)
        keys_h = jnp.repeat(keys_b[:, :, first : first + group_count], per_group, axis=2)
        reads_h = jnp.repeat(reads_c[:, :, first : first + group_count], per_group, axis=2)
        states = jnp.einsum("bshn,bshp->bhnp", keys_h, scaled, preferred_element_type=jnp.float32)
        decay = block_decay[:, part]
        total_state = states[0]
        for member in range(1, blocks):
            total_state = decay[member][:, None, None] * total_state + states[member]
        carried = prefix_states(total_state, levels, part)
        later_cum = jnp.transpose(cum, (0, 2, 1))
        cum_gaps = later_cum[:, :, :, None] - later_cum[:, :, None, :]
        decays = jnp.where(causal_mask, jnp.exp(jnp.minimum(cum_gaps, 0.0)), 0.0)
        scores_h = jnp.repeat(scores[:, first : first + group_count], per_group, axis=1)
        weights = (scores_h * decays * jnp.transpose(steps, (0, 2, 1))[:, :, None, :]).astype(jnp.bfloat16)
        inner_part = jnp.einsum("bhqs,bshp->bqhp", weights, values, preferred_element_type=jnp.float32)
        entering = []
        for member in range(blocks):
            entering.append(carried)
            carried = decay[member][:, None, None] * carried + states[member]
        entering_bf = jnp.stack(entering).astype(jnp.bfloat16)
        outer_part = jnp.exp(cum)[..., None] * jnp.einsum(
            "bqhn,bhnp->bqhp", reads_h, entering_bf, preferred_element_type=jnp.float32
        )
        result = inner_part + outer_part + skip_gain[part, None] * values.astype(jnp.float32)
        return result.reshape(tok_count, heads * P_SIZE).astype(jnp.bfloat16)

    at_once = max(1, groups_here // 2)
    pieces = [finished(first, at_once) for first in range(0, groups_here, at_once)]
    return jnp.concatenate(pieces, axis=1)


def solution(mesh):
    shape = mesh.shape
    split = Mesh(
        mesh.devices.reshape(shape["fsdp"], shape["seq"] // 2, 2, shape["tp"]),
        ("fsdp", "chip", "core", "tp"),
    )
    rows = ("fsdp", "chip", "core")
    return jax.shard_map(
        body,
        mesh=split,
        in_specs=(
            P(rows + ("tp",), None),
            P(rows, "tp"),
            P(None, rows, "tp"),
            P(rows, None, "tp"),
            P(None, rows, None, "tp"),
            P(),
            P(rows, "tp"),
            P("tp"),
            P("tp"),
            P("tp"),
            P(None, "tp"),
            P(None, None, "tp"),
        ),
        out_specs=P(rows, "tp"),
        check_vma=False,
    )
```

```python
import functools

import jax
import jax.numpy as jnp
from jax import lax
from jax.experimental import pallas as pl
from jax.experimental.pallas import tpu as pltpu
from jax.sharding import Mesh, PartitionSpec as P

P_SIZE = 64
N = 128
CONV = 4
SPAN = 128
LANES = 128
RIM = 16
SEQ = ("chip", "core")
F32 = jnp.float32
BF16 = jnp.bfloat16
SMEM = pl.BlockSpec(memory_space=pltpu.SMEM)
VMEM = pl.BlockSpec(memory_space=pltpu.VMEM)


def call(kernel, name, out_shape, flops=0, moved=0, **settings):
    return pl.pallas_call(
        kernel,
        out_shape=out_shape,
        name=name,
        cost_estimate=pl.CostEstimate(flops=flops, bytes_accessed=moved, transcendentals=0),
        compiler_params=pltpu.CompilerParams(vmem_limit_bytes=40 * 1024 * 1024),
        **settings,
    )


def swapped(part, axis, by=1):
    return lax.ppermute(part, axis, [(i, i ^ by) for i in range(lax.axis_size(axis))])


def cut_kernel(chips, at_ref, tokens_ref, own_kept, own_sent, far_kept, far_sent):
    depth = own_kept.shape[1] // chips
    f_at, c_at = at_ref[0], at_ref[1]
    for i in range(chips):
        for f, c, out in (
            (1 - f_at, 1 - c_at, far_sent),
            (1 - f_at, c_at, far_kept),
            (f_at, 1 - c_at, own_sent),
            (f_at, c_at, own_kept),
        ):
            start = pl.multiple_of(((f * chips + at_ref[2 + i]) * 2 + c) * depth, depth)
            out[:, i * depth : (i + 1) * depth] = tokens_ref[:, pl.ds(start, depth)]


def stack_kernel(at_ref, kept, kept_t, got, got_t, rows_ref):
    count = kept.shape[0]
    mine = pl.multiple_of(at_ref[0] * count, count)
    other = pl.multiple_of((1 - at_ref[0]) * count, count)
    rows_ref[pl.ds(mine, count), :] = kept[...]
    rows_ref[pl.ds(other, count), :] = kept_t[...]
    rows_ref[pl.ds(2 * count + mine, count), :] = got[...]
    rows_ref[pl.ds(2 * count + other, count), :] = got_t[...]


def token_rows(kept, got):
    if lax.axis_size("tp") != 2:
        return jnp.concatenate([lax.all_gather(a, "tp", axis=0, tiled=True) for a in (kept, got)], axis=0)
    at = lax.axis_index("tp").astype(jnp.int32).reshape(1)
    shape = jax.ShapeDtypeStruct((4 * kept.shape[0], kept.shape[1]), BF16)
    return call(
        stack_kernel, "stack_rows", shape, moved=2 * 2 * shape.size, in_specs=[SMEM] + [VMEM] * 4, out_specs=VMEM
    )(at, kept, swapped(kept, "tp"), got, swapped(got, "tp"))


def sample_kernel(count, coef_ref, mean_ref, devs_ref, out_ref):
    factor = (2.0 * (count - 1)) ** (-0.5)
    accum = mean_ref[...].astype(F32)
    for member in range(count):
        accum = accum + factor * coef_ref[member] * devs_ref[member].astype(F32)
    out_ref[...] = accum.astype(BF16)


def sampled_cols(mean_part, dev_part, swag_coef, at, width):
    rows, count = mean_part.shape[0], dev_part.shape[0]
    tile = min(rows, 128)
    return call(
        functools.partial(sample_kernel, count),
        "sample",
        jax.ShapeDtypeStruct((rows, width), BF16),
        moved=2 * (count + 2) * rows * width,
        grid=(rows // tile,),
        in_specs=[
            SMEM,
            pl.BlockSpec((tile, width), lambda i: (i, at)),
            pl.BlockSpec((count, tile, width), lambda i: (0, i, at)),
        ],
        out_specs=pl.BlockSpec((tile, width), lambda i: (i, 0)),
    )(swag_coef, mean_part, dev_part)


def sampled(mean_part, dev_part, swag_coef):
    factor = (2.0 * (dev_part.shape[0] - 1)) ** (-0.5)
    accum = mean_part.astype(F32)
    for member in range(dev_part.shape[0]):
        accum = accum + factor * swag_coef[member] * dev_part[member].astype(F32)
    return accum.astype(BF16)


def gathered(weight):
    if lax.axis_size("chip") != 4:
        return [lax.all_gather(weight, "chip", axis=0, tiled=True)]
    half = weight.shape[0] // 2
    by_x = swapped(weight, "chip", 1)
    by_y = swapped(weight, "chip", 2)
    return [weight, by_x, by_y, swapped(by_y[:half], "chip", 1), swapped(by_x[half:], "chip", 2)]


def coded(part, heads):
    high = part.astype(BF16).astype(F32)
    return high + pltpu.roll(part - high, heads, 1)


def decoded(part, heads):
    return part + pltpu.roll(part, LANES - heads, 1)


def multiply_kernel(heads, with_steps, pieces, rows_ref, *refs):
    weights, (sent_ref, kept_ref) = refs[:pieces], refs[pieces:]
    at = 0
    total = None
    for weight in weights:
        depth = weight.shape[0]
        term = jnp.dot(rows_ref[:, at : at + depth], weight[...], preferred_element_type=F32)
        total = term if total is None else total + term
        at += depth
    half = total.shape[0] // 2
    kept_ref[...] = total[:half]
    sent_ref[...] = total[half:].astype(BF16)
    if with_steps:
        @pl.when(pl.program_id(0) == pl.num_programs(0) - 1)
        def _():
            sent_ref[:, -LANES:] = coded(total[half:, -LANES:], heads).astype(BF16)


def multiplied(rows, weights, heads, with_steps):
    width = weights[0].shape[1]
    tile = next(t for t in (256, 384, 128) if width % t == 0)
    half = rows.shape[0] // 2
    return call(
        functools.partial(multiply_kernel, heads, with_steps, len(weights)),
        "multiply",
        (jax.ShapeDtypeStruct((half, width), BF16), jax.ShapeDtypeStruct((half, width), F32)),
        flops=2 * rows.size * width,
        moved=2 * rows.size + 2 * rows.shape[1] * width + 6 * half * width,
        grid=(width // tile,),
        in_specs=[pl.BlockSpec(rows.shape, lambda i: (0, 0))]
        + [pl.BlockSpec((w.shape[0], tile), lambda i: (0, i)) for w in weights],
        out_specs=[pl.BlockSpec((half, tile), lambda i: (0, i))] * 2,
    )(rows, *weights)


def relay_kernel(heads, with_steps, kept_ref, got_ref, out_ref):
    got = got_ref[...].astype(F32)
    out_ref[...] = (kept_ref[...] + got).astype(BF16)
    if with_steps:
        wide = kept_ref[:, -LANES:] + decoded(got[:, -LANES:], heads)
        lane = lax.broadcasted_iota(jnp.int32, wide.shape, 1)
        out_ref[:, -LANES:] = coded(jnp.where(lane < heads, wide, 0.0), heads).astype(BF16)


def relayed(kept, got, heads, with_steps):
    return call(
        functools.partial(relay_kernel, heads, with_steps),
        "relay",
        jax.ShapeDtypeStruct(kept.shape, BF16),
        flops=kept.size,
        moved=8 * kept.size,
        in_specs=[VMEM] * 2,
        out_specs=VMEM,
    )(kept, got)


def convolved(width, kept, got_c, got_f, rim_own, rim_far, taps, padded):
    count = kept.shape[0]
    proj = kept[:, :width] + got_c[:, :width].astype(F32) + got_f[:, :width].astype(F32)
    rim = rim_own[RIM - 8 :, :width] + rim_far[RIM - 8 :, :width].astype(F32)
    padded[8:, :] = proj.astype(BF16).astype(F32)
    padded[:8, :] = rim.astype(BF16).astype(F32)
    first = 8 - (CONV - 1)
    conv_sum = taps[0:1, :] * padded[first : first + count, :]
    for offset in range(1, CONV):
        conv_sum = conv_sum + taps[offset : offset + 1, :] * padded[first + offset : first + offset + count, :]
    return (conv_sum * jax.nn.sigmoid(conv_sum)).astype(BF16)


def state_proj_kernel(heads, kept, got_c, got_f, rim_own, rim_far, taps, out_ref, logits_ref, padded):
    width = out_ref.shape[1]
    out_ref[...] = convolved(width, kept, got_c, got_f, rim_own, rim_far, taps, padded)
    logits_ref[...] = (
        kept[:, width:] + decoded(got_c[:, width:].astype(F32), heads) + decoded(got_f[:, width:].astype(F32), heads)
    )


def pairwise(columns, first):
    shape = (columns.shape[0], 2 * P_SIZE)
    lane = lax.broadcasted_iota(jnp.int32, shape, 1)
    return jnp.where(lane < P_SIZE, columns[:, first : first + 1], columns[:, first + 1 : first + 2])


def over_channels(columns):
    return jnp.concatenate([pairwise(columns, h) for h in range(0, columns.shape[1], 2)], axis=1)


def mix_kernel(
    kept, got_c, got_f, rim_own, rim_far, taps, keys, reads, cum, steps, cum_t, steps_t, skip, y_ref, early_ref, total_ref, padded
):
    width = y_ref.shape[1]
    values = convolved(width, kept, got_c, got_f, rim_own, rim_far, taps, padded)
    heads = cum.shape[1]
    row = lax.broadcasted_iota(jnp.int32, (SPAN, SPAN), 0)
    col = lax.broadcasted_iota(jnp.int32, (SPAN, SPAN), 1)
    causal = row >= col
    lane = lax.broadcasted_iota(jnp.int32, (SPAN, 2 * P_SIZE), 1)
    state = None
    for at in range(0, y_ref.shape[0], SPAN):
        span = slice(at, at + SPAN)
        keys_b, reads_b, values_b = keys[span, :], reads[span, :], values[span, :]
        cum_b, steps_b = cum[span, :], steps[span, :]
        last = cum_b[SPAN - 1 : SPAN, :]
        scores = lax.dot_general(reads_b, keys_b, (((1,), (1,)), ((), ())), preferred_element_type=F32)
        scores = jnp.where(causal, scores, 0.0)
        reach = jnp.exp(last - cum_b) * steps_b
        scaled = []
        for head in range(0, heads, 2):
            chans = slice(head * P_SIZE, (head + 2) * P_SIZE)
            two = []
            for h in (head, head + 1):
                gap = cum_b[:, h : h + 1] - cum_t[h : h + 1, span]
                two.append((scores * jnp.exp(jnp.minimum(gap, 0.0)) * steps_t[h : h + 1, span]).astype(BF16))
            values_h = values_b[:, chans]
            both = jnp.dot(jnp.concatenate(two, axis=0), values_h, preferred_element_type=F32)
            inner = jnp.where(lane < P_SIZE, both[:SPAN], both[SPAN:])
            wide = values_h.astype(F32)
            y_ref[span, chans] = inner + skip[0:1, chans] * wide
            scaled.append((wide * pairwise(reach, head)).astype(BF16))
        fresh = lax.dot_general(
            keys_b, jnp.concatenate(scaled, axis=1), (((0,), (0,)), ((), ())), preferred_element_type=F32
        )
        if at + SPAN == y_ref.shape[0]:
            total_ref[...] = fresh if state is None else over_channels(jnp.exp(last)) * state + fresh
        else:
            state = fresh if state is None else over_channels(jnp.exp(last)) * state + fresh
            early_ref[at // SPAN] = fresh


def read_kernel(y, reads, cum, early, before, out_ref):
    state = before[...]
    for at in range(0, out_ref.shape[0], SPAN):
        span = slice(at, at + SPAN)
        cum_b = cum[span, :]
        seen = jnp.dot(reads[span, :], state.astype(BF16), preferred_element_type=F32)
        out_ref[span, :] = (y[span, :] + over_channels(jnp.exp(cum_b)) * seen).astype(BF16)
        if at + SPAN < out_ref.shape[0]:
            state = over_channels(jnp.exp(cum_b[SPAN - 1 : SPAN, :])) * state + early[at // SPAN]


def prefix_decays(decay):
    place = lax.axis_index(SEQ)
    count = lax.axis_size(SEQ)
    before = jnp.ones_like(decay)
    total = decay
    levels = []
    by = 1
    while by < count:
        other = swapped(total, SEQ, by)
        upper = (place & by) != 0
        levels.append((jnp.where(upper, before, 0.0), jnp.where(upper, 1.0, other), jnp.where(upper, total, 1.0)))
        before = jnp.where(upper, other * before, before)
        total = total * other
        by *= 2
    return levels


def prefix_states(state, levels, part):
    before = None
    total = state
    for level, scales in enumerate(levels):
        gain, keep, take = (jnp.repeat(s[part], P_SIZE)[None, :] for s in scales)
        other = swapped(total.astype(BF16), SEQ, 1 << level).astype(F32)
        before = gain * other if before is None else before + gain * other
        if level + 1 < len(levels):
            total = keep * total + take * other
    return before


def body(
    tokens,
    proj_mean,
    proj_devs,
    bc_mean,
    bc_devs,
    swag_coef,
    dt_weight,
    dt_bias,
    decay_rate,
    skip_gain,
    conv_proj,
    conv_bc,
):
    heads_here = decay_rate.shape[0]
    groups_here = bc_mean.shape[2] // N
    per_group = heads_here // groups_here
    width_bc = 2 * bc_mean.shape[2]
    rows_k = proj_mean.shape[0]
    chips = lax.axis_size("chip")
    count = lax.axis_size(SEQ)

    place = lax.axis_index("chip") if chips == 4 else 0
    at = jnp.stack([lax.axis_index("fsdp"), lax.axis_index("core")] + [place ^ i for i in range(chips)])
    cut = jax.ShapeDtypeStruct((tokens.shape[0], chips * rows_k), BF16)
    own_kept, own_sent, far_kept, far_sent = call(
        functools.partial(cut_kernel, chips),
        "cut_tokens",
        (cut,) * 4,
        moved=4 * tokens.size,
        in_specs=[SMEM, VMEM],
        out_specs=[VMEM] * 4,
    )(at.astype(jnp.int32), tokens)
    far_got = swapped(swapped(far_sent, "fsdp"), "core")
    far_kept = swapped(far_kept, "fsdp")
    rows_own = token_rows(own_kept, swapped(own_sent, "core"))
    rows_far = token_rows(far_kept, far_got)
    tok_count = rows_own.shape[0] // 2
    blocks = tok_count // SPAN

    def projected(pieces, with_steps):
        far_out, far_part = multiplied(rows_far, pieces, heads_here, with_steps)
        own_out, own_part = multiplied(rows_own, pieces, heads_here, with_steps)
        back = relayed(far_part, swapped(far_out, "core"), heads_here, with_steps)
        got_c = swapped(own_out, "core")
        got_f = swapped(back, "fsdp")
        rim = tok_count - RIM
        rim_own = own_part[rim:] + got_c[rim:].astype(F32)
        rim_own = lax.ppermute(rim_own, SEQ, [(i, i + 1) for i in range(count - 1)])
        rim_far = lax.ppermute(
            back[rim:],
            ("fsdp",) + SEQ,
            [(f * count + i, (1 - f) * count + i + 1) for f in range(2) for i in range(count - 1)],
        )
        return own_part, got_c, got_f, rim_own, rim_far

    width = per_group * P_SIZE
    weights = [sampled_cols(proj_mean, proj_devs, swag_coef, g, width) for g in range(groups_here)]
    fill = -heads_here % LANES
    weight_bc = sampled(bc_mean, bc_devs, swag_coef).reshape(rows_k, width_bc)
    weight_bc = jnp.concatenate([weight_bc, dt_weight, jnp.zeros((rows_k, fill), BF16)], axis=1)

    order = [weights[0], weight_bc] + weights[1:]
    pieces = []
    for j, weight in enumerate(order):
        if j >= 2 and chips == 4:
            weight, _ = lax.optimization_barrier((weight, pieces[j - 2][1:3]))
        pieces.append(gathered(weight))
    parts = [projected(chunk, j == 1) for j, chunk in enumerate(pieces)]
    part_bc = parts.pop(1)

    conv_out, logits = call(
        functools.partial(state_proj_kernel, heads_here),
        "state_proj",
        (jax.ShapeDtypeStruct((tok_count, width_bc), BF16), jax.ShapeDtypeStruct((tok_count, LANES), F32)),
        moved=10 * tok_count * width_bc,
        in_specs=[VMEM] * 6,
        out_specs=[VMEM] * 2,
        scratch_shapes=[pltpu.VMEM((tok_count + 8, width_bc), F32)],
    )(*part_bc, conv_bc.reshape(CONV, width_bc))
    step_size = jax.nn.softplus(logits[:, :heads_here] + dt_bias)
    steps_b = step_size.reshape(blocks, SPAN, heads_here)
    cum_log = jnp.cumsum(-steps_b * decay_rate, axis=1)
    levels = prefix_decays(jnp.exp(jnp.sum(cum_log[:, SPAN - 1, :], axis=0)))
    cum_log = cum_log.reshape(tok_count, heads_here)
    cum_t, steps_t = cum_log.T, step_size.T
    skip = jnp.repeat(skip_gain, P_SIZE)[None, :]

    results = []
    for g, part in enumerate(parts):
        heads = slice(g * per_group, (g + 1) * per_group)
        chans = slice(g * width, (g + 1) * width)
        keys = conv_out[:, g * N : (g + 1) * N]
        reads = conv_out[:, width_bc // 2 + g * N : width_bc // 2 + (g + 1) * N]
        cum = cum_log[:, heads]
        y, early, total = call(
            mix_kernel,
            "mix",
            (
                jax.ShapeDtypeStruct((tok_count, width), F32),
                jax.ShapeDtypeStruct((blocks - 1, N, width), F32),
                jax.ShapeDtypeStruct((N, width), F32),
            ),
            flops=8 * tok_count * N * width,
            moved=14 * tok_count * width,
            in_specs=[VMEM] * 13,
            out_specs=[VMEM] * 3,
            scratch_shapes=[pltpu.VMEM((tok_count + 8, width), F32)],
        )(*part, conv_proj[:, chans], keys, reads, cum, step_size[:, heads], cum_t[heads], steps_t[heads], skip[:, chans])
        before = prefix_states(total, levels, heads)
        results.append(
            call(
                read_kernel,
                "read_out",
                jax.ShapeDtypeStruct((tok_count, width), BF16),
                flops=2 * tok_count * N * width,
                moved=10 * tok_count * width,
                in_specs=[VMEM] * 5,
                out_specs=VMEM,
            )(y, reads, cum, early, before)
        )
    return jnp.concatenate(results, axis=1)


def solution(mesh):
    shape = mesh.shape
    split = Mesh(
        mesh.devices.reshape(shape["fsdp"], shape["seq"] // 2, 2, shape["tp"]),
        ("fsdp", "chip", "core", "tp"),
    )
    rows = ("fsdp", "chip", "core")
    return jax.shard_map(
        body,
        mesh=split,
        in_specs=(
            P(rows + ("tp",), None),
            P(rows, "tp"),
            P(None, rows, "tp"),
            P(rows, None, "tp"),
            P(None, rows, None, "tp"),
            P(),
            P(rows, "tp"),
            P("tp"),
            P("tp"),
            P("tp"),
            P(None, "tp"),
            P(None, None, "tp"),
        ),
        out_specs=P(rows, "tp"),
        check_vma=False,
    )
```

```python
import functools

import jax
import jax.numpy as jnp
from jax import lax
from jax.experimental import pallas as pl
from jax.experimental.pallas import tpu as pltpu
from jax.sharding import Mesh, PartitionSpec as P

P_SIZE = 64
N = 128
CONV = 4
SPAN = 128
LANES = 128
RIM = 16
SEQ = ("chip", "core")
F32 = jnp.float32
BF16 = jnp.bfloat16
SMEM = pl.BlockSpec(memory_space=pltpu.SMEM)
VMEM = pl.BlockSpec(memory_space=pltpu.VMEM)


def call(kernel, name, out_shape, flops=0, moved=0, **settings):
    return pl.pallas_call(
        kernel,
        out_shape=out_shape,
        name=name,
        cost_estimate=pl.CostEstimate(flops=flops, bytes_accessed=moved, transcendentals=0),
        compiler_params=pltpu.CompilerParams(vmem_limit_bytes=60 * 1024 * 1024),
        **settings,
    )


def swapped(part, axis, by=1):
    return lax.ppermute(part, axis, [(i, i ^ by) for i in range(lax.axis_size(axis))])


def cut_kernel(chips, at_ref, tokens_ref, own_kept, own_sent, far_kept, far_sent):
    depth = own_kept.shape[1] // chips
    f_at, c_at = at_ref[0], at_ref[1]
    for i in range(chips):
        for f, c, out in (
            (1 - f_at, 1 - c_at, far_sent),
            (1 - f_at, c_at, far_kept),
            (f_at, 1 - c_at, own_sent),
            (f_at, c_at, own_kept),
        ):
            start = pl.multiple_of(((f * chips + at_ref[2 + i]) * 2 + c) * depth, depth)
            out[:, i * depth : (i + 1) * depth] = tokens_ref[:, pl.ds(start, depth)]


def stack_kernel(at_ref, kept, kept_t, got, got_t, rows_ref):
    count = kept.shape[0]
    mine = pl.multiple_of(at_ref[0] * count, count)
    other = pl.multiple_of((1 - at_ref[0]) * count, count)
    rows_ref[pl.ds(mine, count), :] = kept[...]
    rows_ref[pl.ds(other, count), :] = kept_t[...]
    rows_ref[pl.ds(2 * count + mine, count), :] = got[...]
    rows_ref[pl.ds(2 * count + other, count), :] = got_t[...]


def token_rows(kept, got):
    if lax.axis_size("tp") != 2:
        return jnp.concatenate([lax.all_gather(a, "tp", axis=0, tiled=True) for a in (kept, got)], axis=0)
    at = lax.axis_index("tp").astype(jnp.int32).reshape(1)
    shape = jax.ShapeDtypeStruct((4 * kept.shape[0], kept.shape[1]), BF16)
    return call(
        stack_kernel, "stack_rows", shape, moved=2 * 2 * shape.size, in_specs=[SMEM] + [VMEM] * 4, out_specs=VMEM
    )(at, kept, swapped(kept, "tp"), got, swapped(got, "tp"))


def sample_kernel(count, coef_ref, mean_ref, devs_ref, top_ref, low_ref):
    factor = (2.0 * (count - 1)) ** (-0.5)
    accum = mean_ref[...].astype(F32)
    for member in range(count):
        accum = accum + factor * coef_ref[member] * devs_ref[member].astype(F32)
    accum = accum.astype(BF16)
    half = pl.num_programs(0) // 2
    @pl.when(pl.program_id(0) < half)
    def _():
        top_ref[...] = accum
    @pl.when(pl.program_id(0) >= half)
    def _():
        low_ref[...] = accum


def sampled_cols(mean_part, dev_part, swag_coef, at, width):
    rows, count = mean_part.shape[0], dev_part.shape[0]
    tile = rows // 4
    return call(
        functools.partial(sample_kernel, count),
        "sample",
        (jax.ShapeDtypeStruct((rows // 2, width), BF16),) * 2,
        moved=2 * (count + 2) * rows * width,
        grid=(4,),
        in_specs=[
            SMEM,
            pl.BlockSpec((tile, width), lambda i: (i, at)),
            pl.BlockSpec((count, tile, width), lambda i: (0, i, at)),
        ],
        out_specs=[
            pl.BlockSpec((tile, width), lambda i: (jnp.minimum(i, 1), 0)),
            pl.BlockSpec((tile, width), lambda i: (jnp.maximum(i - 2, 0), 0)),
        ],
    )(swag_coef, mean_part, dev_part)


def sampled(mean_part, dev_part, swag_coef):
    factor = (2.0 * (dev_part.shape[0] - 1)) ** (-0.5)
    accum = mean_part.astype(F32)
    for member in range(dev_part.shape[0]):
        accum = accum + factor * swag_coef[member] * dev_part[member].astype(F32)
    return accum.astype(BF16)


def pack_kernel(bc_ref, dt_ref, top_ref, low_ref):
    half, width = top_ref.shape[0], bc_ref.shape[1]
    heads = dt_ref.shape[1]
    for out, at in ((top_ref, 0), (low_ref, half)):
        out[:, :width] = bc_ref[at : at + half, :]
        out[:, width:] = jnp.zeros((half, LANES), BF16)
        out[:, width : width + heads] = dt_ref[at : at + half, :]


def gathered(top, low):
    if lax.axis_size("chip") != 4:
        return [lax.all_gather(jnp.concatenate([top, low], axis=0), "chip", axis=0, tiled=True)]
    top_y, low_x = swapped(top, "chip", 2), swapped(low, "chip", 1)
    top_x, low_y = swapped(top, "chip", 1), swapped(low, "chip", 2)
    return [top, low, top_x, low_x, top_y, low_y, swapped(top_y, "chip", 1), swapped(low_x, "chip", 2)]


def coded(part, heads):
    high = part.astype(BF16).astype(F32)
    return high + pltpu.roll(part - high, heads, 1)


def decoded(part, heads):
    return part + pltpu.roll(part, LANES - heads, 1)


def multiply_kernel(heads, with_steps, pieces, rows_ref, *refs):
    weights, (sent_ref, kept_ref) = refs[:pieces], refs[pieces:]
    at = 0
    total = None
    for weight in weights:
        depth = weight.shape[0]
        term = jnp.dot(rows_ref[:, at : at + depth], weight[...], preferred_element_type=F32)
        total = term if total is None else total + term
        at += depth
    half = total.shape[0] // 2
    kept_ref[...] = total[:half]
    sent_ref[...] = total[half:].astype(BF16)
    if with_steps:
        @pl.when(pl.program_id(0) == pl.num_programs(0) - 1)
        def _():
            sent_ref[:, -LANES:] = coded(total[half:, -LANES:], heads).astype(BF16)


def multiplied(rows, weights, heads, with_steps, first, width):
    tile = next(t for t in (256, 384, 128) if width % t == 0)
    at = first // tile
    half = rows.shape[0] // 2
    return call(
        functools.partial(multiply_kernel, heads, with_steps, len(weights)),
        "multiply",
        (jax.ShapeDtypeStruct((half, width), BF16), jax.ShapeDtypeStruct((half, width), F32)),
        flops=2 * rows.size * width,
        moved=2 * rows.size + 2 * rows.shape[1] * width + 6 * half * width,
        grid=(width // tile,),
        in_specs=[pl.BlockSpec(rows.shape, lambda i: (0, 0))]
        + [pl.BlockSpec((w.shape[0], tile), lambda i: (0, at + i)) for w in weights],
        out_specs=[pl.BlockSpec((half, tile), lambda i: (0, i))] * 2,
    )(rows, *weights)


def relay_kernel(heads, with_steps, kept_ref, got_ref, out_ref, rim_ref):
    got = got_ref[...].astype(F32)
    out_ref[...] = (kept_ref[...] + got).astype(BF16)
    if with_steps:
        wide = kept_ref[:, -LANES:] + decoded(got[:, -LANES:], heads)
        lane = lax.broadcasted_iota(jnp.int32, wide.shape, 1)
        out_ref[:, -LANES:] = coded(jnp.where(lane < heads, wide, 0.0), heads).astype(BF16)
    rim_ref[...] = out_ref[out_ref.shape[0] - RIM :, :]


def relayed(kept, got, heads, with_steps):
    return call(
        functools.partial(relay_kernel, heads, with_steps),
        "relay",
        (jax.ShapeDtypeStruct(kept.shape, BF16), jax.ShapeDtypeStruct((RIM, kept.shape[1]), BF16)),
        flops=kept.size,
        moved=8 * kept.size,
        in_specs=[VMEM] * 2,
        out_specs=[VMEM] * 2,
    )(kept, got)


def rim_kernel(kept_ref, got_ref, rim_ref):
    rim_ref[...] = kept_ref[...] + got_ref[...].astype(F32)


def last_rows(kept, got):
    width, at = kept.shape[1], kept.shape[0] // RIM - 1
    return call(
        rim_kernel,
        "rim",
        jax.ShapeDtypeStruct((RIM, width), F32),
        moved=10 * RIM * width,
        grid=(1,),
        in_specs=[pl.BlockSpec((RIM, width), lambda i: (at, 0))] * 2,
        out_specs=pl.BlockSpec((RIM, width), lambda i: (0, 0)),
    )(kept, got)


def convolved(width, kept, got_c, got_f, rim_own, rim_far, taps, padded):
    count = kept.shape[0]
    proj = kept[:, :width] + got_c[:, :width].astype(F32) + got_f[:, :width].astype(F32)
    rim = rim_own[RIM - 8 :, :width] + rim_far[RIM - 8 :, :width].astype(F32)
    padded[8:, :] = proj.astype(BF16).astype(F32)
    padded[:8, :] = rim.astype(BF16).astype(F32)
    first = 8 - (CONV - 1)
    conv_sum = taps[0:1, :] * padded[first : first + count, :]
    for offset in range(1, CONV):
        conv_sum = conv_sum + taps[offset : offset + 1, :] * padded[first + offset : first + offset + count, :]
    return (conv_sum * jax.nn.sigmoid(conv_sum)).astype(BF16)


def state_proj_kernel(heads, kept, got_c, got_f, rim_own, rim_far, taps, out_ref, logits_ref, padded):
    width = out_ref.shape[1]
    out_ref[...] = convolved(width, kept, got_c, got_f, rim_own, rim_far, taps, padded)
    logits_ref[...] = (
        kept[:, width:] + decoded(got_c[:, width:].astype(F32), heads) + decoded(got_f[:, width:].astype(F32), heads)
    )


def pairwise(columns, first):
    shape = (columns.shape[0], 2 * P_SIZE)
    lane = lax.broadcasted_iota(jnp.int32, shape, 1)
    return jnp.where(lane < P_SIZE, columns[:, first : first + 1], columns[:, first + 1 : first + 2])


def over_channels(columns):
    return jnp.concatenate([pairwise(columns, h) for h in range(0, columns.shape[1], 2)], axis=1)


def mix_kernel(
    kept, got_c, got_f, rim_own, rim_far, taps, keys, reads, cum_g, steps_g, cum_t, steps_t, skip, y_ref, early_ref, total_ref, sent_ref, padded
):
    width = y_ref.shape[1]
    values = convolved(width, kept, got_c, got_f, rim_own, rim_far, taps, padded)
    cum, steps = cum_g[0], steps_g[0]
    heads = cum.shape[1]
    row = lax.broadcasted_iota(jnp.int32, (SPAN, SPAN), 0)
    col = lax.broadcasted_iota(jnp.int32, (SPAN, SPAN), 1)
    causal = row >= col
    lane = lax.broadcasted_iota(jnp.int32, (SPAN, 2 * P_SIZE), 1)
    state = None
    for at in range(0, y_ref.shape[0], SPAN):
        span = slice(at, at + SPAN)
        keys_b, reads_b, values_b = keys[span, :], reads[span, :], values[span, :]
        cum_b, steps_b = cum[span, :], steps[span, :]
        last = cum_b[SPAN - 1 : SPAN, :]
        scores = lax.dot_general(reads_b, keys_b, (((1,), (1,)), ((), ())), preferred_element_type=F32)
        scores = jnp.where(causal, scores, 0.0)
        reach = jnp.exp(last - cum_b) * steps_b
        scaled = []
        for head in range(0, heads, 2):
            chans = slice(head * P_SIZE, (head + 2) * P_SIZE)
            two = []
            for h in (head, head + 1):
                gap = cum_b[:, h : h + 1] - cum_t[h : h + 1, span]
                two.append((scores * jnp.exp(jnp.minimum(gap, 0.0)) * steps_t[h : h + 1, span]).astype(BF16))
            values_h = values_b[:, chans]
            both = jnp.dot(jnp.concatenate(two, axis=0), values_h, preferred_element_type=F32)
            inner = jnp.where(lane < P_SIZE, both[:SPAN], both[SPAN:])
            wide = values_h.astype(F32)
            y_ref[span, chans] = inner + skip[0:1, chans] * wide
            scaled.append((wide * pairwise(reach, head)).astype(BF16))
        fresh = lax.dot_general(
            keys_b, jnp.concatenate(scaled, axis=1), (((0,), (0,)), ((), ())), preferred_element_type=F32
        )
        state = fresh if state is None else over_channels(jnp.exp(last)) * state + fresh
        if at + SPAN < y_ref.shape[0]:
            early_ref[at // SPAN] = fresh
    total_ref[...] = state
    sent_ref[...] = state.astype(BF16)


def combine_kernel(level, scales, total, other, before, total_ref, sent_ref, before_ref):
    gain, keep, take = (scales[3 * level + i : 3 * level + i + 1, :] for i in range(3))
    come = other[...].astype(F32)
    fresh = gain * come
    before_ref[...] = fresh if before is None else before[...] + fresh
    joint = keep * total[...] + take * come
    total_ref[...] = joint
    sent_ref[...] = joint.astype(BF16)


def read_kernel(level, y, reads, cum_g, early, scales, before, other, *refs):
    out_ref = refs[-1]
    state = before[...] + scales[3 * level : 3 * level + 1, :] * other[...].astype(F32)
    cum = cum_g[0]
    for at in range(0, out_ref.shape[0], SPAN):
        span = slice(at, at + SPAN)
        cum_b = cum[span, :]
        seen = jnp.dot(reads[span, :], state.astype(BF16), preferred_element_type=F32)
        out_ref[span, :] = (y[span, :] + over_channels(jnp.exp(cum_b)) * seen).astype(BF16)
        if at + SPAN < out_ref.shape[0]:
            state = over_channels(jnp.exp(cum_b[SPAN - 1 : SPAN, :])) * state + early[at // SPAN]


def prefix_scales(decay):
    place = lax.axis_index(SEQ)
    count = lax.axis_size(SEQ)
    before = jnp.ones_like(decay)
    total = decay
    rows = []
    by = 1
    while by < count:
        other = swapped(total, SEQ, by)
        upper = (place & by) != 0
        rows += [jnp.where(upper, before, 0.0), jnp.where(upper, 1.0, other), jnp.where(upper, total, 1.0)]
        before = jnp.where(upper, other * before, before)
        total = total * other
        by *= 2
    scales = jnp.stack(rows)
    return jnp.broadcast_to(scales[:, :, None], scales.shape + (P_SIZE,)).reshape(len(rows), -1)


def combined(level, scales, total, other, before, first):
    width, wide = total.shape[1], total.shape[1] // first[1]
    block = pl.BlockSpec((N, wide), lambda i: (0, i))
    kernel = functools.partial(combine_kernel, level)
    if before is None:
        kernel = lambda scales, total, other, *outs: combine_kernel(level, scales, total, other, None, *outs)
    return call(
        kernel,
        "combine",
        (
            jax.ShapeDtypeStruct(total.shape, F32),
            jax.ShapeDtypeStruct(total.shape, BF16),
            jax.ShapeDtypeStruct(total.shape, F32),
        ),
        flops=6 * total.size,
        moved=20 * total.size,
        grid=(first[1],),
        in_specs=[pl.BlockSpec((scales.shape[0], wide), lambda i: (0, first[0] + i))]
        + [block] * (2 if before is None else 3),
        out_specs=[block] * 3,
    )(scales, total, other, *(() if before is None else (before,)))


def body(
    tokens,
    proj_mean,
    proj_devs,
    bc_mean,
    bc_devs,
    swag_coef,
    dt_weight,
    dt_bias,
    decay_rate,
    skip_gain,
    conv_proj,
    conv_bc,
):
    heads_here = decay_rate.shape[0]
    groups_here = bc_mean.shape[2] // N
    per_group = heads_here // groups_here
    width_bc = 2 * bc_mean.shape[2]
    rows_k = proj_mean.shape[0]
    chips = lax.axis_size("chip")
    count = lax.axis_size(SEQ)

    place = lax.axis_index("chip") if chips == 4 else 0
    at = jnp.stack([lax.axis_index("fsdp"), lax.axis_index("core")] + [place ^ i for i in range(chips)])
    cut = jax.ShapeDtypeStruct((tokens.shape[0], chips * rows_k), BF16)
    own_kept, own_sent, far_kept, far_sent = call(
        functools.partial(cut_kernel, chips),
        "cut_tokens",
        (cut,) * 4,
        moved=4 * tokens.size,
        in_specs=[SMEM, VMEM],
        out_specs=[VMEM] * 4,
    )(at.astype(jnp.int32), tokens)
    far_got = swapped(swapped(far_sent, "fsdp"), "core")
    far_kept = swapped(far_kept, "fsdp")
    rows_own = token_rows(own_kept, swapped(own_sent, "core"))
    rows_far = token_rows(far_kept, far_got)
    tok_count = rows_own.shape[0] // 2
    blocks = tok_count // SPAN

    def projected(pieces, with_steps, first, width):
        far_out, far_part = multiplied(rows_far, pieces, heads_here, with_steps, first, width)
        own_out, own_part = multiplied(rows_own, pieces, heads_here, with_steps, first, width)
        back, rim_far = relayed(far_part, swapped(far_out, "core"), heads_here, with_steps)
        got_f = swapped(back, "fsdp")
        got_c = swapped(own_out, "core")
        rim_own = lax.ppermute(last_rows(own_part, got_c), SEQ, [(i, i + 1) for i in range(count - 1)])
        rim_far = lax.ppermute(
            rim_far,
            ("fsdp",) + SEQ,
            [(f * count + i, (1 - f) * count + i + 1) for f in range(2) for i in range(count - 1)],
        )
        return (own_part, got_c, got_f, rim_own, rim_far), back

    width = per_group * P_SIZE
    fill = -heads_here % LANES
    early_groups = max(1, groups_here // 2)
    late_groups = groups_here - early_groups

    def sampled_groups(first, groups):
        return sampled_cols(proj_mean, proj_devs, swag_coef, first // groups, groups * width)

    weight_bc = sampled(bc_mean, bc_devs, swag_coef).reshape(rows_k, width_bc)
    weight_bc = call(
        pack_kernel,
        "pack",
        (jax.ShapeDtypeStruct((rows_k // 2, width_bc + LANES), BF16),) * 2,
        moved=4 * weight_bc.size,
        in_specs=[VMEM] * 2,
        out_specs=[VMEM] * 2,
    )(weight_bc, dt_weight)
    pieces_early = gathered(*sampled_groups(0, early_groups))
    pieces_bc = gathered(*weight_bc)
    chunks = [(0, early_groups, pieces_early, 0)]
    if late_groups:
        pieces_late = gathered(*sampled_groups(early_groups, late_groups))
        chunks += [(early_groups + i, 1, pieces_late, i * width) for i in range(late_groups)]

    def after(arrays, earlier):
        return lax.optimization_barrier((arrays, earlier))[0]

    parts = []
    parts_x, back = projected(pieces_early, False, 0, early_groups * width)
    parts.append(parts_x)
    part_bc, back = projected(after(pieces_bc, back), True, 0, width_bc + LANES)
    for first, groups, pieces, col in chunks[1:]:
        parts_x, back = projected(after(pieces, back), False, col, groups * width)
        parts.append(parts_x)

    conv_out, logits = call(
        functools.partial(state_proj_kernel, heads_here),
        "state_proj",
        (jax.ShapeDtypeStruct((tok_count, width_bc), BF16), jax.ShapeDtypeStruct((tok_count, LANES), F32)),
        moved=10 * tok_count * width_bc,
        in_specs=[VMEM] * 6,
        out_specs=[VMEM] * 2,
        scratch_shapes=[pltpu.VMEM((tok_count + 8, width_bc), F32)],
    )(*part_bc, conv_bc.reshape(CONV, width_bc))
    step_size = jax.nn.softplus(logits[:, :heads_here] + dt_bias)
    steps_b = step_size.reshape(blocks, SPAN, heads_here)
    cum_log = jnp.cumsum(-steps_b * decay_rate, axis=1)
    scales = prefix_scales(jnp.exp(jnp.sum(cum_log[:, SPAN - 1, :], axis=0)))
    cum_log = cum_log.reshape(tok_count, heads_here)
    cum_t, steps_t = cum_log.T, step_size.T
    by_group = lambda a: jnp.transpose(a.reshape(tok_count, groups_here, per_group), (1, 0, 2))
    cum_g, steps_g = by_group(cum_log), by_group(step_size)
    skip = jnp.repeat(skip_gain, P_SIZE)[None, :]
    levels = scales.shape[0] // 3

    result = None
    last_total = None
    for (first, groups, _, _), part in zip(chunks, parts):
        if last_total is not None:
            part = after(part, last_total)
        grid = (groups,)
        cols = lambda rows: pl.BlockSpec((rows, width), lambda i: (0, i))
        cols_all = lambda rows: pl.BlockSpec((rows, width), lambda i: (0, first + i))
        heads_g = pl.BlockSpec((1, tok_count, per_group), lambda i: (first + i, 0, 0))
        heads_t = pl.BlockSpec((per_group, tok_count), lambda i: (first + i, 0))
        keys = pl.BlockSpec((tok_count, N), lambda i: (0, first + i))
        reads = pl.BlockSpec((tok_count, N), lambda i: (0, groups_here + first + i))
        early_spec = pl.BlockSpec((blocks - 1, N, width), lambda i: (0, 0, i))
        y, early, total, sent = call(
            mix_kernel,
            "mix",
            (
                jax.ShapeDtypeStruct((tok_count, groups * width), F32),
                jax.ShapeDtypeStruct((blocks - 1, N, groups * width), F32),
                jax.ShapeDtypeStruct((N, groups * width), F32),
                jax.ShapeDtypeStruct((N, groups * width), BF16),
            ),
            flops=8 * tok_count * N * width * groups,
            moved=14 * tok_count * width * groups,
            grid=grid,
            in_specs=[cols(tok_count)] * 3
            + [cols(RIM)] * 2
            + [cols_all(CONV), keys, reads, heads_g, heads_g, heads_t, heads_t, cols_all(1)],
            out_specs=[cols(tok_count), early_spec, cols(N), cols(N)],
            scratch_shapes=[pltpu.VMEM((tok_count + 8, width), F32)],
        )(*part, conv_proj, conv_out, conv_out, cum_g, steps_g, cum_t, steps_t, skip)
        last_total = sent
        before = None
        for level in range(levels - 1):
            other = swapped(sent, SEQ, 1 << level)
            total, sent, before = combined(level, scales, total, other, before, (first, groups))
        other = swapped(sent, SEQ, 1 << (levels - 1))
        operands = [y, conv_out, cum_g, early, scales, before, other]
        specs = [cols(tok_count), reads, heads_g, early_spec, cols_all(scales.shape[0]), cols(N), cols(N)]
        alias = {}
        if result is not None:
            operands.append(result)
            specs.append(pl.BlockSpec(memory_space=pl.ANY))
            alias = {len(operands) - 1: 0}
        result = call(
            functools.partial(read_kernel, levels - 1),
            "read_out",
            jax.ShapeDtypeStruct((tok_count, heads_here * P_SIZE), BF16),
            flops=2 * tok_count * N * width * groups,
            moved=10 * tok_count * width * groups,
            grid=grid,
            in_specs=specs,
            out_specs=cols_all(tok_count),
            input_output_aliases=alias,
        )(*operands)
    return result


def solution(mesh):
    shape = mesh.shape
    split = Mesh(
        mesh.devices.reshape(shape["fsdp"], shape["seq"] // 2, 2, shape["tp"]),
        ("fsdp", "chip", "core", "tp"),
    )
    rows = ("fsdp", "chip", "core")
    return jax.shard_map(
        body,
        mesh=split,
        in_specs=(
            P(rows + ("tp",), None),
            P(rows, "tp"),
            P(None, rows, "tp"),
            P(rows, None, "tp"),
            P(None, rows, None, "tp"),
            P(),
            P(rows, "tp"),
            P("tp"),
            P("tp"),
            P("tp"),
            P(None, "tp"),
            P(None, None, "tp"),
        ),
        out_specs=P(rows, "tp"),
        check_vma=False,
    )
```

```python
import functools

import jax
import jax.numpy as jnp
from jax import lax
from jax.experimental import pallas as pl
from jax.experimental.pallas import tpu as pltpu
from jax.sharding import Mesh, PartitionSpec as P

P_SIZE = 64
N = 128
CONV = 4
SPAN = 128
LANES = 128
RIM = 16
SEQ = ("chip", "core")
F32 = jnp.float32
BF16 = jnp.bfloat16
SMEM = pl.BlockSpec(memory_space=pltpu.SMEM)
VMEM = pl.BlockSpec(memory_space=pltpu.VMEM)


def call(kernel, name, out_shape, flops=0, moved=0, small=False, **settings):
    return pl.pallas_call(
        kernel,
        out_shape=out_shape,
        name=name,
        cost_estimate=pl.CostEstimate(flops=flops // 50, bytes_accessed=moved // 50, transcendentals=0),
        compiler_params=pltpu.CompilerParams(vmem_limit_bytes=(12 if small else 60) * 1024 * 1024),
        **settings,
    )


def swapped(part, axis, by=1):
    return lax.ppermute(part, axis, [(i, i ^ by) for i in range(lax.axis_size(axis))])


def cut_kernel(chips, at_ref, tokens_ref, own_ref, far_kept, far_sent):
    depth = far_kept.shape[1] // chips
    rows = far_kept.shape[0]
    f_at, c_at = at_ref[0], at_ref[1]
    for i in range(chips):
        cols = slice(i * depth, (i + 1) * depth)

        def taken(f, c):
            start = pl.multiple_of(((f * chips + at_ref[3 + i]) * 2 + c) * depth, depth)
            return tokens_ref[:, pl.ds(start, depth)]

        far_sent[:, cols] = taken(1 - f_at, 1 - c_at)
        far_kept[:, cols] = taken(1 - f_at, c_at)
        own_ref[:rows, cols] = taken(f_at, c_at)
        own_ref[rows:, cols] = taken(f_at, 1 - c_at)


def stack_kernel(chips, shares, at_ref, *refs):
    pieces, (rows_ref, tail_ref) = refs[:-2], refs[-2:]
    count = pieces[0].shape[0]
    half = shares * count
    depth = tail_ref.shape[1] // chips
    for at in range(2):
        for share in range(shares):
            place = (at_ref[2] if share == 0 else 1 - at_ref[2]) if shares == 2 else 0
            start = pl.multiple_of(at * half + place * count, count)
            rows_ref[pl.ds(start, count), :] = pieces[at * shares + share][...]
    last = pl.multiple_of((2 - at_ref[1]) * half - RIM, RIM)
    for i in range(chips):
        start = pl.multiple_of(at_ref[3 + i] * depth, depth)
        tail_ref[:, pl.ds(start, depth)] = rows_ref[pl.ds(last, RIM), i * depth : (i + 1) * depth]


def append_kernel(chips, at_ref, tail_ref, rows_ref, out_ref):
    depth = tail_ref.shape[1] // chips
    for i in range(chips):
        start = pl.multiple_of(at_ref[3 + i] * depth, depth)
        out_ref[:, i * depth : (i + 1) * depth] = tail_ref[:, pl.ds(start, depth)]


def token_rows(at, chips, pieces, specs):
    count, depth = specs[0].block_shape
    rows = len(pieces) * count + RIM
    rows_ext, tail = call(
        functools.partial(stack_kernel, chips, len(pieces) // 2),
        "stack_rows",
        (jax.ShapeDtypeStruct((rows, depth), BF16), jax.ShapeDtypeStruct((RIM, depth), BF16)),
        moved=4 * rows * depth,
        grid=(1,),
        in_specs=[SMEM] + specs,
        out_specs=[pl.BlockSpec((rows, depth), lambda i: (0, 0)), pl.BlockSpec((RIM, depth), lambda i: (0, 0))],
    )(at, *pieces)
    tail = lax.ppermute(tail, "chip", [(i, i + 1) for i in range(chips - 1)])
    last = rows // RIM - 1
    return call(
        functools.partial(append_kernel, chips),
        "append_rows",
        jax.ShapeDtypeStruct((rows, depth), BF16),
        moved=4 * RIM * depth,
        grid=(1,),
        in_specs=[SMEM, pl.BlockSpec((RIM, depth), lambda i: (0, 0)), pl.BlockSpec(memory_space=pl.ANY)],
        out_specs=pl.BlockSpec((RIM, depth), lambda i: (last, 0)),
        input_output_aliases={2: 0},
    )(at, tail, rows_ext)


def sample_kernel(count, coef_ref, mean_ref, devs_ref, out_ref):
    factor = (2.0 * (count - 1)) ** (-0.5)
    accum = mean_ref[...].astype(F32)
    for member in range(count):
        accum = accum + factor * coef_ref[member] * devs_ref[member].astype(F32)
    out_ref[...] = accum.astype(BF16)


def sampled_cols(mean_part, dev_part, swag_coef, at, width):
    rows, count = mean_part.shape[0], dev_part.shape[0]
    tile = rows // 4
    return call(
        functools.partial(sample_kernel, count),
        "sample",
        jax.ShapeDtypeStruct((rows, width), BF16),
        moved=2 * (count + 2) * rows * width,
        grid=(4,),
        in_specs=[
            SMEM,
            pl.BlockSpec((tile, width), lambda i: (i, at)),
            pl.BlockSpec((count, tile, width), lambda i: (0, i, at)),
        ],
        out_specs=pl.BlockSpec((tile, width), lambda i: (i, 0)),
    )(swag_coef, mean_part, dev_part)


def sampled(mean_part, dev_part, swag_coef):
    factor = (2.0 * (dev_part.shape[0] - 1)) ** (-0.5)
    accum = mean_part.astype(F32)
    for member in range(dev_part.shape[0]):
        accum = accum + factor * swag_coef[member] * dev_part[member].astype(F32)
    return accum.astype(BF16)


def pack_kernel(bc_ref, dt_ref, out_ref):
    width, heads = bc_ref.shape[1], dt_ref.shape[1]
    out_ref[:, :width] = bc_ref[...]
    out_ref[:, width:] = jnp.zeros((out_ref.shape[0], LANES), BF16)
    out_ref[:, width : width + heads] = dt_ref[...]


def swapped_both(weight):
    return swapped(weight, "chip", 1), swapped(weight, "chip", 2)


def gathered(weight, both, by_x):
    if both is None:
        return [lax.all_gather(weight, "chip", axis=0, tiled=True)]
    return [weight, both[0], both[1], swapped(both[1], "chip", 1) if by_x else swapped(both[0], "chip", 2)]


def coded(part, heads):
    high = part.astype(BF16).astype(F32)
    return high + pltpu.roll(part - high, heads, 1)


def decoded(part, heads):
    return part + pltpu.roll(part, LANES - heads, 1)


def multiply_kernel(heads, with_steps, pieces, at_ref, far_ref, own_ref, *refs):
    weights, (sent_ref, kept_ref) = refs[:pieces], refs[pieces:]
    second = at_ref[1] == 1
    for k, rows_ref in enumerate((far_ref, own_ref)):
        at = 0
        total = None
        for weight in weights:
            depth = weight.shape[0]
            term = jnp.dot(rows_ref[:, at : at + depth], weight[...], preferred_element_type=F32)
            total = term if total is None else total + term
            at += depth
        half = (total.shape[0] - RIM) // 2
        before = total[2 * half :]
        kept_ref[k, :half, :] = total[:half]
        kept_ref[k, half:, :] = jnp.where(second, total[2 * half - RIM : 2 * half], before)
        sent_ref[k, :half, :] = total[half : 2 * half].astype(BF16)
        sent_ref[k, half:, :] = jnp.where(second, before, total[half - RIM : half]).astype(BF16)
        if with_steps:
            @pl.when(pl.program_id(0) == pl.num_programs(0) - 1)
            def _():
                sent_ref[k, :half, -LANES:] = coded(total[half : 2 * half, -LANES:], heads).astype(BF16)


def multiplied(at, rows_far, rows_own, weights, heads, with_steps, first, width):
    tile = next(t for t in (256, 384, 128) if width % t == 0)
    col = first // tile
    half = (rows_far.shape[0] - RIM) // 2 + RIM
    return call(
        functools.partial(multiply_kernel, heads, with_steps, len(weights)),
        "multiply",
        (jax.ShapeDtypeStruct((2, half, width), BF16), jax.ShapeDtypeStruct((2, half, width), F32)),
        flops=4 * rows_far.size * width,
        moved=4 * rows_far.size + 2 * rows_far.shape[1] * width + 12 * half * width,
        grid=(width // tile,),
        in_specs=[SMEM]
        + [pl.BlockSpec(rows_far.shape, lambda i: (0, 0))] * 2
        + [pl.BlockSpec((w.shape[0], tile), lambda i: (0, col + i)) for w in weights],
        out_specs=[pl.BlockSpec((2, half, tile), lambda i: (0, 0, i))] * 2,
    )(at, rows_far, rows_own, *weights)


def relay_kernel(heads, with_steps, kept_ref, got_ref, out_ref):
    kept, got = kept_ref[0], got_ref[0].astype(F32)
    out_ref[...] = (kept + got).astype(BF16)
    if with_steps:
        wide = kept[:, -LANES:] + decoded(got[:, -LANES:], heads)
        lane = lax.broadcasted_iota(jnp.int32, wide.shape, 1)
        out_ref[:, -LANES:] = coded(jnp.where(lane < heads, wide, 0.0), heads).astype(BF16)


def relayed(kept, got, heads, with_steps):
    rows, width = kept.shape[1:]
    return call(
        functools.partial(relay_kernel, heads, with_steps),
        "relay",
        jax.ShapeDtypeStruct((rows, width), BF16),
        moved=8 * rows * width,
        small=True,
        grid=(1,),
        in_specs=[pl.BlockSpec((1, rows, width), lambda i: (0, 0, 0))] * 2,
        out_specs=pl.BlockSpec((rows, width), lambda i: (0, 0)),
    )(kept, got)


def convolved(width, kept, got_c, got_f, taps, padded):
    count = padded.shape[0] - 8
    proj = kept[0, :, :width] + got_c[0, :, :width].astype(F32) + got_f[:, :width].astype(F32)
    proj = proj.astype(BF16).astype(F32)
    padded[8:, :] = proj[:count]
    padded[:8, :] = proj[count + RIM - 8 :]
    first = 8 - (CONV - 1)
    conv_sum = taps[0:1, :] * padded[first : first + count, :]
    for offset in range(1, CONV):
        conv_sum = conv_sum + taps[offset : offset + 1, :] * padded[first + offset : first + offset + count, :]
    return (conv_sum * jax.nn.sigmoid(conv_sum)).astype(BF16)


def state_proj_kernel(heads, kept, got_c, got_f, taps, out_ref, logits_ref, padded):
    count, width = out_ref.shape
    out_ref[...] = convolved(width, kept, got_c, got_f, taps, padded)
    logits_ref[...] = (
        kept[0, :count, width:]
        + decoded(got_c[0, :count, width:].astype(F32), heads)
        + decoded(got_f[:count, width:].astype(F32), heads)
    )


def pairwise(columns, first):
    shape = (columns.shape[0], 2 * P_SIZE)
    lane = lax.broadcasted_iota(jnp.int32, shape, 1)
    return jnp.where(lane < P_SIZE, columns[:, first : first + 1], columns[:, first + 1 : first + 2])


def over_channels(columns):
    return jnp.concatenate([pairwise(columns, h) for h in range(0, columns.shape[1], 2)], axis=1)


def mix_kernel(
    kept, got_c, got_f, taps, keys, reads, cum_g, steps_g, cum_t, steps_t, skip, y_ref, early_ref, total_ref, sent_ref, padded
):
    width = y_ref.shape[1]
    values = convolved(width, kept, got_c, got_f, taps, padded)
    cum, steps = cum_g[0], steps_g[0]
    heads = cum.shape[1]
    row = lax.broadcasted_iota(jnp.int32, (SPAN, SPAN), 0)
    col = lax.broadcasted_iota(jnp.int32, (SPAN, SPAN), 1)
    causal = row >= col
    lane = lax.broadcasted_iota(jnp.int32, (SPAN, 2 * P_SIZE), 1)
    state = None
    for at in range(0, y_ref.shape[0], SPAN):
        span = slice(at, at + SPAN)
        keys_b, reads_b, values_b = keys[span, :], reads[span, :], values[span, :]
        cum_b, steps_b = cum[span, :], steps[span, :]
        last = cum_b[SPAN - 1 : SPAN, :]
        scores = lax.dot_general(reads_b, keys_b, (((1,), (1,)), ((), ())), preferred_element_type=F32)
        scores = jnp.where(causal, scores, 0.0)
        reach = jnp.exp(last - cum_b) * steps_b
        scaled = []
        for head in range(0, heads, 2):
            chans = slice(head * P_SIZE, (head + 2) * P_SIZE)
            two = []
            for h in (head, head + 1):
                gap = cum_b[:, h : h + 1] - cum_t[h : h + 1, span]
                two.append((scores * jnp.exp(jnp.minimum(gap, 0.0)) * steps_t[h : h + 1, span]).astype(BF16))
            values_h = values_b[:, chans]
            both = jnp.dot(jnp.concatenate(two, axis=0), values_h, preferred_element_type=F32)
            inner = jnp.where(lane < P_SIZE, both[:SPAN], both[SPAN:])
            wide = values_h.astype(F32)
            y_ref[span, chans] = inner + skip[0:1, chans] * wide
            scaled.append((wide * pairwise(reach, head)).astype(BF16))
        fresh = lax.dot_general(
            keys_b, jnp.concatenate(scaled, axis=1), (((0,), (0,)), ((), ())), preferred_element_type=F32
        )
        state = fresh if state is None else over_channels(jnp.exp(last)) * state + fresh
        if at + SPAN < y_ref.shape[0]:
            early_ref[at // SPAN] = fresh
    total_ref[...] = state
    sent_ref[...] = state.astype(BF16)


def combine_kernel(level, scales, total, other, before, total_ref, sent_ref, before_ref):
    gain, keep, take = (scales[3 * level + i : 3 * level + i + 1, :] for i in range(3))
    come = other[...].astype(F32)
    fresh = gain * come
    before_ref[...] = fresh if before is None else before[...] + fresh
    joint = keep * total[...] + take * come
    total_ref[...] = joint
    sent_ref[...] = joint.astype(BF16)


def read_kernel(level, y, reads, cum_g, early, scales, before, other, *refs):
    out_ref = refs[-1]
    state = before[...] + scales[3 * level : 3 * level + 1, :] * other[...].astype(F32)
    cum = cum_g[0]
    for at in range(0, out_ref.shape[0], SPAN):
        span = slice(at, at + SPAN)
        cum_b = cum[span, :]
        seen = jnp.dot(reads[span, :], state.astype(BF16), preferred_element_type=F32)
        out_ref[span, :] = (y[span, :] + over_channels(jnp.exp(cum_b)) * seen).astype(BF16)
        if at + SPAN < out_ref.shape[0]:
            state = over_channels(jnp.exp(cum_b[SPAN - 1 : SPAN, :])) * state + early[at // SPAN]


def prefix_scales(decay):
    place = lax.axis_index(SEQ)
    count = lax.axis_size(SEQ)
    before = jnp.ones_like(decay)
    total = decay
    rows = []
    by = 1
    while by < count:
        other = swapped(total, SEQ, by)
        upper = (place & by) != 0
        rows += [jnp.where(upper, before, 0.0), jnp.where(upper, 1.0, other), jnp.where(upper, total, 1.0)]
        before = jnp.where(upper, other * before, before)
        total = total * other
        by *= 2
    scales = jnp.stack(rows)
    return jnp.broadcast_to(scales[:, :, None], scales.shape + (P_SIZE,)).reshape(len(rows), -1)


def combined(level, scales, total, other, before, first):
    width, wide = total.shape[1], total.shape[1] // first[1]
    block = pl.BlockSpec((N, wide), lambda i: (0, i))
    kernel = functools.partial(combine_kernel, level)
    if before is None:
        kernel = lambda scales, total, other, *outs: combine_kernel(level, scales, total, other, None, *outs)
    return call(
        kernel,
        "combine",
        (
            jax.ShapeDtypeStruct(total.shape, F32),
            jax.ShapeDtypeStruct(total.shape, BF16),
            jax.ShapeDtypeStruct(total.shape, F32),
        ),
        flops=6 * total.size,
        moved=20 * total.size,
        small=True,
        grid=(first[1],),
        in_specs=[pl.BlockSpec((scales.shape[0], wide), lambda i: (0, first[0] + i))]
        + [block] * (2 if before is None else 3),
        out_specs=[block] * 3,
    )(scales, total, other, *(() if before is None else (before,)))


def body(
    tokens,
    proj_mean,
    proj_devs,
    bc_mean,
    bc_devs,
    swag_coef,
    dt_weight,
    dt_bias,
    decay_rate,
    skip_gain,
    conv_proj,
    conv_bc,
):
    heads_here = decay_rate.shape[0]
    groups_here = bc_mean.shape[2] // N
    per_group = heads_here // groups_here
    width_bc = 2 * bc_mean.shape[2]
    rows_k = proj_mean.shape[0]
    chips = lax.axis_size("chip")
    count = lax.axis_size(SEQ)

    def after(arrays, earlier):
        return lax.optimization_barrier((arrays, earlier))[0]

    width = per_group * P_SIZE
    early_groups = max(1, groups_here // 2)
    late = list(range(early_groups, groups_here))

    plane = chips == 4
    place = lax.axis_index("chip") if plane else 0
    at = jnp.stack([lax.axis_index(a) for a in ("fsdp", "core", "tp")] + [place ^ i for i in range(chips)]).astype(jnp.int32)
    share, depth = tokens.shape[0], chips * rows_k
    own, far_kept, far_sent = call(
        functools.partial(cut_kernel, chips),
        "cut_tokens",
        (jax.ShapeDtypeStruct((2 * share, depth), BF16),) + (jax.ShapeDtypeStruct((share, depth), BF16),) * 2,
        moved=4 * tokens.size,
        in_specs=[SMEM, VMEM],
        out_specs=[VMEM] * 3,
    )(at, tokens)
    far_sent, far_kept = swapped(far_sent, "fsdp"), swapped(far_kept, "fsdp")

    weights = [sampled_cols(proj_mean, proj_devs, swag_coef, 0, early_groups * width)]
    both = [swapped_both(weights[0]) if plane else None]
    weight_bc = sampled(bc_mean, bc_devs, swag_coef).reshape(rows_k, width_bc)
    weights.append(
        call(
            pack_kernel,
            "pack",
            jax.ShapeDtypeStruct((rows_k, width_bc + LANES), BF16),
            moved=4 * weight_bc.size,
            in_specs=[VMEM] * 2,
            out_specs=VMEM,
        )(weight_bc, dt_weight)
    )
    both.append(swapped_both(weights[1]) if plane else None)
    for j, g in enumerate(late):
        mean_part = proj_mean
        if plane and j < 2:
            mean_part = after(proj_mean, (both[j], weights[-1]))
        weights.append(sampled_cols(mean_part, proj_devs, swag_coef, g, width))
        both.append(swapped_both(weights[-1]) if plane else None)
        if j == 0:
            far_sent, far_kept = after((far_sent, far_kept), weights[-1])
    pieces = [gathered(w, b, j % 2 == 0) for j, (w, b) in enumerate(zip(weights, both))]

    if lax.axis_size("tp") == 2:
        low = pl.BlockSpec((share, depth), lambda i: (0, 0))
        high = pl.BlockSpec((share, depth), lambda i: (1, 0))
        own_t = swapped(own, "tp")
        own_pieces = (own, own_t, swapped(own, "core"), swapped(own_t, "core"))
        rows_own = token_rows(at, chips, own_pieces, [low, low, high, high])
        sent_t = swapped(far_sent, "tp")
        far_pieces = (far_kept, swapped(far_kept, "tp"), swapped(far_sent, "core"), swapped(sent_t, "core"))
        rows_far = token_rows(at, chips, far_pieces, [low] * 4)
    else:
        whole = lambda a: lax.all_gather(a, "tp", axis=0, tiled=True)
        spec = pl.BlockSpec((share * lax.axis_size("tp"), depth), lambda i: (0, 0))
        rows_own = token_rows(at, chips, (whole(own[:share]), whole(swapped(own[share:], "core"))), [spec] * 2)
        rows_far = token_rows(at, chips, (whole(far_kept), whole(swapped(far_sent, "core"))), [spec] * 2)
    tok_count = (rows_own.shape[0] - RIM) // 2
    blocks = tok_count // SPAN

    def projected(pieces, with_steps, width):
        sent, kept = multiplied(at, rows_far, rows_own, pieces, heads_here, with_steps, 0, width)
        got = swapped(sent, "core")
        back = relayed(kept, got, heads_here, with_steps)
        return (kept, got, swapped(back, "fsdp")), back

    parts = []
    back = None
    for j, chunk in enumerate(pieces):
        if back is not None:
            chunk = after(chunk, back)
        part, back = projected(chunk, j == 1, weights[j].shape[1])
        parts.append(part)
    part_bc = parts.pop(1)
    chunks = [(0, early_groups)] + [(g, 1) for g in late]

    rows_ext = tok_count + RIM
    specs_of = lambda width: [pl.BlockSpec((1, rows_ext, width), lambda i: (1, 0, i))] * 2 + [
        pl.BlockSpec((rows_ext, width), lambda i: (0, i))
    ]
    whole_of = lambda *shape: pl.BlockSpec(shape, lambda i: (0,) * len(shape))
    conv_out, logits = call(
        functools.partial(state_proj_kernel, heads_here),
        "state_proj",
        (jax.ShapeDtypeStruct((tok_count, width_bc), BF16), jax.ShapeDtypeStruct((tok_count, LANES), F32)),
        moved=10 * tok_count * width_bc,
        grid=(1,),
        in_specs=specs_of(width_bc + LANES) + [whole_of(CONV, width_bc)],
        out_specs=[whole_of(tok_count, width_bc), whole_of(tok_count, LANES)],
        scratch_shapes=[pltpu.VMEM((tok_count + 8, width_bc), F32)],
    )(*part_bc, conv_bc.reshape(CONV, width_bc))
    step_size = jax.nn.softplus(logits[:, :heads_here] + dt_bias)
    steps_b = step_size.reshape(blocks, SPAN, heads_here)
    cum_log = jnp.cumsum(-steps_b * decay_rate, axis=1)
    scales = prefix_scales(jnp.exp(jnp.sum(cum_log[:, SPAN - 1, :], axis=0)))
    cum_log = cum_log.reshape(tok_count, heads_here)
    cum_t, steps_t = cum_log.T, step_size.T
    by_group = lambda a: jnp.transpose(a.reshape(tok_count, groups_here, per_group), (1, 0, 2))
    cum_g, steps_g = by_group(cum_log), by_group(step_size)
    skip = jnp.repeat(skip_gain, P_SIZE)[None, :]
    levels = scales.shape[0] // 3

    result = None
    last_total = None
    for (first, groups), part in zip(chunks, parts):
        if last_total is not None:
            part = after(part, last_total)
        grid = (groups,)
        cols = lambda rows: pl.BlockSpec((rows, width), lambda i: (0, i))
        cols_all = lambda rows: pl.BlockSpec((rows, width), lambda i: (0, first + i))
        heads_g = pl.BlockSpec((1, tok_count, per_group), lambda i: (first + i, 0, 0))
        heads_t = pl.BlockSpec((per_group, tok_count), lambda i: (first + i, 0))
        keys = pl.BlockSpec((tok_count, N), lambda i: (0, first + i))
        reads = pl.BlockSpec((tok_count, N), lambda i: (0, groups_here + first + i))
        early_spec = pl.BlockSpec((blocks - 1, N, width), lambda i: (0, 0, i))
        y, early, total, sent = call(
            mix_kernel,
            "mix",
            (
                jax.ShapeDtypeStruct((tok_count, groups * width), F32),
                jax.ShapeDtypeStruct((blocks - 1, N, groups * width), F32),
                jax.ShapeDtypeStruct((N, groups * width), F32),
                jax.ShapeDtypeStruct((N, groups * width), BF16),
            ),
            flops=8 * tok_count * N * width * groups,
            moved=14 * tok_count * width * groups,
            grid=grid,
            in_specs=specs_of(width)
            + [cols_all(CONV), keys, reads, heads_g, heads_g, heads_t, heads_t, cols_all(1)],
            out_specs=[cols(tok_count), early_spec, cols(N), cols(N)],
            scratch_shapes=[pltpu.VMEM((tok_count + 8, width), F32)],
        )(*part, conv_proj, conv_out, conv_out, cum_g, steps_g, cum_t, steps_t, skip)
        last_total = sent
        before = None
        for level in range(levels - 1):
            other = swapped(sent, SEQ, 1 << level)
            total, sent, before = combined(level, scales, total, other, before, (first, groups))
        other = swapped(sent, SEQ, 1 << (levels - 1))
        operands = [y, conv_out, cum_g, early, scales, before, other]
        specs = [cols(tok_count), reads, heads_g, early_spec, cols_all(scales.shape[0]), cols(N), cols(N)]
        alias = {}
        if result is not None:
            operands.append(result)
            specs.append(pl.BlockSpec(memory_space=pl.ANY))
            alias = {len(operands) - 1: 0}
        result = call(
            functools.partial(read_kernel, levels - 1),
            "read_out",
            jax.ShapeDtypeStruct((tok_count, heads_here * P_SIZE), BF16),
            flops=2 * tok_count * N * width * groups,
            moved=10 * tok_count * width * groups,
            small=True,
            grid=grid,
            in_specs=specs,
            out_specs=cols_all(tok_count),
            input_output_aliases=alias,
        )(*operands)
    return result


def solution(mesh):
    shape = mesh.shape
    split = Mesh(
        mesh.devices.reshape(shape["fsdp"], shape["seq"] // 2, 2, shape["tp"]),
        ("fsdp", "chip", "core", "tp"),
    )
    rows = ("fsdp", "chip", "core")
    return jax.shard_map(
        body,
        mesh=split,
        in_specs=(
            P(rows + ("tp",), None),
            P(rows, "tp"),
            P(None, rows, "tp"),
            P(rows, None, "tp"),
            P(None, rows, None, "tp"),
            P(),
            P(rows, "tp"),
            P("tp"),
            P("tp"),
            P("tp"),
            P(None, "tp"),
            P(None, None, "tp"),
        ),
        out_specs=P(rows, "tp"),
        check_vma=False,
    )
```

```python
import functools

import jax
import jax.numpy as jnp
from jax import lax
from jax.experimental import pallas as pl
from jax.experimental.pallas import tpu as pltpu
from jax.sharding import Mesh, PartitionSpec as P

P_SIZE = 64
N = 128
CONV = 4
SPAN = 128
LANES = 128
RIM = 16
SEQ = ("chip", "core")
F32 = jnp.float32
BF16 = jnp.bfloat16
SMEM = pl.BlockSpec(memory_space=pltpu.SMEM)
VMEM = pl.BlockSpec(memory_space=pltpu.VMEM)


def call(kernel, name, out_shape, flops=0, moved=0, vmem=60, **settings):
    return pl.pallas_call(
        kernel,
        out_shape=out_shape,
        name=name,
        cost_estimate=pl.CostEstimate(flops=flops // 50, bytes_accessed=moved // 50, transcendentals=0),
        compiler_params=pltpu.CompilerParams(vmem_limit_bytes=vmem * 1024 * 1024),
        **settings,
    )


def swapped(part, axis, by=1):
    return lax.ppermute(part, axis, [(i, i ^ by) for i in range(lax.axis_size(axis))])


def cut_kernel(chips, at_ref, tokens_ref, far_ref, own_ref):
    depth = far_ref.shape[1] // chips
    rows = tokens_ref.shape[0]
    f_at, c_at = at_ref[0], at_ref[1]
    for i in range(chips):
        for out, f in ((far_ref, 1 - f_at), (own_ref, f_at)):
            for k, c in enumerate((c_at, 1 - c_at)):
                start = pl.multiple_of(((f * chips + at_ref[3 + i]) * 2 + c) * depth, depth)
                out[k * rows : (k + 1) * rows, i * depth : (i + 1) * depth] = tokens_ref[:, pl.ds(start, depth)]


def stack_kernel(at_ref, kept, kept_t, got, got_t, rows_ref):
    count = kept.shape[0]
    mine = pl.multiple_of(at_ref[2] * count, count)
    other = pl.multiple_of((1 - at_ref[2]) * count, count)
    rows_ref[pl.ds(mine, count), :] = kept[...]
    rows_ref[pl.ds(other, count), :] = kept_t[...]
    rows_ref[pl.ds(2 * count + mine, count), :] = got[...]
    rows_ref[pl.ds(2 * count + other, count), :] = got_t[...]


def token_rows(at, cut, cut_t):
    share, depth = cut.shape[0] // 2, cut.shape[1]
    if cut_t is None:
        parts = (cut[:share], swapped(cut[share:], "core"))
        return jnp.concatenate([lax.all_gather(a, "tp", axis=0, tiled=True) for a in parts], axis=0)
    low = pl.BlockSpec((share, depth), lambda i: (0, 0))
    high = pl.BlockSpec((share, depth), lambda i: (1, 0))
    return call(
        stack_kernel,
        "stack_rows",
        jax.ShapeDtypeStruct((4 * share, depth), BF16),
        moved=16 * share * depth,
        vmem=40,
        grid=(1,),
        in_specs=[SMEM, low, low, high, high],
        out_specs=pl.BlockSpec((4 * share, depth), lambda i: (0, 0)),
    )(at, cut, cut_t, swapped(cut, "core"), swapped(cut_t, "core"))


def sample_kernel(count, coef_ref, mean_ref, devs_ref, out_ref):
    factor = (2.0 * (count - 1)) ** (-0.5)
    accum = mean_ref[...].astype(F32)
    for member in range(count):
        accum = accum + factor * coef_ref[member] * devs_ref[member].astype(F32)
    out_ref[...] = accum.astype(BF16)


def sampled_cols(mean_part, dev_part, swag_coef, at, width):
    rows, count = mean_part.shape[0], dev_part.shape[0]
    tile = rows // 4
    return call(
        functools.partial(sample_kernel, count),
        "sample",
        jax.ShapeDtypeStruct((rows, width), BF16),
        moved=2 * (count + 2) * rows * width,
        grid=(4,),
        in_specs=[
            SMEM,
            pl.BlockSpec((tile, width), lambda i: (i, at)),
            pl.BlockSpec((count, tile, width), lambda i: (0, i, at)),
        ],
        out_specs=pl.BlockSpec((tile, width), lambda i: (i, 0)),
    )(swag_coef, mean_part, dev_part)


def sampled(mean_part, dev_part, swag_coef):
    factor = (2.0 * (dev_part.shape[0] - 1)) ** (-0.5)
    accum = mean_part.astype(F32)
    for member in range(dev_part.shape[0]):
        accum = accum + factor * swag_coef[member] * dev_part[member].astype(F32)
    return accum.astype(BF16)


def pack_kernel(bc_ref, dt_ref, out_ref):
    width, heads = bc_ref.shape[1], dt_ref.shape[1]
    out_ref[:, :width] = bc_ref[...]
    out_ref[:, width:] = jnp.zeros((out_ref.shape[0], LANES), BF16)
    out_ref[:, width : width + heads] = dt_ref[...]


def gathered(weight):
    if lax.axis_size("chip") != 4:
        return [lax.all_gather(weight, "chip", axis=0, tiled=True)], ()
    half = weight.shape[0] // 2
    by_x, by_y = swapped(weight, "chip", 1), swapped(weight, "chip", 2)
    halves = (by_y[:half], by_x[half:])
    return [weight, by_x, by_y, swapped(halves[0], "chip", 1), swapped(halves[1], "chip", 2)], halves


def coded(part, heads):
    high = part.astype(BF16).astype(F32)
    return high + pltpu.roll(part - high, heads, 1)


def decoded(part, heads):
    return part + pltpu.roll(part, LANES - heads, 1)


def multiply_kernel(heads, with_steps, chips, pieces, at_ref, far_ref, own_ref, *refs):
    weights, (sent_ref, kept_ref) = refs[:pieces], refs[pieces:]
    half = far_ref.shape[0] // 2
    if pieces == 1:
        depth = far_ref.shape[1] // chips
        parts = [weights[0].at[pl.ds(pl.multiple_of(at_ref[3 + i] * depth, depth), depth), :] for i in range(chips)]
    else:
        parts = weights
    for k, rows_ref in enumerate((far_ref, own_ref)):
        at = 0
        total = None
        for part in parts:
            depth = part.shape[0]
            term = jnp.dot(rows_ref[:, at : at + depth], part[...], preferred_element_type=F32)
            total = term if total is None else total + term
            at += depth
        kept_ref[k] = total[:half]
        sent_ref[k] = total[half:].astype(BF16)
        if with_steps:
            @pl.when(pl.program_id(0) == pl.num_programs(0) - 1)
            def _():
                sent_ref[k, :, -LANES:] = coded(total[half:, -LANES:], heads).astype(BF16)


def multiplied(at, rows_far, rows_own, weights, heads, with_steps, first, width):
    tile = next(t for t in (256, 384, 128) if width % t == 0)
    col = first // tile
    half = rows_far.shape[0] // 2
    return call(
        functools.partial(multiply_kernel, heads, with_steps, lax.axis_size("chip"), len(weights)),
        "multiply",
        (jax.ShapeDtypeStruct((2, half, width), BF16), jax.ShapeDtypeStruct((2, half, width), F32)),
        flops=4 * rows_far.size * width,
        moved=4 * rows_far.size + 2 * rows_far.shape[1] * width + 12 * half * width,
        vmem=40,
        grid=(width // tile,),
        in_specs=[SMEM]
        + [pl.BlockSpec(rows_far.shape, lambda i: (0, 0))] * 2
        + [pl.BlockSpec((w.shape[0], tile), lambda i: (0, col + i)) for w in weights],
        out_specs=[pl.BlockSpec((2, half, tile), lambda i: (0, 0, i))] * 2,
    )(at, rows_far, rows_own, *weights)


def relay_kernel(heads, with_steps, kept_ref, got_ref, out_ref):
    kept, got = kept_ref[0], got_ref[0].astype(F32)
    out_ref[...] = (kept + got).astype(BF16)
    if with_steps:
        wide = kept[:, -LANES:] + decoded(got[:, -LANES:], heads)
        lane = lax.broadcasted_iota(jnp.int32, wide.shape, 1)
        out_ref[:, -LANES:] = coded(jnp.where(lane < heads, wide, 0.0), heads).astype(BF16)


def relayed(kept, got, heads, with_steps):
    rows, width = kept.shape[1:]
    return call(
        functools.partial(relay_kernel, heads, with_steps),
        "relay",
        jax.ShapeDtypeStruct((rows, width), BF16),
        moved=8 * rows * width,
        vmem=12,
        grid=(1,),
        in_specs=[pl.BlockSpec((1, rows, width), lambda i: (0, 0, 0))] * 2,
        out_specs=pl.BlockSpec((rows, width), lambda i: (0, 0)),
    )(kept, got)


def rim_kernel(kept, got_c, got_f, rim_ref):
    rim_ref[...] = (kept[0] + got_c[0].astype(F32) + got_f[...].astype(F32)).astype(BF16)


def rows_before(kept, got_c, got_f):
    rows, width = got_f.shape
    at = rows // RIM - 1
    rim = call(
        rim_kernel,
        "rim",
        jax.ShapeDtypeStruct((RIM, width), BF16),
        moved=10 * RIM * width,
        vmem=12,
        grid=(1,),
        in_specs=[pl.BlockSpec((1, RIM, width), lambda i: (1, at, 0))] * 2 + [pl.BlockSpec((RIM, width), lambda i: (at, 0))],
        out_specs=pl.BlockSpec((RIM, width), lambda i: (0, 0)),
    )(kept, got_c, got_f)
    return lax.ppermute(rim, SEQ, [(i, i + 1) for i in range(lax.axis_size(SEQ) - 1)])


def convolved(width, kept, got_c, got_f, rim, taps, padded):
    count = padded.shape[0] - 8
    proj = kept[0, :, :width] + got_c[0, :, :width].astype(F32) + got_f[:, :width].astype(F32)
    padded[8:, :] = proj.astype(BF16).astype(F32)
    padded[:8, :] = rim[:, :width].astype(F32)[RIM - 8 :]
    first = 8 - (CONV - 1)
    conv_sum = taps[0:1, :] * padded[first : first + count, :]
    for offset in range(1, CONV):
        conv_sum = conv_sum + taps[offset : offset + 1, :] * padded[first + offset : first + offset + count, :]
    return (conv_sum * jax.nn.sigmoid(conv_sum)).astype(BF16)


def state_proj_kernel(heads, kept, got_c, got_f, rim, taps, out_ref, logits_ref, padded):
    count, width = out_ref.shape
    out_ref[...] = convolved(width, kept, got_c, got_f, rim, taps, padded)
    logits_ref[...] = (
        kept[0, :, width:]
        + decoded(got_c[0, :, width:].astype(F32), heads)
        + decoded(got_f[:, width:].astype(F32), heads)
    )


def pairwise(columns, first):
    shape = (columns.shape[0], 2 * P_SIZE)
    lane = lax.broadcasted_iota(jnp.int32, shape, 1)
    return jnp.where(lane < P_SIZE, columns[:, first : first + 1], columns[:, first + 1 : first + 2])


def over_channels(columns):
    return jnp.concatenate([pairwise(columns, h) for h in range(0, columns.shape[1], 2)], axis=1)


def mix_kernel(
    kept, got_c, got_f, rim, taps, keys, reads, cum_g, steps_g, cum_t, steps_t, skip, y_ref, early_ref, total_ref, sent_ref, padded
):
    width = y_ref.shape[1]
    values = convolved(width, kept, got_c, got_f, rim, taps, padded)
    cum, steps = cum_g[0], steps_g[0]
    heads = cum.shape[1]
    row = lax.broadcasted_iota(jnp.int32, (SPAN, SPAN), 0)
    col = lax.broadcasted_iota(jnp.int32, (SPAN, SPAN), 1)
    causal = row >= col
    lane = lax.broadcasted_iota(jnp.int32, (SPAN, 2 * P_SIZE), 1)
    state = None
    for at in range(0, y_ref.shape[0], SPAN):
        span = slice(at, at + SPAN)
        keys_b, reads_b, values_b = keys[span, :], reads[span, :], values[span, :]
        cum_b, steps_b = cum[span, :], steps[span, :]
        last = cum_b[SPAN - 1 : SPAN, :]
        scores = lax.dot_general(reads_b, keys_b, (((1,), (1,)), ((), ())), preferred_element_type=F32)
        scores = jnp.where(causal, scores, 0.0)
        reach = jnp.exp(last - cum_b) * steps_b
        scaled = []
        for head in range(0, heads, 2):
            chans = slice(head * P_SIZE, (head + 2) * P_SIZE)
            two = []
            for h in (head, head + 1):
                gap = cum_b[:, h : h + 1] - cum_t[h : h + 1, span]
                two.append((scores * jnp.exp(jnp.minimum(gap, 0.0)) * steps_t[h : h + 1, span]).astype(BF16))
            values_h = values_b[:, chans]
            both = jnp.dot(jnp.concatenate(two, axis=0), values_h, preferred_element_type=F32)
            inner = jnp.where(lane < P_SIZE, both[:SPAN], both[SPAN:])
            wide = values_h.astype(F32)
            y_ref[span, chans] = inner + skip[0:1, chans] * wide
            scaled.append((wide * pairwise(reach, head)).astype(BF16))
        fresh = lax.dot_general(
            keys_b, jnp.concatenate(scaled, axis=1), (((0,), (0,)), ((), ())), preferred_element_type=F32
        )
        state = fresh if state is None else over_channels(jnp.exp(last)) * state + fresh
        if at + SPAN < y_ref.shape[0]:
            early_ref[at // SPAN] = fresh
    total_ref[...] = state
    sent_ref[...] = state.astype(BF16)


def combine_kernel(level, scales, total, other, before, total_ref, sent_ref, before_ref):
    gain, keep, take = (scales[3 * level + i : 3 * level + i + 1, :] for i in range(3))
    come = other[...].astype(F32)
    fresh = gain * come
    before_ref[...] = fresh if before is None else before[...] + fresh
    joint = keep * total[...] + take * come
    total_ref[...] = joint
    sent_ref[...] = joint.astype(BF16)


def read_kernel(level, y, reads, cum_g, early, scales, before, other, *refs):
    out_ref = refs[-1]
    state = before[...] + scales[3 * level : 3 * level + 1, :] * other[...].astype(F32)
    cum = cum_g[0]
    for at in range(0, out_ref.shape[0], SPAN):
        span = slice(at, at + SPAN)
        cum_b = cum[span, :]
        seen = jnp.dot(reads[span, :], state.astype(BF16), preferred_element_type=F32)
        out_ref[span, :] = (y[span, :] + over_channels(jnp.exp(cum_b)) * seen).astype(BF16)
        if at + SPAN < out_ref.shape[0]:
            state = over_channels(jnp.exp(cum_b[SPAN - 1 : SPAN, :])) * state + early[at // SPAN]


def prefix_scales(decay):
    place = lax.axis_index(SEQ)
    count = lax.axis_size(SEQ)
    before = jnp.ones_like(decay)
    total = decay
    rows = []
    by = 1
    while by < count:
        other = swapped(total, SEQ, by)
        upper = (place & by) != 0
        rows += [jnp.where(upper, before, 0.0), jnp.where(upper, 1.0, other), jnp.where(upper, total, 1.0)]
        before = jnp.where(upper, other * before, before)
        total = total * other
        by *= 2
    scales = jnp.stack(rows)
    return jnp.broadcast_to(scales[:, :, None], scales.shape + (P_SIZE,)).reshape(len(rows), -1)


def combined(level, scales, total, other, before, first):
    width, wide = total.shape[1], total.shape[1] // first[1]
    block = pl.BlockSpec((N, wide), lambda i: (0, i))
    kernel = functools.partial(combine_kernel, level)
    if before is None:
        kernel = lambda scales, total, other, *outs: combine_kernel(level, scales, total, other, None, *outs)
    return call(
        kernel,
        "combine",
        (
            jax.ShapeDtypeStruct(total.shape, F32),
            jax.ShapeDtypeStruct(total.shape, BF16),
            jax.ShapeDtypeStruct(total.shape, F32),
        ),
        flops=6 * total.size,
        moved=20 * total.size,
        vmem=12,
        grid=(first[1],),
        in_specs=[pl.BlockSpec((scales.shape[0], wide), lambda i: (0, first[0] + i))]
        + [block] * (2 if before is None else 3),
        out_specs=[block] * 3,
    )(scales, total, other, *(() if before is None else (before,)))


def body(
    tokens,
    proj_mean,
    proj_devs,
    bc_mean,
    bc_devs,
    swag_coef,
    dt_weight,
    dt_bias,
    decay_rate,
    skip_gain,
    conv_proj,
    conv_bc,
):
    heads_here = decay_rate.shape[0]
    groups_here = bc_mean.shape[2] // N
    per_group = heads_here // groups_here
    width_bc = 2 * bc_mean.shape[2]
    rows_k = proj_mean.shape[0]
    chips = lax.axis_size("chip")
    count = lax.axis_size(SEQ)

    def after(arrays, earlier):
        return lax.optimization_barrier((arrays, earlier))[0]

    width = per_group * P_SIZE
    early_groups = max(1, groups_here // 2)
    late = list(range(early_groups, groups_here))

    place = lax.axis_index("chip") if chips == 4 else 0
    at = jnp.stack([lax.axis_index(a) for a in ("fsdp", "core", "tp")] + [place ^ i for i in range(chips)]).astype(jnp.int32)
    cut = jax.ShapeDtypeStruct((2 * tokens.shape[0], chips * rows_k), BF16)
    far, own = call(
        functools.partial(cut_kernel, chips),
        "cut_tokens",
        (cut,) * 2,
        moved=4 * tokens.size,
        in_specs=[SMEM, VMEM],
        out_specs=[VMEM] * 2,
    )(at, tokens)
    far = swapped(far, "fsdp")

    gather = lambda a: [lax.all_gather(a, "chip", axis=0, tiled=True)]
    weights_early = sampled_cols(proj_mean, proj_devs, swag_coef, 0, early_groups * width)
    pieces_early = gather(weights_early)
    weight_bc = sampled(bc_mean, bc_devs, swag_coef).reshape(rows_k, width_bc)
    weight_bc = call(
        pack_kernel,
        "pack",
        jax.ShapeDtypeStruct((rows_k, width_bc + LANES), BF16),
        moved=4 * weight_bc.size,
        in_specs=[VMEM] * 2,
        out_specs=VMEM,
    )(weight_bc, dt_weight)
    pieces_bc, halves_bc = gathered(weight_bc)
    chunks = [(0, early_groups, pieces_early, 0)]
    if late:
        weights_late = sampled_cols(proj_mean, proj_devs, swag_coef, early_groups // len(late), len(late) * width)
        pieces_late = gather(weights_late)
        chunks += [(g, 1, pieces_late, i * width) for i, g in enumerate(late)]
        far = after(far, weights_late)

    two_shares = lax.axis_size("tp") == 2
    rows_own = token_rows(at, own, swapped(own, "tp") if two_shares else None)
    far_t = swapped(far, "tp") if two_shares else None
    far, far_t = after((far, far_t), (rows_own, halves_bc))
    rows_far = token_rows(at, far, far_t)
    tok_count = rows_own.shape[0] // 2
    blocks = tok_count // SPAN

    def projected(pieces, with_steps, first, width):
        sent, kept = multiplied(at, rows_far, rows_own, pieces, heads_here, with_steps, first, width)
        got = swapped(sent, "core")
        back = relayed(kept, got, heads_here, with_steps)
        return (kept, got, swapped(back, "fsdp")), back

    part_bc, back = projected(pieces_bc, True, 0, width_bc + LANES)
    parts = [part_bc]
    for j, (_, groups, pieces, col) in enumerate(chunks):
        earlier = (back, parts[j - 1][2]) if j else back
        part, back = projected(after(pieces, earlier), False, col, groups * width)
        parts.append(part)
    parts = [part + (rows_before(*part),) for part in parts]
    part_bc = parts.pop(0)

    specs_of = lambda width: [pl.BlockSpec((1, tok_count, width), lambda i: (1, 0, i))] * 2 + [
        pl.BlockSpec((tok_count, width), lambda i: (0, i)),
        pl.BlockSpec((RIM, width), lambda i: (0, i)),
    ]
    whole_of = lambda *shape: pl.BlockSpec(shape, lambda i: (0,) * len(shape))
    conv_out, logits = call(
        functools.partial(state_proj_kernel, heads_here),
        "state_proj",
        (jax.ShapeDtypeStruct((tok_count, width_bc), BF16), jax.ShapeDtypeStruct((tok_count, LANES), F32)),
        moved=10 * tok_count * width_bc,
        grid=(1,),
        in_specs=specs_of(width_bc + LANES) + [whole_of(CONV, width_bc)],
        out_specs=[whole_of(tok_count, width_bc), whole_of(tok_count, LANES)],
        scratch_shapes=[pltpu.VMEM((tok_count + 8, width_bc), F32)],
    )(*part_bc, conv_bc.reshape(CONV, width_bc))
    step_size = jax.nn.softplus(logits[:, :heads_here] + dt_bias)
    steps_b = step_size.reshape(blocks, SPAN, heads_here)
    cum_log = jnp.cumsum(-steps_b * decay_rate, axis=1)
    scales = prefix_scales(jnp.exp(jnp.sum(cum_log[:, SPAN - 1, :], axis=0)))
    cum_log = cum_log.reshape(tok_count, heads_here)
    cum_t, steps_t = cum_log.T, step_size.T
    by_group = lambda a: jnp.transpose(a.reshape(tok_count, groups_here, per_group), (1, 0, 2))
    cum_g, steps_g = by_group(cum_log), by_group(step_size)
    skip = jnp.repeat(skip_gain, P_SIZE)[None, :]
    levels = scales.shape[0] // 3

    result = None
    last_total = None
    for (first, groups, _, _), part in zip(chunks, parts):
        if last_total is not None:
            part = after(part, last_total)
        grid = (groups,)
        cols = lambda rows: pl.BlockSpec((rows, width), lambda i: (0, i))
        cols_all = lambda rows: pl.BlockSpec((rows, width), lambda i: (0, first + i))
        heads_g = pl.BlockSpec((1, tok_count, per_group), lambda i: (first + i, 0, 0))
        heads_t = pl.BlockSpec((per_group, tok_count), lambda i: (first + i, 0))
        keys = pl.BlockSpec((tok_count, N), lambda i: (0, first + i))
        reads = pl.BlockSpec((tok_count, N), lambda i: (0, groups_here + first + i))
        early_spec = pl.BlockSpec((blocks - 1, N, width), lambda i: (0, 0, i))
        y, early, total, sent = call(
            mix_kernel,
            "mix",
            (
                jax.ShapeDtypeStruct((tok_count, groups * width), F32),
                jax.ShapeDtypeStruct((blocks - 1, N, groups * width), F32),
                jax.ShapeDtypeStruct((N, groups * width), F32),
                jax.ShapeDtypeStruct((N, groups * width), BF16),
            ),
            flops=8 * tok_count * N * width * groups,
            moved=14 * tok_count * width * groups,
            grid=grid,
            in_specs=specs_of(width)
            + [cols_all(CONV), keys, reads, heads_g, heads_g, heads_t, heads_t, cols_all(1)],
            out_specs=[cols(tok_count), early_spec, cols(N), cols(N)],
            scratch_shapes=[pltpu.VMEM((tok_count + 8, width), F32)],
        )(*part, conv_proj, conv_out, conv_out, cum_g, steps_g, cum_t, steps_t, skip)
        last_total = sent
        before = None
        for level in range(levels - 1):
            other = swapped(sent, SEQ, 1 << level)
            total, sent, before = combined(level, scales, total, other, before, (first, groups))
        other = swapped(sent, SEQ, 1 << (levels - 1))
        operands = [y, conv_out, cum_g, early, scales, before, other]
        specs = [cols(tok_count), reads, heads_g, early_spec, cols_all(scales.shape[0]), cols(N), cols(N)]
        alias = {}
        if result is not None:
            operands.append(result)
            specs.append(pl.BlockSpec(memory_space=pl.ANY))
            alias = {len(operands) - 1: 0}
        result = call(
            functools.partial(read_kernel, levels - 1),
            "read_out",
            jax.ShapeDtypeStruct((tok_count, heads_here * P_SIZE), BF16),
            flops=2 * tok_count * N * width * groups,
            moved=10 * tok_count * width * groups,
            vmem=12,
            grid=grid,
            in_specs=specs,
            out_specs=cols_all(tok_count),
            input_output_aliases=alias,
        )(*operands)
    return result


def solution(mesh):
    shape = mesh.shape
    split = Mesh(
        mesh.devices.reshape(shape["fsdp"], shape["seq"] // 2, 2, shape["tp"]),
        ("fsdp", "chip", "core", "tp"),
    )
    rows = ("fsdp", "chip", "core")
    return jax.shard_map(
        body,
        mesh=split,
        in_specs=(
            P(rows + ("tp",), None),
            P(rows, "tp"),
            P(None, rows, "tp"),
            P(rows, None, "tp"),
            P(None, rows, None, "tp"),
            P(),
            P(rows, "tp"),
            P("tp"),
            P("tp"),
            P("tp"),
            P(None, "tp"),
            P(None, None, "tp"),
        ),
        out_specs=P(rows, "tp"),
        check_vma=False,
    )
```

```python
import functools

import jax
import jax.numpy as jnp
from jax import lax
from jax.experimental import pallas as pl
from jax.experimental.pallas import tpu as pltpu
from jax.sharding import Mesh, PartitionSpec as P

P_SIZE = 64
N = 128
CONV = 4
SPAN = 128
LANES = 128
RIM = 16
SEQ = ("chip", "core")
F32 = jnp.float32
BF16 = jnp.bfloat16
SMEM = pl.BlockSpec(memory_space=pltpu.SMEM)
VMEM = pl.BlockSpec(memory_space=pltpu.VMEM)


def call(kernel, name, out_shape, flops=0, moved=0, vmem=60, **settings):
    return pl.pallas_call(
        kernel,
        out_shape=out_shape,
        name=name,
        cost_estimate=pl.CostEstimate(flops=flops // 50, bytes_accessed=moved // 50, transcendentals=0),
        compiler_params=pltpu.CompilerParams(vmem_limit_bytes=vmem * 1024 * 1024),
        **settings,
    )


def swapped(part, axis, by=1):
    return lax.ppermute(part, axis, [(i, i ^ by) for i in range(lax.axis_size(axis))])


def cut_kernel(chips, at_ref, tokens_ref, far_ref, own_ref):
    depth = far_ref.shape[1] // (2 * chips)
    f_at, c_at = at_ref[0], at_ref[1]
    for out, f in ((far_ref, 1 - f_at), (own_ref, f_at)):
        for k, c in enumerate((c_at, 1 - c_at)):
            for i in range(chips):
                start = pl.multiple_of(((f * chips + at_ref[3 + i]) * 2 + c) * depth, depth)
                to = (k * chips + i) * depth
                out[:, to : to + depth] = tokens_ref[:, pl.ds(start, depth)]


def stack_kernel(at_ref, share, share_t, rows_ref):
    count = share.shape[0]
    rows_ref[pl.ds(pl.multiple_of(at_ref[2] * count, count), count), :] = share[...]
    rows_ref[pl.ds(pl.multiple_of((1 - at_ref[2]) * count, count), count), :] = share_t[...]


def token_rows(at, share, share_t):
    if share_t is None:
        return lax.all_gather(share, "tp", axis=0, tiled=True)
    shape = jax.ShapeDtypeStruct((2 * share.shape[0], share.shape[1]), BF16)
    return call(
        stack_kernel, "stack_rows", shape, moved=4 * shape.size, vmem=40, in_specs=[SMEM] + [VMEM] * 2, out_specs=VMEM
    )(at, share, share_t)


def sample_kernel(count, coef_ref, mean_ref, devs_ref, out_ref):
    factor = (2.0 * (count - 1)) ** (-0.5)
    accum = mean_ref[...].astype(F32)
    for member in range(count):
        accum = accum + factor * coef_ref[member] * devs_ref[member].astype(F32)
    out_ref[...] = accum.astype(BF16)


def sampled_cols(mean_part, dev_part, swag_coef, at, width):
    rows, count = mean_part.shape[0], dev_part.shape[0]
    tile = rows // 4
    return call(
        functools.partial(sample_kernel, count),
        "sample",
        jax.ShapeDtypeStruct((rows, width), BF16),
        moved=2 * (count + 2) * rows * width,
        grid=(4,),
        in_specs=[
            SMEM,
            pl.BlockSpec((tile, width), lambda i: (i, at)),
            pl.BlockSpec((count, tile, width), lambda i: (0, i, at)),
        ],
        out_specs=pl.BlockSpec((tile, width), lambda i: (i, 0)),
    )(swag_coef, mean_part, dev_part)


def sampled(mean_part, dev_part, swag_coef):
    factor = (2.0 * (dev_part.shape[0] - 1)) ** (-0.5)
    accum = mean_part.astype(F32)
    for member in range(dev_part.shape[0]):
        accum = accum + factor * swag_coef[member] * dev_part[member].astype(F32)
    return accum.astype(BF16)


def pack_kernel(bc_ref, dt_ref, out_ref):
    width, heads = bc_ref.shape[1], dt_ref.shape[1]
    out_ref[:, :width] = bc_ref[...]
    out_ref[:, width:] = jnp.zeros((out_ref.shape[0], LANES), BF16)
    out_ref[:, width : width + heads] = dt_ref[...]


def sent_straight(weight):
    return swapped(weight, "chip", 1), swapped(weight, "chip", 2)


def corner_halves(straight):
    half = straight[0].shape[0] // 2
    return straight[1][:half], straight[0][half:]


def sent_on(halves):
    return swapped(halves[0], "chip", 1), swapped(halves[1], "chip", 2)


def of_both_cores(pieces):
    return list(pieces) + [swapped(a, "core") for a in pieces]


def coded(part, heads):
    high = part.astype(BF16).astype(F32)
    return high + pltpu.roll(part - high, heads, 1)


def decoded(part, heads):
    return part + pltpu.roll(part, LANES - heads, 1)


def multiply_kernel(heads, with_steps, pieces, far_ref, own_ref, *refs):
    weights, (far_out, own_out) = refs[:pieces], refs[pieces:]
    totals = []
    for rows_ref in (far_ref, own_ref):
        at = 0
        total = None
        for weight in weights:
            depth = weight.shape[0]
            term = jnp.dot(rows_ref[:, at : at + depth], weight[...], preferred_element_type=F32)
            total = term if total is None else total + term
            at += depth
        totals.append(total)
    far_out[...] = totals[0].astype(BF16)
    own_out[...] = totals[1]
    if with_steps:
        @pl.when(pl.program_id(0) == pl.num_programs(0) - 1)
        def _():
            far_out[:, -LANES:] = coded(totals[0][:, -LANES:], heads).astype(BF16)


def multiplied(rows_far, rows_own, weights, heads, with_steps, first, width):
    tile = next(t for t in (256, 384, 128) if width % t == 0)
    col = first // tile
    rows = rows_far.shape[0]
    return call(
        functools.partial(multiply_kernel, heads, with_steps, len(weights)),
        "multiply",
        (jax.ShapeDtypeStruct((rows, width), BF16), jax.ShapeDtypeStruct((rows, width), F32)),
        flops=4 * rows_far.size * width,
        moved=4 * rows_far.size + 2 * rows_far.shape[1] * width + 6 * rows * width,
        vmem=40,
        grid=(width // tile,),
        in_specs=[pl.BlockSpec(rows_far.shape, lambda i: (0, 0))] * 2
        + [pl.BlockSpec((w.shape[0], tile), lambda i: (0, col + i)) for w in weights],
        out_specs=[pl.BlockSpec((rows, tile), lambda i: (0, i))] * 2,
    )(rows_far, rows_own, *weights)


def rim_kernel(kept, got, rim_ref):
    rim_ref[...] = (kept[...] + got[...].astype(F32)).astype(BF16)


def rows_before(kept, got):
    rows, width = kept.shape
    at = rows // RIM - 1
    rim = call(
        rim_kernel,
        "rim",
        jax.ShapeDtypeStruct((RIM, width), BF16),
        moved=10 * RIM * width,
        vmem=12,
        grid=(1,),
        in_specs=[pl.BlockSpec((RIM, width), lambda i: (at, 0))] * 2,
        out_specs=pl.BlockSpec((RIM, width), lambda i: (0, 0)),
    )(kept, got)
    return lax.ppermute(rim, SEQ, [(i, i + 1) for i in range(lax.axis_size(SEQ) - 1)])


def convolved(width, kept, got, rim, taps, padded):
    count = padded.shape[0] - 8
    proj = kept[:, :width] + got[:, :width].astype(F32)
    padded[8:, :] = proj.astype(BF16).astype(F32)
    padded[:8, :] = rim[:, :width].astype(F32)[RIM - 8 :]
    first = 8 - (CONV - 1)
    conv_sum = taps[0:1, :] * padded[first : first + count, :]
    for offset in range(1, CONV):
        conv_sum = conv_sum + taps[offset : offset + 1, :] * padded[first + offset : first + offset + count, :]
    return (conv_sum * jax.nn.sigmoid(conv_sum)).astype(BF16)


def state_proj_kernel(heads, kept, got, rim, taps, out_ref, logits_ref, padded):
    width = out_ref.shape[1]
    out_ref[...] = convolved(width, kept, got, rim, taps, padded)
    logits_ref[...] = kept[:, width:] + decoded(got[:, width:].astype(F32), heads)


def pairwise(columns, first):
    shape = (columns.shape[0], 2 * P_SIZE)
    lane = lax.broadcasted_iota(jnp.int32, shape, 1)
    return jnp.where(lane < P_SIZE, columns[:, first : first + 1], columns[:, first + 1 : first + 2])


def over_channels(columns):
    return jnp.concatenate([pairwise(columns, h) for h in range(0, columns.shape[1], 2)], axis=1)


def mix_kernel(
    kept, got, rim, taps, keys, reads, cum_g, steps_g, cum_t, steps_t, skip, y_ref, early_ref, total_ref, sent_ref, padded
):
    width = y_ref.shape[1]
    values = convolved(width, kept, got, rim, taps, padded)
    cum, steps = cum_g[0], steps_g[0]
    heads = cum.shape[1]
    row = lax.broadcasted_iota(jnp.int32, (SPAN, SPAN), 0)
    col = lax.broadcasted_iota(jnp.int32, (SPAN, SPAN), 1)
    causal = row >= col
    lane = lax.broadcasted_iota(jnp.int32, (SPAN, 2 * P_SIZE), 1)
    state = None
    for at in range(0, y_ref.shape[0], SPAN):
        span = slice(at, at + SPAN)
        keys_b, reads_b, values_b = keys[span, :], reads[span, :], values[span, :]
        cum_b, steps_b = cum[span, :], steps[span, :]
        last = cum_b[SPAN - 1 : SPAN, :]
        scores = lax.dot_general(reads_b, keys_b, (((1,), (1,)), ((), ())), preferred_element_type=F32)
        scores = jnp.where(causal, scores, 0.0)
        reach = jnp.exp(last - cum_b) * steps_b
        scaled = []
        for head in range(0, heads, 2):
            chans = slice(head * P_SIZE, (head + 2) * P_SIZE)
            two = []
            for h in (head, head + 1):
                gap = cum_b[:, h : h + 1] - cum_t[h : h + 1, span]
                two.append((scores * jnp.exp(jnp.minimum(gap, 0.0)) * steps_t[h : h + 1, span]).astype(BF16))
            values_h = values_b[:, chans]
            both = jnp.dot(jnp.concatenate(two, axis=0), values_h, preferred_element_type=F32)
            inner = jnp.where(lane < P_SIZE, both[:SPAN], both[SPAN:])
            wide = values_h.astype(F32)
            y_ref[span, chans] = inner + skip[0:1, chans] * wide
            scaled.append((wide * pairwise(reach, head)).astype(BF16))
        fresh = lax.dot_general(
            keys_b, jnp.concatenate(scaled, axis=1), (((0,), (0,)), ((), ())), preferred_element_type=F32
        )
        state = fresh if state is None else over_channels(jnp.exp(last)) * state + fresh
        if at + SPAN < y_ref.shape[0]:
            early_ref[at // SPAN] = fresh
    total_ref[...] = state
    sent_ref[...] = state.astype(BF16)


def combine_kernel(level, scales, total, other, before, total_ref, sent_ref, before_ref):
    gain, keep, take = (scales[3 * level + i : 3 * level + i + 1, :] for i in range(3))
    come = other[...].astype(F32)
    fresh = gain * come
    before_ref[...] = fresh if before is None else before[...] + fresh
    joint = keep * total[...] + take * come
    total_ref[...] = joint
    sent_ref[...] = joint.astype(BF16)


def read_kernel(level, y, reads, cum_g, early, scales, before, other, *refs):
    out_ref = refs[-1]
    state = before[...] + scales[3 * level : 3 * level + 1, :] * other[...].astype(F32)
    cum = cum_g[0]
    for at in range(0, out_ref.shape[0], SPAN):
        span = slice(at, at + SPAN)
        cum_b = cum[span, :]
        seen = jnp.dot(reads[span, :], state.astype(BF16), preferred_element_type=F32)
        out_ref[span, :] = (y[span, :] + over_channels(jnp.exp(cum_b)) * seen).astype(BF16)
        if at + SPAN < out_ref.shape[0]:
            state = over_channels(jnp.exp(cum_b[SPAN - 1 : SPAN, :])) * state + early[at // SPAN]


def prefix_scales(decay):
    place = lax.axis_index(SEQ)
    count = lax.axis_size(SEQ)
    before = jnp.ones_like(decay)
    total = decay
    rows = []
    by = 1
    while by < count:
        other = swapped(total, SEQ, by)
        upper = (place & by) != 0
        rows += [jnp.where(upper, before, 0.0), jnp.where(upper, 1.0, other), jnp.where(upper, total, 1.0)]
        before = jnp.where(upper, other * before, before)
        total = total * other
        by *= 2
    scales = jnp.stack(rows)
    return jnp.broadcast_to(scales[:, :, None], scales.shape + (P_SIZE,)).reshape(len(rows), -1)


def combined(level, scales, total, other, before, first):
    width, wide = total.shape[1], total.shape[1] // first[1]
    block = pl.BlockSpec((N, wide), lambda i: (0, i))
    kernel = functools.partial(combine_kernel, level)
    if before is None:
        kernel = lambda scales, total, other, *outs: combine_kernel(level, scales, total, other, None, *outs)
    return call(
        kernel,
        "combine",
        (
            jax.ShapeDtypeStruct(total.shape, F32),
            jax.ShapeDtypeStruct(total.shape, BF16),
            jax.ShapeDtypeStruct(total.shape, F32),
        ),
        flops=6 * total.size,
        moved=20 * total.size,
        vmem=12,
        grid=(first[1],),
        in_specs=[pl.BlockSpec((scales.shape[0], wide), lambda i: (0, first[0] + i))]
        + [block] * (2 if before is None else 3),
        out_specs=[block] * 3,
    )(scales, total, other, *(() if before is None else (before,)))


def body(
    tokens,
    proj_mean,
    proj_devs,
    bc_mean,
    bc_devs,
    swag_coef,
    dt_weight,
    dt_bias,
    decay_rate,
    skip_gain,
    conv_proj,
    conv_bc,
):
    heads_here = decay_rate.shape[0]
    groups_here = bc_mean.shape[2] // N
    per_group = heads_here // groups_here
    width_bc = 2 * bc_mean.shape[2]
    rows_k = proj_mean.shape[0]
    chips = lax.axis_size("chip")
    count = lax.axis_size(SEQ)

    def after(arrays, earlier):
        return lax.optimization_barrier((arrays, earlier))[0]

    width = per_group * P_SIZE
    early_groups = max(1, groups_here // 2)
    late = list(range(early_groups, groups_here))

    plane = chips == 4
    two_shares = lax.axis_size("tp") == 2
    place = lax.axis_index("chip") if plane else 0
    at = jnp.stack([lax.axis_index(a) for a in ("fsdp", "core", "tp")] + [place ^ i for i in range(chips)]).astype(jnp.int32)
    cut = jax.ShapeDtypeStruct((tokens.shape[0], tokens.shape[1] // 2), BF16)
    far, own = call(
        functools.partial(cut_kernel, chips),
        "cut_tokens",
        (cut,) * 2,
        moved=4 * tokens.size,
        in_specs=[SMEM, VMEM],
        out_specs=[VMEM] * 2,
    )(at, tokens)
    bc_mean, proj_mean = after((bc_mean, proj_mean), far)
    far = swapped(far, "fsdp")
    rows_own = token_rows(at, own, swapped(own, "tp") if two_shares else None)

    weight_bc = sampled(bc_mean, bc_devs, swag_coef).reshape(rows_k, width_bc)
    weight_bc = call(
        pack_kernel,
        "pack",
        jax.ShapeDtypeStruct((rows_k, width_bc + LANES), BF16),
        moved=4 * weight_bc.size,
        in_specs=[VMEM] * 2,
        out_specs=VMEM,
    )(weight_bc, dt_weight)
    weight_early = sampled_cols(proj_mean, proj_devs, swag_coef, 0, early_groups * width)
    if late:
        weight_late = sampled_cols(proj_mean, proj_devs, swag_coef, early_groups // len(late), len(late) * width)
    tok_count = rows_own.shape[0]
    blocks = tok_count // SPAN

    def times(pieces, with_steps, first, cols):
        return multiplied(rows_far, rows_own, pieces, heads_here, with_steps, first, cols)

    if plane:
        straight_bc = sent_straight(weight_bc)
        weight_early, weight_late = after((weight_early, weight_late), straight_bc)
        far, straight_bc = lax.optimization_barrier((far, straight_bc))
        halves_bc = corner_halves(straight_bc)
        far_t = swapped(far, "tp")
        on_bc = sent_on(halves_bc)
        weight_early, rows_own = after((weight_early, rows_own), (halves_bc, far))
        straight_early = sent_straight(weight_early)
        pieces_bc = of_both_cores((weight_bc, *straight_bc, *on_bc))
        far, far_t = after((far, far_t), rows_own)
        rows_far = token_rows(at, far, far_t)
    else:
        whole = lambda a: lax.all_gather(a, "chip", axis=0, tiled=True)
        pieces_bc, pieces_early = (of_both_cores((whole(a),)) for a in (weight_bc, weight_early))
        rows_far = token_rows(at, far, swapped(far, "tp") if two_shares else None)
        if late:
            pieces_late = of_both_cores((whole(weight_late),))
    back_bc, kept_bc = times(pieces_bc, True, 0, width_bc + LANES)
    got_bc = swapped(back_bc, "fsdp")
    if plane:
        straight_early, weight_late = after((straight_early, weight_late), back_bc)
        on_early = sent_on(corner_halves(straight_early))
        straight_late = sent_straight(after(weight_late, straight_early))
        pieces_early = of_both_cores((weight_early, *straight_early, *on_early))
    back, kept = times(pieces_early, False, 0, early_groups * width)
    got = swapped(after(back, got_bc), "fsdp")
    parts = [(kept, got)]
    if plane:
        straight_late = after(straight_late, (got_bc, back))
        pieces_late = of_both_cores((weight_late, *straight_late, *sent_on(corner_halves(straight_late))))
    backs = [times(pieces_late, False, i * width, width) for i in range(len(late))]

    rim_bc = rows_before(kept_bc, got_bc)
    specs_of = lambda width: [pl.BlockSpec((tok_count, width), lambda i: (0, i))] * 2 + [
        pl.BlockSpec((RIM, width), lambda i: (0, i)),
    ]
    whole_of = lambda *shape: pl.BlockSpec(shape, lambda i: (0,) * len(shape))
    conv_out, logits = call(
        functools.partial(state_proj_kernel, heads_here),
        "state_proj",
        (jax.ShapeDtypeStruct((tok_count, width_bc), BF16), jax.ShapeDtypeStruct((tok_count, LANES), F32)),
        moved=10 * tok_count * width_bc,
        grid=(1,),
        in_specs=specs_of(width_bc + LANES) + [whole_of(CONV, width_bc)],
        out_specs=[whole_of(tok_count, width_bc), whole_of(tok_count, LANES)],
        scratch_shapes=[pltpu.VMEM((tok_count + 8, width_bc), F32)],
    )(kept_bc, got_bc, rim_bc, conv_bc.reshape(CONV, width_bc))
    step_size = jax.nn.softplus(logits[:, :heads_here] + dt_bias)
    steps_b = step_size.reshape(blocks, SPAN, heads_here)
    cum_log = jnp.cumsum(-steps_b * decay_rate, axis=1)
    scales = prefix_scales(jnp.exp(jnp.sum(cum_log[:, SPAN - 1, :], axis=0)))
    cum_log = cum_log.reshape(tok_count, heads_here)
    cum_t, steps_t = cum_log.T, step_size.T
    by_group = lambda a: jnp.transpose(a.reshape(tok_count, groups_here, per_group), (1, 0, 2))
    cum_g, steps_g = by_group(cum_log), by_group(step_size)
    skip = jnp.repeat(skip_gain, P_SIZE)[None, :]
    levels = scales.shape[0] // 3

    result = None
    mixed = []
    for j, groups in enumerate([early_groups] + [1] * len(late)):
        first = early_groups + j - 1 if j else 0
        if j:
            back, kept = backs[j - 1]
            got = swapped(after(back, (parts[-1][1], mixed[j - 2] if j > 1 else (conv_out, cum_g, cum_t))), "fsdp")
            parts.append((kept, got))
        part = parts[j] + (rows_before(*parts[j]),)
        grid = (groups,)
        cols = lambda rows: pl.BlockSpec((rows, width), lambda i: (0, i))
        cols_all = lambda rows: pl.BlockSpec((rows, width), lambda i: (0, first + i))
        heads_g = pl.BlockSpec((1, tok_count, per_group), lambda i: (first + i, 0, 0))
        heads_t = pl.BlockSpec((per_group, tok_count), lambda i: (first + i, 0))
        keys = pl.BlockSpec((tok_count, N), lambda i: (0, first + i))
        reads = pl.BlockSpec((tok_count, N), lambda i: (0, groups_here + first + i))
        early_spec = pl.BlockSpec((blocks - 1, N, width), lambda i: (0, 0, i))
        y, early, total, sent = call(
            mix_kernel,
            "mix",
            (
                jax.ShapeDtypeStruct((tok_count, groups * width), F32),
                jax.ShapeDtypeStruct((blocks - 1, N, groups * width), F32),
                jax.ShapeDtypeStruct((N, groups * width), F32),
                jax.ShapeDtypeStruct((N, groups * width), BF16),
            ),
            flops=8 * tok_count * N * width * groups,
            moved=14 * tok_count * width * groups,
            grid=grid,
            in_specs=specs_of(width)
            + [cols_all(CONV), keys, reads, heads_g, heads_g, heads_t, heads_t, cols_all(1)],
            out_specs=[cols(tok_count), early_spec, cols(N), cols(N)],
            scratch_shapes=[pltpu.VMEM((tok_count + 8, width), F32)],
        )(*part, conv_proj, conv_out, conv_out, cum_g, steps_g, cum_t, steps_t, skip)
        mixed.append(sent)
        before = None
        for level in range(levels - 1):
            other = swapped(sent, SEQ, 1 << level)
            total, sent, before = combined(level, scales, total, other, before, (first, groups))
        other = swapped(sent, SEQ, 1 << (levels - 1))
        operands = [y, conv_out, cum_g, early, scales, before, other]
        specs = [cols(tok_count), reads, heads_g, early_spec, cols_all(scales.shape[0]), cols(N), cols(N)]
        alias = {}
        if result is not None:
            operands.append(result)
            specs.append(pl.BlockSpec(memory_space=pl.ANY))
            alias = {len(operands) - 1: 0}
        result = call(
            functools.partial(read_kernel, levels - 1),
            "read_out",
            jax.ShapeDtypeStruct((tok_count, heads_here * P_SIZE), BF16),
            flops=2 * tok_count * N * width * groups,
            moved=10 * tok_count * width * groups,
            vmem=12,
            grid=grid,
            in_specs=specs,
            out_specs=cols_all(tok_count),
            input_output_aliases=alias,
        )(*operands)
    return result


def solution(mesh):
    shape = mesh.shape
    split = Mesh(
        mesh.devices.reshape(shape["fsdp"], shape["seq"] // 2, 2, shape["tp"]),
        ("fsdp", "chip", "core", "tp"),
    )
    rows = ("fsdp", "chip", "core")
    return jax.shard_map(
        body,
        mesh=split,
        in_specs=(
            P(rows + ("tp",), None),
            P(rows, "tp"),
            P(None, rows, "tp"),
            P(rows, None, "tp"),
            P(None, rows, None, "tp"),
            P(),
            P(rows, "tp"),
            P("tp"),
            P("tp"),
            P("tp"),
            P(None, "tp"),
            P(None, None, "tp"),
        ),
        out_specs=P(rows, "tp"),
        check_vma=False,
    )
```

```python
import functools

import jax
import jax.numpy as jnp
from jax import lax
from jax.experimental import pallas as pl
from jax.experimental.pallas import tpu as pltpu
from jax.sharding import Mesh, PartitionSpec as P

P_SIZE = 64
N = 128
CONV = 4
SPAN = 128
LANES = 128
RIM = 16
SEQ = ("chip", "core")
F32 = jnp.float32
BF16 = jnp.bfloat16
SMEM = pl.BlockSpec(memory_space=pltpu.SMEM)
VMEM = pl.BlockSpec(memory_space=pltpu.VMEM)


def call(kernel, name, out_shape, flops=0, moved=0, vmem=60, **settings):
    return pl.pallas_call(
        kernel,
        out_shape=out_shape,
        name=name,
        cost_estimate=pl.CostEstimate(flops=flops // 50, bytes_accessed=moved // 50, transcendentals=0),
        compiler_params=pltpu.CompilerParams(vmem_limit_bytes=vmem * 1024 * 1024),
        **settings,
    )


def swapped(part, axis, by=1):
    return lax.ppermute(part, axis, [(i, i ^ by) for i in range(lax.axis_size(axis))])


def cut_kernel(chips, at_ref, tokens_ref, far_sent, far_kept, own_ref):
    depth = far_kept.shape[1] // chips
    rows = tokens_ref.shape[0]
    f_at, c_at = at_ref[0], at_ref[1]
    for i in range(chips):
        cols = slice(i * depth, (i + 1) * depth)

        def taken(f, c):
            start = pl.multiple_of(((f * chips + at_ref[3 + i]) * 2 + c) * depth, depth)
            return tokens_ref[:, pl.ds(start, depth)]

        far_sent[:, cols] = taken(1 - f_at, 1 - c_at)
        far_kept[:, cols] = taken(1 - f_at, c_at)
        own_ref[:rows, cols] = taken(f_at, c_at)
        own_ref[rows:, cols] = taken(f_at, 1 - c_at)


def stack_kernel(at_ref, *refs):
    pieces, rows_ref = refs[:-1], refs[-1]
    count = pieces[0].shape[0]
    for k in range(0, len(pieces), 2):
        rows_ref[pl.ds(pl.multiple_of((k + at_ref[2]) * count, count), count), :] = pieces[k][...]
        rows_ref[pl.ds(pl.multiple_of((k + 1 - at_ref[2]) * count, count), count), :] = pieces[k + 1][...]


def token_rows(at, kept, kept_t, got, got_t, own, own_t, own_c, own_tc):
    count, depth = kept.shape
    low = pl.BlockSpec((count, depth), lambda i: (0, 0))
    high = pl.BlockSpec((count, depth), lambda i: (1, 0))
    return call(
        stack_kernel,
        "stack_rows",
        jax.ShapeDtypeStruct((8 * count, depth), BF16),
        moved=32 * count * depth,
        vmem=40,
        grid=(1,),
        in_specs=[SMEM] + [low] * 6 + [high] * 2,
        out_specs=pl.BlockSpec((8 * count, depth), lambda i: (0, 0)),
    )(at, kept, kept_t, got, got_t, own, own_t, own_c, own_tc)


def sample_kernel(count, coef_ref, mean_ref, devs_ref, out_ref):
    factor = (2.0 * (count - 1)) ** (-0.5)
    accum = mean_ref[...].astype(F32)
    for member in range(count):
        accum = accum + factor * coef_ref[member] * devs_ref[member].astype(F32)
    out_ref[...] = accum.astype(BF16)


def sampled_cols(mean_part, dev_part, swag_coef, at, width):
    rows, count = mean_part.shape[0], dev_part.shape[0]
    tile = rows // 4
    return call(
        functools.partial(sample_kernel, count),
        "sample",
        jax.ShapeDtypeStruct((rows, width), BF16),
        moved=2 * (count + 2) * rows * width,
        grid=(4,),
        in_specs=[
            SMEM,
            pl.BlockSpec((tile, width), lambda i: (i, at)),
            pl.BlockSpec((count, tile, width), lambda i: (0, i, at)),
        ],
        out_specs=pl.BlockSpec((tile, width), lambda i: (i, 0)),
    )(swag_coef, mean_part, dev_part)


def sampled(mean_part, dev_part, swag_coef):
    factor = (2.0 * (dev_part.shape[0] - 1)) ** (-0.5)
    accum = mean_part.astype(F32)
    for member in range(dev_part.shape[0]):
        accum = accum + factor * swag_coef[member] * dev_part[member].astype(F32)
    return accum.astype(BF16)


def pack_kernel(bc_ref, dt_ref, out_ref):
    width, heads = bc_ref.shape[1], dt_ref.shape[1]
    out_ref[:, :width] = bc_ref[...]
    out_ref[:, width:] = jnp.zeros((out_ref.shape[0], LANES), BF16)
    out_ref[:, width : width + heads] = dt_ref[...]


def sent_straight(weight):
    return swapped(weight, "chip", 1), swapped(weight, "chip", 2)


def corner_halves(straight):
    half = straight[0].shape[0] // 2
    return straight[1][:half], straight[0][half:]


def sent_on(halves):
    return swapped(halves[0], "chip", 1), swapped(halves[1], "chip", 2)


def coded(part, heads):
    high = part.astype(BF16).astype(F32)
    return high + pltpu.roll(part - high, heads, 1)


def decoded(part, heads):
    return part + pltpu.roll(part, LANES - heads, 1)


def multiply_kernel(heads, with_steps, pieces, rows_ref, *refs):
    weights, (first_ref, second_ref, sent_ref, kept_ref) = refs[:pieces], refs[pieces:]
    at = 0
    total = None
    for weight in weights:
        depth = weight.shape[0]
        term = jnp.dot(rows_ref[:, at : at + depth], weight[...], preferred_element_type=F32)
        total = term if total is None else total + term
        at += depth
    half = total.shape[0] // 4
    kept_ref[0] = total[:half]
    kept_ref[1] = total[2 * half : 3 * half]
    for out, first in ((first_ref, half), (second_ref, half + half // 2), (sent_ref, 3 * half)):
        sent = total[first : first + out.shape[0]]
        out[...] = sent.astype(BF16)
        if with_steps:
            @pl.when(pl.program_id(0) == pl.num_programs(0) - 1)
            def _():
                out[:, -LANES:] = coded(sent[:, -LANES:], heads).astype(BF16)


def multiplied(rows, weights, heads, with_steps):
    width = weights[0].shape[1]
    tile = next(t for t in (256, 384, 128) if width % t == 0)
    half = rows.shape[0] // 4
    sent = lambda count: jax.ShapeDtypeStruct((count, width), BF16)
    return call(
        functools.partial(multiply_kernel, heads, with_steps, len(weights)),
        "multiply",
        (sent(half // 2), sent(half // 2), sent(half), jax.ShapeDtypeStruct((2, half, width), F32)),
        flops=2 * rows.size * width,
        moved=2 * rows.size + 2 * rows.shape[1] * width + 12 * half * width,
        grid=(width // tile,),
        in_specs=[pl.BlockSpec(rows.shape, lambda i: (0, 0))]
        + [pl.BlockSpec((w.shape[0], tile), lambda i: (0, i)) for w in weights],
        out_specs=[pl.BlockSpec((count, tile), lambda i: (0, i)) for count in (half // 2, half // 2, half)]
        + [pl.BlockSpec((2, half, tile), lambda i: (0, 0, i))],
    )(rows, *weights)


def relay_kernel(heads, with_steps, kept_ref, first_ref, second_ref, out_ref):
    half = first_ref.shape[0]
    for got_ref, rows in ((first_ref, slice(0, half)), (second_ref, slice(half, 2 * half))):
        kept, got = kept_ref[0, rows, :], got_ref[...].astype(F32)
        out_ref[rows, :] = (kept + got).astype(BF16)
        if with_steps:
            wide = kept[:, -LANES:] + decoded(got[:, -LANES:], heads)
            lane = lax.broadcasted_iota(jnp.int32, wide.shape, 1)
            out_ref[rows, -LANES:] = coded(jnp.where(lane < heads, wide, 0.0), heads).astype(BF16)


def relayed(kept, first, second, heads, with_steps):
    rows, width = kept.shape[1:]
    half = pl.BlockSpec((rows // 2, width), lambda i: (0, 0))
    return call(
        functools.partial(relay_kernel, heads, with_steps),
        "relay",
        jax.ShapeDtypeStruct((rows, width), BF16),
        moved=8 * rows * width,
        vmem=12,
        grid=(1,),
        in_specs=[pl.BlockSpec((1, rows, width), lambda i: (0, 0, 0)), half, half],
        out_specs=pl.BlockSpec((rows, width), lambda i: (0, 0)),
    )(kept, first, second)


def rim_kernel(kept, got_c, got_f, rim_ref):
    rim_ref[...] = (kept[0] + got_c[...].astype(F32) + got_f[...].astype(F32)).astype(BF16)


def rows_before(kept, got_c, got_f):
    rows, width = got_f.shape
    at = rows // RIM - 1
    rim = call(
        rim_kernel,
        "rim",
        jax.ShapeDtypeStruct((RIM, width), BF16),
        moved=10 * RIM * width,
        vmem=12,
        grid=(1,),
        in_specs=[pl.BlockSpec((1, RIM, width), lambda i: (1, at, 0))] + [pl.BlockSpec((RIM, width), lambda i: (at, 0))] * 2,
        out_specs=pl.BlockSpec((RIM, width), lambda i: (0, 0)),
    )(kept, got_c, got_f)
    return lax.ppermute(rim, SEQ, [(i, i + 1) for i in range(lax.axis_size(SEQ) - 1)])


def convolved(width, kept, got_c, got_f, rim, taps, padded):
    count = padded.shape[0] - 8
    proj = kept[0, :, :width] + got_c[:, :width].astype(F32) + got_f[:, :width].astype(F32)
    padded[8:, :] = proj.astype(BF16).astype(F32)
    padded[:8, :] = rim[:, :width].astype(F32)[RIM - 8 :]
    first = 8 - (CONV - 1)
    conv_sum = taps[0:1, :] * padded[first : first + count, :]
    for offset in range(1, CONV):
        conv_sum = conv_sum + taps[offset : offset + 1, :] * padded[first + offset : first + offset + count, :]
    return (conv_sum * jax.nn.sigmoid(conv_sum)).astype(BF16)


def state_proj_kernel(
    heads, kept, got_c, got_f, rim, taps, bias, rate, out_ref, cum_ref, steps_ref, cum_t_ref, steps_t_ref, decay_ref, padded
):
    count, width = out_ref.shape
    out_ref[...] = convolved(width, kept, got_c, got_f, rim, taps, padded)
    logits = kept[0, :, width:] + decoded(got_c[:, width:].astype(F32), heads) + decoded(got_f[:, width:].astype(F32), heads)
    steps = jax.nn.softplus(logits + bias[...])
    row = lax.broadcasted_iota(jnp.int32, (SPAN, SPAN), 0)
    col = lax.broadcasted_iota(jnp.int32, (SPAN, SPAN), 1)
    causal = jnp.where(row >= col, 1.0, 0.0)
    groups, per_group = cum_ref.shape[0], cum_ref.shape[2]
    through = jnp.zeros((1, LANES), F32)
    for at in range(0, count, SPAN):
        span = slice(at, at + SPAN)
        steps_b = steps[span, :]
        cum = jnp.dot(
            causal, -steps_b * rate[...], precision=lax.Precision.HIGHEST, preferred_element_type=F32
        )
        through = through + cum[SPAN - 1 : SPAN, :]
        cum_t_ref[:, span] = jnp.transpose(cum)[:heads]
        steps_t_ref[:, span] = jnp.transpose(steps_b)[:heads]
        for g in range(groups):
            cum_ref[g, span, :] = cum[:, g * per_group : (g + 1) * per_group]
            steps_ref[g, span, :] = steps_b[:, g * per_group : (g + 1) * per_group]
    decay_ref[...] = jnp.exp(through)[:, :heads]


def pairwise(columns, first):
    shape = (columns.shape[0], 2 * P_SIZE)
    lane = lax.broadcasted_iota(jnp.int32, shape, 1)
    return jnp.where(lane < P_SIZE, columns[:, first : first + 1], columns[:, first + 1 : first + 2])


def over_channels(columns):
    return jnp.concatenate([pairwise(columns, h) for h in range(0, columns.shape[1], 2)], axis=1)


def mix_kernel(
    kept, got_c, got_f, rim, taps, keys, reads, cum_g, steps_g, cum_t, steps_t, skip, y_ref, early_ref, total_ref, sent_ref, padded
):
    width = y_ref.shape[1]
    values = convolved(width, kept, got_c, got_f, rim, taps, padded)
    cum, steps = cum_g[0], steps_g[0]
    heads = cum.shape[1]
    row = lax.broadcasted_iota(jnp.int32, (SPAN, SPAN), 0)
    col = lax.broadcasted_iota(jnp.int32, (SPAN, SPAN), 1)
    causal = row >= col
    lane = lax.broadcasted_iota(jnp.int32, (SPAN, 2 * P_SIZE), 1)
    state = None
    for at in range(0, y_ref.shape[0], SPAN):
        span = slice(at, at + SPAN)
        keys_b, reads_b, values_b = keys[span, :], reads[span, :], values[span, :]
        cum_b, steps_b = cum[span, :], steps[span, :]
        last = cum_b[SPAN - 1 : SPAN, :]
        scores = lax.dot_general(reads_b, keys_b, (((1,), (1,)), ((), ())), preferred_element_type=F32)
        scores = jnp.where(causal, scores, 0.0)
        reach = jnp.exp(last - cum_b) * steps_b
        scaled = []
        for head in range(0, heads, 2):
            chans = slice(head * P_SIZE, (head + 2) * P_SIZE)
            two = []
            for h in (head, head + 1):
                gap = cum_b[:, h : h + 1] - cum_t[h : h + 1, span]
                two.append((scores * jnp.exp(jnp.minimum(gap, 0.0)) * steps_t[h : h + 1, span]).astype(BF16))
            values_h = values_b[:, chans]
            both = jnp.dot(jnp.concatenate(two, axis=0), values_h, preferred_element_type=F32)
            inner = jnp.where(lane < P_SIZE, both[:SPAN], both[SPAN:])
            wide = values_h.astype(F32)
            y_ref[span, chans] = inner + skip[0:1, chans] * wide
            scaled.append((wide * pairwise(reach, head)).astype(BF16))
        fresh = lax.dot_general(
            keys_b, jnp.concatenate(scaled, axis=1), (((0,), (0,)), ((), ())), preferred_element_type=F32
        )
        state = fresh if state is None else over_channels(jnp.exp(last)) * state + fresh
        if at + SPAN < y_ref.shape[0]:
            early_ref[at // SPAN] = fresh
    total_ref[...] = state
    sent_ref[...] = state.astype(BF16)


def combine_kernel(level, scales, total, other, before, total_ref, sent_ref, before_ref):
    gain, keep, take = (scales[3 * level + i : 3 * level + i + 1, :] for i in range(3))
    come = other[...].astype(F32)
    fresh = gain * come
    before_ref[...] = fresh if before is None else before[...] + fresh
    joint = keep * total[...] + take * come
    total_ref[...] = joint
    sent_ref[...] = joint.astype(BF16)


def read_kernel(level, y, reads, cum_g, early, scales, before, other, *refs):
    out_ref = refs[-1]
    state = before[...] + scales[3 * level : 3 * level + 1, :] * other[...].astype(F32)
    cum = cum_g[0]
    for at in range(0, out_ref.shape[0], SPAN):
        span = slice(at, at + SPAN)
        cum_b = cum[span, :]
        seen = jnp.dot(reads[span, :], state.astype(BF16), preferred_element_type=F32)
        out_ref[span, :] = (y[span, :] + over_channels(jnp.exp(cum_b)) * seen).astype(BF16)
        if at + SPAN < out_ref.shape[0]:
            state = over_channels(jnp.exp(cum_b[SPAN - 1 : SPAN, :])) * state + early[at // SPAN]


def prefix_scales(decay):
    place = lax.axis_index(SEQ)
    count = lax.axis_size(SEQ)
    before = jnp.ones_like(decay)
    total = decay
    rows = []
    by = 1
    while by < count:
        other = swapped(total, SEQ, by)
        upper = (place & by) != 0
        rows += [jnp.where(upper, before, 0.0), jnp.where(upper, 1.0, other), jnp.where(upper, total, 1.0)]
        before = jnp.where(upper, other * before, before)
        total = total * other
        by *= 2
    scales = jnp.stack(rows)
    return jnp.broadcast_to(scales[:, :, None], scales.shape + (P_SIZE,)).reshape(len(rows), -1)


def combined(level, scales, total, other, before, first):
    width, wide = total.shape[1], total.shape[1] // first[1]
    block = pl.BlockSpec((N, wide), lambda i: (0, i))
    kernel = functools.partial(combine_kernel, level)
    if before is None:
        kernel = lambda scales, total, other, *outs: combine_kernel(level, scales, total, other, None, *outs)
    return call(
        kernel,
        "combine",
        (
            jax.ShapeDtypeStruct(total.shape, F32),
            jax.ShapeDtypeStruct(total.shape, BF16),
            jax.ShapeDtypeStruct(total.shape, F32),
        ),
        flops=6 * total.size,
        moved=20 * total.size,
        vmem=12,
        grid=(first[1],),
        in_specs=[pl.BlockSpec((scales.shape[0], wide), lambda i: (0, first[0] + i))]
        + [block] * (2 if before is None else 3),
        out_specs=[block] * 3,
    )(scales, total, other, *(() if before is None else (before,)))


def body(
    tokens,
    proj_mean,
    proj_devs,
    bc_mean,
    bc_devs,
    swag_coef,
    dt_weight,
    dt_bias,
    decay_rate,
    skip_gain,
    conv_proj,
    conv_bc,
):
    heads_here = decay_rate.shape[0]
    groups_here = bc_mean.shape[2] // N
    per_group = heads_here // groups_here
    width_bc = 2 * bc_mean.shape[2]
    rows_k = proj_mean.shape[0]
    chips = lax.axis_size("chip")
    count = lax.axis_size(SEQ)

    def after(arrays, earlier):
        return lax.optimization_barrier((arrays, earlier))[0]

    width = per_group * P_SIZE
    early_groups = max(1, groups_here // 2)
    fill = -heads_here % LANES
    late = list(range(early_groups, groups_here))

    plane = chips == 4
    two_shares = lax.axis_size("tp") == 2
    place = lax.axis_index("chip") if plane else 0
    at = jnp.stack([lax.axis_index(a) for a in ("fsdp", "core", "tp")] + [place ^ i for i in range(chips)]).astype(jnp.int32)
    share, depth = tokens.shape[0], chips * rows_k
    cut = lambda rows: jax.ShapeDtypeStruct((rows, depth), BF16)
    far_sent, far_kept, own = call(
        functools.partial(cut_kernel, chips),
        "cut_tokens",
        (cut(share), cut(share), cut(2 * share)),
        moved=4 * tokens.size,
        in_specs=[SMEM, VMEM],
        out_specs=[VMEM] * 3,
    )(at, tokens)
    proj_mean = after(proj_mean, own)
    far_sent = swapped(far_sent, "fsdp")
    far_kept = swapped(after(far_kept, far_sent), "fsdp")
    bc_mean = after(bc_mean, far_sent)

    weight_early = sampled_cols(proj_mean, proj_devs, swag_coef, 0, early_groups * width)
    weight_bc = sampled(bc_mean, bc_devs, swag_coef).reshape(rows_k, width_bc)
    weight_bc = call(
        pack_kernel,
        "pack",
        jax.ShapeDtypeStruct((rows_k, width_bc + LANES), BF16),
        moved=4 * weight_bc.size,
        vmem=12,
        in_specs=[VMEM] * 2,
        out_specs=VMEM,
    )(weight_bc, dt_weight)
    weight_late = None
    if late:
        weight_late = sampled_cols(proj_mean, proj_devs, swag_coef, early_groups // len(late), len(late) * width)
    tok_count = share * lax.axis_size("tp")
    blocks = tok_count // SPAN

    def partial_sums(rows, pieces, with_steps, earlier=()):
        first, second, sent, kept = multiplied(rows, pieces, heads_here, with_steps)
        first, second = after((first, second), earlier)
        back = relayed(kept, swapped(first, "core"), swapped(second, "core"), heads_here, with_steps)
        return (kept, swapped(after(sent, back), "core")), back

    if plane and two_shares:
        early = [weight_early, *sent_straight(weight_early)]
        early += sent_on(corner_halves(early[1:]))
        own_t = swapped(own, "tp")
        own_c, own_tc = swapped(own, "core"), swapped(own_t, "core")
        far_sent = after(far_sent, own_t)
        sent_t = swapped(far_sent, "tp")
        got, got_t = swapped(far_sent, "core"), swapped(sent_t, "core")
        far_kept = after(far_kept, (own_c, own_tc, got_t, weight_late))
        kept_t = swapped(far_kept, "tp")
        weight_bc = after(weight_bc, (early[3:], far_kept))
        bc = [weight_bc, *sent_straight(weight_bc)]
        rows = token_rows(at, far_kept, kept_t, got, got_t, own, own_t, own_c, own_tc)
        part, back = partial_sums(rows, early, False)
        bc += sent_on(corner_halves(after(bc[1:], back)))
        got = swapped(back, "fsdp")
        weight_late = after(weight_late, (back, bc[3:]))
        part_bc, back_bc = partial_sums(rows, bc, True, got)
        got_bc = swapped(after(back_bc, got), "fsdp")
        straight = sent_straight(weight_late)
        corners = sent_on(after(corner_halves(straight), got))
        part_late, back_late = partial_sums(rows, after([weight_late, *straight, *corners], back_bc), False)
        got_late = swapped(after(back_late, got_bc), "fsdp")
        got_bc = after(got_bc, back_late)
    else:
        whole = lambda a, axis: lax.all_gather(a, axis, axis=0, tiled=True)
        ranges = [far_kept, swapped(far_sent, "core"), own[:share], swapped(own[share:], "core")]
        rows = jnp.concatenate([whole(r, "tp") for r in ranges], axis=0)
        part, back = partial_sums(rows, [whole(weight_early, "chip")], False)
        part_bc, back_bc = partial_sums(rows, [whole(weight_bc, "chip")], True)
        got, got_bc = swapped(back, "fsdp"), swapped(back_bc, "fsdp")
        if late:
            part_late, back_late = partial_sums(rows, [whole(weight_late, "chip")], False)
            got_late = swapped(back_late, "fsdp")
    parts = [part + (got,)]
    if late:
        parts.append(part_late + (got_late,))
    part_bc += (got_bc,)

    specs_of = lambda width: [pl.BlockSpec((1, tok_count, width), lambda i: (1, 0, i))] + [
        pl.BlockSpec((tok_count, width), lambda i: (0, i)),
        pl.BlockSpec((tok_count, width), lambda i: (0, i)),
        pl.BlockSpec((RIM, width), lambda i: (0, i)),
    ]
    whole_of = lambda *shape: pl.BlockSpec(shape, lambda i: (0,) * len(shape))
    by_group = (groups_here, tok_count, per_group)
    by_head = (heads_here, tok_count)
    conv_out, cum_g, steps_g, cum_t, steps_t, decay = call(
        functools.partial(state_proj_kernel, heads_here),
        "state_proj",
        (jax.ShapeDtypeStruct((tok_count, width_bc), BF16),)
        + tuple(jax.ShapeDtypeStruct(a, F32) for a in (by_group, by_group, by_head, by_head, (1, heads_here))),
        moved=10 * tok_count * width_bc,
        grid=(1,),
        in_specs=specs_of(width_bc + LANES) + [whole_of(CONV, width_bc)] + [whole_of(1, LANES)] * 2,
        out_specs=[whole_of(*a) for a in ((tok_count, width_bc), by_group, by_group, by_head, by_head, (1, heads_here))],
        scratch_shapes=[pltpu.VMEM((tok_count + 8, width_bc), F32)],
    )(*part_bc, rows_before(*part_bc), conv_bc.reshape(CONV, width_bc), jnp.pad(dt_bias, (0, fill))[None], jnp.pad(decay_rate, (0, fill))[None])
    scales = prefix_scales(decay[0])
    skip = jnp.repeat(skip_gain, P_SIZE)[None, :]
    levels = scales.shape[0] // 3

    result = None
    for first, groups, part in zip((0, early_groups), (early_groups, len(late)), parts):
        if first:
            part = after(part, first_total)
        part = part + (rows_before(*part),)
        grid = (groups,)
        cols = lambda rows: pl.BlockSpec((rows, width), lambda i: (0, i))
        cols_all = lambda rows: pl.BlockSpec((rows, width), lambda i: (0, first + i))
        heads_g = pl.BlockSpec((1, tok_count, per_group), lambda i: (first + i, 0, 0))
        heads_t = pl.BlockSpec((per_group, tok_count), lambda i: (first + i, 0))
        keys = pl.BlockSpec((tok_count, N), lambda i: (0, first + i))
        reads = pl.BlockSpec((tok_count, N), lambda i: (0, groups_here + first + i))
        early_spec = pl.BlockSpec((blocks - 1, N, width), lambda i: (0, 0, i))
        y, early, total, sent = call(
            mix_kernel,
            "mix",
            (
                jax.ShapeDtypeStruct((tok_count, groups * width), F32),
                jax.ShapeDtypeStruct((blocks - 1, N, groups * width), F32),
                jax.ShapeDtypeStruct((N, groups * width), F32),
                jax.ShapeDtypeStruct((N, groups * width), BF16),
            ),
            flops=8 * tok_count * N * width * groups,
            moved=14 * tok_count * width * groups,
            grid=grid,
            in_specs=specs_of(width)
            + [cols_all(CONV), keys, reads, heads_g, heads_g, heads_t, heads_t, cols_all(1)],
            out_specs=[cols(tok_count), early_spec, cols(N), cols(N)],
            scratch_shapes=[pltpu.VMEM((tok_count + 8, width), F32)],
        )(*part, conv_proj, conv_out, conv_out, cum_g, steps_g, cum_t, steps_t, skip)
        before = None
        first_total = total
        for level in range(levels - 1):
            other = swapped(sent, SEQ, 1 << level)
            total, sent, before = combined(level, scales, total, other, before, (first, groups))
        other = swapped(sent, SEQ, 1 << (levels - 1))
        operands = [y, conv_out, cum_g, early, scales, before, other]
        specs = [cols(tok_count), reads, heads_g, early_spec, cols_all(scales.shape[0]), cols(N), cols(N)]
        alias = {}
        if result is not None:
            operands.append(result)
            specs.append(pl.BlockSpec(memory_space=pl.ANY))
            alias = {len(operands) - 1: 0}
        result = call(
            functools.partial(read_kernel, levels - 1),
            "read_out",
            jax.ShapeDtypeStruct((tok_count, heads_here * P_SIZE), BF16),
            flops=2 * tok_count * N * width * groups,
            moved=10 * tok_count * width * groups,
            vmem=12,
            grid=grid,
            in_specs=specs,
            out_specs=cols_all(tok_count),
            input_output_aliases=alias,
        )(*operands)
    return result


def solution(mesh):
    shape = mesh.shape
    split = Mesh(
        mesh.devices.reshape(shape["fsdp"], shape["seq"] // 2, 2, shape["tp"]),
        ("fsdp", "chip", "core", "tp"),
    )
    rows = ("fsdp", "chip", "core")
    return jax.shard_map(
        body,
        mesh=split,
        in_specs=(
            P(rows + ("tp",), None),
            P(rows, "tp"),
            P(None, rows, "tp"),
            P(rows, None, "tp"),
            P(None, rows, None, "tp"),
            P(),
            P(rows, "tp"),
            P("tp"),
            P("tp"),
            P("tp"),
            P(None, "tp"),
            P(None, None, "tp"),
        ),
        out_specs=P(rows, "tp"),
        check_vma=False,
    )
```

```python
import functools

import jax
import jax.numpy as jnp
from jax import lax
from jax.experimental import pallas as pl
from jax.experimental.pallas import tpu as pltpu
from jax.sharding import Mesh, PartitionSpec as P

P_SIZE = 64
N = 128
CONV = 4
SPAN = 128
LANES = 128
RIM = 16
SEQ = ("chip", "core")
F32 = jnp.float32
BF16 = jnp.bfloat16
SMEM = pl.BlockSpec(memory_space=pltpu.SMEM)
VMEM = pl.BlockSpec(memory_space=pltpu.VMEM)


def call(kernel, name, out_shape, flops=0, moved=0, vmem=60, **settings):
    return pl.pallas_call(
        kernel,
        out_shape=out_shape,
        name=name,
        cost_estimate=pl.CostEstimate(flops=flops // 50, bytes_accessed=moved // 50, transcendentals=0),
        compiler_params=pltpu.CompilerParams(vmem_limit_bytes=vmem * 1024 * 1024),
        **settings,
    )


def swapped(part, axis, by=1):
    return lax.ppermute(part, axis, [(i, i ^ by) for i in range(lax.axis_size(axis))])


def cut_kernel(chips, at_ref, tokens_ref, far_sent, far_kept, own_ref):
    depth = far_kept.shape[1] // chips
    rows = tokens_ref.shape[0]
    f_at, c_at = at_ref[0], at_ref[1]
    for i in range(chips):
        cols = slice(i * depth, (i + 1) * depth)

        def taken(f, c):
            start = pl.multiple_of(((f * chips + at_ref[3 + i]) * 2 + c) * depth, depth)
            return tokens_ref[:, pl.ds(start, depth)]

        far_sent[:, cols] = taken(1 - f_at, 1 - c_at)
        far_kept[:, cols] = taken(1 - f_at, c_at)
        own_ref[:rows, cols] = taken(f_at, c_at)
        own_ref[rows:, cols] = taken(f_at, 1 - c_at)


def stack_kernel(at_ref, *refs):
    pieces, rows_ref = refs[:-1], refs[-1]
    count = pieces[0].shape[0]
    for k in range(0, len(pieces), 2):
        rows_ref[pl.ds(pl.multiple_of((k + at_ref[2]) * count, count), count), :] = pieces[k][...]
        rows_ref[pl.ds(pl.multiple_of((k + 1 - at_ref[2]) * count, count), count), :] = pieces[k + 1][...]


def token_rows(at, kept, kept_t, got, got_t, own, own_t, own_c, own_tc):
    count, depth = kept.shape
    low = pl.BlockSpec((count, depth), lambda i: (0, 0))
    high = pl.BlockSpec((count, depth), lambda i: (1, 0))
    return call(
        stack_kernel,
        "stack_rows",
        jax.ShapeDtypeStruct((8 * count, depth), BF16),
        moved=32 * count * depth,
        vmem=40,
        grid=(1,),
        in_specs=[SMEM] + [low] * 6 + [high] * 2,
        out_specs=pl.BlockSpec((8 * count, depth), lambda i: (0, 0)),
    )(at, kept, kept_t, got, got_t, own, own_t, own_c, own_tc)


def sample_kernel(count, coef_ref, mean_ref, devs_ref, out_ref):
    factor = (2.0 * (count - 1)) ** (-0.5)
    accum = mean_ref[...].astype(F32)
    for member in range(count):
        accum = accum + factor * coef_ref[member] * devs_ref[member].astype(F32)
    out_ref[...] = accum.astype(BF16)


def sampled_cols(mean_part, dev_part, swag_coef, at, width):
    rows, count = mean_part.shape[0], dev_part.shape[0]
    tile = rows // 4
    return call(
        functools.partial(sample_kernel, count),
        "sample",
        jax.ShapeDtypeStruct((rows, width), BF16),
        moved=2 * (count + 2) * rows * width,
        grid=(4,),
        in_specs=[
            SMEM,
            pl.BlockSpec((tile, width), lambda i: (i, at)),
            pl.BlockSpec((count, tile, width), lambda i: (0, i, at)),
        ],
        out_specs=pl.BlockSpec((tile, width), lambda i: (i, 0)),
    )(swag_coef, mean_part, dev_part)


def sampled(mean_part, dev_part, swag_coef):
    factor = (2.0 * (dev_part.shape[0] - 1)) ** (-0.5)
    accum = mean_part.astype(F32)
    for member in range(dev_part.shape[0]):
        accum = accum + factor * swag_coef[member] * dev_part[member].astype(F32)
    return accum.astype(BF16)


def pack_kernel(bc_ref, dt_ref, out_ref):
    width, heads = bc_ref.shape[1], dt_ref.shape[1]
    out_ref[:, :width] = bc_ref[...]
    out_ref[:, width:] = jnp.zeros((out_ref.shape[0], LANES), BF16)
    out_ref[:, width : width + heads] = dt_ref[...]


def sent_straight(weight):
    return swapped(weight, "chip", 1), swapped(weight, "chip", 2)


def corner_parts(straight, each):
    rows = straight[0].shape[0] // (2 * each)
    cut = lambda a, i: a[i * rows : (i + 1) * rows]
    return [cut(straight[1], i) for i in range(each)] + [cut(straight[0], each + i) for i in range(each)]


def sent_on(parts):
    each = len(parts) // 2
    return [swapped(a, "chip", 1) for a in parts[:each]] + [swapped(a, "chip", 2) for a in parts[each:]]


def coded(part, heads):
    high = part.astype(BF16).astype(F32)
    return high + pltpu.roll(part - high, heads, 1)


def decoded(part, heads):
    return part + pltpu.roll(part, LANES - heads, 1)


def multiply_kernel(heads, with_steps, pieces, rows_ref, *refs):
    weights, (first_ref, second_ref, sent_ref, kept_ref) = refs[:pieces], refs[pieces:]
    joined = jnp.concatenate([weight[...] for weight in weights], axis=0)
    total = jnp.dot(rows_ref[...], joined, preferred_element_type=F32)
    half = total.shape[0] // 4
    kept_ref[0] = total[:half]
    kept_ref[1] = total[2 * half : 3 * half]
    for out, first in ((first_ref, half), (second_ref, half + half // 2), (sent_ref, 3 * half)):
        sent = total[first : first + out.shape[0]]
        out[...] = sent.astype(BF16)
        if with_steps:
            @pl.when(pl.program_id(0) == pl.num_programs(0) - 1)
            def _():
                out[:, -LANES:] = coded(sent[:, -LANES:], heads).astype(BF16)


def multiplied(rows, weights, heads, with_steps):
    width = weights[0].shape[1]
    tile = next(t for t in (512, 384, 128) if width % t == 0)
    half = rows.shape[0] // 4
    sent = lambda count: jax.ShapeDtypeStruct((count, width), BF16)
    return call(
        functools.partial(multiply_kernel, heads, with_steps, len(weights)),
        "multiply",
        (sent(half // 2), sent(half // 2), sent(half), jax.ShapeDtypeStruct((2, half, width), F32)),
        flops=2 * rows.size * width,
        moved=2 * rows.size + 2 * rows.shape[1] * width + 12 * half * width,
        grid=(width // tile,),
        in_specs=[pl.BlockSpec(rows.shape, lambda i: (0, 0))]
        + [pl.BlockSpec((w.shape[0], tile), lambda i: (0, i)) for w in weights],
        out_specs=[pl.BlockSpec((count, tile), lambda i: (0, i)) for count in (half // 2, half // 2, half)]
        + [pl.BlockSpec((2, half, tile), lambda i: (0, 0, i))],
    )(rows, *weights)


def relay_kernel(heads, with_steps, kept_ref, first_ref, second_ref, out_ref):
    half = first_ref.shape[0]
    for got_ref, rows in ((first_ref, slice(0, half)), (second_ref, slice(half, 2 * half))):
        kept, got = kept_ref[0, rows, :], got_ref[...].astype(F32)
        out_ref[rows, :] = (kept + got).astype(BF16)
        if with_steps:
            wide = kept[:, -LANES:] + decoded(got[:, -LANES:], heads)
            lane = lax.broadcasted_iota(jnp.int32, wide.shape, 1)
            out_ref[rows, -LANES:] = coded(jnp.where(lane < heads, wide, 0.0), heads).astype(BF16)


def relayed(kept, first, second, heads, with_steps):
    rows, width = kept.shape[1:]
    half = pl.BlockSpec((rows // 2, width), lambda i: (0, 0))
    return call(
        functools.partial(relay_kernel, heads, with_steps),
        "relay",
        jax.ShapeDtypeStruct((rows, width), BF16),
        moved=8 * rows * width,
        vmem=12,
        grid=(1,),
        in_specs=[pl.BlockSpec((1, rows, width), lambda i: (0, 0, 0)), half, half],
        out_specs=pl.BlockSpec((rows, width), lambda i: (0, 0)),
    )(kept, first, second)


def rim_kernel(kept, got_c, got_f, rim_ref):
    rim_ref[...] = (kept[0] + got_c[...].astype(F32) + got_f[...].astype(F32)).astype(BF16)


def rows_before(kept, got_c, got_f):
    rows, width = got_f.shape
    at = rows // RIM - 1
    rim = call(
        rim_kernel,
        "rim",
        jax.ShapeDtypeStruct((RIM, width), BF16),
        moved=10 * RIM * width,
        vmem=12,
        grid=(1,),
        in_specs=[pl.BlockSpec((1, RIM, width), lambda i: (1, at, 0))] + [pl.BlockSpec((RIM, width), lambda i: (at, 0))] * 2,
        out_specs=pl.BlockSpec((RIM, width), lambda i: (0, 0)),
    )(kept, got_c, got_f)
    return lax.ppermute(rim, SEQ, [(i, i + 1) for i in range(lax.axis_size(SEQ) - 1)])


def convolved(width, kept, got_c, got_f, rim, taps, padded):
    count = padded.shape[0] - 8
    proj = kept[0, :, :width] + got_c[:, :width].astype(F32) + got_f[:, :width].astype(F32)
    padded[8:, :] = proj.astype(BF16).astype(F32)
    padded[:8, :] = rim[:, :width].astype(F32)[RIM - 8 :]
    first = 8 - (CONV - 1)
    conv_sum = taps[0:1, :] * padded[first : first + count, :]
    for offset in range(1, CONV):
        conv_sum = conv_sum + taps[offset : offset + 1, :] * padded[first + offset : first + offset + count, :]
    return (conv_sum * jax.nn.sigmoid(conv_sum)).astype(BF16)


def state_proj_kernel(
    heads, kept, got_c, got_f, rim, taps, bias, rate, out_ref, cum_ref, steps_ref, cum_t_ref, steps_t_ref, decay_ref, padded
):
    count, width = out_ref.shape
    out_ref[...] = convolved(width, kept, got_c, got_f, rim, taps, padded)
    logits = kept[0, :, width:] + decoded(got_c[:, width:].astype(F32), heads) + decoded(got_f[:, width:].astype(F32), heads)
    steps = jax.nn.softplus(logits[:, :heads] + bias[...])
    row = lax.broadcasted_iota(jnp.int32, (SPAN, SPAN), 0)
    col = lax.broadcasted_iota(jnp.int32, (SPAN, SPAN), 1)
    causal = jnp.where(row >= col, 1.0, 0.0)
    groups, per_group = cum_ref.shape[0], cum_ref.shape[2]
    through = jnp.zeros((1, heads), F32)
    for at in range(0, count, SPAN):
        span = slice(at, at + SPAN)
        steps_b = steps[span, :]
        cum = jnp.dot(
            causal, -steps_b * rate[...], precision=lax.Precision.HIGHEST, preferred_element_type=F32
        )
        through = through + cum[SPAN - 1 : SPAN, :]
        cum_t_ref[:, span] = jnp.transpose(cum)
        steps_t_ref[:, span] = jnp.transpose(steps_b)
        for g in range(groups):
            cum_ref[g, span, :] = cum[:, g * per_group : (g + 1) * per_group]
            steps_ref[g, span, :] = steps_b[:, g * per_group : (g + 1) * per_group]
    for g in range(groups):
        decay_ref[g] = jnp.exp(through)[:, g * per_group : (g + 1) * per_group]


def pairwise(columns, first):
    shape = (columns.shape[0], 2 * P_SIZE)
    lane = lax.broadcasted_iota(jnp.int32, shape, 1)
    return jnp.where(lane < P_SIZE, columns[:, first : first + 1], columns[:, first + 1 : first + 2])


def over_channels(columns):
    return jnp.concatenate([pairwise(columns, h) for h in range(0, columns.shape[1], 2)], axis=1)


def mix_kernel(
    kept, got_c, got_f, rim, taps, keys, reads, cum_g, steps_g, cum_t, steps_t, skip, decay, y_ref, early_ref, total_ref, decays_ref, sent_ref, padded
):
    width = y_ref.shape[1]
    values = convolved(width, kept, got_c, got_f, rim, taps, padded)
    cum, steps = cum_g[0], steps_g[0]
    heads = cum.shape[1]
    row = lax.broadcasted_iota(jnp.int32, (SPAN, SPAN), 0)
    col = lax.broadcasted_iota(jnp.int32, (SPAN, SPAN), 1)
    causal = row >= col
    lane = lax.broadcasted_iota(jnp.int32, (SPAN, 2 * P_SIZE), 1)
    gain = over_channels(skip[0])
    state = None
    for at in range(0, y_ref.shape[0], SPAN):
        span = slice(at, at + SPAN)
        keys_b, reads_b, values_b = keys[span, :], reads[span, :], values[span, :]
        cum_b, steps_b = cum[span, :], steps[span, :]
        last = cum_b[SPAN - 1 : SPAN, :]
        scores = lax.dot_general(reads_b, keys_b, (((1,), (1,)), ((), ())), preferred_element_type=F32)
        scores = jnp.where(causal, scores, 0.0)
        reach = jnp.exp(last - cum_b) * steps_b
        scaled = []
        for head in range(0, heads, 2):
            chans = slice(head * P_SIZE, (head + 2) * P_SIZE)
            two = []
            for h in (head, head + 1):
                gap = cum_b[:, h : h + 1] - cum_t[h : h + 1, span]
                two.append((scores * jnp.exp(jnp.minimum(gap, 0.0)) * steps_t[h : h + 1, span]).astype(BF16))
            values_h = values_b[:, chans]
            both = jnp.dot(jnp.concatenate(two, axis=0), values_h, preferred_element_type=F32)
            inner = jnp.where(lane < P_SIZE, both[:SPAN], both[SPAN:])
            wide = values_h.astype(F32)
            y_ref[span, chans] = inner + gain[:, chans] * wide
            scaled.append((wide * pairwise(reach, head)).astype(BF16))
        fresh = lax.dot_general(
            keys_b, jnp.concatenate(scaled, axis=1), (((0,), (0,)), ((), ())), preferred_element_type=F32
        )
        state = fresh if state is None else over_channels(jnp.exp(last)) * state + fresh
        if at + SPAN < y_ref.shape[0]:
            early_ref[at // SPAN] = fresh
    total_ref[...] = state
    wide = over_channels(decay[0])
    decays_ref[0:1, :] = wide
    decays_ref[1:2, :] = jnp.ones_like(wide)
    pack_state(sent_ref, state, wide)


def pack_state(sent_ref, state, decay):
    sent_ref[:N, :] = state.astype(BF16)
    high = decay.astype(BF16).astype(F32)
    row = lax.broadcasted_iota(jnp.int32, (RIM, decay.shape[1]), 0)
    sent_ref[N:, :] = jnp.where(row == 0, high, jnp.where(row == 1, decay - high, 0.0)).astype(BF16)


def unpack_state(got_ref):
    rows = got_ref[N:, :].astype(F32)
    return got_ref[:N, :].astype(F32), rows[0:1, :] + rows[1:2, :]


def combine_kernel(level, place_ref, total, decays, other, *refs):
    before, (total_ref, decays_ref, sent_ref, before_ref) = refs[:-4], refs[-4:]
    come, decay = unpack_state(other)
    whole, part = decays[0:1, :], decays[1:2, :]
    upper = (place_ref[0] >> level) & 1 == 1
    fresh = jnp.where(upper, part, 0.0) * come
    before_ref[...] = before[0][...] + fresh if before else fresh
    joint = jnp.where(upper, 1.0, decay) * total[...] + jnp.where(upper, whole, 1.0) * come
    total_ref[...] = joint
    decays_ref[0:1, :] = whole * decay
    decays_ref[1:2, :] = jnp.where(upper, decay * part, part)
    pack_state(sent_ref, joint, whole * decay)


def read_kernel(level, place_ref, y, reads, cum_g, early, decays, before, other, *refs):
    out_ref = refs[-1]
    upper = (place_ref[0] >> level) & 1 == 1
    state = before[...] + jnp.where(upper, decays[1:2, :], 0.0) * unpack_state(other)[0]
    cum = cum_g[0]
    for at in range(0, out_ref.shape[0], SPAN):
        span = slice(at, at + SPAN)
        cum_b = cum[span, :]
        seen = jnp.dot(reads[span, :], state.astype(BF16), preferred_element_type=F32)
        out_ref[span, :] = (y[span, :] + over_channels(jnp.exp(cum_b)) * seen).astype(BF16)
        if at + SPAN < out_ref.shape[0]:
            state = over_channels(jnp.exp(cum_b[SPAN - 1 : SPAN, :])) * state + early[at // SPAN]


def combined(level, place, total, decays, other, before, groups):
    width = total.shape[1] // groups
    block = lambda rows: pl.BlockSpec((rows, width), lambda i: (0, i))
    shape = lambda rows, dtype: jax.ShapeDtypeStruct((rows, total.shape[1]), dtype)
    return call(
        functools.partial(combine_kernel, level),
        "combine",
        (shape(N, F32), shape(8, F32), shape(N + RIM, BF16), shape(N, F32)),
        flops=6 * total.size,
        moved=20 * total.size,
        vmem=12,
        grid=(groups,),
        in_specs=[SMEM, block(N), block(8), block(N + RIM)] + [block(N)] * len(before),
        out_specs=[block(N), block(8), block(N + RIM), block(N)],
    )(place, total, decays, other, *before)


def body(
    tokens,
    proj_mean,
    proj_devs,
    bc_mean,
    bc_devs,
    swag_coef,
    dt_weight,
    dt_bias,
    decay_rate,
    skip_gain,
    conv_proj,
    conv_bc,
):
    heads_here = decay_rate.shape[0]
    groups_here = bc_mean.shape[2] // N
    per_group = heads_here // groups_here
    width_bc = 2 * bc_mean.shape[2]
    rows_k = proj_mean.shape[0]
    chips = lax.axis_size("chip")
    count = lax.axis_size(SEQ)

    def after(arrays, earlier):
        return lax.optimization_barrier((arrays, earlier))[0]

    width = per_group * P_SIZE
    early_groups = max(1, groups_here // 2)
    fill = -heads_here % LANES
    late = list(range(early_groups, groups_here))

    plane = chips == 4
    two_shares = lax.axis_size("tp") == 2
    place = lax.axis_index("chip") if plane else 0
    at = jnp.stack([lax.axis_index(a) for a in ("fsdp", "core", "tp")] + [place ^ i for i in range(chips)]).astype(jnp.int32)
    share, depth = tokens.shape[0], chips * rows_k
    cut = lambda rows: jax.ShapeDtypeStruct((rows, depth), BF16)
    far_sent, far_kept, own = call(
        functools.partial(cut_kernel, chips),
        "cut_tokens",
        (cut(share), cut(share), cut(2 * share)),
        moved=4 * tokens.size,
        in_specs=[SMEM, VMEM],
        out_specs=[VMEM] * 3,
    )(at, tokens)
    proj_mean = after(proj_mean, own)
    far_sent = swapped(far_sent, "fsdp")
    far_kept = swapped(after(far_kept, far_sent), "fsdp")
    bc_mean = after(bc_mean, far_sent)

    weight_early = sampled_cols(proj_mean, proj_devs, swag_coef, 0, early_groups * width)
    weight_bc = sampled(bc_mean, bc_devs, swag_coef).reshape(rows_k, width_bc)
    weight_bc = call(
        pack_kernel,
        "pack",
        jax.ShapeDtypeStruct((rows_k, width_bc + LANES), BF16),
        moved=4 * weight_bc.size,
        vmem=12,
        in_specs=[VMEM] * 2,
        out_specs=VMEM,
    )(weight_bc, dt_weight)
    weight_late = None
    if late:
        weight_late = sampled_cols(proj_mean, proj_devs, swag_coef, early_groups // len(late), len(late) * width)
    tok_count = share * lax.axis_size("tp")
    blocks = tok_count // SPAN

    def partial_sums(rows, pieces, with_steps, earlier=()):
        first, second, sent, kept = multiplied(rows, pieces, heads_here, with_steps)
        first, second = after((first, second), earlier)
        back = relayed(kept, swapped(first, "core"), swapped(second, "core"), heads_here, with_steps)
        return (kept, swapped(after(sent, back), "core")), back

    if plane and two_shares:
        early = [weight_early, *sent_straight(weight_early)]
        early += sent_on(corner_parts(early[1:], 1))
        own_t = swapped(own, "tp")
        far_sent = after(far_sent, own_t)
        sent_t = swapped(far_sent, "tp")
        got, got_t = swapped(far_sent, "core"), swapped(sent_t, "core")
        far_kept = after(far_kept, (got_t, weight_bc, weight_late))
        own, own_t = after((own, own_t), far_kept)
        own_c, own_tc = swapped(own, "core"), swapped(own_t, "core")
        kept_t = swapped(far_kept, "tp")
        weight_bc = after(weight_bc, (early[3:], far_kept))
        bc = [weight_bc, *sent_straight(weight_bc)]
        rows = token_rows(at, far_kept, kept_t, got, got_t, own, own_t, own_c, own_tc)
        part, back = partial_sums(rows, early, False)
        bc += sent_on(corner_parts(after(bc[1:], back), 1))
        got = swapped(back, "fsdp")
        weight_late = after(weight_late, (back, bc[1:3]))
        part_bc, back_bc = partial_sums(rows, bc, True, got)
        got_bc = swapped(after(back_bc, got), "fsdp")
        straight = sent_straight(weight_late)
        corners = sent_on(after(corner_parts(straight, 2), back_bc))
        part_late, back_late = partial_sums(rows, after([weight_late, *straight, *corners], back_bc), False)
        got_late = swapped(after(back_late, got_bc), "fsdp")
        got_bc = after(got_bc, back_late)
    else:
        whole = lambda a, axis: lax.all_gather(a, axis, axis=0, tiled=True)
        ranges = [far_kept, swapped(far_sent, "core"), own[:share], swapped(own[share:], "core")]
        rows = jnp.concatenate([whole(r, "tp") for r in ranges], axis=0)
        part, back = partial_sums(rows, [whole(weight_early, "chip")], False)
        part_bc, back_bc = partial_sums(rows, [whole(weight_bc, "chip")], True)
        got, got_bc = swapped(back, "fsdp"), swapped(back_bc, "fsdp")
        if late:
            part_late, back_late = partial_sums(rows, [whole(weight_late, "chip")], False)
            got_late = swapped(back_late, "fsdp")
    parts = [part + (got,)]
    if late:
        parts.append(part_late + (got_late,))
    part_bc += (got_bc,)

    specs_of = lambda width: [pl.BlockSpec((1, tok_count, width), lambda i: (1, 0, i))] + [
        pl.BlockSpec((tok_count, width), lambda i: (0, i)),
        pl.BlockSpec((tok_count, width), lambda i: (0, i)),
        pl.BlockSpec((RIM, width), lambda i: (0, i)),
    ]
    whole_of = lambda *shape: pl.BlockSpec(shape, lambda i: (0,) * len(shape))
    by_group = (groups_here, tok_count, per_group)
    by_head = (heads_here, tok_count)
    by_decay = (groups_here, 1, per_group)
    conv_out, cum_g, steps_g, cum_t, steps_t, decay = call(
        functools.partial(state_proj_kernel, heads_here),
        "state_proj",
        (jax.ShapeDtypeStruct((tok_count, width_bc), BF16),)
        + tuple(jax.ShapeDtypeStruct(a, F32) for a in (by_group, by_group, by_head, by_head, by_decay)),
        moved=10 * tok_count * width_bc,
        grid=(1,),
        in_specs=specs_of(width_bc + LANES) + [whole_of(CONV, width_bc)] + [whole_of(1, heads_here)] * 2,
        out_specs=[whole_of(*a) for a in ((tok_count, width_bc), by_group, by_group, by_head, by_head, by_decay)],
        scratch_shapes=[pltpu.VMEM((tok_count + 8, width_bc), F32)],
    )(*part_bc, rows_before(*part_bc), conv_bc.reshape(CONV, width_bc), dt_bias[None], decay_rate[None])
    skip = skip_gain.reshape(by_decay)
    levels = count.bit_length() - 1
    seq_place = (2 * lax.axis_index("chip") + lax.axis_index("core")).astype(jnp.int32).reshape(1)

    result = None
    for first, groups, part in zip((0, early_groups), (early_groups, len(late)), parts):
        if first:
            part = after(part, first_total)
        part = part + (rows_before(*part),)
        grid = (groups,)
        cols = lambda rows: pl.BlockSpec((rows, width), lambda i: (0, i))
        cols_all = lambda rows: pl.BlockSpec((rows, width), lambda i: (0, first + i))
        heads_g = pl.BlockSpec((1, tok_count, per_group), lambda i: (first + i, 0, 0))
        heads_t = pl.BlockSpec((per_group, tok_count), lambda i: (first + i, 0))
        heads_1 = pl.BlockSpec((1, 1, per_group), lambda i: (first + i, 0, 0))
        keys = pl.BlockSpec((tok_count, N), lambda i: (0, first + i))
        reads = pl.BlockSpec((tok_count, N), lambda i: (0, groups_here + first + i))
        early_spec = pl.BlockSpec((blocks - 1, N, width), lambda i: (0, 0, i))
        y, early, total, decays, sent = call(
            mix_kernel,
            "mix",
            (
                jax.ShapeDtypeStruct((tok_count, groups * width), F32),
                jax.ShapeDtypeStruct((blocks - 1, N, groups * width), F32),
                jax.ShapeDtypeStruct((N, groups * width), F32),
                jax.ShapeDtypeStruct((8, groups * width), F32),
                jax.ShapeDtypeStruct((N + RIM, groups * width), BF16),
            ),
            flops=8 * tok_count * N * width * groups,
            moved=14 * tok_count * width * groups,
            grid=grid,
            in_specs=specs_of(width) + [cols_all(CONV), keys, reads, heads_g, heads_g, heads_t, heads_t, heads_1, heads_1],
            out_specs=[cols(tok_count), early_spec, cols(N), cols(8), cols(N + RIM)],
            scratch_shapes=[pltpu.VMEM((tok_count + 8, width), F32)],
        )(*part, conv_proj, conv_out, conv_out, cum_g, steps_g, cum_t, steps_t, skip, decay)
        before = ()
        first_total = None
        for level in range(levels - 1):
            other = swapped(sent, SEQ, 1 << level)
            total, decays, sent, fresh = combined(level, seq_place, total, decays, other, before, groups)
            before = (fresh,)
            first_total = total if first_total is None else first_total
        other = swapped(sent, SEQ, 1 << (levels - 1))
        operands = [seq_place, y, conv_out, cum_g, early, decays, *before, other]
        specs = [SMEM, cols(tok_count), reads, heads_g, early_spec, cols(8), cols(N), cols(N + RIM)]
        alias = {}
        if result is not None:
            operands.append(result)
            specs.append(pl.BlockSpec(memory_space=pl.ANY))
            alias = {len(operands) - 1: 0}
        result = call(
            functools.partial(read_kernel, levels - 1),
            "read_out",
            jax.ShapeDtypeStruct((tok_count, heads_here * P_SIZE), BF16),
            flops=2 * tok_count * N * width * groups,
            moved=10 * tok_count * width * groups,
            vmem=12,
            grid=grid,
            in_specs=specs,
            out_specs=cols_all(tok_count),
            input_output_aliases=alias,
        )(*operands)
    return result


def solution(mesh):
    shape = mesh.shape
    split = Mesh(
        mesh.devices.reshape(shape["fsdp"], shape["seq"] // 2, 2, shape["tp"]),
        ("fsdp", "chip", "core", "tp"),
    )
    rows = ("fsdp", "chip", "core")
    return jax.shard_map(
        body,
        mesh=split,
        in_specs=(
            P(rows + ("tp",), None),
            P(rows, "tp"),
            P(None, rows, "tp"),
            P(rows, None, "tp"),
            P(None, rows, None, "tp"),
            P(),
            P(rows, "tp"),
            P("tp"),
            P("tp"),
            P("tp"),
            P(None, "tp"),
            P(None, None, "tp"),
        ),
        out_specs=P(rows, "tp"),
        check_vma=False,
    )
```

```python
import functools

import jax
import jax.numpy as jnp
from jax import lax
from jax.experimental import pallas as pl
from jax.experimental.pallas import tpu as pltpu
from jax.sharding import Mesh, PartitionSpec as P

P_SIZE = 64
N = 128
CONV = 4
SPAN = 128
LANES = 128
RIM = 16
SEQ = ("chip", "core")
F32 = jnp.float32
BF16 = jnp.bfloat16
SMEM = pl.BlockSpec(memory_space=pltpu.SMEM)
VMEM = pl.BlockSpec(memory_space=pltpu.VMEM)


def call(kernel, name, out_shape, flops=0, moved=0, vmem=60, **settings):
    return pl.pallas_call(
        kernel,
        out_shape=out_shape,
        name=name,
        cost_estimate=pl.CostEstimate(flops=flops // 50, bytes_accessed=moved // 50, transcendentals=0),
        compiler_params=pltpu.CompilerParams(vmem_limit_bytes=vmem * 1024 * 1024),
        **settings,
    )


def swapped(part, axis, by=1):
    return lax.ppermute(part, axis, [(i, i ^ by) for i in range(lax.axis_size(axis))])


def cut_kernel(chips, at_ref, tokens_ref, far_sent, far_kept, own_ref):
    depth = far_kept.shape[1] // chips
    rows = tokens_ref.shape[0]
    f_at, c_at = at_ref[0], at_ref[1]
    for i in range(chips):
        cols = slice(i * depth, (i + 1) * depth)

        def taken(f, c):
            start = pl.multiple_of(((f * chips + at_ref[3 + i]) * 2 + c) * depth, depth)
            return tokens_ref[:, pl.ds(start, depth)]

        far_sent[:, cols] = taken(1 - f_at, 1 - c_at)
        far_kept[:, cols] = taken(1 - f_at, c_at)
        own_ref[:rows, cols] = taken(f_at, c_at)
        own_ref[rows:, cols] = taken(f_at, 1 - c_at)


def stack_kernel(at_ref, *refs):
    pieces, rows_ref = refs[:-1], refs[-1]
    count = pieces[0].shape[0]
    for k in range(0, len(pieces), 2):
        rows_ref[pl.ds(pl.multiple_of((k + at_ref[2]) * count, count), count), :] = pieces[k][...]
        rows_ref[pl.ds(pl.multiple_of((k + 1 - at_ref[2]) * count, count), count), :] = pieces[k + 1][...]


def token_rows(at, kept, kept_t, got, got_t, own, own_t, own_c, own_tc):
    count, depth = kept.shape
    low = pl.BlockSpec((count, depth), lambda i: (0, 0))
    high = pl.BlockSpec((count, depth), lambda i: (1, 0))
    return call(
        stack_kernel,
        "stack_rows",
        jax.ShapeDtypeStruct((8 * count, depth), BF16),
        moved=32 * count * depth,
        vmem=40,
        grid=(1,),
        in_specs=[SMEM] + [low] * 6 + [high] * 2,
        out_specs=pl.BlockSpec((8 * count, depth), lambda i: (0, 0)),
    )(at, kept, kept_t, got, got_t, own, own_t, own_c, own_tc)


def sample_kernel(count, coef_ref, mean_ref, devs_ref, out_ref):
    factor = (2.0 * (count - 1)) ** (-0.5)
    accum = mean_ref[...].astype(F32)
    for member in range(count):
        accum = accum + factor * coef_ref[member] * devs_ref[member].astype(F32)
    out_ref[...] = accum.astype(BF16)


def sampled_cols(mean_part, dev_part, swag_coef, at, width):
    rows, count = mean_part.shape[0], dev_part.shape[0]
    tile = rows // 4
    return call(
        functools.partial(sample_kernel, count),
        "sample",
        jax.ShapeDtypeStruct((rows, width), BF16),
        moved=2 * (count + 2) * rows * width,
        grid=(4,),
        in_specs=[
            SMEM,
            pl.BlockSpec((tile, width), lambda i: (i, at)),
            pl.BlockSpec((count, tile, width), lambda i: (0, i, at)),
        ],
        out_specs=pl.BlockSpec((tile, width), lambda i: (i, 0)),
    )(swag_coef, mean_part, dev_part)


def sample_pair_kernel(count, coef_ref, mean_ref, devs_ref, dt_ref, out_ref):
    factor = (2.0 * (count - 1)) ** (-0.5)
    accum = mean_ref[...].astype(F32)
    for member in range(count):
        accum = accum + factor * coef_ref[member] * devs_ref[member].astype(F32)
    width, heads = mean_ref.shape[2], dt_ref.shape[1]
    for k in range(2):
        out_ref[:, k * width : (k + 1) * width] = accum[:, k, :].astype(BF16)
    out_ref[:, 2 * width :] = jnp.zeros((out_ref.shape[0], LANES), BF16)
    out_ref[:, 2 * width : 2 * width + heads] = dt_ref[...]


def sampled_pair(mean_part, dev_part, dt_part, swag_coef):
    rows, _, width = mean_part.shape
    count = dev_part.shape[0]
    tile = rows // 8
    return call(
        functools.partial(sample_pair_kernel, count),
        "sample_pair",
        jax.ShapeDtypeStruct((rows, 2 * width + LANES), BF16),
        moved=4 * (count + 2) * rows * width,
        grid=(8,),
        in_specs=[
            SMEM,
            pl.BlockSpec((tile, 2, width), lambda i: (i, 0, 0)),
            pl.BlockSpec((count, tile, 2, width), lambda i: (0, i, 0, 0)),
            pl.BlockSpec((tile, dt_part.shape[1]), lambda i: (i, 0)),
        ],
        out_specs=pl.BlockSpec((tile, 2 * width + LANES), lambda i: (i, 0)),
    )(swag_coef, mean_part, dev_part, dt_part)


def sent_straight(weight):
    return swapped(weight, "chip", 1), swapped(weight, "chip", 2)


def corner_parts(straight, each):
    rows = straight[0].shape[0] // (2 * each)
    cut = lambda a, i: a[i * rows : (i + 1) * rows]
    return [cut(straight[1], i) for i in range(each)] + [cut(straight[0], each + i) for i in range(each)]


def sent_on(parts):
    each = len(parts) // 2
    return [swapped(a, "chip", 1) for a in parts[:each]] + [swapped(a, "chip", 2) for a in parts[each:]]


def coded(part, heads):
    high = part.astype(BF16).astype(F32)
    return high + pltpu.roll(part - high, heads, 1)


def decoded(part, heads):
    return part + pltpu.roll(part, LANES - heads, 1)


def multiply_kernel(heads, with_steps, pieces, rows_ref, *refs):
    weights, (first_ref, second_ref, sent_ref, kept_ref) = refs[:pieces], refs[pieces:]
    joined = jnp.concatenate([weight[...] for weight in weights], axis=0)
    total = jnp.dot(rows_ref[...], joined, preferred_element_type=F32)
    half = total.shape[0] // 4
    kept_ref[0] = total[:half]
    kept_ref[1] = total[2 * half : 3 * half]
    for out, first in ((first_ref, half), (second_ref, half + half // 2), (sent_ref, 3 * half)):
        sent = total[first : first + out.shape[0]]
        out[...] = sent.astype(BF16)
        if with_steps:
            @pl.when(pl.program_id(0) == pl.num_programs(0) - 1)
            def _():
                out[:, -LANES:] = coded(sent[:, -LANES:], heads).astype(BF16)


def multiplied(rows, weights, heads, with_steps):
    width = weights[0].shape[1]
    tile = next(t for t in (512, 384, 128) if width % t == 0)
    half = rows.shape[0] // 4
    sent = lambda count: jax.ShapeDtypeStruct((count, width), BF16)
    return call(
        functools.partial(multiply_kernel, heads, with_steps, len(weights)),
        "multiply",
        (sent(half // 2), sent(half // 2), sent(half), jax.ShapeDtypeStruct((2, half, width), F32)),
        flops=2 * rows.size * width,
        moved=2 * rows.size + 2 * rows.shape[1] * width + 12 * half * width,
        grid=(width // tile,),
        in_specs=[pl.BlockSpec(rows.shape, lambda i: (0, 0))]
        + [pl.BlockSpec((w.shape[0], tile), lambda i: (0, i)) for w in weights],
        out_specs=[pl.BlockSpec((count, tile), lambda i: (0, i)) for count in (half // 2, half // 2, half)]
        + [pl.BlockSpec((2, half, tile), lambda i: (0, 0, i))],
    )(rows, *weights)


def relay_kernel(heads, with_steps, kept_ref, first_ref, second_ref, out_ref):
    half = first_ref.shape[0]
    for got_ref, rows in ((first_ref, slice(0, half)), (second_ref, slice(half, 2 * half))):
        kept, got = kept_ref[0, rows, :], got_ref[...].astype(F32)
        out_ref[rows, :] = (kept + got).astype(BF16)
        if with_steps:
            wide = kept[:, -LANES:] + decoded(got[:, -LANES:], heads)
            lane = lax.broadcasted_iota(jnp.int32, wide.shape, 1)
            out_ref[rows, -LANES:] = coded(jnp.where(lane < heads, wide, 0.0), heads).astype(BF16)


def relayed(kept, first, second, heads, with_steps):
    rows, width = kept.shape[1:]
    half = pl.BlockSpec((rows // 2, width), lambda i: (0, 0))
    return call(
        functools.partial(relay_kernel, heads, with_steps),
        "relay",
        jax.ShapeDtypeStruct((rows, width), BF16),
        moved=8 * rows * width,
        vmem=12,
        grid=(1,),
        in_specs=[pl.BlockSpec((1, rows, width), lambda i: (0, 0, 0)), half, half],
        out_specs=pl.BlockSpec((rows, width), lambda i: (0, 0)),
    )(kept, first, second)


def rim_kernel(kept, got_c, got_f, rim_ref):
    rim_ref[...] = (kept[0] + got_c[...].astype(F32) + got_f[...].astype(F32)).astype(BF16)


def rows_before(kept, got_c, got_f):
    rows, width = got_f.shape
    at = rows // RIM - 1
    rim = call(
        rim_kernel,
        "rim",
        jax.ShapeDtypeStruct((RIM, width), BF16),
        moved=10 * RIM * width,
        vmem=12,
        grid=(1,),
        in_specs=[pl.BlockSpec((1, RIM, width), lambda i: (1, at, 0))] + [pl.BlockSpec((RIM, width), lambda i: (at, 0))] * 2,
        out_specs=pl.BlockSpec((RIM, width), lambda i: (0, 0)),
    )(kept, got_c, got_f)
    return lax.ppermute(rim, SEQ, [(i, i + 1) for i in range(lax.axis_size(SEQ) - 1)])


def convolved(width, kept, got_c, got_f, rim, taps, padded):
    count = padded.shape[0] - 8
    proj = kept[0, :, :width] + got_c[:, :width].astype(F32) + got_f[:, :width].astype(F32)
    padded[8:, :] = proj.astype(BF16).astype(F32)
    padded[:8, :] = rim[:, :width].astype(F32)[RIM - 8 :]
    first = 8 - (CONV - 1)
    conv_sum = taps[0:1, :] * padded[first : first + count, :]
    for offset in range(1, CONV):
        conv_sum = conv_sum + taps[offset : offset + 1, :] * padded[first + offset : first + offset + count, :]
    return (conv_sum * jax.nn.sigmoid(conv_sum)).astype(BF16)


def state_proj_kernel(
    heads, kept, got_c, got_f, rim, taps, bias, rate, out_ref, cum_ref, steps_ref, cum_t_ref, steps_t_ref, decay_ref, padded
):
    count, width = out_ref.shape
    out_ref[...] = convolved(width, kept, got_c, got_f, rim, taps, padded)
    logits = kept[0, :, width:] + decoded(got_c[:, width:].astype(F32), heads) + decoded(got_f[:, width:].astype(F32), heads)
    steps = jax.nn.softplus(logits[:, :heads] + bias[...])
    row = lax.broadcasted_iota(jnp.int32, (SPAN, SPAN), 0)
    col = lax.broadcasted_iota(jnp.int32, (SPAN, SPAN), 1)
    causal = jnp.where(row >= col, 1.0, 0.0)
    groups, per_group = cum_ref.shape[0], cum_ref.shape[2]
    through = jnp.zeros((1, heads), F32)
    for at in range(0, count, SPAN):
        span = slice(at, at + SPAN)
        steps_b = steps[span, :]
        cum = jnp.dot(
            causal, -steps_b * rate[...], precision=lax.Precision.HIGHEST, preferred_element_type=F32
        )
        through = through + cum[SPAN - 1 : SPAN, :]
        cum_t_ref[:, span] = jnp.transpose(cum)
        steps_t_ref[:, span] = jnp.transpose(steps_b)
        for g in range(groups):
            cum_ref[g, span, :] = cum[:, g * per_group : (g + 1) * per_group]
            steps_ref[g, span, :] = steps_b[:, g * per_group : (g + 1) * per_group]
    for g in range(groups):
        decay_ref[g] = jnp.exp(through)[:, g * per_group : (g + 1) * per_group]


def pairwise(columns, first):
    shape = (columns.shape[0], 2 * P_SIZE)
    lane = lax.broadcasted_iota(jnp.int32, shape, 1)
    return jnp.where(lane < P_SIZE, columns[:, first : first + 1], columns[:, first + 1 : first + 2])


def over_channels(columns):
    return jnp.concatenate([pairwise(columns, h) for h in range(0, columns.shape[1], 2)], axis=1)


def mix_kernel(
    kept, got_c, got_f, rim, taps, keys, reads, cum_g, steps_g, cum_t, steps_t, skip, decay, y_ref, early_ref, total_ref, decays_ref, sent_ref, padded
):
    width = y_ref.shape[1]
    values = convolved(width, kept, got_c, got_f, rim, taps, padded)
    cum, steps = cum_g[0], steps_g[0]
    heads = cum.shape[1]
    row = lax.broadcasted_iota(jnp.int32, (SPAN, SPAN), 0)
    col = lax.broadcasted_iota(jnp.int32, (SPAN, SPAN), 1)
    causal = row >= col
    lane = lax.broadcasted_iota(jnp.int32, (SPAN, 2 * P_SIZE), 1)
    gain = over_channels(skip[0])
    state = None
    for at in range(0, y_ref.shape[0], SPAN):
        span = slice(at, at + SPAN)
        keys_b, reads_b, values_b = keys[span, :], reads[span, :], values[span, :]
        cum_b, steps_b = cum[span, :], steps[span, :]
        last = cum_b[SPAN - 1 : SPAN, :]
        scores = lax.dot_general(reads_b, keys_b, (((1,), (1,)), ((), ())), preferred_element_type=F32)
        scores = jnp.where(causal, scores, 0.0)
        reach = jnp.exp(last - cum_b) * steps_b
        scaled = []
        for head in range(0, heads, 2):
            chans = slice(head * P_SIZE, (head + 2) * P_SIZE)
            two = []
            for h in (head, head + 1):
                gap = cum_b[:, h : h + 1] - cum_t[h : h + 1, span]
                two.append((scores * jnp.exp(jnp.minimum(gap, 0.0)) * steps_t[h : h + 1, span]).astype(BF16))
            values_h = values_b[:, chans]
            both = jnp.dot(jnp.concatenate(two, axis=0), values_h, preferred_element_type=F32)
            inner = jnp.where(lane < P_SIZE, both[:SPAN], both[SPAN:])
            wide = values_h.astype(F32)
            y_ref[span, chans] = inner + gain[:, chans] * wide
            scaled.append((wide * pairwise(reach, head)).astype(BF16))
        fresh = lax.dot_general(
            keys_b, jnp.concatenate(scaled, axis=1), (((0,), (0,)), ((), ())), preferred_element_type=F32
        )
        state = fresh if state is None else over_channels(jnp.exp(last)) * state + fresh
        if at + SPAN < y_ref.shape[0]:
            early_ref[at // SPAN] = fresh
    total_ref[...] = state
    wide = over_channels(decay[0])
    decays_ref[0:1, :] = wide
    decays_ref[1:2, :] = jnp.ones_like(wide)
    pack_state(sent_ref, state, wide)


def pack_state(sent_ref, state, decay):
    sent_ref[:N, :] = state.astype(BF16)
    high = decay.astype(BF16).astype(F32)
    row = lax.broadcasted_iota(jnp.int32, (RIM, decay.shape[1]), 0)
    sent_ref[N:, :] = jnp.where(row == 0, high, jnp.where(row == 1, decay - high, 0.0)).astype(BF16)


def unpack_state(got_ref):
    rows = got_ref[N:, :].astype(F32)
    return got_ref[:N, :].astype(F32), rows[0:1, :] + rows[1:2, :]


def combine_kernel(level, place_ref, total, decays, other, *refs):
    before, (total_ref, decays_ref, sent_ref, before_ref) = refs[:-4], refs[-4:]
    come, decay = unpack_state(other)
    whole, part = decays[0:1, :], decays[1:2, :]
    upper = (place_ref[0] >> level) & 1 == 1
    fresh = jnp.where(upper, part, 0.0) * come
    before_ref[...] = before[0][...] + fresh if before else fresh
    joint = jnp.where(upper, 1.0, decay) * total[...] + jnp.where(upper, whole, 1.0) * come
    total_ref[...] = joint
    decays_ref[0:1, :] = whole * decay
    decays_ref[1:2, :] = jnp.where(upper, decay * part, part)
    pack_state(sent_ref, joint, whole * decay)


def read_kernel(level, place_ref, y, reads, cum_g, early, decays, before, other, *refs):
    out_ref = refs[-1]
    upper = (place_ref[0] >> level) & 1 == 1
    state = before[...] + jnp.where(upper, decays[1:2, :], 0.0) * unpack_state(other)[0]
    cum = cum_g[0]
    for at in range(0, out_ref.shape[0], SPAN):
        span = slice(at, at + SPAN)
        cum_b = cum[span, :]
        seen = jnp.dot(reads[span, :], state.astype(BF16), preferred_element_type=F32)
        out_ref[span, :] = (y[span, :] + over_channels(jnp.exp(cum_b)) * seen).astype(BF16)
        if at + SPAN < out_ref.shape[0]:
            state = over_channels(jnp.exp(cum_b[SPAN - 1 : SPAN, :])) * state + early[at // SPAN]


def combined(level, place, total, decays, other, before, groups):
    width = total.shape[1] // groups
    block = lambda rows: pl.BlockSpec((rows, width), lambda i: (0, i))
    shape = lambda rows, dtype: jax.ShapeDtypeStruct((rows, total.shape[1]), dtype)
    return call(
        functools.partial(combine_kernel, level),
        "combine",
        (shape(N, F32), shape(8, F32), shape(N + RIM, BF16), shape(N, F32)),
        flops=6 * total.size,
        moved=20 * total.size,
        vmem=12,
        grid=(groups,),
        in_specs=[SMEM, block(N), block(8), block(N + RIM)] + [block(N)] * len(before),
        out_specs=[block(N), block(8), block(N + RIM), block(N)],
    )(place, total, decays, other, *before)


def body(
    tokens,
    proj_mean,
    proj_devs,
    bc_mean,
    bc_devs,
    swag_coef,
    dt_weight,
    dt_bias,
    decay_rate,
    skip_gain,
    conv_proj,
    conv_bc,
):
    heads_here = decay_rate.shape[0]
    groups_here = bc_mean.shape[2] // N
    per_group = heads_here // groups_here
    width_bc = 2 * bc_mean.shape[2]
    rows_k = proj_mean.shape[0]
    chips = lax.axis_size("chip")
    count = lax.axis_size(SEQ)

    def after(arrays, earlier):
        return lax.optimization_barrier((arrays, earlier))[0]

    width = per_group * P_SIZE
    early_groups = max(1, groups_here // 2)
    fill = -heads_here % LANES
    late = list(range(early_groups, groups_here))

    plane = chips == 4
    two_shares = lax.axis_size("tp") == 2
    place = lax.axis_index("chip") if plane else 0
    at = jnp.stack([lax.axis_index(a) for a in ("fsdp", "core", "tp")] + [place ^ i for i in range(chips)]).astype(jnp.int32)
    share, depth = tokens.shape[0], chips * rows_k
    cut = lambda rows: jax.ShapeDtypeStruct((rows, depth), BF16)
    far_sent, far_kept, own = call(
        functools.partial(cut_kernel, chips),
        "cut_tokens",
        (cut(share), cut(share), cut(2 * share)),
        moved=4 * tokens.size,
        in_specs=[SMEM, VMEM],
        out_specs=[VMEM] * 3,
    )(at, tokens)
    proj_mean, bc_mean = after((proj_mean, bc_mean), own)
    far_sent = swapped(far_sent, "fsdp")
    far_kept = swapped(after(far_kept, far_sent), "fsdp")

    weight_early = sampled_cols(proj_mean, proj_devs, swag_coef, 0, early_groups * width)
    weight_bc = sampled_pair(bc_mean, bc_devs, dt_weight, swag_coef)
    weight_late = None
    if late:
        weight_late = sampled_cols(proj_mean, proj_devs, swag_coef, early_groups // len(late), len(late) * width)
    tok_count = share * lax.axis_size("tp")
    blocks = tok_count // SPAN

    def partial_sums(rows, pieces, with_steps, earlier=()):
        first, second, sent, kept = multiplied(rows, pieces, heads_here, with_steps)
        first, second = after((first, second), earlier)
        back = relayed(kept, swapped(first, "core"), swapped(second, "core"), heads_here, with_steps)
        return (kept, swapped(after(sent, back), "core")), back

    specs_of = lambda width: [pl.BlockSpec((1, tok_count, width), lambda i: (1, 0, i))] + [
        pl.BlockSpec((tok_count, width), lambda i: (0, i)),
        pl.BlockSpec((tok_count, width), lambda i: (0, i)),
        pl.BlockSpec((RIM, width), lambda i: (0, i)),
    ]
    whole_of = lambda *shape: pl.BlockSpec(shape, lambda i: (0,) * len(shape))
    by_group = (groups_here, tok_count, per_group)
    by_head = (heads_here, tok_count)
    by_decay = (groups_here, 1, per_group)
    state_proj = lambda part: call(
        functools.partial(state_proj_kernel, heads_here),
        "state_proj",
        (jax.ShapeDtypeStruct((tok_count, width_bc), BF16),)
        + tuple(jax.ShapeDtypeStruct(a, F32) for a in (by_group, by_group, by_head, by_head, by_decay)),
        moved=10 * tok_count * width_bc,
        grid=(1,),
        in_specs=specs_of(width_bc + LANES) + [whole_of(CONV, width_bc)] + [whole_of(1, heads_here)] * 2,
        out_specs=[whole_of(*a) for a in ((tok_count, width_bc), by_group, by_group, by_head, by_head, by_decay)],
        scratch_shapes=[pltpu.VMEM((tok_count + 8, width_bc), F32)],
    )(*part, rows_before(*part), conv_bc.reshape(CONV, width_bc), dt_bias[None], decay_rate[None])
    if plane and two_shares:
        bc = [weight_bc, *sent_straight(weight_bc)]
        bc += sent_on(corner_parts(bc[1:], 1))
        own_t = swapped(own, "tp")
        far_sent = after(far_sent, (own_t, weight_early, weight_late))
        sent_t = swapped(far_sent, "tp")
        got, got_t = swapped(far_sent, "core"), swapped(sent_t, "core")
        far_kept = after(far_kept, got_t)
        own, own_t = after((own, own_t), far_kept)
        own_c, own_tc = swapped(own, "core"), swapped(own_t, "core")
        kept_t = swapped(far_kept, "tp")
        weight_early = after(weight_early, (bc[3:], far_kept))
        early = [weight_early, *sent_straight(weight_early)]
        rows = token_rows(at, far_kept, kept_t, got, got_t, own, own_t, own_c, own_tc)
        part_bc, back_bc = partial_sums(rows, bc, True)
        early += sent_on(corner_parts(after(early[1:], back_bc), 1))
        got_bc = swapped(back_bc, "fsdp")
        weight_late = after(weight_late, (back_bc, early[1:3]))
        part, back = partial_sums(rows, early, False, got_bc)
        got = swapped(after(back, got_bc), "fsdp")
        straight = sent_straight(weight_late)
        seen = state_proj(after(part_bc + (got_bc,), back))
        corners = sent_on(after(corner_parts(straight, 2), back))
        part_late, back_late = partial_sums(rows, after([weight_late, *straight, *corners], seen), False)
        got_late = swapped(after(back_late, got), "fsdp")
        got = after(got, back_late)
    else:
        whole = lambda a, axis: lax.all_gather(a, axis, axis=0, tiled=True)
        ranges = [far_kept, swapped(far_sent, "core"), own[:share], swapped(own[share:], "core")]
        rows = jnp.concatenate([whole(r, "tp") for r in ranges], axis=0)
        part, back = partial_sums(rows, [whole(weight_early, "chip")], False)
        part_bc, back_bc = partial_sums(rows, [whole(weight_bc, "chip")], True)
        got, got_bc = swapped(back, "fsdp"), swapped(back_bc, "fsdp")
        if late:
            part_late, back_late = partial_sums(rows, [whole(weight_late, "chip")], False)
            got_late = swapped(back_late, "fsdp")
        seen = state_proj(part_bc + (got_bc,))
    conv_out, cum_g, steps_g, cum_t, steps_t, decay = seen
    parts = [part + (got,)]
    if late:
        parts.append(part_late + (got_late,))

    skip = skip_gain.reshape(by_decay)
    levels = count.bit_length() - 1
    seq_place = (2 * lax.axis_index("chip") + lax.axis_index("core")).astype(jnp.int32).reshape(1)

    result = None
    for first, groups, part in zip((0, early_groups), (early_groups, len(late)), parts):
        if first:
            part = after(part, first_total)
        part = part + (rows_before(*part),)
        grid = (groups,)
        cols = lambda rows: pl.BlockSpec((rows, width), lambda i: (0, i))
        cols_all = lambda rows: pl.BlockSpec((rows, width), lambda i: (0, first + i))
        heads_g = pl.BlockSpec((1, tok_count, per_group), lambda i: (first + i, 0, 0))
        heads_t = pl.BlockSpec((per_group, tok_count), lambda i: (first + i, 0))
        heads_1 = pl.BlockSpec((1, 1, per_group), lambda i: (first + i, 0, 0))
        keys = pl.BlockSpec((tok_count, N), lambda i: (0, first + i))
        reads = pl.BlockSpec((tok_count, N), lambda i: (0, groups_here + first + i))
        early_spec = pl.BlockSpec((blocks - 1, N, width), lambda i: (0, 0, i))
        y, early, total, decays, sent = call(
            mix_kernel,
            "mix",
            (
                jax.ShapeDtypeStruct((tok_count, groups * width), F32),
                jax.ShapeDtypeStruct((blocks - 1, N, groups * width), F32),
                jax.ShapeDtypeStruct((N, groups * width), F32),
                jax.ShapeDtypeStruct((8, groups * width), F32),
                jax.ShapeDtypeStruct((N + RIM, groups * width), BF16),
            ),
            flops=8 * tok_count * N * width * groups,
            moved=14 * tok_count * width * groups,
            grid=grid,
            in_specs=specs_of(width) + [cols_all(CONV), keys, reads, heads_g, heads_g, heads_t, heads_t, heads_1, heads_1],
            out_specs=[cols(tok_count), early_spec, cols(N), cols(8), cols(N + RIM)],
            scratch_shapes=[pltpu.VMEM((tok_count + 8, width), F32)],
        )(*part, conv_proj, conv_out, conv_out, cum_g, steps_g, cum_t, steps_t, skip, decay)
        before = ()
        first_total = None
        for level in range(levels - 1):
            other = swapped(sent, SEQ, 1 << level)
            total, decays, sent, fresh = combined(level, seq_place, total, decays, other, before, groups)
            before = (fresh,)
            first_total = total if first_total is None else first_total
        other = swapped(sent, SEQ, 1 << (levels - 1))
        operands = [seq_place, y, conv_out, cum_g, early, decays, *before, other]
        specs = [SMEM, cols(tok_count), reads, heads_g, early_spec, cols(8), cols(N), cols(N + RIM)]
        alias = {}
        if result is not None:
            operands.append(result)
            specs.append(pl.BlockSpec(memory_space=pl.ANY))
            alias = {len(operands) - 1: 0}
        result = call(
            functools.partial(read_kernel, levels - 1),
            "read_out",
            jax.ShapeDtypeStruct((tok_count, heads_here * P_SIZE), BF16),
            flops=2 * tok_count * N * width * groups,
            moved=10 * tok_count * width * groups,
            vmem=12,
            grid=grid,
            in_specs=specs,
            out_specs=cols_all(tok_count),
            input_output_aliases=alias,
        )(*operands)
    return result


def solution(mesh):
    shape = mesh.shape
    split = Mesh(
        mesh.devices.reshape(shape["fsdp"], shape["seq"] // 2, 2, shape["tp"]),
        ("fsdp", "chip", "core", "tp"),
    )
    rows = ("fsdp", "chip", "core")
    return jax.shard_map(
        body,
        mesh=split,
        in_specs=(
            P(rows + ("tp",), None),
            P(rows, "tp"),
            P(None, rows, "tp"),
            P(rows, None, "tp"),
            P(None, rows, None, "tp"),
            P(),
            P(rows, "tp"),
            P("tp"),
            P("tp"),
            P("tp"),
            P(None, "tp"),
            P(None, None, "tp"),
        ),
        out_specs=P(rows, "tp"),
        check_vma=False,
    )
```

```python
import functools

import jax
import jax.numpy as jnp
from jax import lax
from jax.experimental import pallas as pl
from jax.experimental.pallas import tpu as pltpu
from jax.sharding import Mesh, PartitionSpec as P

P_SIZE = 64
N = 128
CONV = 4
SPAN = 128
LANES = 128
RIM = 16
FAR_PARTS = 4
SEQ = ("chip", "core")
F32 = jnp.float32
BF16 = jnp.bfloat16
SMEM = pl.BlockSpec(memory_space=pltpu.SMEM)
VMEM = pl.BlockSpec(memory_space=pltpu.VMEM)


def call(kernel, name, out_shape, flops=0, moved=0, vmem=60, **settings):
    return pl.pallas_call(
        kernel,
        out_shape=out_shape,
        name=name,
        cost_estimate=pl.CostEstimate(flops=flops // 50, bytes_accessed=moved // 50, transcendentals=0),
        compiler_params=pltpu.CompilerParams(vmem_limit_bytes=vmem * 1024 * 1024),
        **settings,
    )


def swapped(part, axis, by=1):
    return lax.ppermute(part, axis, [(i, i ^ by) for i in range(lax.axis_size(axis))])


def cut_kernel(chips, at_ref, tokens_ref, far_ref, own_ref):
    depth = far_ref.shape[1] // chips
    rows = tokens_ref.shape[0]
    f_at, c_at = at_ref[0], at_ref[1]
    for out, f in ((far_ref, 1 - f_at), (own_ref, f_at)):
        for k, c in enumerate((c_at, 1 - c_at)):
            for i in range(chips):
                start = pl.multiple_of(((f * chips + at_ref[3 + i]) * 2 + c) * depth, depth)
                out[k * rows : (k + 1) * rows, i * depth : (i + 1) * depth] = tokens_ref[:, pl.ds(start, depth)]


def stack_kernel(at_ref, *refs):
    pieces, rows_ref = refs[:-1], refs[-1]
    count = pieces[0].shape[0]
    for k in range(0, len(pieces), 2):
        rows_ref[pl.ds(pl.multiple_of((k + at_ref[2]) * count, count), count), :] = pieces[k][...]
        rows_ref[pl.ds(pl.multiple_of((k + 1 - at_ref[2]) * count, count), count), :] = pieces[k + 1][...]


def token_rows(at, far, far_t, far_c, far_tc, own, own_t, own_c, own_tc):
    count, depth = far.shape[0] // 2, far.shape[1]
    low = pl.BlockSpec((count, depth), lambda i: (0, 0))
    high = pl.BlockSpec((count, depth), lambda i: (1, 0))
    return call(
        stack_kernel,
        "stack_rows",
        jax.ShapeDtypeStruct((8 * count, depth), BF16),
        moved=32 * count * depth,
        vmem=40,
        grid=(1,),
        in_specs=[SMEM] + [low, low, high, high] * 2,
        out_specs=pl.BlockSpec((8 * count, depth), lambda i: (0, 0)),
    )(at, far, far_t, far_c, far_tc, own, own_t, own_c, own_tc)


def sample_kernel(count, coef_ref, mean_ref, devs_ref, out_ref):
    factor = (2.0 * (count - 1)) ** (-0.5)
    accum = mean_ref[...].astype(F32)
    for member in range(count):
        accum = accum + factor * coef_ref[member] * devs_ref[member].astype(F32)
    out_ref[...] = accum.astype(BF16)


def sampled_cols(mean_part, dev_part, swag_coef, at, width):
    rows, count = mean_part.shape[0], dev_part.shape[0]
    tile = rows // 4
    return call(
        functools.partial(sample_kernel, count),
        "sample",
        jax.ShapeDtypeStruct((rows, width), BF16),
        moved=2 * (count + 2) * rows * width,
        grid=(4,),
        in_specs=[
            SMEM,
            pl.BlockSpec((tile, width), lambda i: (i, at)),
            pl.BlockSpec((count, tile, width), lambda i: (0, i, at)),
        ],
        out_specs=pl.BlockSpec((tile, width), lambda i: (i, 0)),
    )(swag_coef, mean_part, dev_part)


def sample_pair_kernel(count, coef_ref, mean_ref, devs_ref, dt_ref, out_ref):
    factor = (2.0 * (count - 1)) ** (-0.5)
    accum = mean_ref[...].astype(F32)
    for member in range(count):
        accum = accum + factor * coef_ref[member] * devs_ref[member].astype(F32)
    width, heads = mean_ref.shape[2], dt_ref.shape[1]
    for k in range(2):
        out_ref[:, k * width : (k + 1) * width] = accum[:, k, :].astype(BF16)
    out_ref[:, 2 * width :] = jnp.zeros((out_ref.shape[0], LANES), BF16)
    out_ref[:, 2 * width : 2 * width + heads] = dt_ref[...]


def sampled_pair(mean_part, dev_part, dt_part, swag_coef):
    rows, _, width = mean_part.shape
    count = dev_part.shape[0]
    tile = rows // 8
    return call(
        functools.partial(sample_pair_kernel, count),
        "sample_pair",
        jax.ShapeDtypeStruct((rows, 2 * width + LANES), BF16),
        moved=4 * (count + 2) * rows * width,
        grid=(8,),
        in_specs=[
            SMEM,
            pl.BlockSpec((tile, 2, width), lambda i: (i, 0, 0)),
            pl.BlockSpec((count, tile, 2, width), lambda i: (0, i, 0, 0)),
            pl.BlockSpec((tile, dt_part.shape[1]), lambda i: (i, 0)),
        ],
        out_specs=pl.BlockSpec((tile, 2 * width + LANES), lambda i: (i, 0)),
    )(swag_coef, mean_part, dev_part, dt_part)


def sent_straight(weight):
    return swapped(weight, "chip", 1), swapped(weight, "chip", 2)


def corner_parts(straight, each):
    rows = straight[0].shape[0] // (2 * each)
    cut = lambda a, i: a[i * rows : (i + 1) * rows]
    return [cut(straight[1], i) for i in range(each)] + [cut(straight[0], each + i) for i in range(each)]


def sent_on(parts):
    each = len(parts) // 2
    return [swapped(a, "chip", 1) for a in parts[:each]] + [swapped(a, "chip", 2) for a in parts[each:]]


def coded(part, heads):
    high = part.astype(BF16).astype(F32)
    return high + pltpu.roll(part - high, heads, 1)


def decoded(part, heads):
    return part + pltpu.roll(part, LANES - heads, 1)


def multiply_kernel(heads, with_steps, pieces, rows_ref, *refs):
    weights, far_refs, (sent_ref, far_ref, own_ref) = refs[:pieces], refs[pieces:-3], refs[-3:]
    joined = jnp.concatenate([weight[...] for weight in weights], axis=0)
    total = jnp.dot(rows_ref[...], joined, preferred_element_type=F32)
    half = total.shape[0] // 4
    far_ref[...] = total[:half]
    own_ref[...] = total[2 * half : 3 * half]
    parts = [(out, half + i * out.shape[0]) for i, out in enumerate(far_refs)]
    for out, first in parts + [(sent_ref, 3 * half)]:
        sent = total[first : first + out.shape[0]]
        out[...] = sent.astype(BF16)
        if with_steps:
            @pl.when(pl.program_id(0) == pl.num_programs(0) - 1)
            def _():
                out[:, -LANES:] = coded(sent[:, -LANES:], heads).astype(BF16)


def multiplied(rows, weights, heads, with_steps):
    width = weights[0].shape[1]
    tile = next(t for t in (512, 384, 128) if width % t == 0)
    half = rows.shape[0] // 4
    sent = lambda count: jax.ShapeDtypeStruct((count, width), BF16)
    return call(
        functools.partial(multiply_kernel, heads, with_steps, len(weights)),
        "multiply",
        (sent(half // FAR_PARTS),) * FAR_PARTS + (sent(half),) + (jax.ShapeDtypeStruct((half, width), F32),) * 2,
        flops=2 * rows.size * width,
        moved=2 * rows.size + 2 * rows.shape[1] * width + 12 * half * width,
        grid=(width // tile,),
        in_specs=[pl.BlockSpec(rows.shape, lambda i: (0, 0))]
        + [pl.BlockSpec((w.shape[0], tile), lambda i: (0, i)) for w in weights],
        out_specs=[pl.BlockSpec((count, tile), lambda i: (0, i)) for count in [half // FAR_PARTS] * FAR_PARTS + [half] * 3],
    )(rows, *weights)


def relay_kernel(heads, with_steps, kept_ref, *refs):
    out_ref, count = refs[-1], refs[0].shape[0]
    for i, got_ref in enumerate(refs[:-1]):
        rows = slice(i * count, (i + 1) * count)
        kept, got = kept_ref[rows, :], got_ref[...].astype(F32)
        out_ref[rows, :] = (kept + got).astype(BF16)
        if with_steps:
            wide = kept[:, -LANES:] + decoded(got[:, -LANES:], heads)
            lane = lax.broadcasted_iota(jnp.int32, wide.shape, 1)
            out_ref[rows, -LANES:] = coded(jnp.where(lane < heads, wide, 0.0), heads).astype(BF16)


def relayed(kept, got, heads, with_steps):
    rows, width = kept.shape
    part = pl.BlockSpec((rows // len(got), width), lambda i: (0, 0))
    return call(
        functools.partial(relay_kernel, heads, with_steps),
        "relay",
        jax.ShapeDtypeStruct((rows, width), BF16),
        moved=8 * rows * width,
        vmem=12,
        grid=(1,),
        in_specs=[pl.BlockSpec((rows, width), lambda i: (0, 0))] + [part] * len(got),
        out_specs=pl.BlockSpec((rows, width), lambda i: (0, 0)),
    )(kept, *got)


def rim_kernel(kept, got_c, got_f, rim_ref):
    rim_ref[...] = (kept[...] + got_c[...].astype(F32) + got_f[...].astype(F32)).astype(BF16)


def rows_before(kept, got_c, got_f):
    rows, width = got_f.shape
    at = rows // RIM - 1
    rim = call(
        rim_kernel,
        "rim",
        jax.ShapeDtypeStruct((RIM, width), BF16),
        moved=10 * RIM * width,
        vmem=12,
        grid=(1,),
        in_specs=[pl.BlockSpec((RIM, width), lambda i: (at, 0))] * 3,
        out_specs=pl.BlockSpec((RIM, width), lambda i: (0, 0)),
    )(kept, got_c, got_f)
    return lax.ppermute(rim, SEQ, [(i, i + 1) for i in range(lax.axis_size(SEQ) - 1)])


def convolved(width, kept, got_c, got_f, rim, taps, padded):
    count = padded.shape[0] - 8
    proj = kept[:, :width] + got_c[:, :width].astype(F32) + got_f[:, :width].astype(F32)
    padded[8:, :] = proj.astype(BF16).astype(F32)
    padded[:8, :] = rim[:, :width].astype(F32)[RIM - 8 :]
    first = 8 - (CONV - 1)
    conv_sum = taps[0:1, :] * padded[first : first + count, :]
    for offset in range(1, CONV):
        conv_sum = conv_sum + taps[offset : offset + 1, :] * padded[first + offset : first + offset + count, :]
    return (conv_sum * jax.nn.sigmoid(conv_sum)).astype(BF16)


def state_proj_kernel(
    heads, kept, got_c, got_f, rim, taps, bias, rate, out_ref, cum_ref, steps_ref, cum_t_ref, steps_t_ref, decay_ref, padded
):
    count, width = out_ref.shape
    out_ref[...] = convolved(width, kept, got_c, got_f, rim, taps, padded)
    logits = kept[:, width:] + decoded(got_c[:, width:].astype(F32), heads) + decoded(got_f[:, width:].astype(F32), heads)
    steps = jax.nn.softplus(logits[:, :heads] + bias[...])
    row = lax.broadcasted_iota(jnp.int32, (SPAN, SPAN), 0)
    col = lax.broadcasted_iota(jnp.int32, (SPAN, SPAN), 1)
    causal = jnp.where(row >= col, 1.0, 0.0)
    groups, per_group = cum_ref.shape[0], cum_ref.shape[2]
    through = jnp.zeros((1, heads), F32)
    for at in range(0, count, SPAN):
        span = slice(at, at + SPAN)
        steps_b = steps[span, :]
        cum = jnp.dot(
            causal, -steps_b * rate[...], precision=lax.Precision.HIGHEST, preferred_element_type=F32
        )
        through = through + cum[SPAN - 1 : SPAN, :]
        cum_t_ref[:, span] = jnp.transpose(cum)
        steps_t_ref[:, span] = jnp.transpose(steps_b)
        for g in range(groups):
            cum_ref[g, span, :] = cum[:, g * per_group : (g + 1) * per_group]
            steps_ref[g, span, :] = steps_b[:, g * per_group : (g + 1) * per_group]
    for g in range(groups):
        decay_ref[g] = jnp.exp(through)[:, g * per_group : (g + 1) * per_group]


def pairwise(columns, first):
    shape = (columns.shape[0], 2 * P_SIZE)
    lane = lax.broadcasted_iota(jnp.int32, shape, 1)
    return jnp.where(lane < P_SIZE, columns[:, first : first + 1], columns[:, first + 1 : first + 2])


def over_channels(columns):
    return jnp.concatenate([pairwise(columns, h) for h in range(0, columns.shape[1], 2)], axis=1)


def mix_kernel(
    kept, got_c, got_f, rim, taps, keys, reads, cum_g, steps_g, cum_t, steps_t, skip, decay, y_ref, early_ref, total_ref, decays_ref, sent_ref, padded
):
    width = y_ref.shape[1]
    values = convolved(width, kept, got_c, got_f, rim, taps, padded)
    cum, steps = cum_g[0], steps_g[0]
    heads = cum.shape[1]
    row = lax.broadcasted_iota(jnp.int32, (SPAN, SPAN), 0)
    col = lax.broadcasted_iota(jnp.int32, (SPAN, SPAN), 1)
    causal = row >= col
    lane = lax.broadcasted_iota(jnp.int32, (SPAN, 2 * P_SIZE), 1)
    gain = over_channels(skip[0])
    state = None
    for at in range(0, y_ref.shape[0], SPAN):
        span = slice(at, at + SPAN)
        keys_b, reads_b, values_b = keys[span, :], reads[span, :], values[span, :]
        cum_b, steps_b = cum[span, :], steps[span, :]
        last = cum_b[SPAN - 1 : SPAN, :]
        scores = lax.dot_general(reads_b, keys_b, (((1,), (1,)), ((), ())), preferred_element_type=F32)
        scores = jnp.where(causal, scores, 0.0)
        reach = jnp.exp(last - cum_b) * steps_b
        scaled = []
        for head in range(0, heads, 2):
            chans = slice(head * P_SIZE, (head + 2) * P_SIZE)
            two = []
            for h in (head, head + 1):
                gap = cum_b[:, h : h + 1] - cum_t[h : h + 1, span]
                two.append((scores * jnp.exp(jnp.minimum(gap, 0.0)) * steps_t[h : h + 1, span]).astype(BF16))
            values_h = values_b[:, chans]
            both = jnp.dot(jnp.concatenate(two, axis=0), values_h, preferred_element_type=F32)
            inner = jnp.where(lane < P_SIZE, both[:SPAN], both[SPAN:])
            wide = values_h.astype(F32)
            y_ref[span, chans] = inner + gain[:, chans] * wide
            scaled.append((wide * pairwise(reach, head)).astype(BF16))
        fresh = lax.dot_general(
            keys_b, jnp.concatenate(scaled, axis=1), (((0,), (0,)), ((), ())), preferred_element_type=F32
        )
        state = fresh if state is None else over_channels(jnp.exp(last)) * state + fresh
        if at + SPAN < y_ref.shape[0]:
            early_ref[at // SPAN] = fresh
    total_ref[...] = state
    wide = over_channels(decay[0])
    decays_ref[0:1, :] = wide
    decays_ref[1:2, :] = jnp.ones_like(wide)
    pack_state(sent_ref, state, wide)


def pack_state(sent_ref, state, decay):
    sent_ref[:N, :] = state.astype(BF16)
    high = decay.astype(BF16).astype(F32)
    row = lax.broadcasted_iota(jnp.int32, (RIM, decay.shape[1]), 0)
    sent_ref[N:, :] = jnp.where(row == 0, high, jnp.where(row == 1, decay - high, 0.0)).astype(BF16)


def unpack_state(got_ref):
    rows = got_ref[N:, :].astype(F32)
    return got_ref[:N, :].astype(F32), rows[0:1, :] + rows[1:2, :]


def combine_kernel(level, place_ref, total, decays, other, *refs):
    before, (total_ref, decays_ref, sent_ref, before_ref) = refs[:-4], refs[-4:]
    come, decay = unpack_state(other)
    whole, part = decays[0:1, :], decays[1:2, :]
    upper = (place_ref[0] >> level) & 1 == 1
    fresh = jnp.where(upper, part, 0.0) * come
    before_ref[...] = before[0][...] + fresh if before else fresh
    joint = jnp.where(upper, 1.0, decay) * total[...] + jnp.where(upper, whole, 1.0) * come
    total_ref[...] = joint
    decays_ref[0:1, :] = whole * decay
    decays_ref[1:2, :] = jnp.where(upper, decay * part, part)
    pack_state(sent_ref, joint, whole * decay)


def read_kernel(level, place_ref, y, reads, cum_g, early, decays, before, other, *refs):
    out_ref = refs[-1]
    upper = (place_ref[0] >> level) & 1 == 1
    state = before[...] + jnp.where(upper, decays[1:2, :], 0.0) * unpack_state(other)[0]
    cum = cum_g[0]
    for at in range(0, out_ref.shape[0], SPAN):
        span = slice(at, at + SPAN)
        cum_b = cum[span, :]
        seen = jnp.dot(reads[span, :], state.astype(BF16), preferred_element_type=F32)
        out_ref[span, :] = (y[span, :] + over_channels(jnp.exp(cum_b)) * seen).astype(BF16)
        if at + SPAN < out_ref.shape[0]:
            state = over_channels(jnp.exp(cum_b[SPAN - 1 : SPAN, :])) * state + early[at // SPAN]


def combined(level, place, total, decays, other, before, groups):
    width = total.shape[1] // groups
    block = lambda rows: pl.BlockSpec((rows, width), lambda i: (0, i))
    shape = lambda rows, dtype: jax.ShapeDtypeStruct((rows, total.shape[1]), dtype)
    return call(
        functools.partial(combine_kernel, level),
        "combine",
        (shape(N, F32), shape(8, F32), shape(N + RIM, BF16), shape(N, F32)),
        flops=6 * total.size,
        moved=20 * total.size,
        vmem=12,
        grid=(groups,),
        in_specs=[SMEM, block(N), block(8), block(N + RIM)] + [block(N)] * len(before),
        out_specs=[block(N), block(8), block(N + RIM), block(N)],
    )(place, total, decays, other, *before)


def body(
    tokens,
    proj_mean,
    proj_devs,
    bc_mean,
    bc_devs,
    swag_coef,
    dt_weight,
    dt_bias,
    decay_rate,
    skip_gain,
    conv_proj,
    conv_bc,
):
    heads_here = decay_rate.shape[0]
    groups_here = bc_mean.shape[2] // N
    per_group = heads_here // groups_here
    width_bc = 2 * bc_mean.shape[2]
    rows_k = proj_mean.shape[0]
    chips = lax.axis_size("chip")
    count = lax.axis_size(SEQ)

    def after(arrays, earlier):
        return lax.optimization_barrier((arrays, earlier))[0]

    width = per_group * P_SIZE
    early_groups = max(1, groups_here // 2)
    fill = -heads_here % LANES
    late = list(range(early_groups, groups_here))

    plane = chips == 4
    two_shares = lax.axis_size("tp") == 2
    place = lax.axis_index("chip") if plane else 0
    at = jnp.stack([lax.axis_index(a) for a in ("fsdp", "core", "tp")] + [place ^ i for i in range(chips)]).astype(jnp.int32)
    share, depth = tokens.shape[0], chips * rows_k
    weight_bc = sampled_pair(bc_mean, bc_devs, dt_weight, swag_coef)
    tokens = after(tokens, weight_bc)
    cut = jax.ShapeDtypeStruct((2 * share, depth), BF16)
    far, own = call(
        functools.partial(cut_kernel, chips),
        "cut_tokens",
        (cut,) * 2,
        moved=4 * tokens.size,
        in_specs=[SMEM, VMEM],
        out_specs=[VMEM] * 2,
    )(at, tokens)
    proj_mean = after(proj_mean, own)
    far = swapped(far, "fsdp")

    weight_early = sampled_cols(proj_mean, proj_devs, swag_coef, 0, early_groups * width)
    weight_late = None
    if late:
        weight_late = sampled_cols(proj_mean, proj_devs, swag_coef, early_groups // len(late), len(late) * width)
    tok_count = share * lax.axis_size("tp")
    blocks = tok_count // SPAN

    def partial_sums(rows, pieces, with_steps, earlier=()):
        *far_sent, sent, far_kept, kept = multiplied(rows, pieces, heads_here, with_steps)
        far_sent = after(far_sent, earlier)
        back = relayed(far_kept, [swapped(a, "core") for a in far_sent], heads_here, with_steps)
        return (kept, swapped(after(sent, back), "core")), back

    specs_of = lambda width: [pl.BlockSpec((tok_count, width), lambda i: (0, i))] * 3 + [
        pl.BlockSpec((RIM, width), lambda i: (0, i)),
    ]
    whole_of = lambda *shape: pl.BlockSpec(shape, lambda i: (0,) * len(shape))
    by_group = (groups_here, tok_count, per_group)
    by_head = (heads_here, tok_count)
    by_decay = (groups_here, 1, per_group)
    state_proj = lambda part: call(
        functools.partial(state_proj_kernel, heads_here),
        "state_proj",
        (jax.ShapeDtypeStruct((tok_count, width_bc), BF16),)
        + tuple(jax.ShapeDtypeStruct(a, F32) for a in (by_group, by_group, by_head, by_head, by_decay)),
        moved=10 * tok_count * width_bc,
        grid=(1,),
        in_specs=specs_of(width_bc + LANES) + [whole_of(CONV, width_bc)] + [whole_of(1, heads_here)] * 2,
        out_specs=[whole_of(*a) for a in ((tok_count, width_bc), by_group, by_group, by_head, by_head, by_decay)],
        scratch_shapes=[pltpu.VMEM((tok_count + 8, width_bc), F32)],
    )(*part, rows_before(*part), conv_bc.reshape(CONV, width_bc), dt_bias[None], decay_rate[None])
    if plane and two_shares:
        bc = [weight_bc, *sent_straight(weight_bc)]
        bc += sent_on(corner_parts(bc[1:], 1))
        own_t = swapped(own, "tp")
        weight_early = after(weight_early, bc[3:])
        early = [weight_early, *sent_straight(weight_early)]
        far = after(far, (own_t, bc[3:], weight_late))
        far_t = swapped(far, "tp")
        own, own_t = after((own, own_t), far)
        own_c, own_tc = swapped(own, "core"), swapped(own_t, "core")
        halves = corner_parts(early[1:], 1)
        far_c, far_tc = swapped(far, "core"), swapped(after(far_t, halves), "core")
        rows = token_rows(at, far, far_t, far_c, far_tc, own, own_t, own_c, own_tc)
        part_bc, back_bc = partial_sums(rows, bc, True)
        early += sent_on(halves)
        got_bc = swapped(back_bc, "fsdp")
        weight_late = after(weight_late, (back_bc, early[3:]))
        part, back = partial_sums(rows, early, False, got_bc)
        got = swapped(after(back, got_bc), "fsdp")
        straight = sent_straight(weight_late)
        corners = sent_on(after(corner_parts(straight, 2), back))
        part_late, back_late = partial_sums(rows, after([weight_late, *straight, *corners], back), False)
        seen = state_proj(after(part_bc + (got_bc,), back_late))
        got_late = swapped(after(back_late, got), "fsdp")
        got = after(got, back_late)
    else:
        whole = lambda a, axis: lax.all_gather(a, axis, axis=0, tiled=True)
        ranges = [r for a in (far, own) for r in (a[:share], swapped(a[share:], "core"))]
        rows = jnp.concatenate([whole(r, "tp") for r in ranges], axis=0)
        part, back = partial_sums(rows, [whole(weight_early, "chip")], False)
        part_bc, back_bc = partial_sums(rows, [whole(weight_bc, "chip")], True)
        got, got_bc = swapped(back, "fsdp"), swapped(back_bc, "fsdp")
        if late:
            part_late, back_late = partial_sums(rows, [whole(weight_late, "chip")], False)
            got_late = swapped(back_late, "fsdp")
        seen = state_proj(part_bc + (got_bc,))
    conv_out, cum_g, steps_g, cum_t, steps_t, decay = seen
    parts = [part + (got,)]
    if late:
        parts.append(part_late + (got_late,))

    skip = skip_gain.reshape(by_decay)
    levels = count.bit_length() - 1
    seq_place = (2 * lax.axis_index("chip") + lax.axis_index("core")).astype(jnp.int32).reshape(1)

    result = None
    for first, groups, part in zip((0, early_groups), (early_groups, len(late)), parts):
        if first:
            part = after(part, first_total)
        part = part + (rows_before(*part),)
        grid = (groups,)
        cols = lambda rows: pl.BlockSpec((rows, width), lambda i: (0, i))
        cols_all = lambda rows: pl.BlockSpec((rows, width), lambda i: (0, first + i))
        heads_g = pl.BlockSpec((1, tok_count, per_group), lambda i: (first + i, 0, 0))
        heads_t = pl.BlockSpec((per_group, tok_count), lambda i: (first + i, 0))
        heads_1 = pl.BlockSpec((1, 1, per_group), lambda i: (first + i, 0, 0))
        keys = pl.BlockSpec((tok_count, N), lambda i: (0, first + i))
        reads = pl.BlockSpec((tok_count, N), lambda i: (0, groups_here + first + i))
        early_spec = pl.BlockSpec((blocks - 1, N, width), lambda i: (0, 0, i))
        y, early, total, decays, sent = call(
            mix_kernel,
            "mix",
            (
                jax.ShapeDtypeStruct((tok_count, groups * width), F32),
                jax.ShapeDtypeStruct((blocks - 1, N, groups * width), F32),
                jax.ShapeDtypeStruct((N, groups * width), F32),
                jax.ShapeDtypeStruct((8, groups * width), F32),
                jax.ShapeDtypeStruct((N + RIM, groups * width), BF16),
            ),
            flops=8 * tok_count * N * width * groups,
            moved=14 * tok_count * width * groups,
            grid=grid,
            in_specs=specs_of(width) + [cols_all(CONV), keys, reads, heads_g, heads_g, heads_t, heads_t, heads_1, heads_1],
            out_specs=[cols(tok_count), early_spec, cols(N), cols(8), cols(N + RIM)],
            scratch_shapes=[pltpu.VMEM((tok_count + 8, width), F32)],
        )(*part, conv_proj, conv_out, conv_out, cum_g, steps_g, cum_t, steps_t, skip, decay)
        before = ()
        first_total = None
        for level in range(levels - 1):
            other = swapped(sent, SEQ, 1 << level)
            total, decays, sent, fresh = combined(level, seq_place, total, decays, other, before, groups)
            before = (fresh,)
            first_total = total if first_total is None else first_total
        other = swapped(sent, SEQ, 1 << (levels - 1))
        operands = [seq_place, y, conv_out, cum_g, early, decays, *before, other]
        specs = [SMEM, cols(tok_count), reads, heads_g, early_spec, cols(8), cols(N), cols(N + RIM)]
        alias = {}
        if result is not None:
            operands.append(result)
            specs.append(pl.BlockSpec(memory_space=pl.ANY))
            alias = {len(operands) - 1: 0}
        result = call(
            functools.partial(read_kernel, levels - 1),
            "read_out",
            jax.ShapeDtypeStruct((tok_count, heads_here * P_SIZE), BF16),
            flops=2 * tok_count * N * width * groups,
            moved=10 * tok_count * width * groups,
            vmem=12,
            grid=grid,
            in_specs=specs,
            out_specs=cols_all(tok_count),
            input_output_aliases=alias,
        )(*operands)
    return result


def solution(mesh):
    shape = mesh.shape
    split = Mesh(
        mesh.devices.reshape(shape["fsdp"], shape["seq"] // 2, 2, shape["tp"]),
        ("fsdp", "chip", "core", "tp"),
    )
    rows = ("fsdp", "chip", "core")
    return jax.shard_map(
        body,
        mesh=split,
        in_specs=(
            P(rows + ("tp",), None),
            P(rows, "tp"),
            P(None, rows, "tp"),
            P(rows, None, "tp"),
            P(None, rows, None, "tp"),
            P(),
            P(rows, "tp"),
            P("tp"),
            P("tp"),
            P("tp"),
            P(None, "tp"),
            P(None, None, "tp"),
        ),
        out_specs=P(rows, "tp"),
        check_vma=False,
    )
```

```python
import functools

import jax
import jax.numpy as jnp
from jax import lax
from jax.experimental import pallas as pl
from jax.experimental.pallas import tpu as pltpu
from jax.sharding import Mesh, PartitionSpec as P

P_SIZE = 64
N = 128
CONV = 4
SPAN = 128
LANES = 128
RIM = 16
FAR_PARTS = 2
SEQ = ("chip", "core")
F32 = jnp.float32
BF16 = jnp.bfloat16
SMEM = pl.BlockSpec(memory_space=pltpu.SMEM)
VMEM = pl.BlockSpec(memory_space=pltpu.VMEM)


def call(kernel, name, out_shape, flops=0, moved=0, vmem=60, **settings):
    return pl.pallas_call(
        kernel,
        out_shape=out_shape,
        name=name,
        cost_estimate=pl.CostEstimate(flops=flops // 50, bytes_accessed=moved // 50, transcendentals=0),
        compiler_params=pltpu.CompilerParams(vmem_limit_bytes=vmem * 1024 * 1024),
        **settings,
    )


def swapped(part, axis, by=1):
    return lax.ppermute(part, axis, [(i, i ^ by) for i in range(lax.axis_size(axis))])


def cut_kernel(chips, at_ref, tokens_ref, far_ref, own_ref):
    depth = far_ref.shape[1] // chips
    rows = tokens_ref.shape[0]
    f_at, c_at = at_ref[0], at_ref[1]
    for out, f in ((far_ref, 1 - f_at), (own_ref, f_at)):
        for k, c in enumerate((c_at, 1 - c_at)):
            for i in range(chips):
                start = pl.multiple_of(((f * chips + at_ref[3 + i]) * 2 + c) * depth, depth)
                out[k * rows : (k + 1) * rows, i * depth : (i + 1) * depth] = tokens_ref[:, pl.ds(start, depth)]


def stack_kernel(at_ref, *refs):
    pieces, rows_ref = refs[:-1], refs[-1]
    count = pieces[0].shape[0]
    for k in range(0, len(pieces), 2):
        rows_ref[pl.ds(pl.multiple_of((k + at_ref[2]) * count, count), count), :] = pieces[k][...]
        rows_ref[pl.ds(pl.multiple_of((k + 1 - at_ref[2]) * count, count), count), :] = pieces[k + 1][...]


def token_rows(at, far, far_t, far_c, far_tc, own, own_t, own_c, own_tc):
    count, depth = far.shape[0] // 2, far.shape[1]
    low = pl.BlockSpec((count, depth), lambda i: (0, 0))
    high = pl.BlockSpec((count, depth), lambda i: (1, 0))
    return call(
        stack_kernel,
        "stack_rows",
        jax.ShapeDtypeStruct((8 * count, depth), BF16),
        moved=32 * count * depth,
        vmem=40,
        grid=(1,),
        in_specs=[SMEM] + [low, low, high, high] * 2,
        out_specs=pl.BlockSpec((8 * count, depth), lambda i: (0, 0)),
    )(at, far, far_t, far_c, far_tc, own, own_t, own_c, own_tc)


def sample_kernel(count, coef_ref, mean_ref, devs_ref, out_ref):
    factor = (2.0 * (count - 1)) ** (-0.5)
    accum = mean_ref[...].astype(F32)
    for member in range(count):
        accum = accum + factor * coef_ref[member] * devs_ref[member].astype(F32)
    out_ref[...] = accum.astype(BF16)


def sampled_cols(mean_part, dev_part, swag_coef, at, width):
    rows, count = mean_part.shape[0], dev_part.shape[0]
    tile = rows // 4
    return call(
        functools.partial(sample_kernel, count),
        "sample",
        jax.ShapeDtypeStruct((rows, width), BF16),
        moved=2 * (count + 2) * rows * width,
        grid=(4,),
        in_specs=[
            SMEM,
            pl.BlockSpec((tile, width), lambda i: (i, at)),
            pl.BlockSpec((count, tile, width), lambda i: (0, i, at)),
        ],
        out_specs=pl.BlockSpec((tile, width), lambda i: (i, 0)),
    )(swag_coef, mean_part, dev_part)


def sample_pair_kernel(count, coef_ref, mean_ref, devs_ref, dt_ref, out_ref):
    factor = (2.0 * (count - 1)) ** (-0.5)
    accum = mean_ref[...].astype(F32)
    for member in range(count):
        accum = accum + factor * coef_ref[member] * devs_ref[member].astype(F32)
    width, heads = mean_ref.shape[2], dt_ref.shape[1]
    for k in range(2):
        out_ref[:, k * width : (k + 1) * width] = accum[:, k, :].astype(BF16)
    out_ref[:, 2 * width :] = jnp.zeros((out_ref.shape[0], LANES), BF16)
    out_ref[:, 2 * width : 2 * width + heads] = dt_ref[...]


def sampled_pair(mean_part, dev_part, dt_part, swag_coef):
    rows, _, width = mean_part.shape
    count = dev_part.shape[0]
    tile = rows // 8
    return call(
        functools.partial(sample_pair_kernel, count),
        "sample_pair",
        jax.ShapeDtypeStruct((rows, 2 * width + LANES), BF16),
        moved=4 * (count + 2) * rows * width,
        grid=(8,),
        in_specs=[
            SMEM,
            pl.BlockSpec((tile, 2, width), lambda i: (i, 0, 0)),
            pl.BlockSpec((count, tile, 2, width), lambda i: (0, i, 0, 0)),
            pl.BlockSpec((tile, dt_part.shape[1]), lambda i: (i, 0)),
        ],
        out_specs=pl.BlockSpec((tile, 2 * width + LANES), lambda i: (i, 0)),
    )(swag_coef, mean_part, dev_part, dt_part)


def sent_straight(weight):
    return swapped(weight, "chip", 1), swapped(weight, "chip", 2)


def corner_parts(straight, each):
    rows = straight[0].shape[0] // (2 * each)
    cut = lambda a, i: a[i * rows : (i + 1) * rows]
    return [cut(straight[1], i) for i in range(each)] + [cut(straight[0], each + i) for i in range(each)]


def sent_on(parts):
    each = len(parts) // 2
    return [swapped(a, "chip", 1) for a in parts[:each]] + [swapped(a, "chip", 2) for a in parts[each:]]


def coded(part, heads):
    high = part.astype(BF16).astype(F32)
    return high + pltpu.roll(part - high, heads, 1)


def decoded(part, heads):
    return part + pltpu.roll(part, LANES - heads, 1)


def multiply_kernel(heads, with_steps, pieces, plan, rows_ref, *refs):
    weights, outs = refs[:pieces], refs[pieces:]
    joined = jnp.concatenate([weight[...] for weight in weights], axis=0)
    total = jnp.dot(rows_ref[...], joined, preferred_element_type=F32)
    for out, (first, sent) in zip(outs, plan):
        part = total[first : first + out.shape[0]]
        out[...] = part.astype(out.dtype)
        if with_steps and sent:
            @pl.when(pl.program_id(0) == pl.num_programs(0) - 1)
            def _():
                out[:, -LANES:] = coded(part[:, -LANES:], heads).astype(BF16)


def multiplied(rows, weights, heads, with_steps, document=None):
    width = weights[0].shape[1]
    tile = next(t for t in (512, 384, 128) if width % t == 0)
    half = rows.shape[0] // 4
    part = half // FAR_PARTS
    plan, shapes = [], []
    count = rows.shape[0] if document is None else 2 * half
    if document != 1:
        plan += [(half + i * part, True) for i in range(FAR_PARTS)] + [(0, False)]
        shapes += [(part, BF16)] * FAR_PARTS + [(half, F32)]
    if document != 0:
        plan += [(count - half, True), (count - 2 * half, False)]
        shapes += [(half, BF16), (half, F32)]
    return call(
        functools.partial(multiply_kernel, heads, with_steps, len(weights), plan),
        "multiply",
        tuple(jax.ShapeDtypeStruct((r, width), dtype) for r, dtype in shapes),
        flops=2 * count * rows.shape[1] * width,
        moved=2 * rows.size + 2 * rows.shape[1] * width + 12 * half * width,
        grid=(width // tile,),
        in_specs=[pl.BlockSpec((count, rows.shape[1]), lambda i: (document or 0, 0))]
        + [pl.BlockSpec((w.shape[0], tile), lambda i: (0, i)) for w in weights],
        out_specs=[pl.BlockSpec((r, tile), lambda i: (0, i)) for r, _ in shapes],
    )(rows, *weights)


def relay_kernel(heads, with_steps, kept_ref, *refs):
    out_ref, count = refs[-1], refs[0].shape[0]
    for i, got_ref in enumerate(refs[:-1]):
        rows = slice(i * count, (i + 1) * count)
        kept, got = kept_ref[rows, :], got_ref[...].astype(F32)
        out_ref[rows, :] = (kept + got).astype(BF16)
        if with_steps:
            wide = kept[:, -LANES:] + decoded(got[:, -LANES:], heads)
            lane = lax.broadcasted_iota(jnp.int32, wide.shape, 1)
            out_ref[rows, -LANES:] = coded(jnp.where(lane < heads, wide, 0.0), heads).astype(BF16)


def relayed(kept, got, heads, with_steps):
    rows, width = kept.shape
    part = pl.BlockSpec((rows // len(got), width), lambda i: (0, 0))
    return call(
        functools.partial(relay_kernel, heads, with_steps),
        "relay",
        jax.ShapeDtypeStruct((rows, width), BF16),
        moved=8 * rows * width,
        vmem=12,
        grid=(1,),
        in_specs=[pl.BlockSpec((rows, width), lambda i: (0, 0))] + [part] * len(got),
        out_specs=pl.BlockSpec((rows, width), lambda i: (0, 0)),
    )(kept, *got)


def rim_kernel(kept, got_c, got_f, rim_ref):
    rim_ref[...] = (kept[...] + got_c[...].astype(F32) + got_f[...].astype(F32)).astype(BF16)


def rows_before(kept, got_c, got_f):
    rows, width = got_f.shape
    at = rows // RIM - 1
    rim = call(
        rim_kernel,
        "rim",
        jax.ShapeDtypeStruct((RIM, width), BF16),
        moved=10 * RIM * width,
        vmem=12,
        grid=(1,),
        in_specs=[pl.BlockSpec((RIM, width), lambda i: (at, 0))] * 3,
        out_specs=pl.BlockSpec((RIM, width), lambda i: (0, 0)),
    )(kept, got_c, got_f)
    return lax.ppermute(rim, SEQ, [(i, i + 1) for i in range(lax.axis_size(SEQ) - 1)])


def convolved(width, kept, got_c, got_f, rim, taps, padded):
    count = padded.shape[0] - 8
    proj = kept[:, :width] + got_c[:, :width].astype(F32) + got_f[:, :width].astype(F32)
    padded[8:, :] = proj.astype(BF16).astype(F32)
    padded[:8, :] = rim[:, :width].astype(F32)[RIM - 8 :]
    first = 8 - (CONV - 1)
    conv_sum = taps[0:1, :] * padded[first : first + count, :]
    for offset in range(1, CONV):
        conv_sum = conv_sum + taps[offset : offset + 1, :] * padded[first + offset : first + offset + count, :]
    return (conv_sum * jax.nn.sigmoid(conv_sum)).astype(BF16)


def state_proj_kernel(
    heads, kept, got_c, got_f, rim, taps, bias, rate, out_ref, cum_ref, steps_ref, cum_t_ref, steps_t_ref, decay_ref, padded
):
    count, width = out_ref.shape
    out_ref[...] = convolved(width, kept, got_c, got_f, rim, taps, padded)
    logits = kept[:, width:] + decoded(got_c[:, width:].astype(F32), heads) + decoded(got_f[:, width:].astype(F32), heads)
    steps = jax.nn.softplus(logits[:, :heads] + bias[...])
    row = lax.broadcasted_iota(jnp.int32, (SPAN, SPAN), 0)
    col = lax.broadcasted_iota(jnp.int32, (SPAN, SPAN), 1)
    causal = jnp.where(row >= col, 1.0, 0.0)
    groups, per_group = cum_ref.shape[0], cum_ref.shape[2]
    through = jnp.zeros((1, heads), F32)
    for at in range(0, count, SPAN):
        span = slice(at, at + SPAN)
        steps_b = steps[span, :]
        cum = jnp.dot(
            causal, -steps_b * rate[...], precision=lax.Precision.HIGHEST, preferred_element_type=F32
        )
        through = through + cum[SPAN - 1 : SPAN, :]
        cum_t_ref[:, span] = jnp.transpose(cum)
        steps_t_ref[:, span] = jnp.transpose(steps_b)
        for g in range(groups):
            cum_ref[g, span, :] = cum[:, g * per_group : (g + 1) * per_group]
            steps_ref[g, span, :] = steps_b[:, g * per_group : (g + 1) * per_group]
    for g in range(groups):
        decay_ref[g] = jnp.exp(through)[:, g * per_group : (g + 1) * per_group]


def pairwise(columns, first):
    shape = (columns.shape[0], 2 * P_SIZE)
    lane = lax.broadcasted_iota(jnp.int32, shape, 1)
    return jnp.where(lane < P_SIZE, columns[:, first : first + 1], columns[:, first + 1 : first + 2])


def over_channels(columns):
    return jnp.concatenate([pairwise(columns, h) for h in range(0, columns.shape[1], 2)], axis=1)


def mix_kernel(
    kept, got_c, got_f, rim, taps, keys, reads, cum_g, steps_g, cum_t, steps_t, skip, decay, y_ref, early_ref, total_ref, decays_ref, sent_ref, padded
):
    width = y_ref.shape[1]
    values = convolved(width, kept, got_c, got_f, rim, taps, padded)
    cum, steps = cum_g[0], steps_g[0]
    heads = cum.shape[1]
    row = lax.broadcasted_iota(jnp.int32, (SPAN, SPAN), 0)
    col = lax.broadcasted_iota(jnp.int32, (SPAN, SPAN), 1)
    causal = row >= col
    lane = lax.broadcasted_iota(jnp.int32, (SPAN, 2 * P_SIZE), 1)
    gain = over_channels(skip[0])
    state = None
    for at in range(0, y_ref.shape[0], SPAN):
        span = slice(at, at + SPAN)
        keys_b, reads_b, values_b = keys[span, :], reads[span, :], values[span, :]
        cum_b, steps_b = cum[span, :], steps[span, :]
        last = cum_b[SPAN - 1 : SPAN, :]
        scores = lax.dot_general(reads_b, keys_b, (((1,), (1,)), ((), ())), preferred_element_type=F32)
        scores = jnp.where(causal, scores, 0.0)
        reach = jnp.exp(last - cum_b) * steps_b
        scaled = []
        for head in range(0, heads, 2):
            chans = slice(head * P_SIZE, (head + 2) * P_SIZE)
            two = []
            for h in (head, head + 1):
                gap = cum_b[:, h : h + 1] - cum_t[h : h + 1, span]
                two.append((scores * jnp.exp(jnp.minimum(gap, 0.0)) * steps_t[h : h + 1, span]).astype(BF16))
            values_h = values_b[:, chans]
            both = jnp.dot(jnp.concatenate(two, axis=0), values_h, preferred_element_type=F32)
            inner = jnp.where(lane < P_SIZE, both[:SPAN], both[SPAN:])
            wide = values_h.astype(F32)
            y_ref[span, chans] = inner + gain[:, chans] * wide
            scaled.append((wide * pairwise(reach, head)).astype(BF16))
        fresh = lax.dot_general(
            keys_b, jnp.concatenate(scaled, axis=1), (((0,), (0,)), ((), ())), preferred_element_type=F32
        )
        state = fresh if state is None else over_channels(jnp.exp(last)) * state + fresh
        if at + SPAN < y_ref.shape[0]:
            early_ref[at // SPAN] = fresh
    total_ref[...] = state
    wide = over_channels(decay[0])
    decays_ref[0:1, :] = wide
    decays_ref[1:2, :] = jnp.ones_like(wide)
    pack_state(sent_ref, state, wide)


def pack_state(sent_ref, state, decay):
    sent_ref[:N, :] = state.astype(BF16)
    high = decay.astype(BF16).astype(F32)
    row = lax.broadcasted_iota(jnp.int32, (RIM, decay.shape[1]), 0)
    sent_ref[N:, :] = jnp.where(row == 0, high, jnp.where(row == 1, decay - high, 0.0)).astype(BF16)


def unpack_state(got_ref):
    rows = got_ref[N:, :].astype(F32)
    return got_ref[:N, :].astype(F32), rows[0:1, :] + rows[1:2, :]


def combine_kernel(level, place_ref, total, decays, other, *refs):
    before, (total_ref, decays_ref, sent_ref, before_ref) = refs[:-4], refs[-4:]
    come, decay = unpack_state(other)
    whole, part = decays[0:1, :], decays[1:2, :]
    upper = (place_ref[0] >> level) & 1 == 1
    fresh = jnp.where(upper, part, 0.0) * come
    before_ref[...] = before[0][...] + fresh if before else fresh
    joint = jnp.where(upper, 1.0, decay) * total[...] + jnp.where(upper, whole, 1.0) * come
    total_ref[...] = joint
    decays_ref[0:1, :] = whole * decay
    decays_ref[1:2, :] = jnp.where(upper, decay * part, part)
    pack_state(sent_ref, joint, whole * decay)


def read_kernel(level, place_ref, y, reads, cum_g, early, decays, before, other, *refs):
    out_ref = refs[-1]
    upper = (place_ref[0] >> level) & 1 == 1
    state = before[...] + jnp.where(upper, decays[1:2, :], 0.0) * unpack_state(other)[0]
    cum = cum_g[0]
    for at in range(0, out_ref.shape[0], SPAN):
        span = slice(at, at + SPAN)
        cum_b = cum[span, :]
        seen = jnp.dot(reads[span, :], state.astype(BF16), preferred_element_type=F32)
        out_ref[span, :] = (y[span, :] + over_channels(jnp.exp(cum_b)) * seen).astype(BF16)
        if at + SPAN < out_ref.shape[0]:
            state = over_channels(jnp.exp(cum_b[SPAN - 1 : SPAN, :])) * state + early[at // SPAN]


def combined(level, place, total, decays, other, before, groups):
    width = total.shape[1] // groups
    block = lambda rows: pl.BlockSpec((rows, width), lambda i: (0, i))
    shape = lambda rows, dtype: jax.ShapeDtypeStruct((rows, total.shape[1]), dtype)
    return call(
        functools.partial(combine_kernel, level),
        "combine",
        (shape(N, F32), shape(8, F32), shape(N + RIM, BF16), shape(N, F32)),
        flops=6 * total.size,
        moved=20 * total.size,
        vmem=12,
        grid=(groups,),
        in_specs=[SMEM, block(N), block(8), block(N + RIM)] + [block(N)] * len(before),
        out_specs=[block(N), block(8), block(N + RIM), block(N)],
    )(place, total, decays, other, *before)


def body(
    tokens,
    proj_mean,
    proj_devs,
    bc_mean,
    bc_devs,
    swag_coef,
    dt_weight,
    dt_bias,
    decay_rate,
    skip_gain,
    conv_proj,
    conv_bc,
):
    heads_here = decay_rate.shape[0]
    groups_here = bc_mean.shape[2] // N
    per_group = heads_here // groups_here
    width_bc = 2 * bc_mean.shape[2]
    rows_k = proj_mean.shape[0]
    chips = lax.axis_size("chip")
    count = lax.axis_size(SEQ)

    def after(arrays, earlier):
        return lax.optimization_barrier((arrays, earlier))[0]

    width = per_group * P_SIZE
    early_groups = max(1, groups_here // 2)
    fill = -heads_here % LANES
    late = list(range(early_groups, groups_here))

    plane = chips == 4
    two_shares = lax.axis_size("tp") == 2
    place = lax.axis_index("chip") if plane else 0
    at = jnp.stack([lax.axis_index(a) for a in ("fsdp", "core", "tp")] + [place ^ i for i in range(chips)]).astype(jnp.int32)
    share, depth = tokens.shape[0], chips * rows_k
    weight_bc = sampled_pair(bc_mean, bc_devs, dt_weight, swag_coef)
    tokens = after(tokens, weight_bc)
    cut = jax.ShapeDtypeStruct((2 * share, depth), BF16)
    far, own = call(
        functools.partial(cut_kernel, chips),
        "cut_tokens",
        (cut,) * 2,
        moved=4 * tokens.size,
        in_specs=[SMEM, VMEM],
        out_specs=[VMEM] * 2,
    )(at, tokens)
    proj_mean = after(proj_mean, own)
    far = swapped(far, "fsdp")

    weight_early = sampled_cols(proj_mean, proj_devs, swag_coef, 0, early_groups * width)
    weight_late = None
    if late:
        weight_late = sampled_cols(proj_mean, proj_devs, swag_coef, early_groups // len(late), len(late) * width)
    tok_count = share * lax.axis_size("tp")
    blocks = tok_count // SPAN

    def partial_sums(rows, pieces, with_steps, before_send=(), before_relay=()):
        *far_sent, far_kept, sent, kept = multiplied(rows, pieces, heads_here, with_steps)
        far_got = [swapped(a, "core") for a in after(far_sent, before_send)]
        back = relayed(far_kept, after(far_got, before_relay), heads_here, with_steps)
        return (kept, swapped(after(sent, back), "core")), back

    specs_of = lambda width: [pl.BlockSpec((tok_count, width), lambda i: (0, i))] * 3 + [
        pl.BlockSpec((RIM, width), lambda i: (0, i)),
    ]
    whole_of = lambda *shape: pl.BlockSpec(shape, lambda i: (0,) * len(shape))
    by_group = (groups_here, tok_count, per_group)
    by_head = (heads_here, tok_count)
    by_decay = (groups_here, 1, per_group)
    state_proj = lambda part: call(
        functools.partial(state_proj_kernel, heads_here),
        "state_proj",
        (jax.ShapeDtypeStruct((tok_count, width_bc), BF16),)
        + tuple(jax.ShapeDtypeStruct(a, F32) for a in (by_group, by_group, by_head, by_head, by_decay)),
        moved=10 * tok_count * width_bc,
        grid=(1,),
        in_specs=specs_of(width_bc + LANES) + [whole_of(CONV, width_bc)] + [whole_of(1, heads_here)] * 2,
        out_specs=[whole_of(*a) for a in ((tok_count, width_bc), by_group, by_group, by_head, by_head, by_decay)],
        scratch_shapes=[pltpu.VMEM((tok_count + 8, width_bc), F32)],
    )(*part, rows_before(*part), conv_bc.reshape(CONV, width_bc), dt_bias[None], decay_rate[None])
    if plane and two_shares:
        bc = [weight_bc, *sent_straight(weight_bc)]
        bc += sent_on(corner_parts(bc[1:], 1))
        own_t = swapped(own, "tp")
        weight_early = after(weight_early, bc[3:])
        early = [weight_early, *sent_straight(weight_early)]
        far = after(far, (own_t, bc[3:], weight_late))
        far_t = swapped(far, "tp")
        own, own_t = after((own, own_t), far)
        own_c, own_tc = swapped(own, "core"), swapped(own_t, "core")
        halves = corner_parts(early[1:], 1)
        far_c, far_tc = swapped(far, "core"), swapped(after(far_t, halves), "core")
        rows = token_rows(at, far, far_t, far_c, far_tc, own, own_t, own_c, own_tc)
        part_bc, back_bc = partial_sums(rows, bc, True)
        early += sent_on(halves)
        got_bc = swapped(back_bc, "fsdp")
        weight_late = after(weight_late, (back_bc, early[3:]))
        part, back = partial_sums(rows, early, False, before_relay=got_bc)
        got = swapped(after(back, got_bc), "fsdp")
        straight = sent_straight(weight_late)
        corners = sent_on(corner_parts(straight, 1))
        seen = state_proj(after(part_bc + (got_bc,), back))
        part_late, back_late = partial_sums(rows, [weight_late, *straight, *corners], False, before_send=seen)
        got_late = swapped(after(back_late, got), "fsdp")
        got = after(got, back_late)
    else:
        whole = lambda a, axis: lax.all_gather(a, axis, axis=0, tiled=True)
        ranges = [r for a in (far, own) for r in (a[:share], swapped(a[share:], "core"))]
        rows = jnp.concatenate([whole(r, "tp") for r in ranges], axis=0)
        part, back = partial_sums(rows, [whole(weight_early, "chip")], False)
        part_bc, back_bc = partial_sums(rows, [whole(weight_bc, "chip")], True)
        got, got_bc = swapped(back, "fsdp"), swapped(back_bc, "fsdp")
        if late:
            part_late, back_late = partial_sums(rows, [whole(weight_late, "chip")], False)
            got_late = swapped(back_late, "fsdp")
        seen = state_proj(part_bc + (got_bc,))
    conv_out, cum_g, steps_g, cum_t, steps_t, decay = seen
    parts = [part + (got,)]
    if late:
        parts.append(part_late + (got_late,))

    skip = skip_gain.reshape(by_decay)
    levels = count.bit_length() - 1
    seq_place = (2 * lax.axis_index("chip") + lax.axis_index("core")).astype(jnp.int32).reshape(1)

    result = None
    for first, groups, part in zip((0, early_groups), (early_groups, len(late)), parts):
        if first:
            part = after(part, first_sent)
        part = part + (rows_before(*part),)
        grid = (groups,)
        cols = lambda rows: pl.BlockSpec((rows, width), lambda i: (0, i))
        cols_all = lambda rows: pl.BlockSpec((rows, width), lambda i: (0, first + i))
        heads_g = pl.BlockSpec((1, tok_count, per_group), lambda i: (first + i, 0, 0))
        heads_t = pl.BlockSpec((per_group, tok_count), lambda i: (first + i, 0))
        heads_1 = pl.BlockSpec((1, 1, per_group), lambda i: (first + i, 0, 0))
        keys = pl.BlockSpec((tok_count, N), lambda i: (0, first + i))
        reads = pl.BlockSpec((tok_count, N), lambda i: (0, groups_here + first + i))
        early_spec = pl.BlockSpec((blocks - 1, N, width), lambda i: (0, 0, i))
        y, early, total, decays, sent = call(
            mix_kernel,
            "mix",
            (
                jax.ShapeDtypeStruct((tok_count, groups * width), F32),
                jax.ShapeDtypeStruct((blocks - 1, N, groups * width), F32),
                jax.ShapeDtypeStruct((N, groups * width), F32),
                jax.ShapeDtypeStruct((8, groups * width), F32),
                jax.ShapeDtypeStruct((N + RIM, groups * width), BF16),
            ),
            flops=8 * tok_count * N * width * groups,
            moved=14 * tok_count * width * groups,
            grid=grid,
            in_specs=specs_of(width) + [cols_all(CONV), keys, reads, heads_g, heads_g, heads_t, heads_t, heads_1, heads_1],
            out_specs=[cols(tok_count), early_spec, cols(N), cols(8), cols(N + RIM)],
            scratch_shapes=[pltpu.VMEM((tok_count + 8, width), F32)],
        )(*part, conv_proj, conv_out, conv_out, cum_g, steps_g, cum_t, steps_t, skip, decay)
        before, first_sent = (), None
        for level in range(levels - 1):
            other = swapped(sent, SEQ, 1 << level)
            total, decays, sent, fresh = combined(level, seq_place, total, decays, other, before, groups)
            before = (fresh,)
            first_sent = first_sent if level else sent
        other = swapped(sent, SEQ, 1 << (levels - 1))
        operands = [seq_place, y, conv_out, cum_g, early, decays, *before, other]
        specs = [SMEM, cols(tok_count), reads, heads_g, early_spec, cols(8), cols(N), cols(N + RIM)]
        alias = {}
        if result is not None:
            operands.append(result)
            specs.append(pl.BlockSpec(memory_space=pl.ANY))
            alias = {len(operands) - 1: 0}
        result = call(
            functools.partial(read_kernel, levels - 1),
            "read_out",
            jax.ShapeDtypeStruct((tok_count, heads_here * P_SIZE), BF16),
            flops=2 * tok_count * N * width * groups,
            moved=10 * tok_count * width * groups,
            vmem=12,
            grid=grid,
            in_specs=specs,
            out_specs=cols_all(tok_count),
            input_output_aliases=alias,
        )(*operands)
    return result


def solution(mesh):
    shape = mesh.shape
    split = Mesh(
        mesh.devices.reshape(shape["fsdp"], shape["seq"] // 2, 2, shape["tp"]),
        ("fsdp", "chip", "core", "tp"),
    )
    rows = ("fsdp", "chip", "core")
    return jax.shard_map(
        body,
        mesh=split,
        in_specs=(
            P(rows + ("tp",), None),
            P(rows, "tp"),
            P(None, rows, "tp"),
            P(rows, None, "tp"),
            P(None, rows, None, "tp"),
            P(),
            P(rows, "tp"),
            P("tp"),
            P("tp"),
            P("tp"),
            P(None, "tp"),
            P(None, None, "tp"),
        ),
        out_specs=P(rows, "tp"),
        check_vma=False,
    )
```

```python
import functools

import jax
import jax.numpy as jnp
from jax import lax
from jax.experimental import pallas as pl
from jax.experimental.pallas import tpu as pltpu
from jax.sharding import Mesh, PartitionSpec as P

P_SIZE = 64
N = 128
CONV = 4
SPAN = 128
LANES = 128
RIM = 16
FAR_PARTS = 2
SEQ = ("chip", "core")
F32 = jnp.float32
BF16 = jnp.bfloat16
SMEM = pl.BlockSpec(memory_space=pltpu.SMEM)
VMEM = pl.BlockSpec(memory_space=pltpu.VMEM)


def call(kernel, name, out_shape, flops=0, moved=0, vmem=60, **settings):
    return pl.pallas_call(
        kernel,
        out_shape=out_shape,
        name=name,
        cost_estimate=pl.CostEstimate(flops=flops // 50, bytes_accessed=moved // 50, transcendentals=0),
        compiler_params=pltpu.CompilerParams(vmem_limit_bytes=vmem * 1024 * 1024),
        **settings,
    )


def swapped(part, axis, by=1):
    return lax.ppermute(part, axis, [(i, i ^ by) for i in range(lax.axis_size(axis))])


def cut_kernel(chips, at_ref, tokens_ref, far_ref, own_ref):
    depth = far_ref.shape[1] // chips
    rows = tokens_ref.shape[0]
    f_at, c_at = at_ref[0], at_ref[1]
    for out, f in ((far_ref, 1 - f_at), (own_ref, f_at)):
        for k, c in enumerate((c_at, 1 - c_at)):
            for i in range(chips):
                start = pl.multiple_of(((f * chips + at_ref[3 + i]) * 2 + c) * depth, depth)
                out[k * rows : (k + 1) * rows, i * depth : (i + 1) * depth] = tokens_ref[:, pl.ds(start, depth)]


def stack_kernel(at_ref, *refs):
    pieces, rows_ref = refs[:-1], refs[-1]
    count = pieces[0].shape[0]
    for k in range(0, len(pieces), 2):
        rows_ref[pl.ds(pl.multiple_of((k + at_ref[2]) * count, count), count), :] = pieces[k][...]
        rows_ref[pl.ds(pl.multiple_of((k + 1 - at_ref[2]) * count, count), count), :] = pieces[k + 1][...]


def token_rows(at, far, far_t, far_c, far_tc, own, own_t, own_c, own_tc):
    count, depth = far.shape[0] // 2, far.shape[1]
    low = pl.BlockSpec((count, depth), lambda i: (0, 0))
    high = pl.BlockSpec((count, depth), lambda i: (1, 0))
    return call(
        stack_kernel,
        "stack_rows",
        jax.ShapeDtypeStruct((8 * count, depth), BF16),
        moved=32 * count * depth,
        grid=(1,),
        in_specs=[SMEM] + [low, low, high, high] * 2,
        out_specs=pl.BlockSpec((8 * count, depth), lambda i: (0, 0)),
    )(at, far, far_t, far_c, far_tc, own, own_t, own_c, own_tc)


def sample_kernel(count, coef_ref, mean_ref, devs_ref, out_ref):
    factor = (2.0 * (count - 1)) ** (-0.5)
    accum = mean_ref[...].astype(F32)
    for member in range(count):
        accum = accum + factor * coef_ref[member] * devs_ref[member].astype(F32)
    out_ref[...] = accum.astype(BF16)


def sampled_cols(mean_part, dev_part, swag_coef, at, width):
    rows, count = mean_part.shape[0], dev_part.shape[0]
    tile = rows // 4
    return call(
        functools.partial(sample_kernel, count),
        "sample",
        jax.ShapeDtypeStruct((rows, width), BF16),
        moved=2 * (count + 2) * rows * width,
        grid=(4,),
        in_specs=[
            SMEM,
            pl.BlockSpec((tile, width), lambda i: (i, at)),
            pl.BlockSpec((count, tile, width), lambda i: (0, i, at)),
        ],
        out_specs=pl.BlockSpec((tile, width), lambda i: (i, 0)),
    )(swag_coef, mean_part, dev_part)


def sample_pair_kernel(count, coef_ref, mean_ref, devs_ref, dt_ref, out_ref):
    factor = (2.0 * (count - 1)) ** (-0.5)
    accum = mean_ref[...].astype(F32)
    for member in range(count):
        accum = accum + factor * coef_ref[member] * devs_ref[member].astype(F32)
    width, heads = mean_ref.shape[2], dt_ref.shape[0]
    for k in range(2):
        out_ref[:, k * width : (k + 1) * width] = accum[:, k, :].astype(BF16)
    out_ref[:, 2 * width :] = jnp.zeros((out_ref.shape[0], LANES), BF16)
    rows = out_ref.shape[0]
    steps = dt_ref[:, pl.ds(pl.multiple_of(pl.program_id(0) * rows, rows), rows)]
    out_ref[:, 2 * width : 2 * width + heads] = jnp.transpose(steps.astype(F32)).astype(BF16)


def sampled_pair(mean_part, dev_part, dt_part, swag_coef):
    rows, _, width = mean_part.shape
    count = dev_part.shape[0]
    tile = min(rows, LANES)
    return call(
        functools.partial(sample_pair_kernel, count),
        "sample_pair",
        jax.ShapeDtypeStruct((rows, 2 * width + LANES), BF16),
        moved=4 * (count + 2) * rows * width,
        grid=(rows // tile,),
        in_specs=[
            SMEM,
            pl.BlockSpec((tile, 2, width), lambda i: (i, 0, 0)),
            pl.BlockSpec((count, tile, 2, width), lambda i: (0, i, 0, 0)),
            pl.BlockSpec((dt_part.shape[1], rows), lambda i: (0, 0)),
        ],
        out_specs=pl.BlockSpec((tile, 2 * width + LANES), lambda i: (i, 0)),
    )(swag_coef, mean_part, dev_part, dt_part.T)


def sent_straight(weight):
    return swapped(weight, "chip", 1), swapped(weight, "chip", 2)


def corner_parts(straight, each):
    rows = straight[0].shape[0] // (2 * each)
    cut = lambda a, i: a[i * rows : (i + 1) * rows]
    return [cut(straight[1], i) for i in range(each)] + [cut(straight[0], each + i) for i in range(each)]


def sent_on(parts):
    each = len(parts) // 2
    return [swapped(a, "chip", 1) for a in parts[:each]] + [swapped(a, "chip", 2) for a in parts[each:]]


def coded(part, heads):
    high = part.astype(BF16).astype(F32)
    return high + pltpu.roll(part - high, heads, 1)


def decoded(part, heads):
    return part + pltpu.roll(part, LANES - heads, 1)


def multiply_kernel(heads, with_steps, pieces, plan, rows_ref, *refs):
    weights, outs = refs[:pieces], refs[pieces:]
    joined = jnp.concatenate([weight[...] for weight in weights], axis=0)
    total = jnp.dot(rows_ref[...], joined, preferred_element_type=F32)
    for out, (first, sent) in zip(outs, plan):
        part = total[first : first + out.shape[0]]
        out[...] = part.astype(out.dtype)
        if with_steps and sent:
            @pl.when(pl.program_id(0) == pl.num_programs(0) - 1)
            def _():
                out[:, -LANES:] = coded(part[:, -LANES:], heads).astype(BF16)


def multiplied(rows, weights, heads, with_steps, document=None):
    width = weights[0].shape[1]
    tile = next(t for t in (512, 384, 128) if width % t == 0)
    half = rows.shape[0] // 4
    part = half // FAR_PARTS
    plan, shapes = [], []
    count = rows.shape[0] if document is None else 2 * half
    if document != 1:
        plan += [(half + i * part, True) for i in range(FAR_PARTS)] + [(0, False)]
        shapes += [(part, BF16)] * FAR_PARTS + [(half, F32)]
    if document != 0:
        plan += [(count - half, True), (count - 2 * half, False)]
        shapes += [(half, BF16), (half, F32)]
    return call(
        functools.partial(multiply_kernel, heads, with_steps, len(weights), plan),
        "multiply",
        tuple(jax.ShapeDtypeStruct((r, width), dtype) for r, dtype in shapes),
        flops=2 * count * rows.shape[1] * width,
        moved=2 * rows.size + 2 * rows.shape[1] * width + 12 * half * width,
        grid=(width // tile,),
        in_specs=[pl.BlockSpec((count, rows.shape[1]), lambda i: (document or 0, 0))]
        + [pl.BlockSpec((w.shape[0], tile), lambda i: (0, i)) for w in weights],
        out_specs=[pl.BlockSpec((r, tile), lambda i: (0, i)) for r, _ in shapes],
    )(rows, *weights)


def relay_kernel(heads, with_steps, kept_ref, *refs):
    out_ref, count = refs[-1], refs[0].shape[0]
    for i, got_ref in enumerate(refs[:-1]):
        rows = slice(i * count, (i + 1) * count)
        kept, got = kept_ref[rows, :], got_ref[...].astype(F32)
        out_ref[rows, :] = (kept + got).astype(BF16)
        if with_steps:
            wide = kept[:, -LANES:] + decoded(got[:, -LANES:], heads)
            lane = lax.broadcasted_iota(jnp.int32, wide.shape, 1)
            out_ref[rows, -LANES:] = coded(jnp.where(lane < heads, wide, 0.0), heads).astype(BF16)


def relayed(kept, got, heads, with_steps):
    rows, width = kept.shape
    part = pl.BlockSpec((rows // len(got), width), lambda i: (0, 0))
    return call(
        functools.partial(relay_kernel, heads, with_steps),
        "relay",
        jax.ShapeDtypeStruct((rows, width), BF16),
        moved=8 * rows * width,
        vmem=12,
        grid=(1,),
        in_specs=[pl.BlockSpec((rows, width), lambda i: (0, 0))] + [part] * len(got),
        out_specs=pl.BlockSpec((rows, width), lambda i: (0, 0)),
    )(kept, *got)


def rim_kernel(kept, got_c, got_f, rim_ref):
    rim_ref[...] = (kept[...] + got_c[...].astype(F32) + got_f[...].astype(F32)).astype(BF16)


def rows_before(kept, got_c, got_f):
    rows, width = got_f.shape
    at = rows // RIM - 1
    rim = call(
        rim_kernel,
        "rim",
        jax.ShapeDtypeStruct((RIM, width), BF16),
        moved=10 * RIM * width,
        vmem=12,
        grid=(1,),
        in_specs=[pl.BlockSpec((RIM, width), lambda i: (at, 0))] * 3,
        out_specs=pl.BlockSpec((RIM, width), lambda i: (0, 0)),
    )(kept, got_c, got_f)
    return lax.ppermute(rim, SEQ, [(i, i + 1) for i in range(lax.axis_size(SEQ) - 1)])


def convolved(width, kept, got_c, got_f, rim, taps, padded):
    count = padded.shape[0] - 8
    proj = kept[:, :width] + got_c[:, :width].astype(F32) + got_f[:, :width].astype(F32)
    padded[8:, :] = proj.astype(BF16).astype(F32)
    padded[:8, :] = rim[:, :width].astype(F32)[RIM - 8 :]
    first = 8 - (CONV - 1)
    conv_sum = taps[0:1, :] * padded[first : first + count, :]
    for offset in range(1, CONV):
        conv_sum = conv_sum + taps[offset : offset + 1, :] * padded[first + offset : first + offset + count, :]
    return (conv_sum * jax.nn.sigmoid(conv_sum)).astype(BF16)


def state_proj_kernel(
    heads, kept, got_c, got_f, rim, taps, bias, rate, out_ref, cum_ref, steps_ref, cum_t_ref, steps_t_ref, decay_ref, padded
):
    count, width = out_ref.shape
    out_ref[...] = convolved(width, kept, got_c, got_f, rim, taps, padded)
    logits = kept[:, width:] + decoded(got_c[:, width:].astype(F32), heads) + decoded(got_f[:, width:].astype(F32), heads)
    steps = jax.nn.softplus(logits[:, :heads] + bias[...])
    row = lax.broadcasted_iota(jnp.int32, (SPAN, SPAN), 0)
    col = lax.broadcasted_iota(jnp.int32, (SPAN, SPAN), 1)
    causal = jnp.where(row >= col, 1.0, 0.0)
    groups, per_group = cum_ref.shape[0], cum_ref.shape[2]
    through = jnp.zeros((1, heads), F32)
    for at in range(0, count, SPAN):
        span = slice(at, at + SPAN)
        steps_b = steps[span, :]
        cum = jnp.dot(
            causal, -steps_b * rate[...], precision=lax.Precision.HIGHEST, preferred_element_type=F32
        )
        through = through + cum[SPAN - 1 : SPAN, :]
        cum_t_ref[:, span] = jnp.transpose(cum)
        steps_t_ref[:, span] = jnp.transpose(steps_b)
        for g in range(groups):
            cum_ref[g, span, :] = cum[:, g * per_group : (g + 1) * per_group]
            steps_ref[g, span, :] = steps_b[:, g * per_group : (g + 1) * per_group]
    for g in range(groups):
        decay_ref[g] = jnp.exp(through)[:, g * per_group : (g + 1) * per_group]


def pairwise(columns, first):
    shape = (columns.shape[0], 2 * P_SIZE)
    lane = lax.broadcasted_iota(jnp.int32, shape, 1)
    return jnp.where(lane < P_SIZE, columns[:, first : first + 1], columns[:, first + 1 : first + 2])


def over_channels(columns):
    return jnp.concatenate([pairwise(columns, h) for h in range(0, columns.shape[1], 2)], axis=1)


def mix_kernel(
    kept, got_c, got_f, rim, taps, keys, reads, cum_g, steps_g, cum_t, steps_t, skip, decay, y_ref, early_ref, total_ref, decays_ref, sent_ref, padded
):
    width = y_ref.shape[1]
    values = convolved(width, kept, got_c, got_f, rim, taps, padded)
    cum, steps = cum_g[0], steps_g[0]
    heads = cum.shape[1]
    row = lax.broadcasted_iota(jnp.int32, (SPAN, SPAN), 0)
    col = lax.broadcasted_iota(jnp.int32, (SPAN, SPAN), 1)
    causal = row >= col
    lane = lax.broadcasted_iota(jnp.int32, (SPAN, 2 * P_SIZE), 1)
    gain = over_channels(skip[0])
    state = None
    for at in range(0, y_ref.shape[0], SPAN):
        span = slice(at, at + SPAN)
        keys_b, reads_b, values_b = keys[span, :], reads[span, :], values[span, :]
        cum_b, steps_b = cum[span, :], steps[span, :]
        last = cum_b[SPAN - 1 : SPAN, :]
        scores = lax.dot_general(reads_b, keys_b, (((1,), (1,)), ((), ())), preferred_element_type=F32)
        scores = jnp.where(causal, scores, 0.0)
        reach = jnp.exp(last - cum_b) * steps_b
        scaled = []
        for head in range(0, heads, 2):
            chans = slice(head * P_SIZE, (head + 2) * P_SIZE)
            two = []
            for h in (head, head + 1):
                gap = cum_b[:, h : h + 1] - cum_t[h : h + 1, span]
                two.append((scores * jnp.exp(jnp.minimum(gap, 0.0)) * steps_t[h : h + 1, span]).astype(BF16))
            values_h = values_b[:, chans]
            both = jnp.dot(jnp.concatenate(two, axis=0), values_h, preferred_element_type=F32)
            inner = jnp.where(lane < P_SIZE, both[:SPAN], both[SPAN:])
            wide = values_h.astype(F32)
            y_ref[span, chans] = inner + gain[:, chans] * wide
            scaled.append((wide * pairwise(reach, head)).astype(BF16))
        fresh = lax.dot_general(
            keys_b, jnp.concatenate(scaled, axis=1), (((0,), (0,)), ((), ())), preferred_element_type=F32
        )
        state = fresh if state is None else over_channels(jnp.exp(last)) * state + fresh
        if at + SPAN < y_ref.shape[0]:
            early_ref[at // SPAN] = fresh
    total_ref[...] = state
    wide = over_channels(decay[0])
    decays_ref[0:1, :] = wide
    decays_ref[1:2, :] = jnp.ones_like(wide)
    pack_state([sent_ref], state, wide)


def pack_state(sent_refs, state, decay):
    high = decay.astype(BF16).astype(F32)
    row = lax.broadcasted_iota(jnp.int32, (RIM, decay.shape[1]), 0)
    tail = jnp.where(row == 0, high, jnp.where(row == 1, decay - high, 0.0)).astype(BF16)
    state = state.astype(BF16)
    at = 0
    for sent_ref in sent_refs[:-1]:
        sent_ref[...] = state[at : at + sent_ref.shape[0]]
        at += sent_ref.shape[0]
    sent_refs[-1][: N - at, :] = state[at:]
    sent_refs[-1][N - at :, :] = tail


def unpack_state(got_refs):
    rows = jnp.concatenate([ref[...] for ref in got_refs], axis=0).astype(F32)
    return rows[:N], rows[N : N + 1, :] + rows[N + 1 : N + 2, :]


def combine_kernel(level, got, has_before, place_ref, total, decays, *refs):
    other, refs = refs[:got], refs[got:]
    if has_before:
        before, refs = refs[0][...], refs[1:]
    total_ref, decays_ref, before_ref, *sent_refs = refs
    come, decay = unpack_state(other)
    whole, part = decays[0:1, :], decays[1:2, :]
    upper = (place_ref[0] >> level) & 1 == 1
    fresh = jnp.where(upper, part, 0.0) * come
    before_ref[...] = before + fresh if has_before else fresh
    joint = jnp.where(upper, 1.0, decay) * total[...] + jnp.where(upper, whole, 1.0) * come
    total_ref[...] = joint
    decays_ref[0:1, :] = whole * decay
    decays_ref[1:2, :] = jnp.where(upper, decay * part, part)
    pack_state(sent_refs, joint, whole * decay)


def read_kernel(level, place_ref, y, reads, cum_g, early, decays, before, other, *refs):
    out_ref = refs[-1]
    upper = (place_ref[0] >> level) & 1 == 1
    state = before[...] + jnp.where(upper, decays[1:2, :], 0.0) * unpack_state([other])[0]
    cum = cum_g[0]
    for at in range(0, out_ref.shape[0], SPAN):
        span = slice(at, at + SPAN)
        cum_b = cum[span, :]
        seen = jnp.dot(reads[span, :], state.astype(BF16), preferred_element_type=F32)
        out_ref[span, :] = (y[span, :] + over_channels(jnp.exp(cum_b)) * seen).astype(BF16)
        if at + SPAN < out_ref.shape[0]:
            state = over_channels(jnp.exp(cum_b[SPAN - 1 : SPAN, :])) * state + early[at // SPAN]


def combined(level, place, total, decays, other, before, groups, cut):
    width = total.shape[1] // groups
    block = lambda rows: pl.BlockSpec((rows, width), lambda i: (0, i))
    shape = lambda rows, dtype: jax.ShapeDtypeStruct((rows, total.shape[1]), dtype)
    total, decays, before, *sent = call(
        functools.partial(combine_kernel, level, len(other), bool(before)),
        "combine",
        (shape(N, F32), shape(8, F32), shape(N, F32)) + tuple(shape(rows, BF16) for rows in cut),
        flops=6 * total.size,
        moved=20 * total.size,
        vmem=12,
        grid=(groups,),
        in_specs=[SMEM, block(N), block(8)] + [block(a.shape[0]) for a in other] + [block(N)] * len(before),
        out_specs=[block(N), block(8), block(N)] + [block(rows) for rows in cut],
    )(place, total, decays, *other, *before)
    return total, decays, before, sent


def body(
    tokens,
    proj_mean,
    proj_devs,
    bc_mean,
    bc_devs,
    swag_coef,
    dt_weight,
    dt_bias,
    decay_rate,
    skip_gain,
    conv_proj,
    conv_bc,
):
    heads_here = decay_rate.shape[0]
    groups_here = bc_mean.shape[2] // N
    per_group = heads_here // groups_here
    width_bc = 2 * bc_mean.shape[2]
    rows_k = proj_mean.shape[0]
    chips = lax.axis_size("chip")
    count = lax.axis_size(SEQ)

    def after(arrays, earlier):
        return lax.optimization_barrier((arrays, earlier))[0]

    width = per_group * P_SIZE
    early_groups = max(1, groups_here // 2)
    fill = -heads_here % LANES
    late = list(range(early_groups, groups_here))

    plane = chips == 4
    two_shares = lax.axis_size("tp") == 2
    place = lax.axis_index("chip") if plane else 0
    at = jnp.stack([lax.axis_index(a) for a in ("fsdp", "core", "tp")] + [place ^ i for i in range(chips)]).astype(jnp.int32)
    share, depth = tokens.shape[0], chips * rows_k
    weight_bc = sampled_pair(bc_mean, bc_devs, dt_weight, swag_coef)
    tokens = after(tokens, weight_bc)
    cut = jax.ShapeDtypeStruct((2 * share, depth), BF16)
    far, own = call(
        functools.partial(cut_kernel, chips),
        "cut_tokens",
        (cut,) * 2,
        moved=4 * tokens.size,
        in_specs=[SMEM, VMEM],
        out_specs=[VMEM] * 2,
    )(at, tokens)
    proj_mean = after(proj_mean, own)
    far = swapped(far, "fsdp")

    weight_early = sampled_cols(proj_mean, proj_devs, swag_coef, 0, early_groups * width)
    weight_late = None
    if late:
        weight_late = sampled_cols(proj_mean, proj_devs, swag_coef, early_groups // len(late), len(late) * width)
    tok_count = share * lax.axis_size("tp")
    blocks = tok_count // SPAN

    def partial_sums(rows, pieces, with_steps, before_send=(), before_relay=()):
        *far_sent, far_kept, sent, kept = multiplied(rows, pieces, heads_here, with_steps)
        far_got = [swapped(a, "core") for a in after(far_sent, before_send)]
        back = relayed(far_kept, after(far_got, before_relay), heads_here, with_steps)
        return (kept, swapped(after(sent, back), "core")), back

    specs_of = lambda width: [pl.BlockSpec((tok_count, width), lambda i: (0, i))] * 3 + [
        pl.BlockSpec((RIM, width), lambda i: (0, i)),
    ]
    whole_of = lambda *shape: pl.BlockSpec(shape, lambda i: (0,) * len(shape))
    by_group = (groups_here, tok_count, per_group)
    by_head = (heads_here, tok_count)
    by_decay = (groups_here, 1, per_group)
    state_proj = lambda part: call(
        functools.partial(state_proj_kernel, heads_here),
        "state_proj",
        (jax.ShapeDtypeStruct((tok_count, width_bc), BF16),)
        + tuple(jax.ShapeDtypeStruct(a, F32) for a in (by_group, by_group, by_head, by_head, by_decay)),
        moved=10 * tok_count * width_bc,
        grid=(1,),
        in_specs=specs_of(width_bc + LANES) + [whole_of(CONV, width_bc)] + [whole_of(1, heads_here)] * 2,
        out_specs=[whole_of(*a) for a in ((tok_count, width_bc), by_group, by_group, by_head, by_head, by_decay)],
        scratch_shapes=[pltpu.VMEM((tok_count + 8, width_bc), F32)],
    )(*part, rows_before(*part), conv_bc.reshape(CONV, width_bc), dt_bias[None], decay_rate[None])
    if plane and two_shares:
        bc = [weight_bc, *sent_straight(weight_bc)]
        bc += sent_on(corner_parts(bc[1:], 1))
        own_t = swapped(own, "tp")
        weight_early = after(weight_early, bc[3:])
        early = [weight_early, *sent_straight(weight_early)]
        far = after(far, (own_t, bc[3:], weight_late))
        far_t = swapped(far, "tp")
        own, own_t = after((own, own_t), far)
        own_c, own_tc = swapped(own, "core"), swapped(own_t, "core")
        halves = corner_parts(early[1:], 1)
        far_c, far_tc = swapped(far, "core"), swapped(after(far_t, halves), "core")
        rows = token_rows(at, far, far_t, far_c, far_tc, own, own_t, own_c, own_tc)
        part_bc, back_bc = partial_sums(rows, bc, True)
        early += sent_on(halves)
        got_bc = swapped(back_bc, "fsdp")
        weight_late = after(weight_late, (back_bc, early[3:]))
        part, back = partial_sums(rows, early, False, before_relay=got_bc)
        got = swapped(after(back, got_bc), "fsdp")
        straight = sent_straight(weight_late)
        corners = sent_on(corner_parts(straight, 1))
        seen = state_proj(after(part_bc + (got_bc,), back))
        part_late, back_late = partial_sums(rows, [weight_late, *straight, *corners], False, before_send=seen)
        got_late = swapped(after(back_late, got), "fsdp")
        got = after(got, back_late)
    else:
        whole = lambda a, axis: lax.all_gather(a, axis, axis=0, tiled=True)
        ranges = [r for a in (far, own) for r in (a[:share], swapped(a[share:], "core"))]
        rows = jnp.concatenate([whole(r, "tp") for r in ranges], axis=0)
        part, back = partial_sums(rows, [whole(weight_early, "chip")], False)
        part_bc, back_bc = partial_sums(rows, [whole(weight_bc, "chip")], True)
        got, got_bc = swapped(back, "fsdp"), swapped(back_bc, "fsdp")
        if late:
            part_late, back_late = partial_sums(rows, [whole(weight_late, "chip")], False)
            got_late = swapped(back_late, "fsdp")
        seen = state_proj(part_bc + (got_bc,))
    conv_out, cum_g, steps_g, cum_t, steps_t, decay = seen
    parts = [part + (got,)]
    if late:
        parts.append(part_late + (got_late,))

    skip = skip_gain.reshape(by_decay)
    levels = count.bit_length() - 1
    seq_place = (2 * lax.axis_index("chip") + lax.axis_index("core")).astype(jnp.int32).reshape(1)

    result = None
    for first, groups, part in zip((0, early_groups), (early_groups, len(late)), parts):
        part = part + (rows_before(*part),)
        if first:
            part = after(part, sent)
        grid = (groups,)
        cols = lambda rows: pl.BlockSpec((rows, width), lambda i: (0, i))
        cols_all = lambda rows: pl.BlockSpec((rows, width), lambda i: (0, first + i))
        heads_g = pl.BlockSpec((1, tok_count, per_group), lambda i: (first + i, 0, 0))
        heads_t = pl.BlockSpec((per_group, tok_count), lambda i: (first + i, 0))
        heads_1 = pl.BlockSpec((1, 1, per_group), lambda i: (first + i, 0, 0))
        keys = pl.BlockSpec((tok_count, N), lambda i: (0, first + i))
        reads = pl.BlockSpec((tok_count, N), lambda i: (0, groups_here + first + i))
        early_spec = pl.BlockSpec((blocks - 1, N, width), lambda i: (0, 0, i))
        y, early, total, decays, sent = call(
            mix_kernel,
            "mix",
            (
                jax.ShapeDtypeStruct((tok_count, groups * width), F32),
                jax.ShapeDtypeStruct((blocks - 1, N, groups * width), F32),
                jax.ShapeDtypeStruct((N, groups * width), F32),
                jax.ShapeDtypeStruct((8, groups * width), F32),
                jax.ShapeDtypeStruct((N + RIM, groups * width), BF16),
            ),
            flops=8 * tok_count * N * width * groups,
            moved=14 * tok_count * width * groups,
            grid=grid,
            in_specs=specs_of(width) + [cols_all(CONV), keys, reads, heads_g, heads_g, heads_t, heads_t, heads_1, heads_1],
            out_specs=[cols(tok_count), early_spec, cols(N), cols(8), cols(N + RIM)],
            scratch_shapes=[pltpu.VMEM((tok_count + 8, width), F32)],
        )(*part, conv_proj, conv_out, conv_out, cum_g, steps_g, cum_t, steps_t, skip, decay)
        before, sent = (), [sent]
        for level in range(levels - 1):
            other = [swapped(a, SEQ, 1 << level) for a in sent]
            cut = (N // 2, N // 2 + RIM) if not first and level + 2 < levels else (N + RIM,)
            total, decays, fresh, sent = combined(level, seq_place, total, decays, other, before, groups, cut)
            before = (fresh,)
        (other,) = [swapped(a, SEQ, 1 << (levels - 1)) for a in sent]
        operands = [seq_place, y, conv_out, cum_g, early, decays, *before, other]
        specs = [SMEM, cols(tok_count), reads, heads_g, early_spec, cols(8), cols(N), cols(N + RIM)]
        alias = {}
        if result is not None:
            operands.append(result)
            specs.append(pl.BlockSpec(memory_space=pl.ANY))
            alias = {len(operands) - 1: 0}
        result = call(
            functools.partial(read_kernel, levels - 1),
            "read_out",
            jax.ShapeDtypeStruct((tok_count, heads_here * P_SIZE), BF16),
            flops=2 * tok_count * N * width * groups,
            moved=10 * tok_count * width * groups,
            vmem=12,
            grid=grid,
            in_specs=specs,
            out_specs=cols_all(tok_count),
            input_output_aliases=alias,
        )(*operands)
    return result


def solution(mesh):
    shape = mesh.shape
    split = Mesh(
        mesh.devices.reshape(shape["fsdp"], shape["seq"] // 2, 2, shape["tp"]),
        ("fsdp", "chip", "core", "tp"),
    )
    rows = ("fsdp", "chip", "core")
    return jax.shard_map(
        body,
        mesh=split,
        in_specs=(
            P(rows + ("tp",), None),
            P(rows, "tp"),
            P(None, rows, "tp"),
            P(rows, None, "tp"),
            P(None, rows, None, "tp"),
            P(),
            P(rows, "tp"),
            P("tp"),
            P("tp"),
            P("tp"),
            P(None, "tp"),
            P(None, None, "tp"),
        ),
        out_specs=P(rows, "tp"),
        check_vma=False,
    )
```

```python
import functools

import jax
import jax.numpy as jnp
from jax import lax
from jax.experimental import pallas as pl
from jax.experimental.pallas import tpu as pltpu
from jax.sharding import Mesh, PartitionSpec as P

P_SIZE = 64
N = 128
CONV = 4
SPAN = 128
LANES = 128
RIM = 16
FAR_PARTS = 2
SEQ = ("chip", "core")
F32 = jnp.float32
BF16 = jnp.bfloat16
SMEM = pl.BlockSpec(memory_space=pltpu.SMEM)
VMEM = pl.BlockSpec(memory_space=pltpu.VMEM)


def call(kernel, name, out_shape, flops=0, moved=0, vmem=60, **settings):
    return pl.pallas_call(
        kernel,
        out_shape=out_shape,
        name=name,
        cost_estimate=pl.CostEstimate(flops=flops // 50, bytes_accessed=moved // 50, transcendentals=0),
        compiler_params=pltpu.CompilerParams(vmem_limit_bytes=vmem * 1024 * 1024),
        **settings,
    )


def swapped(part, axis, by=1):
    return lax.ppermute(part, axis, [(i, i ^ by) for i in range(lax.axis_size(axis))])


def cut_kernel(chips, at_ref, tokens_ref, far_ref, own_ref):
    depth = far_ref.shape[1] // chips
    rows = tokens_ref.shape[0]
    f_at, c_at = at_ref[0], at_ref[1]
    for out, f in ((far_ref, 1 - f_at), (own_ref, f_at)):
        for k, c in enumerate((c_at, 1 - c_at)):
            for i in range(chips):
                start = pl.multiple_of(((f * chips + at_ref[3 + i]) * 2 + c) * depth, depth)
                out[k * rows : (k + 1) * rows, i * depth : (i + 1) * depth] = tokens_ref[:, pl.ds(start, depth)]


def stack_rows(at_ref, pieces, rows_ref):
    count = pieces[0].shape[0]
    for k in range(0, len(pieces), 2):
        rows_ref[pl.ds(pl.multiple_of((k + at_ref[2]) * count, count), count), :] = pieces[k][...]
        rows_ref[pl.ds(pl.multiple_of((k + 1 - at_ref[2]) * count, count), count), :] = pieces[k + 1][...]


def sample_kernel(count, coef_ref, mean_ref, devs_ref, out_ref):
    factor = (2.0 * (count - 1)) ** (-0.5)
    accum = mean_ref[...].astype(F32)
    for member in range(count):
        accum = accum + factor * coef_ref[member] * devs_ref[member].astype(F32)
    out_ref[...] = accum.astype(BF16)


def sampled_cols(mean_part, dev_part, swag_coef, at, width):
    rows, count = mean_part.shape[0], dev_part.shape[0]
    tile = rows // 4
    return call(
        functools.partial(sample_kernel, count),
        "sample",
        jax.ShapeDtypeStruct((rows, width), BF16),
        moved=2 * (count + 2) * rows * width,
        grid=(4,),
        in_specs=[
            SMEM,
            pl.BlockSpec((tile, width), lambda i: (i, at)),
            pl.BlockSpec((count, tile, width), lambda i: (0, i, at)),
        ],
        out_specs=pl.BlockSpec((tile, width), lambda i: (i, 0)),
    )(swag_coef, mean_part, dev_part)


def sample_pair_kernel(count, coef_ref, mean_ref, devs_ref, dt_ref, out_ref):
    factor = (2.0 * (count - 1)) ** (-0.5)
    width, heads = mean_ref.shape[2], dt_ref.shape[0]
    for k in range(2):
        accum = mean_ref[:, k, :].astype(F32)
        for member in range(count):
            accum = accum + factor * coef_ref[member] * devs_ref[member, :, k, :].astype(F32)
        out_ref[:, k * width : (k + 1) * width] = accum.astype(BF16)
    out_ref[:, 2 * width :] = jnp.zeros((out_ref.shape[0], LANES), BF16)
    rows = out_ref.shape[0]
    steps = dt_ref[:, pl.ds(pl.multiple_of(pl.program_id(0) * rows, rows), rows)]
    out_ref[:, 2 * width : 2 * width + heads] = jnp.transpose(steps.astype(F32)).astype(BF16)


def sampled_pair(mean_part, dev_part, dt_part, swag_coef):
    rows, _, width = mean_part.shape
    count = dev_part.shape[0]
    tile = min(rows, LANES)
    return call(
        functools.partial(sample_pair_kernel, count),
        "sample_pair",
        jax.ShapeDtypeStruct((rows, 2 * width + LANES), BF16),
        moved=4 * (count + 2) * rows * width,
        grid=(rows // tile,),
        in_specs=[
            SMEM,
            pl.BlockSpec((tile, 2, width), lambda i: (i, 0, 0)),
            pl.BlockSpec((count, tile, 2, width), lambda i: (0, i, 0, 0)),
            pl.BlockSpec((dt_part.shape[1], rows), lambda i: (0, 0)),
        ],
        out_specs=pl.BlockSpec((tile, 2 * width + LANES), lambda i: (i, 0)),
    )(swag_coef, mean_part, dev_part, dt_part.T)


def sent_straight(weight):
    return swapped(weight, "chip", 1), swapped(weight, "chip", 2)


def corner_parts(straight, each):
    rows = straight[0].shape[0] // (2 * each)
    cut = lambda a, i: a[i * rows : (i + 1) * rows]
    return [cut(straight[1], i) for i in range(each)] + [cut(straight[0], each + i) for i in range(each)]


def sent_on(parts):
    each = len(parts) // 2
    return [swapped(a, "chip", 1) for a in parts[:each]] + [swapped(a, "chip", 2) for a in parts[each:]]


def coded(part, heads):
    high = part.astype(BF16).astype(F32)
    return high + pltpu.roll(part - high, heads, 1)


def decoded(part, heads):
    return part + pltpu.roll(part, LANES - heads, 1)


def multiply_kernel(heads, with_steps, shares, pieces, plan, at_ref, *refs):
    shares, weights, outs, rows_ref = refs[:shares], refs[shares : shares + pieces], refs[shares + pieces : -1], refs[-1]

    @pl.when(pl.program_id(0) == 0)
    def _():
        if len(shares) == 1:
            rows_ref[...] = shares[0][...]
        else:
            stack_rows(at_ref, shares, rows_ref)

    joined = jnp.concatenate([weight[...] for weight in weights], axis=0)
    total = jnp.dot(rows_ref[...], joined, preferred_element_type=F32)
    for out, (first, sent) in zip(outs, plan):
        part = total[first : first + out.shape[0]]
        out[...] = part.astype(out.dtype)
        if with_steps and sent:
            @pl.when(pl.program_id(0) == pl.num_programs(0) - 1)
            def _():
                out[:, -LANES:] = coded(part[:, -LANES:], heads).astype(BF16)


def multiplied(at, rows, weights, heads, with_steps):
    width = weights[0].shape[1]
    tile = next(t for t in (512, 384, 128) if width % t == 0)
    depth = rows[0].shape[1]
    if len(rows) == 1:
        count = rows[0].shape[0]
        row_specs = [pl.BlockSpec(rows[0].shape, lambda i: (0, 0))]
    else:
        share = rows[0].shape[0] // 2
        count = len(rows) * share
        low = pl.BlockSpec((share, depth), lambda i: (0, 0))
        high = pl.BlockSpec((share, depth), lambda i: (1, 0))
        row_specs = [low, low, high, high] * 2
    half = count // 4
    part = half // FAR_PARTS
    plan = [(half + i * part, True) for i in range(FAR_PARTS)] + [(0, False), (3 * half, True), (2 * half, False)]
    shapes = [(part, BF16)] * FAR_PARTS + [(half, F32), (half, BF16), (half, F32)]
    return call(
        functools.partial(multiply_kernel, heads, with_steps, len(rows), len(weights), plan),
        "multiply",
        tuple(jax.ShapeDtypeStruct((r, width), dtype) for r, dtype in shapes),
        flops=2 * count * depth * width,
        moved=2 * count * depth + 2 * depth * width + 12 * half * width,
        vmem=34,
        grid=(width // tile,),
        in_specs=[SMEM] + row_specs + [pl.BlockSpec((w.shape[0], tile), lambda i: (0, i)) for w in weights],
        out_specs=[pl.BlockSpec((r, tile), lambda i: (0, i)) for r, _ in shapes],
        scratch_shapes=[pltpu.VMEM((count, depth), BF16)],
    )(at, *rows, *weights)


def relay_kernel(heads, with_steps, kept_ref, *refs):
    out_ref, count = refs[-1], refs[0].shape[0]
    for i, got_ref in enumerate(refs[:-1]):
        rows = slice(i * count, (i + 1) * count)
        kept, got = kept_ref[rows, :], got_ref[...].astype(F32)
        out_ref[rows, :] = (kept + got).astype(BF16)
        if with_steps:
            wide = kept[:, -LANES:] + decoded(got[:, -LANES:], heads)
            lane = lax.broadcasted_iota(jnp.int32, wide.shape, 1)
            out_ref[rows, -LANES:] = coded(jnp.where(lane < heads, wide, 0.0), heads).astype(BF16)


def relayed(kept, got, heads, with_steps):
    rows, width = kept.shape
    part = pl.BlockSpec((rows // len(got), width), lambda i: (0, 0))
    return call(
        functools.partial(relay_kernel, heads, with_steps),
        "relay",
        jax.ShapeDtypeStruct((rows, width), BF16),
        moved=8 * rows * width,
        vmem=12,
        grid=(1,),
        in_specs=[pl.BlockSpec((rows, width), lambda i: (0, 0))] + [part] * len(got),
        out_specs=pl.BlockSpec((rows, width), lambda i: (0, 0)),
    )(kept, *got)


def rim_kernel(kept, got_c, got_f, rim_ref):
    rim_ref[...] = (kept[...] + got_c[...].astype(F32) + got_f[...].astype(F32)).astype(BF16)


def rows_before(kept, got_c, got_f):
    rows, width = got_f.shape
    at = rows // RIM - 1
    rim = call(
        rim_kernel,
        "rim",
        jax.ShapeDtypeStruct((RIM, width), BF16),
        moved=10 * RIM * width,
        vmem=12,
        grid=(1,),
        in_specs=[pl.BlockSpec((RIM, width), lambda i: (at, 0))] * 3,
        out_specs=pl.BlockSpec((RIM, width), lambda i: (0, 0)),
    )(kept, got_c, got_f)
    return lax.ppermute(rim, SEQ, [(i, i + 1) for i in range(lax.axis_size(SEQ) - 1)])


def convolved(width, kept, got_c, got_f, rim, taps, padded):
    count = padded.shape[0] - 8
    proj = kept[:, :width] + got_c[:, :width].astype(F32) + got_f[:, :width].astype(F32)
    padded[8:, :] = proj.astype(BF16).astype(F32)
    padded[:8, :] = rim[:, :width].astype(F32)[RIM - 8 :]
    first = 8 - (CONV - 1)
    conv_sum = taps[0:1, :] * padded[first : first + count, :]
    for offset in range(1, CONV):
        conv_sum = conv_sum + taps[offset : offset + 1, :] * padded[first + offset : first + offset + count, :]
    return (conv_sum * jax.nn.sigmoid(conv_sum)).astype(BF16)


def state_proj_kernel(
    heads, kept, got_c, got_f, rim, taps, bias, rate, out_ref, cum_ref, steps_ref, cum_t_ref, steps_t_ref, decay_ref, padded
):
    count, width = out_ref.shape
    out_ref[...] = convolved(width, kept, got_c, got_f, rim, taps, padded)
    logits = kept[:, width:] + decoded(got_c[:, width:].astype(F32), heads) + decoded(got_f[:, width:].astype(F32), heads)
    steps = jax.nn.softplus(logits[:, :heads] + bias[...])
    row = lax.broadcasted_iota(jnp.int32, (SPAN, SPAN), 0)
    col = lax.broadcasted_iota(jnp.int32, (SPAN, SPAN), 1)
    causal = jnp.where(row >= col, 1.0, 0.0)
    groups, per_group = cum_ref.shape[0], cum_ref.shape[2]
    through = jnp.zeros((1, heads), F32)
    for at in range(0, count, SPAN):
        span = slice(at, at + SPAN)
        steps_b = steps[span, :]
        cum = jnp.dot(
            causal, -steps_b * rate[...], precision=lax.Precision.HIGHEST, preferred_element_type=F32
        )
        through = through + cum[SPAN - 1 : SPAN, :]
        cum_t_ref[:, span] = jnp.transpose(cum)
        steps_t_ref[:, span] = jnp.transpose(steps_b)
        for g in range(groups):
            cum_ref[g, span, :] = cum[:, g * per_group : (g + 1) * per_group]
            steps_ref[g, span, :] = steps_b[:, g * per_group : (g + 1) * per_group]
    for g in range(groups):
        decay_ref[g] = jnp.exp(through)[:, g * per_group : (g + 1) * per_group]


def pairwise(columns, first):
    shape = (columns.shape[0], 2 * P_SIZE)
    lane = lax.broadcasted_iota(jnp.int32, shape, 1)
    return jnp.where(lane < P_SIZE, columns[:, first : first + 1], columns[:, first + 1 : first + 2])


def over_channels(columns):
    return jnp.concatenate([pairwise(columns, h) for h in range(0, columns.shape[1], 2)], axis=1)


def mix_kernel(
    kept, got_c, got_f, rim, taps, keys, reads, cum_g, steps_g, cum_t, steps_t, skip, decay, y_ref, early_ref, total_ref, decays_ref, sent_ref, padded
):
    width = y_ref.shape[1]
    values = convolved(width, kept, got_c, got_f, rim, taps, padded)
    cum, steps = cum_g[0], steps_g[0]
    heads = cum.shape[1]
    row = lax.broadcasted_iota(jnp.int32, (SPAN, SPAN), 0)
    col = lax.broadcasted_iota(jnp.int32, (SPAN, SPAN), 1)
    causal = row >= col
    lane = lax.broadcasted_iota(jnp.int32, (SPAN, 2 * P_SIZE), 1)
    gain = over_channels(skip[0])
    state = None
    for at in range(0, y_ref.shape[0], SPAN):
        span = slice(at, at + SPAN)
        keys_b, reads_b, values_b = keys[span, :], reads[span, :], values[span, :]
        cum_b, steps_b = cum[span, :], steps[span, :]
        last = cum_b[SPAN - 1 : SPAN, :]
        scores = lax.dot_general(reads_b, keys_b, (((1,), (1,)), ((), ())), preferred_element_type=F32)
        scores = jnp.where(causal, scores, 0.0)
        reach = jnp.exp(last - cum_b) * steps_b
        scaled = []
        for head in range(0, heads, 2):
            chans = slice(head * P_SIZE, (head + 2) * P_SIZE)
            two = []
            for h in (head, head + 1):
                gap = cum_b[:, h : h + 1] - cum_t[h : h + 1, span]
                two.append((scores * jnp.exp(jnp.minimum(gap, 0.0)) * steps_t[h : h + 1, span]).astype(BF16))
            values_h = values_b[:, chans]
            both = jnp.dot(jnp.concatenate(two, axis=0), values_h, preferred_element_type=F32)
            inner = jnp.where(lane < P_SIZE, both[:SPAN], both[SPAN:])
            wide = values_h.astype(F32)
            y_ref[span, chans] = inner + gain[:, chans] * wide
            scaled.append((wide * pairwise(reach, head)).astype(BF16))
        fresh = lax.dot_general(
            keys_b, jnp.concatenate(scaled, axis=1), (((0,), (0,)), ((), ())), preferred_element_type=F32
        )
        state = fresh if state is None else over_channels(jnp.exp(last)) * state + fresh
        if at + SPAN < y_ref.shape[0]:
            early_ref[at // SPAN] = fresh
    total_ref[...] = state
    wide = over_channels(decay[0])
    decays_ref[0:1, :] = wide
    decays_ref[1:2, :] = jnp.ones_like(wide)
    pack_state([sent_ref], state, wide)


def pack_state(sent_refs, state, decay):
    high = decay.astype(BF16).astype(F32)
    row = lax.broadcasted_iota(jnp.int32, (RIM, decay.shape[1]), 0)
    tail = jnp.where(row == 0, high, jnp.where(row == 1, decay - high, 0.0)).astype(BF16)
    state = state.astype(BF16)
    at = 0
    for sent_ref in sent_refs[:-1]:
        sent_ref[...] = state[at : at + sent_ref.shape[0]]
        at += sent_ref.shape[0]
    sent_refs[-1][: N - at, :] = state[at:]
    sent_refs[-1][N - at :, :] = tail


def unpack_state(got_refs):
    rows = jnp.concatenate([ref[...] for ref in got_refs], axis=0).astype(F32)
    return rows[:N], rows[N : N + 1, :] + rows[N + 1 : N + 2, :]


def combine_kernel(level, got, has_before, place_ref, total, decays, *refs):
    other, refs = refs[:got], refs[got:]
    if has_before:
        before, refs = refs[0][...], refs[1:]
    total_ref, decays_ref, before_ref, *sent_refs = refs
    come, decay = unpack_state(other)
    whole, part = decays[0:1, :], decays[1:2, :]
    upper = (place_ref[0] >> level) & 1 == 1
    fresh = jnp.where(upper, part, 0.0) * come
    before_ref[...] = before + fresh if has_before else fresh
    joint = jnp.where(upper, 1.0, decay) * total[...] + jnp.where(upper, whole, 1.0) * come
    total_ref[...] = joint
    decays_ref[0:1, :] = whole * decay
    decays_ref[1:2, :] = jnp.where(upper, decay * part, part)
    pack_state(sent_refs, joint, whole * decay)


def read_kernel(level, place_ref, y, reads, cum_g, early, decays, before, other, *refs):
    out_ref = refs[-1]
    upper = (place_ref[0] >> level) & 1 == 1
    state = before[...] + jnp.where(upper, decays[1:2, :], 0.0) * unpack_state([other])[0]
    cum = cum_g[0]
    for at in range(0, out_ref.shape[0], SPAN):
        span = slice(at, at + SPAN)
        cum_b = cum[span, :]
        seen = jnp.dot(reads[span, :], state.astype(BF16), preferred_element_type=F32)
        out_ref[span, :] = (y[span, :] + over_channels(jnp.exp(cum_b)) * seen).astype(BF16)
        if at + SPAN < out_ref.shape[0]:
            state = over_channels(jnp.exp(cum_b[SPAN - 1 : SPAN, :])) * state + early[at // SPAN]


def combined(level, place, total, decays, other, before, groups, cut):
    width = total.shape[1] // groups
    block = lambda rows: pl.BlockSpec((rows, width), lambda i: (0, i))
    shape = lambda rows, dtype: jax.ShapeDtypeStruct((rows, total.shape[1]), dtype)
    total, decays, before, *sent = call(
        functools.partial(combine_kernel, level, len(other), bool(before)),
        "combine",
        (shape(N, F32), shape(8, F32), shape(N, F32)) + tuple(shape(rows, BF16) for rows in cut),
        flops=6 * total.size,
        moved=20 * total.size,
        vmem=12,
        grid=(groups,),
        in_specs=[SMEM, block(N), block(8)] + [block(a.shape[0]) for a in other] + [block(N)] * len(before),
        out_specs=[block(N), block(8), block(N)] + [block(rows) for rows in cut],
    )(place, total, decays, *other, *before)
    return total, decays, before, sent


def body(
    tokens,
    proj_mean,
    proj_devs,
    bc_mean,
    bc_devs,
    swag_coef,
    dt_weight,
    dt_bias,
    decay_rate,
    skip_gain,
    conv_proj,
    conv_bc,
):
    heads_here = decay_rate.shape[0]
    groups_here = bc_mean.shape[2] // N
    per_group = heads_here // groups_here
    width_bc = 2 * bc_mean.shape[2]
    rows_k = proj_mean.shape[0]
    chips = lax.axis_size("chip")
    count = lax.axis_size(SEQ)

    def after(arrays, earlier):
        return lax.optimization_barrier((arrays, earlier))[0]

    width = per_group * P_SIZE
    early_groups = max(1, groups_here // 2)
    fill = -heads_here % LANES
    late = list(range(early_groups, groups_here))

    plane = chips == 4
    two_shares = lax.axis_size("tp") == 2
    place = lax.axis_index("chip") if plane else 0
    at = jnp.stack([lax.axis_index(a) for a in ("fsdp", "core", "tp")] + [place ^ i for i in range(chips)]).astype(jnp.int32)
    share, depth = tokens.shape[0], chips * rows_k
    weight_bc = sampled_pair(bc_mean, bc_devs, dt_weight, swag_coef)
    tokens = after(tokens, weight_bc)
    cut = jax.ShapeDtypeStruct((2 * share, depth), BF16)
    far, own = call(
        functools.partial(cut_kernel, chips),
        "cut_tokens",
        (cut,) * 2,
        moved=4 * tokens.size,
        in_specs=[SMEM, VMEM],
        out_specs=[VMEM] * 2,
    )(at, tokens)
    proj_mean = after(proj_mean, own)
    far = swapped(far, "fsdp")

    weight_early = sampled_cols(proj_mean, proj_devs, swag_coef, 0, early_groups * width)
    weight_late = None
    if late:
        weight_late = sampled_cols(proj_mean, proj_devs, swag_coef, early_groups // len(late), len(late) * width)
    tok_count = share * lax.axis_size("tp")
    blocks = tok_count // SPAN

    def partial_sums(rows, pieces, with_steps, before_send=(), before_relay=()):
        *far_sent, far_kept, sent, kept = multiplied(at, rows, pieces, heads_here, with_steps)
        far_got = [swapped(a, "core") for a in after(far_sent, before_send)]
        back = relayed(far_kept, after(far_got, before_relay), heads_here, with_steps)
        return (kept, swapped(after(sent, back), "core")), back

    specs_of = lambda width: [pl.BlockSpec((tok_count, width), lambda i: (0, i))] * 3 + [
        pl.BlockSpec((RIM, width), lambda i: (0, i)),
    ]
    whole_of = lambda *shape: pl.BlockSpec(shape, lambda i: (0,) * len(shape))
    by_group = (groups_here, tok_count, per_group)
    by_head = (heads_here, tok_count)
    by_decay = (groups_here, 1, per_group)
    state_proj = lambda part: call(
        functools.partial(state_proj_kernel, heads_here),
        "state_proj",
        (jax.ShapeDtypeStruct((tok_count, width_bc), BF16),)
        + tuple(jax.ShapeDtypeStruct(a, F32) for a in (by_group, by_group, by_head, by_head, by_decay)),
        moved=10 * tok_count * width_bc,
        vmem=30,
        grid=(1,),
        in_specs=specs_of(width_bc + LANES) + [whole_of(CONV, width_bc)] + [whole_of(1, heads_here)] * 2,
        out_specs=[whole_of(*a) for a in ((tok_count, width_bc), by_group, by_group, by_head, by_head, by_decay)],
        scratch_shapes=[pltpu.VMEM((tok_count + 8, width_bc), F32)],
    )(*part, rows_before(*part), conv_bc.reshape(CONV, width_bc), dt_bias[None], decay_rate[None])
    if plane and two_shares:
        bc = [weight_bc, *sent_straight(weight_bc)]
        bc += sent_on(corner_parts(bc[1:], 1))
        own_t = swapped(own, "tp")
        weight_early = after(weight_early, bc[3:])
        early = [weight_early, *sent_straight(weight_early)]
        far = after(far, (own_t, bc[3:], weight_late))
        far_t = swapped(far, "tp")
        own, own_t = after((own, own_t), far)
        own_c, own_tc = swapped(own, "core"), swapped(own_t, "core")
        halves = corner_parts(early[1:], 1)
        far_c, far_tc = swapped(far, "core"), swapped(after(far_t, halves), "core")
        rows = (far, far_t, far_c, far_tc, own, own_t, own_c, own_tc)
        part_bc, back_bc = partial_sums(rows, bc, True)
        early += sent_on(halves)
        got_bc = swapped(back_bc, "fsdp")
        weight_late = after(weight_late, (back_bc, early[3:]))
        part, back = partial_sums(rows, early, False, before_relay=got_bc)
        got = swapped(after(back, got_bc), "fsdp")
        straight = sent_straight(weight_late)
        corners = sent_on(corner_parts(straight, 1))
        seen = state_proj(after(part_bc + (got_bc,), back))
        part_late, back_late = partial_sums(rows, [weight_late, *straight, *corners], False, before_send=seen)
        got_late = swapped(after(back_late, got), "fsdp")
        got = after(got, back_late)
    else:
        whole = lambda a, axis: lax.all_gather(a, axis, axis=0, tiled=True)
        ranges = [r for a in (far, own) for r in (a[:share], swapped(a[share:], "core"))]
        rows = (jnp.concatenate([whole(r, "tp") for r in ranges], axis=0),)
        part, back = partial_sums(rows, [whole(weight_early, "chip")], False)
        part_bc, back_bc = partial_sums(rows, [whole(weight_bc, "chip")], True)
        got, got_bc = swapped(back, "fsdp"), swapped(back_bc, "fsdp")
        if late:
            part_late, back_late = partial_sums(rows, [whole(weight_late, "chip")], False)
            got_late = swapped(back_late, "fsdp")
        seen = state_proj(part_bc + (got_bc,))
    conv_out, cum_g, steps_g, cum_t, steps_t, decay = seen
    parts = [part + (got,)]
    if late:
        parts.append(part_late + (got_late,))

    skip = skip_gain.reshape(by_decay)
    levels = count.bit_length() - 1
    seq_place = (2 * lax.axis_index("chip") + lax.axis_index("core")).astype(jnp.int32).reshape(1)

    result = None
    for first, groups, part in zip((0, early_groups), (early_groups, len(late)), parts):
        part = part + (rows_before(*part),)
        if first:
            part = after(part, sent)
        grid = (groups,)
        cols = lambda rows: pl.BlockSpec((rows, width), lambda i: (0, i))
        cols_all = lambda rows: pl.BlockSpec((rows, width), lambda i: (0, first + i))
        heads_g = pl.BlockSpec((1, tok_count, per_group), lambda i: (first + i, 0, 0))
        heads_t = pl.BlockSpec((per_group, tok_count), lambda i: (first + i, 0))
        heads_1 = pl.BlockSpec((1, 1, per_group), lambda i: (first + i, 0, 0))
        keys = pl.BlockSpec((tok_count, N), lambda i: (0, first + i))
        reads = pl.BlockSpec((tok_count, N), lambda i: (0, groups_here + first + i))
        early_spec = pl.BlockSpec((blocks - 1, N, width), lambda i: (0, 0, i))
        y, early, total, decays, sent = call(
            mix_kernel,
            "mix",
            (
                jax.ShapeDtypeStruct((tok_count, groups * width), F32),
                jax.ShapeDtypeStruct((blocks - 1, N, groups * width), F32),
                jax.ShapeDtypeStruct((N, groups * width), F32),
                jax.ShapeDtypeStruct((8, groups * width), F32),
                jax.ShapeDtypeStruct((N + RIM, groups * width), BF16),
            ),
            flops=8 * tok_count * N * width * groups,
            moved=14 * tok_count * width * groups,
            vmem=24,
            grid=grid,
            in_specs=specs_of(width) + [cols_all(CONV), keys, reads, heads_g, heads_g, heads_t, heads_t, heads_1, heads_1],
            out_specs=[cols(tok_count), early_spec, cols(N), cols(8), cols(N + RIM)],
            scratch_shapes=[pltpu.VMEM((tok_count + 8, width), F32)],
        )(*part, conv_proj, conv_out, conv_out, cum_g, steps_g, cum_t, steps_t, skip, decay)
        before, sent = (), [sent]
        for level in range(levels - 1):
            other = [swapped(a, SEQ, 1 << level) for a in sent]
            cut = (N // 2, N // 2 + RIM) if not first and level + 2 < levels else (N + RIM,)
            total, decays, fresh, sent = combined(level, seq_place, total, decays, other, before, groups, cut)
            before = (fresh,)
        (other,) = [swapped(a, SEQ, 1 << (levels - 1)) for a in sent]
        operands = [seq_place, y, conv_out, cum_g, early, decays, *before, other]
        specs = [SMEM, cols(tok_count), reads, heads_g, early_spec, cols(8), cols(N), cols(N + RIM)]
        alias = {}
        if result is not None:
            operands.append(result)
            specs.append(pl.BlockSpec(memory_space=pl.ANY))
            alias = {len(operands) - 1: 0}
        result = call(
            functools.partial(read_kernel, levels - 1),
            "read_out",
            jax.ShapeDtypeStruct((tok_count, heads_here * P_SIZE), BF16),
            flops=2 * tok_count * N * width * groups,
            moved=10 * tok_count * width * groups,
            vmem=12,
            grid=grid,
            in_specs=specs,
            out_specs=cols_all(tok_count),
            input_output_aliases=alias,
        )(*operands)
    return result


def solution(mesh):
    shape = mesh.shape
    split = Mesh(
        mesh.devices.reshape(shape["fsdp"], shape["seq"] // 2, 2, shape["tp"]),
        ("fsdp", "chip", "core", "tp"),
    )
    rows = ("fsdp", "chip", "core")
    return jax.shard_map(
        body,
        mesh=split,
        in_specs=(
            P(rows + ("tp",), None),
            P(rows, "tp"),
            P(None, rows, "tp"),
            P(rows, None, "tp"),
            P(None, rows, None, "tp"),
            P(),
            P(rows, "tp"),
            P("tp"),
            P("tp"),
            P("tp"),
            P(None, "tp"),
            P(None, None, "tp"),
        ),
        out_specs=P(rows, "tp"),
        check_vma=False,
    )
```

```python
import functools

import jax
import jax.numpy as jnp
from jax import lax
from jax.experimental import pallas as pl
from jax.experimental.pallas import tpu as pltpu
from jax.sharding import Mesh, PartitionSpec as P

P_SIZE = 64
N = 128
CONV = 4
SPAN = 128
LANES = 128
RIM = 16
FAR_PARTS = 2
SEQ = ("chip", "core")
F32 = jnp.float32
BF16 = jnp.bfloat16
SMEM = pl.BlockSpec(memory_space=pltpu.SMEM)
VMEM = pl.BlockSpec(memory_space=pltpu.VMEM)


def call(kernel, name, out_shape, flops=0, moved=0, vmem=60, **settings):
    return pl.pallas_call(
        kernel,
        out_shape=out_shape,
        name=name,
        cost_estimate=pl.CostEstimate(flops=flops // 50, bytes_accessed=moved // 50, transcendentals=0),
        compiler_params=pltpu.CompilerParams(vmem_limit_bytes=vmem * 1024 * 1024),
        **settings,
    )


def swapped(part, axis, by=1):
    return lax.ppermute(part, axis, [(i, i ^ by) for i in range(lax.axis_size(axis))])


def cut_kernel(chips, at_ref, tokens_ref, far_ref, own_ref):
    depth = far_ref.shape[1] // chips
    rows = tokens_ref.shape[0]
    f_at, c_at = at_ref[0], at_ref[1]
    for out, f in ((far_ref, 1 - f_at), (own_ref, f_at)):
        for k, c in enumerate((c_at, 1 - c_at)):
            for i in range(chips):
                start = pl.multiple_of(((f * chips + at_ref[3 + i]) * 2 + c) * depth, depth)
                out[k * rows : (k + 1) * rows, i * depth : (i + 1) * depth] = tokens_ref[:, pl.ds(start, depth)]


def stack_rows(at_ref, pieces, rows_ref):
    count = pieces[0].shape[0]
    for k in range(0, len(pieces), 2):
        rows_ref[pl.ds(pl.multiple_of((k + at_ref[2]) * count, count), count), :] = pieces[k][...]
        rows_ref[pl.ds(pl.multiple_of((k + 1 - at_ref[2]) * count, count), count), :] = pieces[k + 1][...]


def sample_kernel(count, coef_ref, mean_ref, devs_ref, out_ref):
    factor = (2.0 * (count - 1)) ** (-0.5)
    accum = mean_ref[...].astype(F32)
    for member in range(count):
        accum = accum + factor * coef_ref[member] * devs_ref[member].astype(F32)
    out_ref[...] = accum.astype(BF16)


def sampled_cols(mean_part, dev_part, swag_coef, at, width):
    rows, count = mean_part.shape[0], dev_part.shape[0]
    tile = rows // 4
    return call(
        functools.partial(sample_kernel, count),
        "sample",
        jax.ShapeDtypeStruct((rows, width), BF16),
        moved=2 * (count + 2) * rows * width,
        vmem=24,
        grid=(4,),
        in_specs=[
            SMEM,
            pl.BlockSpec((tile, width), lambda i: (i, at)),
            pl.BlockSpec((count, tile, width), lambda i: (0, i, at)),
        ],
        out_specs=pl.BlockSpec((tile, width), lambda i: (i, 0)),
    )(swag_coef, mean_part, dev_part)


def sample_pair_kernel(count, coef_ref, mean_ref, devs_ref, dt_ref, out_ref):
    factor = (2.0 * (count - 1)) ** (-0.5)
    accum = mean_ref[...].astype(F32)
    for member in range(count):
        accum = accum + factor * coef_ref[member] * devs_ref[member].astype(F32)
    width, heads = mean_ref.shape[2], dt_ref.shape[0]
    for k in range(2):
        out_ref[:, k * width : (k + 1) * width] = accum[:, k, :].astype(BF16)
    out_ref[:, 2 * width :] = jnp.zeros((out_ref.shape[0], LANES), BF16)
    rows = out_ref.shape[0]
    steps = dt_ref[:, pl.ds(pl.multiple_of(pl.program_id(0) * rows, rows), rows)]
    out_ref[:, 2 * width : 2 * width + heads] = jnp.transpose(steps.astype(F32)).astype(BF16)


def sampled_pair(mean_part, dev_part, dt_part, swag_coef):
    rows, _, width = mean_part.shape
    count = dev_part.shape[0]
    tile = min(rows, LANES)
    return call(
        functools.partial(sample_pair_kernel, count),
        "sample_pair",
        jax.ShapeDtypeStruct((rows, 2 * width + LANES), BF16),
        moved=4 * (count + 2) * rows * width,
        grid=(rows // tile,),
        in_specs=[
            SMEM,
            pl.BlockSpec((tile, 2, width), lambda i: (i, 0, 0)),
            pl.BlockSpec((count, tile, 2, width), lambda i: (0, i, 0, 0)),
            pl.BlockSpec((dt_part.shape[1], rows), lambda i: (0, 0)),
        ],
        out_specs=pl.BlockSpec((tile, 2 * width + LANES), lambda i: (i, 0)),
    )(swag_coef, mean_part, dev_part, dt_part.T)


def sent_straight(weight):
    return swapped(weight, "chip", 1), swapped(weight, "chip", 2)


def corner_parts(straight, each):
    rows = straight[0].shape[0] // (2 * each)
    cut = lambda a, i: a[i * rows : (i + 1) * rows]
    return [cut(straight[1], i) for i in range(each)] + [cut(straight[0], each + i) for i in range(each)]


def sent_on(parts):
    each = len(parts) // 2
    return [swapped(a, "chip", 1) for a in parts[:each]] + [swapped(a, "chip", 2) for a in parts[each:]]


def coded(part, heads):
    high = part.astype(BF16).astype(F32)
    return high + pltpu.roll(part - high, heads, 1)


def decoded(part, heads):
    return part + pltpu.roll(part, LANES - heads, 1)


def multiply_kernel(heads, with_steps, shares, pieces, plan, at_ref, *refs):
    shares, weights, outs, rows_ref = refs[:shares], refs[shares : shares + pieces], refs[shares + pieces : -1], refs[-1]

    @pl.when(pl.program_id(0) == 0)
    def _():
        if len(shares) == 1:
            rows_ref[...] = shares[0][...]
        else:
            stack_rows(at_ref, shares, rows_ref)

    joined = jnp.concatenate([weight[...] for weight in weights], axis=0)
    total = jnp.dot(rows_ref[...], joined, preferred_element_type=F32)
    for out, (first, sent) in zip(outs, plan):
        part = total[first : first + out.shape[0]]
        out[...] = part.astype(out.dtype)
        if with_steps and sent:
            @pl.when(pl.program_id(0) == pl.num_programs(0) - 1)
            def _():
                out[:, -LANES:] = coded(part[:, -LANES:], heads).astype(BF16)


def multiplied(at, rows, weights, heads, with_steps):
    width = weights[0].shape[1]
    tile = next(t for t in (512, 384, 128) if width % t == 0)
    depth = rows[0].shape[1]
    if len(rows) == 1:
        count = rows[0].shape[0]
        row_specs = [pl.BlockSpec(rows[0].shape, lambda i: (0, 0))]
    else:
        share = rows[0].shape[0] // 2
        count = len(rows) * share
        low = pl.BlockSpec((share, depth), lambda i: (0, 0))
        high = pl.BlockSpec((share, depth), lambda i: (1, 0))
        row_specs = [low, low, high, high] * 2
    half = count // 4
    part = half // FAR_PARTS
    plan = [(half + i * part, True) for i in range(FAR_PARTS)] + [(0, False), (3 * half, True), (2 * half, False)]
    shapes = [(part, BF16)] * FAR_PARTS + [(half, F32), (half, BF16), (half, F32)]
    return call(
        functools.partial(multiply_kernel, heads, with_steps, len(rows), len(weights), plan),
        "multiply",
        tuple(jax.ShapeDtypeStruct((r, width), dtype) for r, dtype in shapes),
        flops=2 * count * depth * width,
        moved=2 * count * depth + 2 * depth * width + 12 * half * width,
        vmem=34,
        grid=(width // tile,),
        in_specs=[SMEM] + row_specs + [pl.BlockSpec((w.shape[0], tile), lambda i: (0, i)) for w in weights],
        out_specs=[pl.BlockSpec((r, tile), lambda i: (0, i)) for r, _ in shapes],
        scratch_shapes=[pltpu.VMEM((count, depth), BF16)],
    )(at, *rows, *weights)


def relay_kernel(heads, with_steps, kept_ref, *refs):
    out_ref, count = refs[-1], refs[0].shape[0]
    for i, got_ref in enumerate(refs[:-1]):
        rows = slice(i * count, (i + 1) * count)
        kept, got = kept_ref[rows, :], got_ref[...].astype(F32)
        out_ref[rows, :] = (kept + got).astype(BF16)
        if with_steps:
            wide = kept[:, -LANES:] + decoded(got[:, -LANES:], heads)
            lane = lax.broadcasted_iota(jnp.int32, wide.shape, 1)
            out_ref[rows, -LANES:] = coded(jnp.where(lane < heads, wide, 0.0), heads).astype(BF16)


def relayed(kept, got, heads, with_steps):
    rows, width = kept.shape
    part = pl.BlockSpec((rows // len(got), width), lambda i: (0, 0))
    return call(
        functools.partial(relay_kernel, heads, with_steps),
        "relay",
        jax.ShapeDtypeStruct((rows, width), BF16),
        moved=8 * rows * width,
        vmem=12,
        grid=(1,),
        in_specs=[pl.BlockSpec((rows, width), lambda i: (0, 0))] + [part] * len(got),
        out_specs=pl.BlockSpec((rows, width), lambda i: (0, 0)),
    )(kept, *got)


def rim_kernel(kept, got_c, got_f, rim_ref):
    rim_ref[...] = (kept[...] + got_c[...].astype(F32) + got_f[...].astype(F32)).astype(BF16)


def rows_before(kept, got_c, got_f):
    rows, width = got_f.shape
    at = rows // RIM - 1
    rim = call(
        rim_kernel,
        "rim",
        jax.ShapeDtypeStruct((RIM, width), BF16),
        moved=10 * RIM * width,
        vmem=12,
        grid=(1,),
        in_specs=[pl.BlockSpec((RIM, width), lambda i: (at, 0))] * 3,
        out_specs=pl.BlockSpec((RIM, width), lambda i: (0, 0)),
    )(kept, got_c, got_f)
    return lax.ppermute(rim, SEQ, [(i, i + 1) for i in range(lax.axis_size(SEQ) - 1)])


def convolved(width, kept, got_c, got_f, rim, taps, padded):
    count = padded.shape[0] - 8
    proj = kept[:, :width] + got_c[:, :width].astype(F32) + got_f[:, :width].astype(F32)
    padded[8:, :] = proj.astype(BF16).astype(F32)
    padded[:8, :] = rim[:, :width].astype(F32)[RIM - 8 :]
    first = 8 - (CONV - 1)
    conv_sum = taps[0:1, :] * padded[first : first + count, :]
    for offset in range(1, CONV):
        conv_sum = conv_sum + taps[offset : offset + 1, :] * padded[first + offset : first + offset + count, :]
    return (conv_sum * jax.nn.sigmoid(conv_sum)).astype(BF16)


def state_proj_kernel(
    heads, kept, got_c, got_f, rim, taps, bias, rate, out_ref, cum_ref, steps_ref, cum_t_ref, steps_t_ref, decay_ref, padded
):
    count, width = out_ref.shape
    out_ref[...] = convolved(width, kept, got_c, got_f, rim, taps, padded)
    logits = kept[:, width:] + decoded(got_c[:, width:].astype(F32), heads) + decoded(got_f[:, width:].astype(F32), heads)
    steps = jax.nn.softplus(logits[:, :heads] + bias[...])
    row = lax.broadcasted_iota(jnp.int32, (SPAN, SPAN), 0)
    col = lax.broadcasted_iota(jnp.int32, (SPAN, SPAN), 1)
    causal = jnp.where(row >= col, 1.0, 0.0)
    groups, per_group = cum_ref.shape[0], cum_ref.shape[2]
    through = jnp.zeros((1, heads), F32)
    for at in range(0, count, SPAN):
        span = slice(at, at + SPAN)
        steps_b = steps[span, :]
        cum = jnp.dot(
            causal, -steps_b * rate[...], precision=lax.Precision.HIGHEST, preferred_element_type=F32
        )
        through = through + cum[SPAN - 1 : SPAN, :]
        cum_t_ref[:, span] = jnp.transpose(cum)
        steps_t_ref[:, span] = jnp.transpose(steps_b)
        for g in range(groups):
            cum_ref[g, span, :] = cum[:, g * per_group : (g + 1) * per_group]
            steps_ref[g, span, :] = steps_b[:, g * per_group : (g + 1) * per_group]
    for g in range(groups):
        decay_ref[g] = jnp.exp(through)[:, g * per_group : (g + 1) * per_group]


def pairwise(columns, first):
    shape = (columns.shape[0], 2 * P_SIZE)
    lane = lax.broadcasted_iota(jnp.int32, shape, 1)
    return jnp.where(lane < P_SIZE, columns[:, first : first + 1], columns[:, first + 1 : first + 2])


def over_channels(columns):
    return jnp.concatenate([pairwise(columns, h) for h in range(0, columns.shape[1], 2)], axis=1)


def mix_kernel(
    kept, got_c, got_f, rim, taps, keys, reads, cum_g, steps_g, cum_t, steps_t, skip, decay, y_ref, early_ref, total_ref, decays_ref, sent_ref, padded
):
    width = y_ref.shape[1]
    values = convolved(width, kept, got_c, got_f, rim, taps, padded)
    cum, steps = cum_g[0], steps_g[0]
    heads = cum.shape[1]
    row = lax.broadcasted_iota(jnp.int32, (SPAN, SPAN), 0)
    col = lax.broadcasted_iota(jnp.int32, (SPAN, SPAN), 1)
    causal = row >= col
    lane = lax.broadcasted_iota(jnp.int32, (SPAN, 2 * P_SIZE), 1)
    gain = over_channels(skip[0])
    state = None
    for at in range(0, y_ref.shape[0], SPAN):
        span = slice(at, at + SPAN)
        keys_b, reads_b, values_b = keys[span, :], reads[span, :], values[span, :]
        cum_b, steps_b = cum[span, :], steps[span, :]
        last = cum_b[SPAN - 1 : SPAN, :]
        scores = lax.dot_general(reads_b, keys_b, (((1,), (1,)), ((), ())), preferred_element_type=F32)
        scores = jnp.where(causal, scores, 0.0)
        reach = jnp.exp(last - cum_b) * steps_b
        scaled = []
        for head in range(0, heads, 2):
            chans = slice(head * P_SIZE, (head + 2) * P_SIZE)
            two = []
            for h in (head, head + 1):
                gap = cum_b[:, h : h + 1] - cum_t[h : h + 1, span]
                two.append((scores * jnp.exp(jnp.minimum(gap, 0.0)) * steps_t[h : h + 1, span]).astype(BF16))
            values_h = values_b[:, chans]
            both = jnp.dot(jnp.concatenate(two, axis=0), values_h, preferred_element_type=F32)
            inner = jnp.where(lane < P_SIZE, both[:SPAN], both[SPAN:])
            wide = values_h.astype(F32)
            y_ref[span, chans] = inner + gain[:, chans] * wide
            scaled.append((wide * pairwise(reach, head)).astype(BF16))
        fresh = lax.dot_general(
            keys_b, jnp.concatenate(scaled, axis=1), (((0,), (0,)), ((), ())), preferred_element_type=F32
        )
        state = fresh if state is None else over_channels(jnp.exp(last)) * state + fresh
        if at + SPAN < y_ref.shape[0]:
            early_ref[at // SPAN] = fresh
    total_ref[...] = state
    wide = over_channels(decay[0])
    decays_ref[0:1, :] = wide
    decays_ref[1:2, :] = jnp.ones_like(wide)
    pack_state([sent_ref], state, wide)


def pack_state(sent_refs, state, decay):
    high = decay.astype(BF16).astype(F32)
    row = lax.broadcasted_iota(jnp.int32, (RIM, decay.shape[1]), 0)
    tail = jnp.where(row == 0, high, jnp.where(row == 1, decay - high, 0.0)).astype(BF16)
    state = state.astype(BF16)
    at = 0
    for sent_ref in sent_refs[:-1]:
        sent_ref[...] = state[at : at + sent_ref.shape[0]]
        at += sent_ref.shape[0]
    sent_refs[-1][: N - at, :] = state[at:]
    sent_refs[-1][N - at :, :] = tail


def unpack_state(got_refs):
    rows = jnp.concatenate([ref[...] for ref in got_refs], axis=0).astype(F32)
    return rows[:N], rows[N : N + 1, :] + rows[N + 1 : N + 2, :]


def combine_kernel(level, got, has_before, place_ref, total, decays, *refs):
    other, refs = refs[:got], refs[got:]
    if has_before:
        before, refs = refs[0][...], refs[1:]
    total_ref, decays_ref, before_ref, *sent_refs = refs
    come, decay = unpack_state(other)
    whole, part = decays[0:1, :], decays[1:2, :]
    upper = (place_ref[0] >> level) & 1 == 1
    fresh = jnp.where(upper, part, 0.0) * come
    before_ref[...] = before + fresh if has_before else fresh
    joint = jnp.where(upper, 1.0, decay) * total[...] + jnp.where(upper, whole, 1.0) * come
    total_ref[...] = joint
    decays_ref[0:1, :] = whole * decay
    decays_ref[1:2, :] = jnp.where(upper, decay * part, part)
    pack_state(sent_refs, joint, whole * decay)


def read_kernel(level, place_ref, y, reads, cum_g, early, decays, before, other, *refs):
    out_ref = refs[-1]
    upper = (place_ref[0] >> level) & 1 == 1
    state = before[...] + jnp.where(upper, decays[1:2, :], 0.0) * unpack_state([other])[0]
    cum = cum_g[0]
    for at in range(0, out_ref.shape[0], SPAN):
        span = slice(at, at + SPAN)
        cum_b = cum[span, :]
        seen = jnp.dot(reads[span, :], state.astype(BF16), preferred_element_type=F32)
        out_ref[span, :] = (y[span, :] + over_channels(jnp.exp(cum_b)) * seen).astype(BF16)
        if at + SPAN < out_ref.shape[0]:
            state = over_channels(jnp.exp(cum_b[SPAN - 1 : SPAN, :])) * state + early[at // SPAN]


def combined(level, place, total, decays, other, before, groups, cut):
    width = total.shape[1] // groups
    block = lambda rows: pl.BlockSpec((rows, width), lambda i: (0, i))
    shape = lambda rows, dtype: jax.ShapeDtypeStruct((rows, total.shape[1]), dtype)
    total, decays, before, *sent = call(
        functools.partial(combine_kernel, level, len(other), bool(before)),
        "combine",
        (shape(N, F32), shape(8, F32), shape(N, F32)) + tuple(shape(rows, BF16) for rows in cut),
        flops=6 * total.size,
        moved=20 * total.size,
        vmem=12,
        grid=(groups,),
        in_specs=[SMEM, block(N), block(8)] + [block(a.shape[0]) for a in other] + [block(N)] * len(before),
        out_specs=[block(N), block(8), block(N)] + [block(rows) for rows in cut],
    )(place, total, decays, *other, *before)
    return total, decays, before, sent


def body(
    tokens,
    proj_mean,
    proj_devs,
    bc_mean,
    bc_devs,
    swag_coef,
    dt_weight,
    dt_bias,
    decay_rate,
    skip_gain,
    conv_proj,
    conv_bc,
):
    heads_here = decay_rate.shape[0]
    groups_here = bc_mean.shape[2] // N
    per_group = heads_here // groups_here
    width_bc = 2 * bc_mean.shape[2]
    rows_k = proj_mean.shape[0]
    chips = lax.axis_size("chip")
    count = lax.axis_size(SEQ)

    def after(arrays, earlier):
        return lax.optimization_barrier((arrays, earlier))[0]

    width = per_group * P_SIZE
    early_groups = max(1, groups_here // 2)
    fill = -heads_here % LANES
    late = list(range(early_groups, groups_here))

    plane = chips == 4
    two_shares = lax.axis_size("tp") == 2
    place = lax.axis_index("chip") if plane else 0
    at = jnp.stack([lax.axis_index(a) for a in ("fsdp", "core", "tp")] + [place ^ i for i in range(chips)]).astype(jnp.int32)
    share, depth = tokens.shape[0], chips * rows_k
    weight_bc = sampled_pair(bc_mean, bc_devs, dt_weight, swag_coef)
    tokens = after(tokens, weight_bc)
    cut = jax.ShapeDtypeStruct((2 * share, depth), BF16)
    far, own = call(
        functools.partial(cut_kernel, chips),
        "cut_tokens",
        (cut,) * 2,
        moved=4 * tokens.size,
        vmem=24,
        in_specs=[SMEM, VMEM],
        out_specs=[VMEM] * 2,
    )(at, tokens)
    proj_mean = after(proj_mean, own)
    far = swapped(far, "fsdp")

    weight_early = sampled_cols(proj_mean, proj_devs, swag_coef, 0, early_groups * width)
    weight_late = None
    if late:
        weight_late = sampled_cols(proj_mean, proj_devs, swag_coef, early_groups // len(late), len(late) * width)
    tok_count = share * lax.axis_size("tp")
    blocks = tok_count // SPAN

    def partial_sums(rows, pieces, with_steps, before_send=(), before_relay=()):
        *far_sent, far_kept, sent, kept = multiplied(at, rows, pieces, heads_here, with_steps)
        far_got = [swapped(a, "core") for a in after(far_sent, before_send)]
        back = relayed(far_kept, after(far_got, before_relay), heads_here, with_steps)
        return (kept, swapped(after(sent, back), "core")), back

    specs_of = lambda width: [pl.BlockSpec((tok_count, width), lambda i: (0, i))] * 3 + [
        pl.BlockSpec((RIM, width), lambda i: (0, i)),
    ]
    whole_of = lambda *shape: pl.BlockSpec(shape, lambda i: (0,) * len(shape))
    by_group = (groups_here, tok_count, per_group)
    by_head = (heads_here, tok_count)
    by_decay = (groups_here, 1, per_group)
    state_proj = lambda part: call(
        functools.partial(state_proj_kernel, heads_here),
        "state_proj",
        (jax.ShapeDtypeStruct((tok_count, width_bc), BF16),)
        + tuple(jax.ShapeDtypeStruct(a, F32) for a in (by_group, by_group, by_head, by_head, by_decay)),
        moved=10 * tok_count * width_bc,
        vmem=30,
        grid=(1,),
        in_specs=specs_of(width_bc + LANES) + [whole_of(CONV, width_bc)] + [whole_of(1, heads_here)] * 2,
        out_specs=[whole_of(*a) for a in ((tok_count, width_bc), by_group, by_group, by_head, by_head, by_decay)],
        scratch_shapes=[pltpu.VMEM((tok_count + 8, width_bc), F32)],
    )(*part, rows_before(*part), conv_bc.reshape(CONV, width_bc), dt_bias[None], decay_rate[None])
    if plane and two_shares:
        bc = [weight_bc, *sent_straight(weight_bc)]
        bc += sent_on(corner_parts(bc[1:], 1))
        own_t = swapped(own, "tp")
        weight_early = after(weight_early, bc[3:])
        early = [weight_early, *sent_straight(weight_early)]
        far = after(far, (own_t, bc[3:], weight_late))
        far_t = swapped(far, "tp")
        own, own_t = after((own, own_t), far)
        own_c, own_tc = swapped(own, "core"), swapped(own_t, "core")
        halves = corner_parts(early[1:], 1)
        far_c, far_tc = swapped(far, "core"), swapped(after(far_t, halves), "core")
        rows = (far, far_t, far_c, far_tc, own, own_t, own_c, own_tc)
        part_bc, back_bc = partial_sums(rows, bc, True)
        early += sent_on(halves)
        got_bc = swapped(back_bc, "fsdp")
        weight_late = after(weight_late, (back_bc, early[3:]))
        part, back = partial_sums(rows, early, False, before_relay=got_bc)
        got = swapped(after(back, got_bc), "fsdp")
        straight = sent_straight(weight_late)
        corners = sent_on(corner_parts(straight, 1))
        seen = state_proj(after(part_bc + (got_bc,), back))
        part_late, back_late = partial_sums(rows, [weight_late, *straight, *corners], False, before_send=seen)
        got_late = swapped(after(back_late, got), "fsdp")
        got = after(got, back_late)
    else:
        whole = lambda a, axis: lax.all_gather(a, axis, axis=0, tiled=True)
        ranges = [r for a in (far, own) for r in (a[:share], swapped(a[share:], "core"))]
        rows = (jnp.concatenate([whole(r, "tp") for r in ranges], axis=0),)
        part, back = partial_sums(rows, [whole(weight_early, "chip")], False)
        part_bc, back_bc = partial_sums(rows, [whole(weight_bc, "chip")], True)
        got, got_bc = swapped(back, "fsdp"), swapped(back_bc, "fsdp")
        if late:
            part_late, back_late = partial_sums(rows, [whole(weight_late, "chip")], False)
            got_late = swapped(back_late, "fsdp")
        seen = state_proj(part_bc + (got_bc,))
    conv_out, cum_g, steps_g, cum_t, steps_t, decay = seen
    parts = [part + (got,)]
    if late:
        parts.append(part_late + (got_late,))

    skip = skip_gain.reshape(by_decay)
    levels = count.bit_length() - 1
    seq_place = (2 * lax.axis_index("chip") + lax.axis_index("core")).astype(jnp.int32).reshape(1)

    result = None
    for first, groups, part in zip((0, early_groups), (early_groups, len(late)), parts):
        part = part + (rows_before(*part),)
        if first:
            part = after(part, sent)
        grid = (groups,)
        cols = lambda rows: pl.BlockSpec((rows, width), lambda i: (0, i))
        cols_all = lambda rows: pl.BlockSpec((rows, width), lambda i: (0, first + i))
        heads_g = pl.BlockSpec((1, tok_count, per_group), lambda i: (first + i, 0, 0))
        heads_t = pl.BlockSpec((per_group, tok_count), lambda i: (first + i, 0))
        heads_1 = pl.BlockSpec((1, 1, per_group), lambda i: (first + i, 0, 0))
        keys = pl.BlockSpec((tok_count, N), lambda i: (0, first + i))
        reads = pl.BlockSpec((tok_count, N), lambda i: (0, groups_here + first + i))
        early_spec = pl.BlockSpec((blocks - 1, N, width), lambda i: (0, 0, i))
        y, early, total, decays, sent = call(
            mix_kernel,
            "mix",
            (
                jax.ShapeDtypeStruct((tok_count, groups * width), F32),
                jax.ShapeDtypeStruct((blocks - 1, N, groups * width), F32),
                jax.ShapeDtypeStruct((N, groups * width), F32),
                jax.ShapeDtypeStruct((8, groups * width), F32),
                jax.ShapeDtypeStruct((N + RIM, groups * width), BF16),
            ),
            flops=8 * tok_count * N * width * groups,
            moved=14 * tok_count * width * groups,
            vmem=24,
            grid=grid,
            in_specs=specs_of(width) + [cols_all(CONV), keys, reads, heads_g, heads_g, heads_t, heads_t, heads_1, heads_1],
            out_specs=[cols(tok_count), early_spec, cols(N), cols(8), cols(N + RIM)],
            scratch_shapes=[pltpu.VMEM((tok_count + 8, width), F32)],
        )(*part, conv_proj, conv_out, conv_out, cum_g, steps_g, cum_t, steps_t, skip, decay)
        before, sent = (), [sent]
        for level in range(levels - 1):
            other = [swapped(a, SEQ, 1 << level) for a in sent]
            cut = (N // 2, N // 2 + RIM) if not first and level + 2 < levels else (N + RIM,)
            total, decays, fresh, sent = combined(level, seq_place, total, decays, other, before, groups, cut)
            before = (fresh,)
        (other,) = [swapped(a, SEQ, 1 << (levels - 1)) for a in sent]
        operands = [seq_place, y, conv_out, cum_g, early, decays, *before, other]
        specs = [SMEM, cols(tok_count), reads, heads_g, early_spec, cols(8), cols(N), cols(N + RIM)]
        alias = {}
        if result is not None:
            operands.append(result)
            specs.append(pl.BlockSpec(memory_space=pl.ANY))
            alias = {len(operands) - 1: 0}
        result = call(
            functools.partial(read_kernel, levels - 1),
            "read_out",
            jax.ShapeDtypeStruct((tok_count, heads_here * P_SIZE), BF16),
            flops=2 * tok_count * N * width * groups,
            moved=10 * tok_count * width * groups,
            vmem=12,
            grid=grid,
            in_specs=specs,
            out_specs=cols_all(tok_count),
            input_output_aliases=alias,
        )(*operands)
    return result


def solution(mesh):
    shape = mesh.shape
    split = Mesh(
        mesh.devices.reshape(shape["fsdp"], shape["seq"] // 2, 2, shape["tp"]),
        ("fsdp", "chip", "core", "tp"),
    )
    rows = ("fsdp", "chip", "core")
    return jax.shard_map(
        body,
        mesh=split,
        in_specs=(
            P(rows + ("tp",), None),
            P(rows, "tp"),
            P(None, rows, "tp"),
            P(rows, None, "tp"),
            P(None, rows, None, "tp"),
            P(),
            P(rows, "tp"),
            P("tp"),
            P("tp"),
            P("tp"),
            P(None, "tp"),
            P(None, None, "tp"),
        ),
        out_specs=P(rows, "tp"),
        check_vma=False,
    )
```

```python
import functools

import jax
import jax.numpy as jnp
from jax import lax
from jax.experimental import pallas as pl
from jax.experimental.pallas import tpu as pltpu
from jax.sharding import Mesh, PartitionSpec as P

P_SIZE = 64
N = 128
CONV = 4
SPAN = 128
LANES = 128
RIM = 16
FAR_PARTS = 2
SEQ = ("chip", "core")
F32 = jnp.float32
BF16 = jnp.bfloat16
SMEM = pl.BlockSpec(memory_space=pltpu.SMEM)
VMEM = pl.BlockSpec(memory_space=pltpu.VMEM)


def call(kernel, name, out_shape, flops=0, moved=0, vmem=60, **settings):
    return pl.pallas_call(
        kernel,
        out_shape=out_shape,
        name=name,
        cost_estimate=pl.CostEstimate(flops=flops // 50, bytes_accessed=moved // 50, transcendentals=0),
        compiler_params=pltpu.CompilerParams(vmem_limit_bytes=vmem * 1024 * 1024),
        **settings,
    )


def swapped(part, axis, by=1):
    return lax.ppermute(part, axis, [(i, i ^ by) for i in range(lax.axis_size(axis))])


def cut_kernel(chips, at_ref, tokens_ref, far_ref, own_ref):
    depth = far_ref.shape[1] // chips
    rows = tokens_ref.shape[0]
    f_at, c_at = at_ref[0], at_ref[1]
    for out, f in ((far_ref, 1 - f_at), (own_ref, f_at)):
        for k, c in enumerate((c_at, 1 - c_at)):
            for i in range(chips):
                start = pl.multiple_of(((f * chips + at_ref[3 + i]) * 2 + c) * depth, depth)
                out[k * rows : (k + 1) * rows, i * depth : (i + 1) * depth] = tokens_ref[:, pl.ds(start, depth)]


def stack_rows(at_ref, pieces, rows_ref):
    count = pieces[0].shape[0]
    for k in range(0, len(pieces), 2):
        rows_ref[pl.ds(pl.multiple_of((k + at_ref[2]) * count, count), count), :] = pieces[k][...]
        rows_ref[pl.ds(pl.multiple_of((k + 1 - at_ref[2]) * count, count), count), :] = pieces[k + 1][...]


def sample_kernel(count, coef_ref, mean_ref, devs_ref, out_ref):
    factor = (2.0 * (count - 1)) ** (-0.5)
    accum = mean_ref[...].astype(F32)
    for member in range(count):
        accum = accum + factor * coef_ref[member] * devs_ref[member].astype(F32)
    out_ref[...] = accum.astype(BF16)


def sampled_cols(mean_part, dev_part, swag_coef, at, width):
    rows, count = mean_part.shape[0], dev_part.shape[0]
    tile = rows // 4
    return call(
        functools.partial(sample_kernel, count),
        "sample",
        jax.ShapeDtypeStruct((rows, width), BF16),
        moved=2 * (count + 2) * rows * width,
        vmem=24,
        grid=(4,),
        in_specs=[
            SMEM,
            pl.BlockSpec((tile, width), lambda i: (i, at)),
            pl.BlockSpec((count, tile, width), lambda i: (0, i, at)),
        ],
        out_specs=pl.BlockSpec((tile, width), lambda i: (i, 0)),
    )(swag_coef, mean_part, dev_part)


def sample_pair_kernel(count, coef_ref, mean_ref, devs_ref, dt_ref, out_ref):
    factor = (2.0 * (count - 1)) ** (-0.5)
    accum = mean_ref[...].astype(F32)
    for member in range(count):
        accum = accum + factor * coef_ref[member] * devs_ref[member].astype(F32)
    width, heads = mean_ref.shape[2], dt_ref.shape[0]
    for k in range(2):
        out_ref[:, k * width : (k + 1) * width] = accum[:, k, :].astype(BF16)
    out_ref[:, 2 * width :] = jnp.zeros((out_ref.shape[0], LANES), BF16)
    rows = out_ref.shape[0]
    steps = dt_ref[:, pl.ds(pl.multiple_of(pl.program_id(0) * rows, rows), rows)]
    out_ref[:, 2 * width : 2 * width + heads] = jnp.transpose(steps.astype(F32)).astype(BF16)


def sampled_pair(mean_part, dev_part, dt_part, swag_coef):
    rows, _, width = mean_part.shape
    count = dev_part.shape[0]
    tile = min(rows, LANES)
    return call(
        functools.partial(sample_pair_kernel, count),
        "sample_pair",
        jax.ShapeDtypeStruct((rows, 2 * width + LANES), BF16),
        moved=4 * (count + 2) * rows * width,
        grid=(rows // tile,),
        in_specs=[
            SMEM,
            pl.BlockSpec((tile, 2, width), lambda i: (i, 0, 0)),
            pl.BlockSpec((count, tile, 2, width), lambda i: (0, i, 0, 0)),
            pl.BlockSpec((dt_part.shape[1], rows), lambda i: (0, 0)),
        ],
        out_specs=pl.BlockSpec((tile, 2 * width + LANES), lambda i: (i, 0)),
    )(swag_coef, mean_part, dev_part, dt_part.T)


def sent_straight(weight):
    return swapped(weight, "chip", 1), swapped(weight, "chip", 2)


def corner_parts(straight, each):
    rows = straight[0].shape[0] // (2 * each)
    cut = lambda a, i: a[i * rows : (i + 1) * rows]
    return [cut(straight[1], i) for i in range(each)] + [cut(straight[0], each + i) for i in range(each)]


def sent_on(parts):
    each = len(parts) // 2
    return [swapped(a, "chip", 1) for a in parts[:each]] + [swapped(a, "chip", 2) for a in parts[each:]]


def coded(part, heads):
    high = part.astype(BF16).astype(F32)
    return high + pltpu.roll(part - high, heads, 1)


def decoded(part, heads):
    return part + pltpu.roll(part, LANES - heads, 1)


def multiply_kernel(heads, with_steps, shares, pieces, plan, at_ref, *refs):
    shares, weights, outs, rows_ref = refs[:shares], refs[shares : shares + pieces], refs[shares + pieces : -1], refs[-1]

    @pl.when(pl.program_id(0) == 0)
    def _():
        if len(shares) == 1:
            rows_ref[...] = shares[0][...]
        else:
            stack_rows(at_ref, shares, rows_ref)

    joined = jnp.concatenate([weight[...] for weight in weights], axis=0)
    total = jnp.dot(rows_ref[...], joined, preferred_element_type=F32)
    for out, (first, sent) in zip(outs, plan):
        part = total[first : first + out.shape[0]]
        out[...] = part.astype(out.dtype)
        if with_steps and sent:
            @pl.when(pl.program_id(0) == pl.num_programs(0) - 1)
            def _():
                out[:, -LANES:] = coded(part[:, -LANES:], heads).astype(BF16)


def multiplied(at, rows, weights, heads, with_steps):
    width = weights[0].shape[1]
    tile = next(t for t in (512, 384, 128) if width % t == 0)
    depth = rows[0].shape[1]
    if len(rows) == 1:
        count = rows[0].shape[0]
        row_specs = [pl.BlockSpec(rows[0].shape, lambda i: (0, 0))]
    else:
        share = rows[0].shape[0] // 2
        count = len(rows) * share
        low = pl.BlockSpec((share, depth), lambda i: (0, 0))
        high = pl.BlockSpec((share, depth), lambda i: (1, 0))
        row_specs = [low, low, high, high] * 2
    half = count // 4
    part = half // FAR_PARTS
    plan = [(half + i * part, True) for i in range(FAR_PARTS)] + [(0, False), (3 * half, True), (2 * half, False)]
    shapes = [(part, BF16)] * FAR_PARTS + [(half, F32), (half, BF16), (half, F32)]
    return call(
        functools.partial(multiply_kernel, heads, with_steps, len(rows), len(weights), plan),
        "multiply",
        tuple(jax.ShapeDtypeStruct((r, width), dtype) for r, dtype in shapes),
        flops=2 * count * depth * width,
        moved=2 * count * depth + 2 * depth * width + 12 * half * width,
        vmem=34,
        grid=(width // tile,),
        in_specs=[SMEM] + row_specs + [pl.BlockSpec((w.shape[0], tile), lambda i: (0, i)) for w in weights],
        out_specs=[pl.BlockSpec((r, tile), lambda i: (0, i)) for r, _ in shapes],
        scratch_shapes=[pltpu.VMEM((count, depth), BF16)],
    )(at, *rows, *weights)


def relay_kernel(heads, with_steps, kept_ref, *refs):
    out_ref, count = refs[-1], refs[0].shape[0]
    for i, got_ref in enumerate(refs[:-1]):
        rows = slice(i * count, (i + 1) * count)
        kept, got = kept_ref[rows, :], got_ref[...].astype(F32)
        out_ref[rows, :] = (kept + got).astype(BF16)
        if with_steps:
            wide = kept[:, -LANES:] + decoded(got[:, -LANES:], heads)
            lane = lax.broadcasted_iota(jnp.int32, wide.shape, 1)
            out_ref[rows, -LANES:] = coded(jnp.where(lane < heads, wide, 0.0), heads).astype(BF16)


def relayed(kept, got, heads, with_steps):
    rows, width = kept.shape
    part = pl.BlockSpec((rows // len(got), width), lambda i: (0, 0))
    return call(
        functools.partial(relay_kernel, heads, with_steps),
        "relay",
        jax.ShapeDtypeStruct((rows, width), BF16),
        moved=8 * rows * width,
        vmem=12,
        grid=(1,),
        in_specs=[pl.BlockSpec((rows, width), lambda i: (0, 0))] + [part] * len(got),
        out_specs=pl.BlockSpec((rows, width), lambda i: (0, 0)),
    )(kept, *got)


def rim_kernel(kept, got_c, got_f, rim_ref):
    rim_ref[...] = (kept[...] + got_c[...].astype(F32) + got_f[...].astype(F32)).astype(BF16)


def rows_before(kept, got_c, got_f):
    rows, width = got_f.shape
    at = rows // RIM - 1
    rim = call(
        rim_kernel,
        "rim",
        jax.ShapeDtypeStruct((RIM, width), BF16),
        moved=10 * RIM * width,
        vmem=12,
        grid=(1,),
        in_specs=[pl.BlockSpec((RIM, width), lambda i: (at, 0))] * 3,
        out_specs=pl.BlockSpec((RIM, width), lambda i: (0, 0)),
    )(kept, got_c, got_f)
    return lax.ppermute(rim, SEQ, [(i, i + 1) for i in range(lax.axis_size(SEQ) - 1)])


def convolved(width, kept, got_c, got_f, rim, taps, padded):
    count = padded.shape[0] - 8
    proj = kept[:, :width] + got_c[:, :width].astype(F32) + got_f[:, :width].astype(F32)
    padded[8:, :] = proj.astype(BF16).astype(F32)
    padded[:8, :] = rim[:, :width].astype(F32)[RIM - 8 :]
    first = 8 - (CONV - 1)
    conv_sum = taps[0:1, :] * padded[first : first + count, :]
    for offset in range(1, CONV):
        conv_sum = conv_sum + taps[offset : offset + 1, :] * padded[first + offset : first + offset + count, :]
    return (conv_sum * jax.nn.sigmoid(conv_sum)).astype(BF16)


def state_proj_kernel(
    heads, kept, got_c, got_f, rim, taps, bias, rate, out_ref, cum_ref, steps_ref, cum_t_ref, steps_t_ref, decay_ref, padded
):
    count, width = out_ref.shape
    out_ref[...] = convolved(width, kept, got_c, got_f, rim, taps, padded)
    logits = kept[:, width:] + decoded(got_c[:, width:].astype(F32), heads) + decoded(got_f[:, width:].astype(F32), heads)
    steps = jax.nn.softplus(logits[:, :heads] + bias[...])
    row = lax.broadcasted_iota(jnp.int32, (SPAN, SPAN), 0)
    col = lax.broadcasted_iota(jnp.int32, (SPAN, SPAN), 1)
    causal = jnp.where(row >= col, 1.0, 0.0)
    groups, per_group = cum_ref.shape[0], cum_ref.shape[2]
    through = jnp.zeros((1, heads), F32)
    for at in range(0, count, SPAN):
        span = slice(at, at + SPAN)
        steps_b = steps[span, :]
        cum = jnp.dot(
            causal, -steps_b * rate[...], precision=lax.Precision.HIGHEST, preferred_element_type=F32
        )
        through = through + cum[SPAN - 1 : SPAN, :]
        cum_t_ref[:, span] = jnp.transpose(cum)
        steps_t_ref[:, span] = jnp.transpose(steps_b)
        for g in range(groups):
            cum_ref[g, span, :] = cum[:, g * per_group : (g + 1) * per_group]
            steps_ref[g, span, :] = steps_b[:, g * per_group : (g + 1) * per_group]
    for g in range(groups):
        decay_ref[g] = jnp.exp(through)[:, g * per_group : (g + 1) * per_group]


def pairwise(columns, first):
    shape = (columns.shape[0], 2 * P_SIZE)
    lane = lax.broadcasted_iota(jnp.int32, shape, 1)
    return jnp.where(lane < P_SIZE, columns[:, first : first + 1], columns[:, first + 1 : first + 2])


def over_channels(columns):
    return jnp.concatenate([pairwise(columns, h) for h in range(0, columns.shape[1], 2)], axis=1)


def mix_kernel(
    kept, got_c, got_f, rim, taps, keys, reads, cum_g, steps_g, cum_t, steps_t, skip, decay, y_ref, early_ref, total_ref, decays_ref, sent_ref, padded
):
    width = y_ref.shape[1]
    values = convolved(width, kept, got_c, got_f, rim, taps, padded)
    cum, steps = cum_g[0], steps_g[0]
    heads = cum.shape[1]
    row = lax.broadcasted_iota(jnp.int32, (SPAN, SPAN), 0)
    col = lax.broadcasted_iota(jnp.int32, (SPAN, SPAN), 1)
    causal = row >= col
    lane = lax.broadcasted_iota(jnp.int32, (SPAN, 2 * P_SIZE), 1)
    gain = over_channels(skip[0])
    state = None
    for at in range(0, y_ref.shape[0], SPAN):
        span = slice(at, at + SPAN)
        keys_b, reads_b, values_b = keys[span, :], reads[span, :], values[span, :]
        cum_b, steps_b = cum[span, :], steps[span, :]
        last = cum_b[SPAN - 1 : SPAN, :]
        scores = lax.dot_general(reads_b, keys_b, (((1,), (1,)), ((), ())), preferred_element_type=F32)
        scores = jnp.where(causal, scores, 0.0)
        reach = jnp.exp(last - cum_b) * steps_b
        scaled = []
        for head in range(0, heads, 2):
            chans = slice(head * P_SIZE, (head + 2) * P_SIZE)
            two = []
            for h in (head, head + 1):
                gap = cum_b[:, h : h + 1] - cum_t[h : h + 1, span]
                two.append((scores * jnp.exp(jnp.minimum(gap, 0.0)) * steps_t[h : h + 1, span]).astype(BF16))
            values_h = values_b[:, chans]
            both = jnp.dot(jnp.concatenate(two, axis=0), values_h, preferred_element_type=F32)
            inner = jnp.where(lane < P_SIZE, both[:SPAN], both[SPAN:])
            wide = values_h.astype(F32)
            y_ref[span, chans] = inner + gain[:, chans] * wide
            scaled.append((wide * pairwise(reach, head)).astype(BF16))
        fresh = lax.dot_general(
            keys_b, jnp.concatenate(scaled, axis=1), (((0,), (0,)), ((), ())), preferred_element_type=F32
        )
        state = fresh if state is None else over_channels(jnp.exp(last)) * state + fresh
        if at + SPAN < y_ref.shape[0]:
            early_ref[at // SPAN] = fresh
    total_ref[...] = state
    wide = over_channels(decay[0])
    decays_ref[0:1, :] = wide
    decays_ref[1:2, :] = jnp.ones_like(wide)
    pack_state([sent_ref], state, wide)


def pack_state(sent_refs, state, decay):
    high = decay.astype(BF16).astype(F32)
    row = lax.broadcasted_iota(jnp.int32, (RIM, decay.shape[1]), 0)
    tail = jnp.where(row == 0, high, jnp.where(row == 1, decay - high, 0.0)).astype(BF16)
    state = state.astype(BF16)
    at = 0
    for sent_ref in sent_refs[:-1]:
        sent_ref[...] = state[at : at + sent_ref.shape[0]]
        at += sent_ref.shape[0]
    sent_refs[-1][: N - at, :] = state[at:]
    sent_refs[-1][N - at :, :] = tail


def unpack_state(got_refs):
    rows = jnp.concatenate([ref[...] for ref in got_refs], axis=0).astype(F32)
    return rows[:N], rows[N : N + 1, :] + rows[N + 1 : N + 2, :]


def combine_kernel(level, got, has_before, place_ref, total, decays, *refs):
    other, refs = refs[:got], refs[got:]
    if has_before:
        before, refs = refs[0][...], refs[1:]
    total_ref, decays_ref, before_ref, *sent_refs = refs
    come, decay = unpack_state(other)
    whole, part = decays[0:1, :], decays[1:2, :]
    upper = (place_ref[0] >> level) & 1 == 1
    fresh = jnp.where(upper, part, 0.0) * come
    before_ref[...] = before + fresh if has_before else fresh
    joint = jnp.where(upper, 1.0, decay) * total[...] + jnp.where(upper, whole, 1.0) * come
    total_ref[...] = joint
    decays_ref[0:1, :] = whole * decay
    decays_ref[1:2, :] = jnp.where(upper, decay * part, part)
    pack_state(sent_refs, joint, whole * decay)


def pair_kernel(place_ref, total, decays, other, total_ref, decays_ref, sent_ref, before_ref, part_ref):
    come, decay = unpack_state([other])
    whole = decays[0:1, :]
    upper = place_ref[0] & 1 == 1
    before_ref[...] = jnp.where(upper, come, 0.0)
    part_ref[0:1, :] = jnp.where(upper, decay, 1.0)
    joint = jnp.where(upper, 1.0, decay) * total[...] + jnp.where(upper, whole, 1.0) * come
    half = joint.shape[1] // 2
    picked = lambda a: jnp.where(upper, a[:, half:], a[:, :half])
    joint, whole = picked(joint), picked(whole * decay)
    total_ref[...] = joint
    decays_ref[0:1, :] = whole
    decays_ref[1:2, :] = jnp.ones_like(whole)
    pack_state([sent_ref], joint, whole)


def settle_kernel(level, has_before, place_ref, decays, other, *refs):
    upper = (place_ref[0] >> level) & 1 == 1
    state = jnp.where(upper, decays[1:2, :], 0.0) * unpack_state([other])[0]
    refs[-1][...] = (refs[0][...] + state if has_before else state).astype(BF16)


def read_kernel(place_ref, y, reads, cum_g, early, part, before, mine, theirs, *refs):
    out_ref = refs[-1]
    upper = place_ref[0] & 1 == 1
    mine, theirs = mine[...].astype(F32), theirs[...].astype(F32)
    chip = jnp.concatenate([jnp.where(upper, theirs, mine), jnp.where(upper, mine, theirs)], axis=1)
    whole = before[...] + part[0:1, :] * chip
    width = whole.shape[1] // cum_g.shape[0]
    for g in range(cum_g.shape[0]):
        chans, state = slice(g * width, (g + 1) * width), whole[:, g * width : (g + 1) * width]
        for at in range(0, out_ref.shape[0], SPAN):
            span = slice(at, at + SPAN)
            cum_b = cum_g[g, span, :]
            seen = jnp.dot(reads[span, g * N : (g + 1) * N], state.astype(BF16), preferred_element_type=F32)
            out_ref[span, chans] = (y[span, chans] + over_channels(jnp.exp(cum_b)) * seen).astype(BF16)
            if at + SPAN < out_ref.shape[0]:
                state = over_channels(jnp.exp(cum_b[SPAN - 1 : SPAN, :])) * state + early[at // SPAN, :, chans]


def combined(level, place, total, decays, other, before, groups, cut):
    width = total.shape[1] // groups
    block = lambda rows: pl.BlockSpec((rows, width), lambda i: (0, i))
    shape = lambda rows, dtype: jax.ShapeDtypeStruct((rows, total.shape[1]), dtype)
    total, decays, before, *sent = call(
        functools.partial(combine_kernel, level, len(other), bool(before)),
        "combine",
        (shape(N, F32), shape(8, F32), shape(N, F32)) + tuple(shape(rows, BF16) for rows in cut),
        flops=6 * total.size,
        moved=20 * total.size,
        vmem=12,
        grid=(groups,),
        in_specs=[SMEM, block(N), block(8)] + [block(a.shape[0]) for a in other] + [block(N)] * len(before),
        out_specs=[block(N), block(8), block(N)] + [block(rows) for rows in cut],
    )(place, total, decays, *other, *before)
    return total, decays, before, sent


def body(
    tokens,
    proj_mean,
    proj_devs,
    bc_mean,
    bc_devs,
    swag_coef,
    dt_weight,
    dt_bias,
    decay_rate,
    skip_gain,
    conv_proj,
    conv_bc,
):
    heads_here = decay_rate.shape[0]
    groups_here = bc_mean.shape[2] // N
    per_group = heads_here // groups_here
    width_bc = 2 * bc_mean.shape[2]
    rows_k = proj_mean.shape[0]
    chips = lax.axis_size("chip")
    count = lax.axis_size(SEQ)

    def after(arrays, earlier):
        return lax.optimization_barrier((arrays, earlier))[0]

    width = per_group * P_SIZE
    early_groups = max(1, groups_here // 2)
    fill = -heads_here % LANES
    late = list(range(early_groups, groups_here))

    plane = chips == 4
    two_shares = lax.axis_size("tp") == 2
    place = lax.axis_index("chip") if plane else 0
    at = jnp.stack([lax.axis_index(a) for a in ("fsdp", "core", "tp")] + [place ^ i for i in range(chips)]).astype(jnp.int32)
    share, depth = tokens.shape[0], chips * rows_k
    weight_bc = sampled_pair(bc_mean, bc_devs, dt_weight, swag_coef)
    tokens = after(tokens, weight_bc)
    cut = jax.ShapeDtypeStruct((2 * share, depth), BF16)
    far, own = call(
        functools.partial(cut_kernel, chips),
        "cut_tokens",
        (cut,) * 2,
        moved=4 * tokens.size,
        vmem=24,
        in_specs=[SMEM, VMEM],
        out_specs=[VMEM] * 2,
    )(at, tokens)
    proj_mean = after(proj_mean, own)
    far = swapped(far, "fsdp")

    weight_early = sampled_cols(proj_mean, proj_devs, swag_coef, 0, early_groups * width)
    weight_late = None
    if late:
        weight_late = sampled_cols(proj_mean, proj_devs, swag_coef, early_groups // len(late), len(late) * width)
    tok_count = share * lax.axis_size("tp")
    blocks = tok_count // SPAN

    def partial_sums(rows, pieces, with_steps, before_send=(), before_relay=()):
        *far_sent, far_kept, sent, kept = multiplied(at, rows, pieces, heads_here, with_steps)
        far_got = [swapped(a, "core") for a in after(far_sent, before_send)]
        back = relayed(far_kept, after(far_got, before_relay), heads_here, with_steps)
        return (kept, swapped(after(sent, back), "core")), back

    specs_of = lambda width: [pl.BlockSpec((tok_count, width), lambda i: (0, i))] * 3 + [
        pl.BlockSpec((RIM, width), lambda i: (0, i)),
    ]
    whole_of = lambda *shape: pl.BlockSpec(shape, lambda i: (0,) * len(shape))
    by_group = (groups_here, tok_count, per_group)
    by_head = (heads_here, tok_count)
    by_decay = (groups_here, 1, per_group)
    state_proj = lambda part: call(
        functools.partial(state_proj_kernel, heads_here),
        "state_proj",
        (jax.ShapeDtypeStruct((tok_count, width_bc), BF16),)
        + tuple(jax.ShapeDtypeStruct(a, F32) for a in (by_group, by_group, by_head, by_head, by_decay)),
        moved=10 * tok_count * width_bc,
        vmem=30,
        grid=(1,),
        in_specs=specs_of(width_bc + LANES) + [whole_of(CONV, width_bc)] + [whole_of(1, heads_here)] * 2,
        out_specs=[whole_of(*a) for a in ((tok_count, width_bc), by_group, by_group, by_head, by_head, by_decay)],
        scratch_shapes=[pltpu.VMEM((tok_count + 8, width_bc), F32)],
    )(*part, rows_before(*part), conv_bc.reshape(CONV, width_bc), dt_bias[None], decay_rate[None])
    if plane and two_shares:
        bc = [weight_bc, *sent_straight(weight_bc)]
        bc += sent_on(corner_parts(bc[1:], 1))
        own_t = swapped(own, "tp")
        weight_early = after(weight_early, bc[3:])
        early = [weight_early, *sent_straight(weight_early)]
        far = after(far, (own_t, bc[3:], weight_late))
        far_t = swapped(far, "tp")
        own, own_t = after((own, own_t), far)
        own_c, own_tc = swapped(own, "core"), swapped(own_t, "core")
        halves = corner_parts(early[1:], 1)
        far_c, far_tc = swapped(far, "core"), swapped(after(far_t, halves), "core")
        rows = (far, far_t, far_c, far_tc, own, own_t, own_c, own_tc)
        part_bc, back_bc = partial_sums(rows, bc, True)
        early += sent_on(halves)
        got_bc = swapped(back_bc, "fsdp")
        weight_late = after(weight_late, (back_bc, early[3:]))
        part, back = partial_sums(rows, early, False, before_relay=got_bc)
        got = swapped(after(back, got_bc), "fsdp")
        straight = sent_straight(weight_late)
        corners = sent_on(corner_parts(straight, 1))
        seen = state_proj(after(part_bc + (got_bc,), back))
        part_late, back_late = partial_sums(rows, [weight_late, *straight, *corners], False, before_send=seen)
        got_late = swapped(after(back_late, got), "fsdp")
        got = after(got, back_late)
    else:
        whole = lambda a, axis: lax.all_gather(a, axis, axis=0, tiled=True)
        ranges = [r for a in (far, own) for r in (a[:share], swapped(a[share:], "core"))]
        rows = (jnp.concatenate([whole(r, "tp") for r in ranges], axis=0),)
        part, back = partial_sums(rows, [whole(weight_early, "chip")], False)
        part_bc, back_bc = partial_sums(rows, [whole(weight_bc, "chip")], True)
        got, got_bc = swapped(back, "fsdp"), swapped(back_bc, "fsdp")
        if late:
            part_late, back_late = partial_sums(rows, [whole(weight_late, "chip")], False)
            got_late = swapped(back_late, "fsdp")
        seen = state_proj(part_bc + (got_bc,))
    conv_out, cum_g, steps_g, cum_t, steps_t, decay = seen
    parts = [part + (got,)]
    if late:
        parts.append(part_late + (got_late,))

    skip = skip_gain.reshape(by_decay)
    levels = count.bit_length() - 1
    seq_place = (2 * lax.axis_index("chip") + lax.axis_index("core")).astype(jnp.int32).reshape(1)

    result = None
    for first, groups, part in zip((0, early_groups), (early_groups, len(late)), parts):
        part = part + (rows_before(*part),)
        if first:
            part = after(part, sent)
        grid = (groups,)
        cols = lambda rows: pl.BlockSpec((rows, width), lambda i: (0, i))
        cols_all = lambda rows: pl.BlockSpec((rows, width), lambda i: (0, first + i))
        heads_g = pl.BlockSpec((1, tok_count, per_group), lambda i: (first + i, 0, 0))
        heads_t = pl.BlockSpec((per_group, tok_count), lambda i: (first + i, 0))
        heads_1 = pl.BlockSpec((1, 1, per_group), lambda i: (first + i, 0, 0))
        keys = pl.BlockSpec((tok_count, N), lambda i: (0, first + i))
        reads = pl.BlockSpec((tok_count, N), lambda i: (0, groups_here + first + i))
        early_spec = pl.BlockSpec((blocks - 1, N, width), lambda i: (0, 0, i))
        y, early, total, decays, sent = call(
            mix_kernel,
            "mix",
            (
                jax.ShapeDtypeStruct((tok_count, groups * width), F32),
                jax.ShapeDtypeStruct((blocks - 1, N, groups * width), F32),
                jax.ShapeDtypeStruct((N, groups * width), F32),
                jax.ShapeDtypeStruct((8, groups * width), F32),
                jax.ShapeDtypeStruct((N + RIM, groups * width), BF16),
            ),
            flops=8 * tok_count * N * width * groups,
            moved=14 * tok_count * width * groups,
            vmem=24,
            grid=grid,
            in_specs=specs_of(width) + [cols_all(CONV), keys, reads, heads_g, heads_g, heads_t, heads_t, heads_1, heads_1],
            out_specs=[cols(tok_count), early_spec, cols(N), cols(8), cols(N + RIM)],
            scratch_shapes=[pltpu.VMEM((tok_count + 8, width), F32)],
        )(*part, conv_proj, conv_out, conv_out, cum_g, steps_g, cum_t, steps_t, skip, decay)
        wide = groups * width
        shape = lambda rows, cols, dtype=F32: jax.ShapeDtypeStruct((rows, cols), dtype)
        total, decays, sent, core_before, core_part = call(
            pair_kernel,
            "pair",
            (shape(N, wide // 2), shape(8, wide // 2), shape(N + RIM, wide // 2, BF16), shape(N, wide), shape(8, wide)),
            moved=20 * N * wide,
            vmem=12,
            in_specs=[SMEM] + [VMEM] * 3,
            out_specs=[VMEM] * 5,
        )(seq_place, total, decays, swapped(sent, SEQ, 1))
        before, sent = (), [sent]
        for level in range(1, levels - 1):
            other = [swapped(a, SEQ, 1 << level) for a in sent]
            total, decays, fresh, sent = combined(level, seq_place, total, decays, other, before, 1, (N + RIM,))
            before = (fresh,)
        mine = call(
            functools.partial(settle_kernel, levels - 1, bool(before)),
            "settle",
            shape(N, wide // 2, BF16),
            moved=6 * N * wide,
            vmem=12,
            in_specs=[SMEM] + [VMEM] * (2 + len(before)),
            out_specs=VMEM,
        )(seq_place, decays, swapped(sent[0], SEQ, 1 << (levels - 1)), *before)
        operands = [seq_place, y, conv_out, cum_g, early, core_part, core_before, mine, swapped(mine, "core")]
        at_block = first // groups
        specs = [
            SMEM,
            whole_of(tok_count, wide),
            pl.BlockSpec((tok_count, groups * N), lambda i: (0, groups_here // groups + at_block)),
            pl.BlockSpec((groups, tok_count, per_group), lambda i: (at_block, 0, 0)),
            whole_of(blocks - 1, N, wide),
            whole_of(8, wide),
            whole_of(N, wide),
            whole_of(N, wide // 2),
            whole_of(N, wide // 2),
        ]
        alias = {}
        if result is not None:
            operands.append(result)
            specs.append(pl.BlockSpec(memory_space=pl.ANY))
            alias = {len(operands) - 1: 0}
        result = call(
            read_kernel,
            "read_out",
            jax.ShapeDtypeStruct((tok_count, heads_here * P_SIZE), BF16),
            flops=2 * tok_count * N * width * groups,
            moved=10 * tok_count * width * groups,
            vmem=12,
            grid=(1,),
            in_specs=specs,
            out_specs=pl.BlockSpec((tok_count, wide), lambda i: (0, at_block)),
            input_output_aliases=alias,
        )(*operands)
    return result


def solution(mesh):
    shape = mesh.shape
    split = Mesh(
        mesh.devices.reshape(shape["fsdp"], shape["seq"] // 2, 2, shape["tp"]),
        ("fsdp", "chip", "core", "tp"),
    )
    rows = ("fsdp", "chip", "core")
    return jax.shard_map(
        body,
        mesh=split,
        in_specs=(
            P(rows + ("tp",), None),
            P(rows, "tp"),
            P(None, rows, "tp"),
            P(rows, None, "tp"),
            P(None, rows, None, "tp"),
            P(),
            P(rows, "tp"),
            P("tp"),
            P("tp"),
            P("tp"),
            P(None, "tp"),
            P(None, None, "tp"),
        ),
        out_specs=P(rows, "tp"),
        check_vma=False,
    )
```

```python
import functools

import jax
import jax.numpy as jnp
from jax import lax
from jax.experimental import pallas as pl
from jax.experimental.pallas import tpu as pltpu
from jax.sharding import Mesh, PartitionSpec as P

P_SIZE = 64
N = 128
CONV = 4
SPAN = 128
LANES = 128
RIM = 16
FAR_PARTS = 2
SEQ = ("chip", "core")
F32 = jnp.float32
BF16 = jnp.bfloat16
SMEM = pl.BlockSpec(memory_space=pltpu.SMEM)
VMEM = pl.BlockSpec(memory_space=pltpu.VMEM)


def call(kernel, name, out_shape, flops=0, moved=0, vmem=60, **settings):
    return pl.pallas_call(
        kernel,
        out_shape=out_shape,
        name=name,
        cost_estimate=pl.CostEstimate(flops=flops // 50, bytes_accessed=moved // 50, transcendentals=0),
        compiler_params=pltpu.CompilerParams(vmem_limit_bytes=vmem * 1024 * 1024),
        **settings,
    )


def swapped(part, axis, by=1):
    return lax.ppermute(part, axis, [(i, i ^ by) for i in range(lax.axis_size(axis))])


def cut_kernel(chips, at_ref, tokens_ref, far_ref, own_ref):
    depth = far_ref.shape[1] // chips
    rows = tokens_ref.shape[0]
    f_at, c_at = at_ref[0], at_ref[1]
    for out, f in ((far_ref, 1 - f_at), (own_ref, f_at)):
        for k, c in enumerate((c_at, 1 - c_at)):
            for i in range(chips):
                start = pl.multiple_of(((f * chips + at_ref[3 + i]) * 2 + c) * depth, depth)
                out[k * rows : (k + 1) * rows, i * depth : (i + 1) * depth] = tokens_ref[:, pl.ds(start, depth)]


def stack_rows(at_ref, pieces, rows_ref):
    count = pieces[0].shape[0]
    for k in range(0, len(pieces), 2):
        rows_ref[pl.ds(pl.multiple_of((k + at_ref[2]) * count, count), count), :] = pieces[k][...]
        rows_ref[pl.ds(pl.multiple_of((k + 1 - at_ref[2]) * count, count), count), :] = pieces[k + 1][...]


def sample_kernel(count, coef_ref, mean_ref, devs_ref, out_ref):
    factor = (2.0 * (count - 1)) ** (-0.5)
    accum = mean_ref[...].astype(F32)
    for member in range(count):
        accum = accum + factor * coef_ref[member] * devs_ref[member].astype(F32)
    out_ref[...] = accum.astype(BF16)


def sampled_cols(mean_part, dev_part, swag_coef, at, width):
    rows, count = mean_part.shape[0], dev_part.shape[0]
    tile = rows // 4
    return call(
        functools.partial(sample_kernel, count),
        "sample",
        jax.ShapeDtypeStruct((rows, width), BF16),
        moved=2 * (count + 2) * rows * width,
        vmem=24,
        grid=(4,),
        in_specs=[
            SMEM,
            pl.BlockSpec((tile, width), lambda i: (i, at)),
            pl.BlockSpec((count, tile, width), lambda i: (0, i, at)),
        ],
        out_specs=pl.BlockSpec((tile, width), lambda i: (i, 0)),
    )(swag_coef, mean_part, dev_part)


def sample_pair_kernel(count, coef_ref, mean_ref, devs_ref, dt_ref, out_ref):
    factor = (2.0 * (count - 1)) ** (-0.5)
    rows, _, width = mean_ref.shape
    heads = dt_ref.shape[0]
    flat = lambda a: a.reshape(2 * rows, width).astype(F32)
    accum = flat(mean_ref[...])
    for member in range(count):
        accum = accum + factor * coef_ref[member] * flat(devs_ref[member])
    accum = accum.astype(BF16)
    row = lax.broadcasted_iota(jnp.int32, (rows, 2 * rows), 0)
    col = lax.broadcasted_iota(jnp.int32, (rows, 2 * rows), 1)
    for k in range(2):
        picks = jnp.where(col == 2 * row + k, 1.0, 0.0).astype(BF16)
        part = jnp.dot(picks, accum, preferred_element_type=F32)
        out_ref[:, k * width : (k + 1) * width] = part.astype(BF16)
    out_ref[:, 2 * width :] = jnp.zeros((out_ref.shape[0], LANES), BF16)
    rows = out_ref.shape[0]
    steps = dt_ref[:, pl.ds(pl.multiple_of(pl.program_id(0) * rows, rows), rows)]
    out_ref[:, 2 * width : 2 * width + heads] = jnp.transpose(steps.astype(F32)).astype(BF16)


def sampled_pair(mean_part, dev_part, dt_part, swag_coef):
    rows, _, width = mean_part.shape
    count = dev_part.shape[0]
    tile = min(rows, LANES)
    return call(
        functools.partial(sample_pair_kernel, count),
        "sample_pair",
        jax.ShapeDtypeStruct((rows, 2 * width + LANES), BF16),
        moved=4 * (count + 2) * rows * width,
        grid=(rows // tile,),
        in_specs=[
            SMEM,
            pl.BlockSpec((tile, 2, width), lambda i: (i, 0, 0)),
            pl.BlockSpec((count, tile, 2, width), lambda i: (0, i, 0, 0)),
            pl.BlockSpec((dt_part.shape[1], rows), lambda i: (0, 0)),
        ],
        out_specs=pl.BlockSpec((tile, 2 * width + LANES), lambda i: (i, 0)),
    )(swag_coef, mean_part, dev_part, dt_part.T)


def sent_straight(weight):
    return swapped(weight, "chip", 1), swapped(weight, "chip", 2)


def corner_parts(straight, each):
    rows = straight[0].shape[0] // (2 * each)
    cut = lambda a, i: a[i * rows : (i + 1) * rows]
    return [cut(straight[1], i) for i in range(each)] + [cut(straight[0], each + i) for i in range(each)]


def sent_on(parts):
    each = len(parts) // 2
    return [swapped(a, "chip", 1) for a in parts[:each]] + [swapped(a, "chip", 2) for a in parts[each:]]


def coded(part, heads):
    high = part.astype(BF16).astype(F32)
    return high + pltpu.roll(part - high, heads, 1)


def decoded(part, heads):
    return part + pltpu.roll(part, LANES - heads, 1)


def multiply_kernel(heads, with_steps, shares, pieces, plan, at_ref, *refs):
    shares, weights, outs, rows_ref = refs[:shares], refs[shares : shares + pieces], refs[shares + pieces : -1], refs[-1]

    @pl.when(pl.program_id(0) == 0)
    def _():
        if len(shares) == 1:
            rows_ref[...] = shares[0][...]
        else:
            stack_rows(at_ref, shares, rows_ref)

    joined = jnp.concatenate([weight[...] for weight in weights], axis=0)
    total = jnp.dot(rows_ref[...], joined, preferred_element_type=F32)
    for out, (first, sent) in zip(outs, plan):
        part = total[first : first + out.shape[0]]
        out[...] = part.astype(out.dtype)
        if with_steps and sent:
            @pl.when(pl.program_id(0) == pl.num_programs(0) - 1)
            def _():
                out[:, -LANES:] = coded(part[:, -LANES:], heads).astype(BF16)


def multiplied(at, rows, weights, heads, with_steps):
    width = weights[0].shape[1]
    tile = next(t for t in (512, 384, 128) if width % t == 0)
    depth = rows[0].shape[1]
    if len(rows) == 1:
        count = rows[0].shape[0]
        row_specs = [pl.BlockSpec(rows[0].shape, lambda i: (0, 0))]
    else:
        share = rows[0].shape[0] // 2
        count = len(rows) * share
        low = pl.BlockSpec((share, depth), lambda i: (0, 0))
        high = pl.BlockSpec((share, depth), lambda i: (1, 0))
        row_specs = [low, low, high, high] * 2
    half = count // 4
    part = half // FAR_PARTS
    plan = [(half + i * part, True) for i in range(FAR_PARTS)] + [(0, False), (3 * half, True), (2 * half, False)]
    shapes = [(part, BF16)] * FAR_PARTS + [(half, F32), (half, BF16), (half, F32)]
    return call(
        functools.partial(multiply_kernel, heads, with_steps, len(rows), len(weights), plan),
        "multiply",
        tuple(jax.ShapeDtypeStruct((r, width), dtype) for r, dtype in shapes),
        flops=2 * count * depth * width,
        moved=2 * count * depth + 2 * depth * width + 12 * half * width,
        vmem=34,
        grid=(width // tile,),
        in_specs=[SMEM] + row_specs + [pl.BlockSpec((w.shape[0], tile), lambda i: (0, i)) for w in weights],
        out_specs=[pl.BlockSpec((r, tile), lambda i: (0, i)) for r, _ in shapes],
        scratch_shapes=[pltpu.VMEM((count, depth), BF16)],
    )(at, *rows, *weights)


def relay_kernel(heads, with_steps, kept_ref, *refs):
    out_ref, count = refs[-1], refs[0].shape[0]
    for i, got_ref in enumerate(refs[:-1]):
        rows = slice(i * count, (i + 1) * count)
        kept, got = kept_ref[rows, :], got_ref[...].astype(F32)
        out_ref[rows, :] = (kept + got).astype(BF16)
        if with_steps:
            wide = kept[:, -LANES:] + decoded(got[:, -LANES:], heads)
            lane = lax.broadcasted_iota(jnp.int32, wide.shape, 1)
            out_ref[rows, -LANES:] = coded(jnp.where(lane < heads, wide, 0.0), heads).astype(BF16)


def relayed(kept, got, heads, with_steps):
    rows, width = kept.shape
    part = pl.BlockSpec((rows // len(got), width), lambda i: (0, 0))
    return call(
        functools.partial(relay_kernel, heads, with_steps),
        "relay",
        jax.ShapeDtypeStruct((rows, width), BF16),
        moved=8 * rows * width,
        vmem=12,
        grid=(1,),
        in_specs=[pl.BlockSpec((rows, width), lambda i: (0, 0))] + [part] * len(got),
        out_specs=pl.BlockSpec((rows, width), lambda i: (0, 0)),
    )(kept, *got)


def rim_kernel(kept, got_c, got_f, rim_ref):
    rim_ref[...] = (kept[...] + got_c[...].astype(F32) + got_f[...].astype(F32)).astype(BF16)


def rows_before(kept, got_c, got_f):
    rows, width = got_f.shape
    at = rows // RIM - 1
    rim = call(
        rim_kernel,
        "rim",
        jax.ShapeDtypeStruct((RIM, width), BF16),
        moved=10 * RIM * width,
        vmem=12,
        grid=(1,),
        in_specs=[pl.BlockSpec((RIM, width), lambda i: (at, 0))] * 3,
        out_specs=pl.BlockSpec((RIM, width), lambda i: (0, 0)),
    )(kept, got_c, got_f)
    return lax.ppermute(rim, SEQ, [(i, i + 1) for i in range(lax.axis_size(SEQ) - 1)])


def convolved(width, kept, got_c, got_f, rim, taps, padded):
    count = padded.shape[0] - 8
    proj = kept[:, :width] + got_c[:, :width].astype(F32) + got_f[:, :width].astype(F32)
    padded[8:, :] = proj.astype(BF16).astype(F32)
    padded[:8, :] = rim[:, :width].astype(F32)[RIM - 8 :]
    first = 8 - (CONV - 1)
    conv_sum = taps[0:1, :] * padded[first : first + count, :]
    for offset in range(1, CONV):
        conv_sum = conv_sum + taps[offset : offset + 1, :] * padded[first + offset : first + offset + count, :]
    return (conv_sum * jax.nn.sigmoid(conv_sum)).astype(BF16)


def state_proj_kernel(
    heads, kept, got_c, got_f, rim, taps, bias, rate, out_ref, cum_ref, steps_ref, cum_t_ref, steps_t_ref, decay_ref, padded
):
    count, width = out_ref.shape
    out_ref[...] = convolved(width, kept, got_c, got_f, rim, taps, padded)
    logits = kept[:, width:] + decoded(got_c[:, width:].astype(F32), heads) + decoded(got_f[:, width:].astype(F32), heads)
    steps = jax.nn.softplus(logits[:, :heads] + bias[...])
    row = lax.broadcasted_iota(jnp.int32, (SPAN, SPAN), 0)
    col = lax.broadcasted_iota(jnp.int32, (SPAN, SPAN), 1)
    causal = jnp.where(row >= col, 1.0, 0.0)
    groups, per_group = cum_ref.shape[0], cum_ref.shape[2]
    through = jnp.zeros((1, heads), F32)
    for at in range(0, count, SPAN):
        span = slice(at, at + SPAN)
        steps_b = steps[span, :]
        cum = jnp.dot(
            causal, -steps_b * rate[...], precision=lax.Precision.HIGHEST, preferred_element_type=F32
        )
        through = through + cum[SPAN - 1 : SPAN, :]
        cum_t_ref[:, span] = jnp.transpose(cum)
        steps_t_ref[:, span] = jnp.transpose(steps_b)
        for g in range(groups):
            cum_ref[g, span, :] = cum[:, g * per_group : (g + 1) * per_group]
            steps_ref[g, span, :] = steps_b[:, g * per_group : (g + 1) * per_group]
    for g in range(groups):
        decay_ref[g] = jnp.exp(through)[:, g * per_group : (g + 1) * per_group]


def pairwise(columns, first):
    shape = (columns.shape[0], 2 * P_SIZE)
    lane = lax.broadcasted_iota(jnp.int32, shape, 1)
    return jnp.where(lane < P_SIZE, columns[:, first : first + 1], columns[:, first + 1 : first + 2])


def over_channels(columns):
    return jnp.concatenate([pairwise(columns, h) for h in range(0, columns.shape[1], 2)], axis=1)


def mix_kernel(
    kept, got_c, got_f, rim, taps, keys, reads, cum_g, steps_g, cum_t, steps_t, skip, decay, y_ref, early_ref, total_ref, decays_ref, sent_ref, padded
):
    width = y_ref.shape[1]
    values = convolved(width, kept, got_c, got_f, rim, taps, padded)
    cum, steps = cum_g[0], steps_g[0]
    heads = cum.shape[1]
    row = lax.broadcasted_iota(jnp.int32, (SPAN, SPAN), 0)
    col = lax.broadcasted_iota(jnp.int32, (SPAN, SPAN), 1)
    causal = row >= col
    lane = lax.broadcasted_iota(jnp.int32, (SPAN, 2 * P_SIZE), 1)
    gain = over_channels(skip[0])
    state = None
    for at in range(0, y_ref.shape[0], SPAN):
        span = slice(at, at + SPAN)
        keys_b, reads_b, values_b = keys[span, :], reads[span, :], values[span, :]
        cum_b, steps_b = cum[span, :], steps[span, :]
        last = cum_b[SPAN - 1 : SPAN, :]
        scores = lax.dot_general(reads_b, keys_b, (((1,), (1,)), ((), ())), preferred_element_type=F32)
        scores = jnp.where(causal, scores, 0.0)
        reach = jnp.exp(last - cum_b) * steps_b
        scaled = []
        for head in range(0, heads, 2):
            chans = slice(head * P_SIZE, (head + 2) * P_SIZE)
            two = []
            for h in (head, head + 1):
                gap = cum_b[:, h : h + 1] - cum_t[h : h + 1, span]
                two.append((scores * jnp.exp(jnp.minimum(gap, 0.0)) * steps_t[h : h + 1, span]).astype(BF16))
            values_h = values_b[:, chans]
            both = jnp.dot(jnp.concatenate(two, axis=0), values_h, preferred_element_type=F32)
            inner = jnp.where(lane < P_SIZE, both[:SPAN], both[SPAN:])
            wide = values_h.astype(F32)
            y_ref[span, chans] = inner + gain[:, chans] * wide
            scaled.append((wide * pairwise(reach, head)).astype(BF16))
        fresh = lax.dot_general(
            keys_b, jnp.concatenate(scaled, axis=1), (((0,), (0,)), ((), ())), preferred_element_type=F32
        )
        state = fresh if state is None else over_channels(jnp.exp(last)) * state + fresh
        if at + SPAN < y_ref.shape[0]:
            early_ref[at // SPAN] = fresh
    total_ref[...] = state
    wide = over_channels(decay[0])
    decays_ref[0:1, :] = wide
    decays_ref[1:2, :] = jnp.ones_like(wide)
    pack_state([sent_ref], state, wide)


def pack_state(sent_refs, state, decay):
    high = decay.astype(BF16).astype(F32)
    row = lax.broadcasted_iota(jnp.int32, (RIM, decay.shape[1]), 0)
    tail = jnp.where(row == 0, high, jnp.where(row == 1, decay - high, 0.0)).astype(BF16)
    state = state.astype(BF16)
    at = 0
    for sent_ref in sent_refs[:-1]:
        sent_ref[...] = state[at : at + sent_ref.shape[0]]
        at += sent_ref.shape[0]
    sent_refs[-1][: N - at, :] = state[at:]
    sent_refs[-1][N - at :, :] = tail


def unpack_state(got_refs):
    rows = jnp.concatenate([ref[...] for ref in got_refs], axis=0).astype(F32)
    return rows[:N], rows[N : N + 1, :] + rows[N + 1 : N + 2, :]


def combine_kernel(level, got, has_before, place_ref, total, decays, *refs):
    other, refs = refs[:got], refs[got:]
    if has_before:
        before, refs = refs[0][...], refs[1:]
    total_ref, decays_ref, before_ref, *sent_refs = refs
    come, decay = unpack_state(other)
    whole, part = decays[0:1, :], decays[1:2, :]
    upper = (place_ref[0] >> level) & 1 == 1
    fresh = jnp.where(upper, part, 0.0) * come
    before_ref[...] = before + fresh if has_before else fresh
    joint = jnp.where(upper, 1.0, decay) * total[...] + jnp.where(upper, whole, 1.0) * come
    total_ref[...] = joint
    decays_ref[0:1, :] = whole * decay
    decays_ref[1:2, :] = jnp.where(upper, decay * part, part)
    pack_state(sent_refs, joint, whole * decay)


def pair_kernel(place_ref, total, decays, other, total_ref, decays_ref, sent_ref, before_ref, part_ref):
    come, decay = unpack_state([other])
    whole = decays[0:1, :]
    upper = place_ref[0] & 1 == 1
    before_ref[...] = jnp.where(upper, come, 0.0)
    part_ref[0:1, :] = jnp.where(upper, decay, 1.0)
    joint = jnp.where(upper, 1.0, decay) * total[...] + jnp.where(upper, whole, 1.0) * come
    half = joint.shape[1] // 2
    picked = lambda a: jnp.where(upper, a[:, half:], a[:, :half])
    joint, whole = picked(joint), picked(whole * decay)
    total_ref[...] = joint
    decays_ref[0:1, :] = whole
    decays_ref[1:2, :] = jnp.ones_like(whole)
    pack_state([sent_ref], joint, whole)


def settle_kernel(level, has_before, place_ref, decays, other, *refs):
    upper = (place_ref[0] >> level) & 1 == 1
    state = jnp.where(upper, decays[1:2, :], 0.0) * unpack_state([other])[0]
    refs[-1][...] = (refs[0][...] + state if has_before else state).astype(BF16)


def read_kernel(place_ref, y, reads, cum_g, early, part, before, mine, theirs, *refs):
    out_ref = refs[-1]
    upper = place_ref[0] & 1 == 1
    mine, theirs = mine[...].astype(F32), theirs[...].astype(F32)
    chip = jnp.concatenate([jnp.where(upper, theirs, mine), jnp.where(upper, mine, theirs)], axis=1)
    whole = before[...] + part[0:1, :] * chip
    width = whole.shape[1] // cum_g.shape[0]
    for g in range(cum_g.shape[0]):
        chans, state = slice(g * width, (g + 1) * width), whole[:, g * width : (g + 1) * width]
        for at in range(0, out_ref.shape[0], SPAN):
            span = slice(at, at + SPAN)
            cum_b = cum_g[g, span, :]
            seen = jnp.dot(reads[span, g * N : (g + 1) * N], state.astype(BF16), preferred_element_type=F32)
            out_ref[span, chans] = (y[span, chans] + over_channels(jnp.exp(cum_b)) * seen).astype(BF16)
            if at + SPAN < out_ref.shape[0]:
                state = over_channels(jnp.exp(cum_b[SPAN - 1 : SPAN, :])) * state + early[at // SPAN, :, chans]


def combined(level, place, total, decays, other, before, groups, cut):
    width = total.shape[1] // groups
    block = lambda rows: pl.BlockSpec((rows, width), lambda i: (0, i))
    shape = lambda rows, dtype: jax.ShapeDtypeStruct((rows, total.shape[1]), dtype)
    total, decays, before, *sent = call(
        functools.partial(combine_kernel, level, len(other), bool(before)),
        "combine",
        (shape(N, F32), shape(8, F32), shape(N, F32)) + tuple(shape(rows, BF16) for rows in cut),
        flops=6 * total.size,
        moved=20 * total.size,
        vmem=12,
        grid=(groups,),
        in_specs=[SMEM, block(N), block(8)] + [block(a.shape[0]) for a in other] + [block(N)] * len(before),
        out_specs=[block(N), block(8), block(N)] + [block(rows) for rows in cut],
    )(place, total, decays, *other, *before)
    return total, decays, before, sent


def body(
    tokens,
    proj_mean,
    proj_devs,
    bc_mean,
    bc_devs,
    swag_coef,
    dt_weight,
    dt_bias,
    decay_rate,
    skip_gain,
    conv_proj,
    conv_bc,
):
    heads_here = decay_rate.shape[0]
    groups_here = bc_mean.shape[2] // N
    per_group = heads_here // groups_here
    width_bc = 2 * bc_mean.shape[2]
    rows_k = proj_mean.shape[0]
    chips = lax.axis_size("chip")
    count = lax.axis_size(SEQ)

    def after(arrays, earlier):
        return lax.optimization_barrier((arrays, earlier))[0]

    width = per_group * P_SIZE
    early_groups = max(1, groups_here // 2)
    fill = -heads_here % LANES
    late = list(range(early_groups, groups_here))

    plane = chips == 4
    two_shares = lax.axis_size("tp") == 2
    place = lax.axis_index("chip") if plane else 0
    at = jnp.stack([lax.axis_index(a) for a in ("fsdp", "core", "tp")] + [place ^ i for i in range(chips)]).astype(jnp.int32)
    share, depth = tokens.shape[0], chips * rows_k
    weight_bc = sampled_pair(bc_mean, bc_devs, dt_weight, swag_coef)
    tokens = after(tokens, weight_bc)
    cut = jax.ShapeDtypeStruct((2 * share, depth), BF16)
    far, own = call(
        functools.partial(cut_kernel, chips),
        "cut_tokens",
        (cut,) * 2,
        moved=4 * tokens.size,
        vmem=24,
        in_specs=[SMEM, VMEM],
        out_specs=[VMEM] * 2,
    )(at, tokens)
    proj_mean = after(proj_mean, own)
    far = swapped(far, "fsdp")

    weight_early = sampled_cols(proj_mean, proj_devs, swag_coef, 0, early_groups * width)
    weight_late = None
    if late:
        weight_late = sampled_cols(proj_mean, proj_devs, swag_coef, early_groups // len(late), len(late) * width)
    tok_count = share * lax.axis_size("tp")
    blocks = tok_count // SPAN

    def partial_sums(rows, pieces, with_steps, before_send=(), before_relay=()):
        *far_sent, far_kept, sent, kept = multiplied(at, rows, pieces, heads_here, with_steps)
        far_got = [swapped(a, "core") for a in after(far_sent, before_send)]
        back = relayed(far_kept, after(far_got, before_relay), heads_here, with_steps)
        return (kept, swapped(after(sent, back), "core")), back

    specs_of = lambda width: [pl.BlockSpec((tok_count, width), lambda i: (0, i))] * 3 + [
        pl.BlockSpec((RIM, width), lambda i: (0, i)),
    ]
    whole_of = lambda *shape: pl.BlockSpec(shape, lambda i: (0,) * len(shape))
    by_group = (groups_here, tok_count, per_group)
    by_head = (heads_here, tok_count)
    by_decay = (groups_here, 1, per_group)
    state_proj = lambda part: call(
        functools.partial(state_proj_kernel, heads_here),
        "state_proj",
        (jax.ShapeDtypeStruct((tok_count, width_bc), BF16),)
        + tuple(jax.ShapeDtypeStruct(a, F32) for a in (by_group, by_group, by_head, by_head, by_decay)),
        moved=10 * tok_count * width_bc,
        vmem=30,
        grid=(1,),
        in_specs=specs_of(width_bc + LANES) + [whole_of(CONV, width_bc)] + [whole_of(1, heads_here)] * 2,
        out_specs=[whole_of(*a) for a in ((tok_count, width_bc), by_group, by_group, by_head, by_head, by_decay)],
        scratch_shapes=[pltpu.VMEM((tok_count + 8, width_bc), F32)],
    )(*part, rows_before(*part), conv_bc.reshape(CONV, width_bc), dt_bias[None], decay_rate[None])
    if plane and two_shares:
        bc = [weight_bc, *sent_straight(weight_bc)]
        bc += sent_on(corner_parts(bc[1:], 1))
        own_t = swapped(own, "tp")
        weight_early = after(weight_early, bc[3:])
        early = [weight_early, *sent_straight(weight_early)]
        far = after(far, (own_t, bc[3:], weight_late))
        far_t = swapped(far, "tp")
        own, own_t = after((own, own_t), far)
        own_c, own_tc = swapped(own, "core"), swapped(own_t, "core")
        halves = corner_parts(early[1:], 1)
        far_c, far_tc = swapped(far, "core"), swapped(after(far_t, halves), "core")
        rows = (far, far_t, far_c, far_tc, own, own_t, own_c, own_tc)
        part_bc, back_bc = partial_sums(rows, bc, True)
        early += sent_on(halves)
        got_bc = swapped(back_bc, "fsdp")
        weight_late = after(weight_late, (back_bc, early[3:]))
        part, back = partial_sums(rows, early, False, before_relay=got_bc)
        got = swapped(after(back, got_bc), "fsdp")
        straight = sent_straight(weight_late)
        corners = sent_on(corner_parts(straight, 1))
        seen = state_proj(after(part_bc + (got_bc,), back))
        part_late, back_late = partial_sums(rows, [weight_late, *straight, *corners], False, before_send=seen)
        got_late = swapped(after(back_late, got), "fsdp")
        got = after(got, back_late)
    else:
        whole = lambda a, axis: lax.all_gather(a, axis, axis=0, tiled=True)
        ranges = [r for a in (far, own) for r in (a[:share], swapped(a[share:], "core"))]
        rows = (jnp.concatenate([whole(r, "tp") for r in ranges], axis=0),)
        part, back = partial_sums(rows, [whole(weight_early, "chip")], False)
        part_bc, back_bc = partial_sums(rows, [whole(weight_bc, "chip")], True)
        got, got_bc = swapped(back, "fsdp"), swapped(back_bc, "fsdp")
        if late:
            part_late, back_late = partial_sums(rows, [whole(weight_late, "chip")], False)
            got_late = swapped(back_late, "fsdp")
        seen = state_proj(part_bc + (got_bc,))
    conv_out, cum_g, steps_g, cum_t, steps_t, decay = seen
    parts = [part + (got,)]
    if late:
        parts.append(part_late + (got_late,))

    skip = skip_gain.reshape(by_decay)
    levels = count.bit_length() - 1
    seq_place = (2 * lax.axis_index("chip") + lax.axis_index("core")).astype(jnp.int32).reshape(1)

    result = None
    for first, groups, part in zip((0, early_groups), (early_groups, len(late)), parts):
        part = part + (rows_before(*part),)
        if first:
            part = after(part, sent)
        grid = (groups,)
        cols = lambda rows: pl.BlockSpec((rows, width), lambda i: (0, i))
        cols_all = lambda rows: pl.BlockSpec((rows, width), lambda i: (0, first + i))
        heads_g = pl.BlockSpec((1, tok_count, per_group), lambda i: (first + i, 0, 0))
        heads_t = pl.BlockSpec((per_group, tok_count), lambda i: (first + i, 0))
        heads_1 = pl.BlockSpec((1, 1, per_group), lambda i: (first + i, 0, 0))
        keys = pl.BlockSpec((tok_count, N), lambda i: (0, first + i))
        reads = pl.BlockSpec((tok_count, N), lambda i: (0, groups_here + first + i))
        early_spec = pl.BlockSpec((blocks - 1, N, width), lambda i: (0, 0, i))
        y, early, total, decays, sent = call(
            mix_kernel,
            "mix",
            (
                jax.ShapeDtypeStruct((tok_count, groups * width), F32),
                jax.ShapeDtypeStruct((blocks - 1, N, groups * width), F32),
                jax.ShapeDtypeStruct((N, groups * width), F32),
                jax.ShapeDtypeStruct((8, groups * width), F32),
                jax.ShapeDtypeStruct((N + RIM, groups * width), BF16),
            ),
            flops=8 * tok_count * N * width * groups,
            moved=14 * tok_count * width * groups,
            vmem=24,
            grid=grid,
            in_specs=specs_of(width) + [cols_all(CONV), keys, reads, heads_g, heads_g, heads_t, heads_t, heads_1, heads_1],
            out_specs=[cols(tok_count), early_spec, cols(N), cols(8), cols(N + RIM)],
            scratch_shapes=[pltpu.VMEM((tok_count + 8, width), F32)],
        )(*part, conv_proj, conv_out, conv_out, cum_g, steps_g, cum_t, steps_t, skip, decay)
        wide = groups * width
        shape = lambda rows, cols, dtype=F32: jax.ShapeDtypeStruct((rows, cols), dtype)
        total, decays, sent, core_before, core_part = call(
            pair_kernel,
            "pair",
            (shape(N, wide // 2), shape(8, wide // 2), shape(N + RIM, wide // 2, BF16), shape(N, wide), shape(8, wide)),
            moved=20 * N * wide,
            vmem=12,
            in_specs=[SMEM] + [VMEM] * 3,
            out_specs=[VMEM] * 5,
        )(seq_place, total, decays, swapped(sent, SEQ, 1))
        before, sent = (), [sent]
        for level in range(1, levels - 1):
            other = [swapped(a, SEQ, 1 << level) for a in sent]
            total, decays, fresh, sent = combined(level, seq_place, total, decays, other, before, 1, (N + RIM,))
            before = (fresh,)
        mine = call(
            functools.partial(settle_kernel, levels - 1, bool(before)),
            "settle",
            shape(N, wide // 2, BF16),
            moved=6 * N * wide,
            vmem=12,
            in_specs=[SMEM] + [VMEM] * (2 + len(before)),
            out_specs=VMEM,
        )(seq_place, decays, swapped(sent[0], SEQ, 1 << (levels - 1)), *before)
        operands = [seq_place, y, conv_out, cum_g, early, core_part, core_before, mine, swapped(mine, "core")]
        at_block = first // groups
        specs = [
            SMEM,
            whole_of(tok_count, wide),
            pl.BlockSpec((tok_count, groups * N), lambda i: (0, groups_here // groups + at_block)),
            pl.BlockSpec((groups, tok_count, per_group), lambda i: (at_block, 0, 0)),
            whole_of(blocks - 1, N, wide),
            whole_of(8, wide),
            whole_of(N, wide),
            whole_of(N, wide // 2),
            whole_of(N, wide // 2),
        ]
        alias = {}
        if result is not None:
            operands.append(result)
            specs.append(pl.BlockSpec(memory_space=pl.ANY))
            alias = {len(operands) - 1: 0}
        result = call(
            read_kernel,
            "read_out",
            jax.ShapeDtypeStruct((tok_count, heads_here * P_SIZE), BF16),
            flops=2 * tok_count * N * width * groups,
            moved=10 * tok_count * width * groups,
            vmem=12,
            grid=(1,),
            in_specs=specs,
            out_specs=pl.BlockSpec((tok_count, wide), lambda i: (0, at_block)),
            input_output_aliases=alias,
        )(*operands)
    return result


def solution(mesh):
    shape = mesh.shape
    split = Mesh(
        mesh.devices.reshape(shape["fsdp"], shape["seq"] // 2, 2, shape["tp"]),
        ("fsdp", "chip", "core", "tp"),
    )
    rows = ("fsdp", "chip", "core")
    return jax.shard_map(
        body,
        mesh=split,
        in_specs=(
            P(rows + ("tp",), None),
            P(rows, "tp"),
            P(None, rows, "tp"),
            P(rows, None, "tp"),
            P(None, rows, None, "tp"),
            P(),
            P(rows, "tp"),
            P("tp"),
            P("tp"),
            P("tp"),
            P(None, "tp"),
            P(None, None, "tp"),
        ),
        out_specs=P(rows, "tp"),
        check_vma=False,
    )
```

```python
import functools

import jax
import jax.numpy as jnp
from jax import lax
from jax.experimental import pallas as pl
from jax.experimental.pallas import tpu as pltpu
from jax.sharding import Mesh, PartitionSpec as P

P_SIZE = 64
N = 128
CONV = 4
SPAN = 128
LANES = 128
RIM = 16
FAR_PARTS = 2
SEQ = ("chip", "core")
F32 = jnp.float32
BF16 = jnp.bfloat16
SMEM = pl.BlockSpec(memory_space=pltpu.SMEM)
VMEM = pl.BlockSpec(memory_space=pltpu.VMEM)


def call(kernel, name, out_shape, flops=0, moved=0, vmem=60, **settings):
    return pl.pallas_call(
        kernel,
        out_shape=out_shape,
        name=name,
        cost_estimate=pl.CostEstimate(flops=flops // 50, bytes_accessed=moved // 50, transcendentals=0),
        compiler_params=pltpu.CompilerParams(vmem_limit_bytes=vmem * 1024 * 1024),
        **settings,
    )


def swapped(part, axis, by=1):
    return lax.ppermute(part, axis, [(i, i ^ by) for i in range(lax.axis_size(axis))])


def cut_kernel(chips, at_ref, tokens_ref, far_ref, own_ref):
    depth = far_ref.shape[1] // chips
    rows = tokens_ref.shape[0]
    f_at, c_at = at_ref[0], at_ref[1]
    for out, f in ((far_ref, 1 - f_at), (own_ref, f_at)):
        for k, c in enumerate((c_at, 1 - c_at)):
            for i in range(chips):
                start = pl.multiple_of(((f * chips + at_ref[3 + i]) * 2 + c) * depth, depth)
                out[k * rows : (k + 1) * rows, i * depth : (i + 1) * depth] = tokens_ref[:, pl.ds(start, depth)]


def stack_rows(at_ref, pieces, rows_ref):
    count = pieces[0].shape[0]
    for k in range(0, len(pieces), 2):
        rows_ref[pl.ds(pl.multiple_of((k + at_ref[2]) * count, count), count), :] = pieces[k][...]
        rows_ref[pl.ds(pl.multiple_of((k + 1 - at_ref[2]) * count, count), count), :] = pieces[k + 1][...]


def sample_kernel(count, coef_ref, mean_ref, devs_ref, out_ref):
    factor = (2.0 * (count - 1)) ** (-0.5)
    accum = mean_ref[...].astype(F32)
    for member in range(count):
        accum = accum + factor * coef_ref[member] * devs_ref[member].astype(F32)
    out_ref[...] = accum.astype(BF16)


def sampled_cols(mean_part, dev_part, swag_coef, at, width):
    rows, count = mean_part.shape[0], dev_part.shape[0]
    tile = rows // 4
    return call(
        functools.partial(sample_kernel, count),
        "sample",
        jax.ShapeDtypeStruct((rows, width), BF16),
        moved=2 * (count + 2) * rows * width,
        vmem=24,
        grid=(4,),
        in_specs=[
            SMEM,
            pl.BlockSpec((tile, width), lambda i: (i, at)),
            pl.BlockSpec((count, tile, width), lambda i: (0, i, at)),
        ],
        out_specs=pl.BlockSpec((tile, width), lambda i: (i, 0)),
    )(swag_coef, mean_part, dev_part)


def sample_steps_kernel(count, coef_ref, mean_ref, devs_ref, dt_ref, out_ref):
    rows, width = mean_ref.shape
    heads = dt_ref.shape[0]
    sample_kernel(count, coef_ref, mean_ref, devs_ref, out_ref.at[:, :width])
    steps = dt_ref[:, pl.ds(pl.multiple_of(pl.program_id(0) * rows, rows), rows)]
    out_ref[:, width:] = jnp.zeros((rows, LANES), BF16)
    out_ref[:, width : width + heads] = jnp.transpose(steps.astype(F32)).astype(BF16)


def sampled_steps(mean_part, dev_part, dt_part, swag_coef, width):
    rows, count = mean_part.shape[0], dev_part.shape[0]
    tile = min(rows, LANES)
    return call(
        functools.partial(sample_steps_kernel, count),
        "sample_steps",
        jax.ShapeDtypeStruct((rows, width + LANES), BF16),
        moved=2 * (count + 2) * rows * width,
        vmem=24,
        grid=(rows // tile,),
        in_specs=[
            SMEM,
            pl.BlockSpec((tile, width), lambda i: (i, 0)),
            pl.BlockSpec((count, tile, width), lambda i: (0, i, 0)),
            pl.BlockSpec((dt_part.shape[1], rows), lambda i: (0, 0)),
        ],
        out_specs=pl.BlockSpec((tile, width + LANES), lambda i: (i, 0)),
    )(swag_coef, mean_part, dev_part, dt_part.T)


def sample_pair_kernel(count, coef_ref, mean_ref, devs_ref, out_ref):
    factor = (2.0 * (count - 1)) ** (-0.5)
    rows, _, width = mean_ref.shape
    flat = lambda a: a.reshape(2 * rows, width).astype(F32)
    accum = flat(mean_ref[...])
    for member in range(count):
        accum = accum + factor * coef_ref[member] * flat(devs_ref[member])
    accum = accum.astype(BF16)
    row = lax.broadcasted_iota(jnp.int32, (rows, 2 * rows), 0)
    col = lax.broadcasted_iota(jnp.int32, (rows, 2 * rows), 1)
    for k in range(2):
        picks = jnp.where(col == 2 * row + k, 1.0, 0.0).astype(BF16)
        part = jnp.dot(picks, accum, preferred_element_type=F32)
        out_ref[:, k * width : (k + 1) * width] = part.astype(BF16)


def sampled_pair(mean_part, dev_part, swag_coef):
    rows, _, width = mean_part.shape
    count = dev_part.shape[0]
    tile = min(rows, LANES)
    return call(
        functools.partial(sample_pair_kernel, count),
        "sample_pair",
        jax.ShapeDtypeStruct((rows, 2 * width), BF16),
        moved=4 * (count + 2) * rows * width,
        grid=(rows // tile,),
        in_specs=[
            SMEM,
            pl.BlockSpec((tile, 2, width), lambda i: (i, 0, 0)),
            pl.BlockSpec((count, tile, 2, width), lambda i: (0, i, 0, 0)),
        ],
        out_specs=pl.BlockSpec((tile, 2 * width), lambda i: (i, 0)),
    )(swag_coef, mean_part, dev_part)


def sent_straight(weight):
    return swapped(weight, "chip", 1), swapped(weight, "chip", 2)


def corner_parts(straight, each):
    rows = straight[0].shape[0] // (2 * each)
    cut = lambda a, i: a[i * rows : (i + 1) * rows]
    return [cut(straight[1], i) for i in range(each)] + [cut(straight[0], each + i) for i in range(each)]


def sent_on(parts):
    each = len(parts) // 2
    return [swapped(a, "chip", 1) for a in parts[:each]] + [swapped(a, "chip", 2) for a in parts[each:]]


def coded(part, heads):
    high = part.astype(BF16).astype(F32)
    return high + pltpu.roll(part - high, heads, 1)


def decoded(part, heads):
    return part + pltpu.roll(part, LANES - heads, 1)


def multiply_kernel(heads, with_steps, shares, pieces, plan, at_ref, *refs):
    shares, weights, outs, rows_ref = refs[:shares], refs[shares : shares + pieces], refs[shares + pieces : -1], refs[-1]

    @pl.when(pl.program_id(0) == 0)
    def _():
        if len(shares) == 1:
            rows_ref[...] = shares[0][...]
        else:
            stack_rows(at_ref, shares, rows_ref)

    joined = jnp.concatenate([weight[...] for weight in weights], axis=0)
    total = jnp.dot(rows_ref[...], joined, preferred_element_type=F32)
    for out, (first, sent) in zip(outs, plan):
        part = total[first : first + out.shape[0]]
        out[...] = part.astype(out.dtype)
        if with_steps and sent:
            @pl.when(pl.program_id(0) == pl.num_programs(0) - 1)
            def _():
                out[:, -LANES:] = coded(part[:, -LANES:], heads).astype(BF16)


def multiplied(at, rows, weights, heads, with_steps):
    width = weights[0].shape[1]
    tile = next(t for t in (512, 384, 128) if width % t == 0)
    depth = rows[0].shape[1]
    if len(rows) == 1:
        count = rows[0].shape[0]
        row_specs = [pl.BlockSpec(rows[0].shape, lambda i: (0, 0))]
    else:
        share = rows[0].shape[0] // 2
        count = len(rows) * share
        low = pl.BlockSpec((share, depth), lambda i: (0, 0))
        high = pl.BlockSpec((share, depth), lambda i: (1, 0))
        row_specs = [low, low, high, high] * 2
    half = count // 4
    part = half // FAR_PARTS
    plan = [(half + i * part, True) for i in range(FAR_PARTS)] + [(0, False), (3 * half, True), (2 * half, False)]
    shapes = [(part, BF16)] * FAR_PARTS + [(half, F32), (half, BF16), (half, F32)]
    return call(
        functools.partial(multiply_kernel, heads, with_steps, len(rows), len(weights), plan),
        "multiply",
        tuple(jax.ShapeDtypeStruct((r, width), dtype) for r, dtype in shapes),
        flops=2 * count * depth * width,
        moved=2 * count * depth + 2 * depth * width + 12 * half * width,
        vmem=34,
        grid=(width // tile,),
        in_specs=[SMEM] + row_specs + [pl.BlockSpec((w.shape[0], tile), lambda i: (0, i)) for w in weights],
        out_specs=[pl.BlockSpec((r, tile), lambda i: (0, i)) for r, _ in shapes],
        scratch_shapes=[pltpu.VMEM((count, depth), BF16)],
    )(at, *rows, *weights)


def relay_kernel(heads, with_steps, kept_ref, *refs):
    out_ref, count = refs[-1], refs[0].shape[0]
    for i, got_ref in enumerate(refs[:-1]):
        rows = slice(i * count, (i + 1) * count)
        kept, got = kept_ref[rows, :], got_ref[...].astype(F32)
        out_ref[rows, :] = (kept + got).astype(BF16)
        if with_steps:
            wide = kept[:, -LANES:] + decoded(got[:, -LANES:], heads)
            lane = lax.broadcasted_iota(jnp.int32, wide.shape, 1)
            out_ref[rows, -LANES:] = coded(jnp.where(lane < heads, wide, 0.0), heads).astype(BF16)


def relayed(kept, got, heads, with_steps):
    rows, width = kept.shape
    part = pl.BlockSpec((rows // len(got), width), lambda i: (0, 0))
    return call(
        functools.partial(relay_kernel, heads, with_steps),
        "relay",
        jax.ShapeDtypeStruct((rows, width), BF16),
        moved=8 * rows * width,
        vmem=12,
        grid=(1,),
        in_specs=[pl.BlockSpec((rows, width), lambda i: (0, 0))] + [part] * len(got),
        out_specs=pl.BlockSpec((rows, width), lambda i: (0, 0)),
    )(kept, *got)


def rim_kernel(kept, got_c, got_f, rim_ref):
    rim_ref[...] = (kept[...] + got_c[...].astype(F32) + got_f[...].astype(F32)).astype(BF16)


def rows_before(kept, got_c, got_f):
    rows, width = got_f.shape
    at = rows // RIM - 1
    rim = call(
        rim_kernel,
        "rim",
        jax.ShapeDtypeStruct((RIM, width), BF16),
        moved=10 * RIM * width,
        vmem=12,
        grid=(1,),
        in_specs=[pl.BlockSpec((RIM, width), lambda i: (at, 0))] * 3,
        out_specs=pl.BlockSpec((RIM, width), lambda i: (0, 0)),
    )(kept, got_c, got_f)
    return lax.ppermute(rim, SEQ, [(i, i + 1) for i in range(lax.axis_size(SEQ) - 1)])


def convolved(width, kept, got_c, got_f, rim, taps, padded):
    count = padded.shape[0] - 8
    proj = kept[:, :width] + got_c[:, :width].astype(F32) + got_f[:, :width].astype(F32)
    padded[8:, :] = proj.astype(BF16).astype(F32)
    padded[:8, :] = rim[:, :width].astype(F32)[RIM - 8 :]
    first = 8 - (CONV - 1)
    conv_sum = taps[0:1, :] * padded[first : first + count, :]
    for offset in range(1, CONV):
        conv_sum = conv_sum + taps[offset : offset + 1, :] * padded[first + offset : first + offset + count, :]
    return (conv_sum * jax.nn.sigmoid(conv_sum)).astype(BF16)


def state_proj_kernel(kept, got_c, got_f, rim, taps, out_ref, padded):
    out_ref[...] = convolved(out_ref.shape[1], kept, got_c, got_f, rim, taps, padded)


def steps_kernel(heads, kept, got_c, got_f, bias, rate, cum_ref, steps_ref, cum_t_ref, steps_t_ref, decay_ref):
    count = kept.shape[0]
    logits = kept[...] + decoded(got_c[...].astype(F32), heads) + decoded(got_f[...].astype(F32), heads)
    steps = jax.nn.softplus(logits[:, :heads] + bias[...])
    row = lax.broadcasted_iota(jnp.int32, (SPAN, SPAN), 0)
    col = lax.broadcasted_iota(jnp.int32, (SPAN, SPAN), 1)
    causal = jnp.where(row >= col, 1.0, 0.0)
    groups, per_group = cum_ref.shape[0], cum_ref.shape[2]
    through = jnp.zeros((1, heads), F32)
    for at in range(0, count, SPAN):
        span = slice(at, at + SPAN)
        steps_b = steps[span, :]
        cum = jnp.dot(
            causal, -steps_b * rate[...], precision=lax.Precision.HIGHEST, preferred_element_type=F32
        )
        through = through + cum[SPAN - 1 : SPAN, :]
        cum_t_ref[:, span] = jnp.transpose(cum)
        steps_t_ref[:, span] = jnp.transpose(steps_b)
        for g in range(groups):
            cum_ref[g, span, :] = cum[:, g * per_group : (g + 1) * per_group]
            steps_ref[g, span, :] = steps_b[:, g * per_group : (g + 1) * per_group]
    for g in range(groups):
        decay_ref[g] = jnp.exp(through)[:, g * per_group : (g + 1) * per_group]


def pairwise(columns, first):
    shape = (columns.shape[0], 2 * P_SIZE)
    lane = lax.broadcasted_iota(jnp.int32, shape, 1)
    return jnp.where(lane < P_SIZE, columns[:, first : first + 1], columns[:, first + 1 : first + 2])


def over_channels(columns):
    return jnp.concatenate([pairwise(columns, h) for h in range(0, columns.shape[1], 2)], axis=1)


def mix_kernel(
    kept, got_c, got_f, rim, taps, keys, reads, cum_g, steps_g, cum_t, steps_t, skip, decay, y_ref, early_ref, total_ref, decays_ref, sent_ref, padded
):
    width = y_ref.shape[1]
    values = convolved(width, kept, got_c, got_f, rim, taps, padded)
    cum, steps = cum_g[0], steps_g[0]
    heads = cum.shape[1]
    row = lax.broadcasted_iota(jnp.int32, (SPAN, SPAN), 0)
    col = lax.broadcasted_iota(jnp.int32, (SPAN, SPAN), 1)
    causal = row >= col
    lane = lax.broadcasted_iota(jnp.int32, (SPAN, 2 * P_SIZE), 1)
    gain = over_channels(skip[0])
    state = None
    for at in range(0, y_ref.shape[0], SPAN):
        span = slice(at, at + SPAN)
        keys_b, reads_b, values_b = keys[span, :], reads[span, :], values[span, :]
        cum_b, steps_b = cum[span, :], steps[span, :]
        last = cum_b[SPAN - 1 : SPAN, :]
        scores = lax.dot_general(reads_b, keys_b, (((1,), (1,)), ((), ())), preferred_element_type=F32)
        scores = jnp.where(causal, scores, 0.0)
        reach = jnp.exp(last - cum_b) * steps_b
        scaled = []
        for head in range(0, heads, 2):
            chans = slice(head * P_SIZE, (head + 2) * P_SIZE)
            two = []
            for h in (head, head + 1):
                gap = cum_b[:, h : h + 1] - cum_t[h : h + 1, span]
                two.append((scores * jnp.exp(jnp.minimum(gap, 0.0)) * steps_t[h : h + 1, span]).astype(BF16))
            values_h = values_b[:, chans]
            both = jnp.dot(jnp.concatenate(two, axis=0), values_h, preferred_element_type=F32)
            inner = jnp.where(lane < P_SIZE, both[:SPAN], both[SPAN:])
            wide = values_h.astype(F32)
            y_ref[span, chans] = inner + gain[:, chans] * wide
            scaled.append((wide * pairwise(reach, head)).astype(BF16))
        fresh = lax.dot_general(
            keys_b, jnp.concatenate(scaled, axis=1), (((0,), (0,)), ((), ())), preferred_element_type=F32
        )
        state = fresh if state is None else over_channels(jnp.exp(last)) * state + fresh
        if at + SPAN < y_ref.shape[0]:
            early_ref[at // SPAN] = fresh
    total_ref[...] = state
    wide = over_channels(decay[0])
    decays_ref[0:1, :] = wide
    decays_ref[1:2, :] = jnp.ones_like(wide)
    pack_state([sent_ref], state, wide)


def pack_state(sent_refs, state, decay):
    high = decay.astype(BF16).astype(F32)
    row = lax.broadcasted_iota(jnp.int32, (RIM, decay.shape[1]), 0)
    tail = jnp.where(row == 0, high, jnp.where(row == 1, decay - high, 0.0)).astype(BF16)
    state = state.astype(BF16)
    at = 0
    for sent_ref in sent_refs[:-1]:
        sent_ref[...] = state[at : at + sent_ref.shape[0]]
        at += sent_ref.shape[0]
    sent_refs[-1][: N - at, :] = state[at:]
    sent_refs[-1][N - at :, :] = tail


def unpack_state(got_refs):
    rows = jnp.concatenate([ref[...] for ref in got_refs], axis=0).astype(F32)
    return rows[:N], rows[N : N + 1, :] + rows[N + 1 : N + 2, :]


def combine_kernel(level, got, has_before, place_ref, total, decays, *refs):
    other, refs = refs[:got], refs[got:]
    if has_before:
        before, refs = refs[0][...], refs[1:]
    total_ref, decays_ref, before_ref, *sent_refs = refs
    come, decay = unpack_state(other)
    whole, part = decays[0:1, :], decays[1:2, :]
    upper = (place_ref[0] >> level) & 1 == 1
    fresh = jnp.where(upper, part, 0.0) * come
    before_ref[...] = before + fresh if has_before else fresh
    joint = jnp.where(upper, 1.0, decay) * total[...] + jnp.where(upper, whole, 1.0) * come
    total_ref[...] = joint
    decays_ref[0:1, :] = whole * decay
    decays_ref[1:2, :] = jnp.where(upper, decay * part, part)
    pack_state(sent_refs, joint, whole * decay)


def pair_kernel(place_ref, total, decays, other, total_ref, decays_ref, sent_ref, before_ref, part_ref):
    come, decay = unpack_state([other])
    whole = decays[0:1, :]
    upper = place_ref[0] & 1 == 1
    before_ref[...] = jnp.where(upper, come, 0.0)
    part_ref[0:1, :] = jnp.where(upper, decay, 1.0)
    joint = jnp.where(upper, 1.0, decay) * total[...] + jnp.where(upper, whole, 1.0) * come
    half = joint.shape[1] // 2
    picked = lambda a: jnp.where(upper, a[:, half:], a[:, :half])
    joint, whole = picked(joint), picked(whole * decay)
    total_ref[...] = joint
    decays_ref[0:1, :] = whole
    decays_ref[1:2, :] = jnp.ones_like(whole)
    pack_state([sent_ref], joint, whole)


def settle_kernel(level, has_before, place_ref, decays, other, *refs):
    upper = (place_ref[0] >> level) & 1 == 1
    state = jnp.where(upper, decays[1:2, :], 0.0) * unpack_state([other])[0]
    refs[-1][...] = (refs[0][...] + state if has_before else state).astype(BF16)


def read_kernel(place_ref, y, reads, cum_g, early, part, before, mine, theirs, *refs):
    out_ref = refs[-1]
    upper = place_ref[0] & 1 == 1
    mine, theirs = mine[...].astype(F32), theirs[...].astype(F32)
    chip = jnp.concatenate([jnp.where(upper, theirs, mine), jnp.where(upper, mine, theirs)], axis=1)
    whole = before[...] + part[0:1, :] * chip
    width = whole.shape[1] // cum_g.shape[0]
    for g in range(cum_g.shape[0]):
        chans, state = slice(g * width, (g + 1) * width), whole[:, g * width : (g + 1) * width]
        for at in range(0, out_ref.shape[0], SPAN):
            span = slice(at, at + SPAN)
            cum_b = cum_g[g, span, :]
            seen = jnp.dot(reads[span, g * N : (g + 1) * N], state.astype(BF16), preferred_element_type=F32)
            out_ref[span, chans] = (y[span, chans] + over_channels(jnp.exp(cum_b)) * seen).astype(BF16)
            if at + SPAN < out_ref.shape[0]:
                state = over_channels(jnp.exp(cum_b[SPAN - 1 : SPAN, :])) * state + early[at // SPAN, :, chans]


def combined(level, place, total, decays, other, before, groups, cut):
    width = total.shape[1] // groups
    block = lambda rows: pl.BlockSpec((rows, width), lambda i: (0, i))
    shape = lambda rows, dtype: jax.ShapeDtypeStruct((rows, total.shape[1]), dtype)
    total, decays, before, *sent = call(
        functools.partial(combine_kernel, level, len(other), bool(before)),
        "combine",
        (shape(N, F32), shape(8, F32), shape(N, F32)) + tuple(shape(rows, BF16) for rows in cut),
        flops=6 * total.size,
        moved=20 * total.size,
        vmem=12,
        grid=(groups,),
        in_specs=[SMEM, block(N), block(8)] + [block(a.shape[0]) for a in other] + [block(N)] * len(before),
        out_specs=[block(N), block(8), block(N)] + [block(rows) for rows in cut],
    )(place, total, decays, *other, *before)
    return total, decays, before, sent


def body(
    tokens,
    proj_mean,
    proj_devs,
    bc_mean,
    bc_devs,
    swag_coef,
    dt_weight,
    dt_bias,
    decay_rate,
    skip_gain,
    conv_proj,
    conv_bc,
):
    heads_here = decay_rate.shape[0]
    groups_here = bc_mean.shape[2] // N
    per_group = heads_here // groups_here
    width_bc = 2 * bc_mean.shape[2]
    rows_k = proj_mean.shape[0]
    chips = lax.axis_size("chip")
    count = lax.axis_size(SEQ)

    def after(arrays, earlier):
        return lax.optimization_barrier((arrays, earlier))[0]

    width = per_group * P_SIZE
    early_groups = max(1, groups_here // 2)
    fill = -heads_here % LANES
    late = list(range(early_groups, groups_here))

    plane = chips == 4
    two_shares = lax.axis_size("tp") == 2
    place = lax.axis_index("chip") if plane else 0
    at = jnp.stack([lax.axis_index(a) for a in ("fsdp", "core", "tp")] + [place ^ i for i in range(chips)]).astype(jnp.int32)
    share, depth = tokens.shape[0], chips * rows_k
    weight_bc = sampled_pair(bc_mean, bc_devs, swag_coef)
    tokens = after(tokens, weight_bc)
    cut = jax.ShapeDtypeStruct((2 * share, depth), BF16)
    far, own = call(
        functools.partial(cut_kernel, chips),
        "cut_tokens",
        (cut,) * 2,
        moved=4 * tokens.size,
        vmem=24,
        in_specs=[SMEM, VMEM],
        out_specs=[VMEM] * 2,
    )(at, tokens)
    proj_mean = after(proj_mean, own)
    far = swapped(far, "fsdp")

    weight_early = sampled_steps(proj_mean, proj_devs, dt_weight, swag_coef, early_groups * width)
    weight_late = None
    if late:
        weight_late = sampled_cols(proj_mean, proj_devs, swag_coef, early_groups // len(late), len(late) * width)
    tok_count = share * lax.axis_size("tp")
    blocks = tok_count // SPAN

    def partial_sums(rows, pieces, with_steps, before_send=(), before_relay=()):
        *far_sent, far_kept, sent, kept = multiplied(at, rows, pieces, heads_here, with_steps)
        far_got = [swapped(a, "core") for a in after(far_sent, before_send)]
        back = relayed(far_kept, after(far_got, before_relay), heads_here, with_steps)
        return (kept, swapped(after(sent, back), "core")), back

    specs_of = lambda width: [pl.BlockSpec((tok_count, width), lambda i: (0, i))] * 3 + [
        pl.BlockSpec((RIM, width), lambda i: (0, i)),
    ]
    whole_of = lambda *shape: pl.BlockSpec(shape, lambda i: (0,) * len(shape))
    by_group = (groups_here, tok_count, per_group)
    by_head = (heads_here, tok_count)
    by_decay = (groups_here, 1, per_group)
    state_proj = lambda part: call(
        state_proj_kernel,
        "state_proj",
        jax.ShapeDtypeStruct((tok_count, width_bc), BF16),
        moved=10 * tok_count * width_bc,
        vmem=30,
        grid=(1,),
        in_specs=specs_of(width_bc) + [whole_of(CONV, width_bc)],
        out_specs=whole_of(tok_count, width_bc),
        scratch_shapes=[pltpu.VMEM((tok_count + 8, width_bc), F32)],
    )(*part, rows_before(*part), conv_bc.reshape(CONV, width_bc))
    steps_at = early_groups * width // LANES
    steps_of = lambda part: call(
        functools.partial(steps_kernel, heads_here),
        "steps",
        tuple(jax.ShapeDtypeStruct(a, F32) for a in (by_group, by_group, by_head, by_head, by_decay)),
        moved=10 * tok_count * LANES,
        vmem=12,
        grid=(1,),
        in_specs=[pl.BlockSpec((tok_count, LANES), lambda i: (0, steps_at))] * 3 + [whole_of(1, heads_here)] * 2,
        out_specs=[whole_of(*a) for a in (by_group, by_group, by_head, by_head, by_decay)],
    )(*part, dt_bias[None], decay_rate[None])

    if plane and two_shares:
        bc = [weight_bc, *sent_straight(weight_bc)]
        bc += sent_on(corner_parts(bc[1:], 1))
        own_t = swapped(own, "tp")
        weight_early = after(weight_early, bc[3:])
        early = [weight_early, *sent_straight(weight_early)]
        far = after(far, (own_t, bc[3:], weight_late))
        far_t = swapped(far, "tp")
        own, own_t = after((own, own_t), far)
        own_c, own_tc = swapped(own, "core"), swapped(own_t, "core")
        halves = corner_parts(early[1:], 1)
        far_c, far_tc = swapped(far, "core"), swapped(after(far_t, halves), "core")
        rows = (far, far_t, far_c, far_tc, own, own_t, own_c, own_tc)
        part_bc, back_bc = partial_sums(rows, bc, False)
        early += sent_on(halves)
        got_bc = swapped(back_bc, "fsdp")
        weight_late = after(weight_late, (back_bc, early[3:]))
        part, back = partial_sums(rows, early, True, before_relay=got_bc)
        got = swapped(after(back, got_bc), "fsdp")
        straight = sent_straight(weight_late)
        corners = sent_on(corner_parts(straight, 1))
        seen = state_proj(after(part_bc + (got_bc,), back))
        part_late, back_late = partial_sums(rows, [weight_late, *straight, *corners], False, before_send=seen)
        got_late = swapped(after(back_late, got), "fsdp")
        got = after(got, back_late)
    else:
        whole = lambda a, axis: lax.all_gather(a, axis, axis=0, tiled=True)
        ranges = [r for a in (far, own) for r in (a[:share], swapped(a[share:], "core"))]
        rows = (jnp.concatenate([whole(r, "tp") for r in ranges], axis=0),)
        part, back = partial_sums(rows, [whole(weight_early, "chip")], True)
        part_bc, back_bc = partial_sums(rows, [whole(weight_bc, "chip")], False)
        got, got_bc = swapped(back, "fsdp"), swapped(back_bc, "fsdp")
        if late:
            part_late, back_late = partial_sums(rows, [whole(weight_late, "chip")], False)
            got_late = swapped(back_late, "fsdp")
        seen = state_proj(part_bc + (got_bc,))
    conv_out = seen
    parts = [part + (got,)]
    cum_g, steps_g, cum_t, steps_t, decay = steps_of(parts[0])
    if late:
        parts.append(part_late + (got_late,))

    skip = skip_gain.reshape(by_decay)
    levels = count.bit_length() - 1
    seq_place = (2 * lax.axis_index("chip") + lax.axis_index("core")).astype(jnp.int32).reshape(1)

    result = None
    for first, groups, part in zip((0, early_groups), (early_groups, len(late)), parts):
        part = part + (rows_before(*part),)
        if first:
            part = after(part, sent)
        grid = (groups,)
        cols = lambda rows: pl.BlockSpec((rows, width), lambda i: (0, i))
        cols_all = lambda rows: pl.BlockSpec((rows, width), lambda i: (0, first + i))
        heads_g = pl.BlockSpec((1, tok_count, per_group), lambda i: (first + i, 0, 0))
        heads_t = pl.BlockSpec((per_group, tok_count), lambda i: (first + i, 0))
        heads_1 = pl.BlockSpec((1, 1, per_group), lambda i: (first + i, 0, 0))
        keys = pl.BlockSpec((tok_count, N), lambda i: (0, first + i))
        reads = pl.BlockSpec((tok_count, N), lambda i: (0, groups_here + first + i))
        early_spec = pl.BlockSpec((blocks - 1, N, width), lambda i: (0, 0, i))
        y, early, total, decays, sent = call(
            mix_kernel,
            "mix",
            (
                jax.ShapeDtypeStruct((tok_count, groups * width), F32),
                jax.ShapeDtypeStruct((blocks - 1, N, groups * width), F32),
                jax.ShapeDtypeStruct((N, groups * width), F32),
                jax.ShapeDtypeStruct((8, groups * width), F32),
                jax.ShapeDtypeStruct((N + RIM, groups * width), BF16),
            ),
            flops=8 * tok_count * N * width * groups,
            moved=14 * tok_count * width * groups,
            vmem=24,
            grid=grid,
            in_specs=specs_of(width) + [cols_all(CONV), keys, reads, heads_g, heads_g, heads_t, heads_t, heads_1, heads_1],
            out_specs=[cols(tok_count), early_spec, cols(N), cols(8), cols(N + RIM)],
            scratch_shapes=[pltpu.VMEM((tok_count + 8, width), F32)],
        )(*part, conv_proj, conv_out, conv_out, cum_g, steps_g, cum_t, steps_t, skip, decay)
        wide = groups * width
        shape = lambda rows, cols, dtype=F32: jax.ShapeDtypeStruct((rows, cols), dtype)
        total, decays, sent, core_before, core_part = call(
            pair_kernel,
            "pair",
            (shape(N, wide // 2), shape(8, wide // 2), shape(N + RIM, wide // 2, BF16), shape(N, wide), shape(8, wide)),
            moved=20 * N * wide,
            vmem=12,
            in_specs=[SMEM] + [VMEM] * 3,
            out_specs=[VMEM] * 5,
        )(seq_place, total, decays, swapped(sent, SEQ, 1))
        before, sent = (), [sent]
        for level in range(1, levels - 1):
            other = [swapped(a, SEQ, 1 << level) for a in sent]
            total, decays, fresh, sent = combined(level, seq_place, total, decays, other, before, 1, (N + RIM,))
            before = (fresh,)
        mine = call(
            functools.partial(settle_kernel, levels - 1, bool(before)),
            "settle",
            shape(N, wide // 2, BF16),
            moved=6 * N * wide,
            vmem=12,
            in_specs=[SMEM] + [VMEM] * (2 + len(before)),
            out_specs=VMEM,
        )(seq_place, decays, swapped(sent[0], SEQ, 1 << (levels - 1)), *before)
        operands = [seq_place, y, conv_out, cum_g, early, core_part, core_before, mine, swapped(mine, "core")]
        at_block = first // groups
        specs = [
            SMEM,
            whole_of(tok_count, wide),
            pl.BlockSpec((tok_count, groups * N), lambda i: (0, groups_here // groups + at_block)),
            pl.BlockSpec((groups, tok_count, per_group), lambda i: (at_block, 0, 0)),
            whole_of(blocks - 1, N, wide),
            whole_of(8, wide),
            whole_of(N, wide),
            whole_of(N, wide // 2),
            whole_of(N, wide // 2),
        ]
        alias = {}
        if result is not None:
            operands.append(result)
            specs.append(pl.BlockSpec(memory_space=pl.ANY))
            alias = {len(operands) - 1: 0}
        result = call(
            read_kernel,
            "read_out",
            jax.ShapeDtypeStruct((tok_count, heads_here * P_SIZE), BF16),
            flops=2 * tok_count * N * width * groups,
            moved=10 * tok_count * width * groups,
            vmem=12,
            grid=(1,),
            in_specs=specs,
            out_specs=pl.BlockSpec((tok_count, wide), lambda i: (0, at_block)),
            input_output_aliases=alias,
        )(*operands)
    return result


def solution(mesh):
    shape = mesh.shape
    split = Mesh(
        mesh.devices.reshape(shape["fsdp"], shape["seq"] // 2, 2, shape["tp"]),
        ("fsdp", "chip", "core", "tp"),
    )
    rows = ("fsdp", "chip", "core")
    return jax.shard_map(
        body,
        mesh=split,
        in_specs=(
            P(rows + ("tp",), None),
            P(rows, "tp"),
            P(None, rows, "tp"),
            P(rows, None, "tp"),
            P(None, rows, None, "tp"),
            P(),
            P(rows, "tp"),
            P("tp"),
            P("tp"),
            P("tp"),
            P(None, "tp"),
            P(None, None, "tp"),
        ),
        out_specs=P(rows, "tp"),
        check_vma=False,
    )
```
